32 devices in a mesh: dp: 8 (over z, core), tensor: 4 (over y, x).
Axes of the slice: x: 2, y: 2, z: 4, core: 2. Of those that a mesh axis runs over, the one named last changes fastest.
Arguments:
- residual: bfloat16 [8192, 2048], P(('dp', 'tensor')), may hold values from -6 to 6
- segment_ids: int32 [8, 1024], P('dp'), may hold values from 0 to 16, as said below
- norm_gain: float32 [2048], replicated, may hold values from 0.1 to 1.9
- inner_weight: bfloat16 [2048, 2, 4096], P('dp', None, 'tensor'), may hold values from -0.125 to 0.125
- state_weight: bfloat16 [2048, 256], replicated, may hold values from -0.125 to 0.125
- step_weight: bfloat16 [2048, 64], P('dp', 'tensor'), may hold values from -0.125 to 0.125
- conv_weight: float32 [4, 4352], replicated, may hold values from -3 to 3
- conv_bias: float32 [4352], replicated, may hold values from -3 to 3
- step_bias: float32 [64], replicated, may hold values from -6 to -2.5
- decay_log: float32 [64], replicated, may hold values from 0 to 2.77
- skip_gain: float32 [64], replicated, may hold values from 0.5 to 2
- gated_gain: float32 [4096], replicated, may hold values from 0.1 to 1.9
- out_weight: bfloat16 [4096, 2048], P('tensor', 'dp'), may hold values from -0.09375 to 0.09375
- cotangent: bfloat16 [8192, 2048], P(('dp', 'tensor')), may hold values from -6 to 6
Outputs:
- block_out: float32 [8192, 2048], P(('dp', 'tensor'))
- residual_grad: float32 [8192, 2048], P(('dp', 'tensor'))
- norm_gain_grad: float32 [2048], replicated
- inner_weight_grad: float32 [2048, 2, 4096], P('dp', None, 'tensor')
- state_weight_grad: float32 [2048, 256], replicated
- step_weight_grad: float32 [2048, 64], P('dp', 'tensor')
- conv_weight_grad: float32 [4, 4352], replicated
- conv_bias_grad: float32 [4352], replicated
- step_bias_grad: float32 [64], replicated
- decay_log_grad: float32 [64], replicated
- skip_gain_grad: float32 [64], replicated
- gated_gain_grad: float32 [4096], replicated
- out_weight_grad: float32 [4096, 2048], P('tensor', 'dp')
The draws below stay inside these ranges and needn't reach their ends.
Inputs may be any that keep to these rules, and one draw needn't show every extreme that they name: `segment_ids`: numbers start at 0 in each row and rise by one at each new document; each document has 60 to 800 tokens; some row has a document of exactly 800 tokens, and some row reaches the largest number.
All inputs are finite; a program needn't handle non-finite values.
Results may differ from the reference program's by a relative error of at most 0.014.
Values may be sent and summed in bfloat16 or wider, within the bound.
A program may use at most 192 MiB of HBM per device.

```python
from functools import partial
import jax
import jax.numpy as jnp
from jax import lax

D = 2048
HEADS = 64
STATE = 128
CONV = 4
BLOCK_LEN = 256
SEQ_LEN = 1024
MIN_DOC = 60
MAX_DOC = 800
DOCS = 17
INNER = 4096
NSEQ = 8
TOKENS = 8192


def one_row(row_key, first_full, dense_row):
    drawn = jax.random.randint(row_key, (DOCS,), MIN_DOC, MAX_DOC + 1).astype(jnp.int32)
    drawn = jnp.where(dense_row, jnp.full((DOCS,), MIN_DOC, jnp.int32), drawn)
    drawn = drawn.at[0].set(jnp.where(first_full, jnp.int32(MAX_DOC), drawn[0]))

    def take_doc(remaining, wanted):
        length = jnp.minimum(wanted, remaining)
        short = remaining - length < MIN_DOC
        length = jnp.where(short, jnp.where(remaining <= MAX_DOC, remaining, remaining - MIN_DOC), length)
        return (remaining - length, length)
    _, lengths = lax.scan(take_doc, jnp.int32(SEQ_LEN), drawn)
    starts = jnp.cumsum(lengths) - lengths
    live = lengths > 0
    positions = jnp.arange(SEQ_LEN, dtype=jnp.int32)
    begun = live[:, None] & (starts[:, None] <= positions[None, :])
    return (jnp.sum(begun.astype(jnp.int32), axis=0) - 1).astype(jnp.int32)


def draw_segment_ids(key, part):
    key = jax.random.fold_in(key, 11)
    row_keys = jax.random.split(key, NSEQ)
    full_row = jax.random.randint(jax.random.fold_in(key, 5), (), 0, NSEQ)
    dense_pick = (full_row + 1 + jax.random.randint(jax.random.fold_in(key, 7), (), 0, NSEQ - 1)) % NSEQ
    rows = jnp.arange(NSEQ)
    flags = rows == full_row
    dense_flags = rows == dense_pick
    return jax.vmap(one_row)(row_keys, flags, dense_flags)


def block_levels(stream_key, shape, cuts, low, largest):
    def one(position, blocks):
        heights = jax.random.uniform(jax.random.fold_in(jax.random.fold_in(stream_key, 6), position), (blocks,), jnp.float32, low / len(cuts), largest / len(cuts))
        return jnp.repeat(jnp.exp(heights), shape[position] // blocks).reshape((-1,) + (1,) * (len(shape) - position - 1))

    loudness = one(*cuts[0])
    for cut in cuts[1:]:
        loudness = loudness * one(*cut)
    return loudness


def normal_values(own_key, shape, width, most, cuts=(), kind=jnp.bfloat16):
    entries = width * jax.random.normal(own_key, shape, jnp.float32)
    if cuts:
        entries = entries * block_levels(own_key, shape, cuts, -0.22, 0.18)
    return jnp.clip(entries, -most, most).astype(kind)


def setup_inputs(seed: int = 0) -> dict:
    seeds = jax.random.split(jax.random.key(seed), 15)
    residual = normal_values(seeds[0], (TOKENS, D), 1.0, 6.0, ((0, 32),))
    segment_ids = draw_segment_ids(jax.random.fold_in(seeds[14], 71), 0)
    norm_gain = jnp.clip(1.0 + 0.18 * jax.random.normal(seeds[2], (D,), jnp.float32), 0.1, 1.9)
    inner_weight = normal_values(seeds[3], (D, 2, INNER), D ** -0.5, 0.125, ((0, 8), (2, 4)))
    state_weight = normal_values(seeds[4], (D, 2 * STATE), D ** -0.5, 0.125)
    step_weight = normal_values(seeds[5], (D, HEADS), D ** -0.5, 0.125, ((0, 8), (1, 4)))
    conv_weight = normal_values(seeds[6], (CONV, INNER + 2 * STATE), CONV ** -0.5, 3.0, (), jnp.float32)
    conv_bias = normal_values(seeds[7], (INNER + 2 * STATE,), 0.5, 3.0, (), jnp.float32)
    step_bias = jnp.clip(jax.random.uniform(seeds[8], (HEADS,), jnp.float32, -6.0, -2.5), -6.0, -2.5)
    decay_log = jnp.clip(jax.random.uniform(seeds[9], (HEADS,), jnp.float32, 0.0, 2.77), 0.0, 2.77)
    skip_gain = jnp.clip(jax.random.uniform(seeds[10], (HEADS,), jnp.float32, 0.5, 2.0), 0.5, 2.0)
    gated_gain = jnp.clip(1.0 + 0.18 * jax.random.normal(seeds[11], (INNER,), jnp.float32), 0.1, 1.9)
    out_weight = normal_values(seeds[12], (INNER, D), INNER ** -0.5, 0.09375, ((0, 4), (1, 8)))
    cotangent = normal_values(seeds[13], (TOKENS, D), 1.0, 6.0, ((0, 32),))
    return {"residual": residual, "segment_ids": segment_ids, "norm_gain": norm_gain, "inner_weight": inner_weight, "state_weight": state_weight, "step_weight": step_weight, "conv_weight": conv_weight, "conv_bias": conv_bias, "step_bias": step_bias, "decay_log": decay_log, "skip_gain": skip_gain, "gated_gain": gated_gain, "out_weight": out_weight, "cotangent": cotangent}


epsilon = 1e-05
highest = lax.Precision.HIGHEST

@jax.custom_vjp
def low(v):
    return lax.optimization_barrier(v.astype(jnp.bfloat16)).astype(jnp.float32)

@jax.custom_vjp
def low_back(v):
    return v

def low_keep(v):
    return (low(v), None)

def low_pass(kept, grad):
    return (grad,)

def back_keep(v):
    return (v, None)

def back_low(kept, grad):
    return (low(grad),)
low.defvjp(low_keep, low_pass)
low_back.defvjp(back_keep, back_low)

def conv_sequence(channels, segments, kernel, bias_row):
    length = channels.shape[0]
    tap_count = kernel.shape[0]
    result = bias_row + kernel[tap_count - 1] * channels
    for offset in range(1, tap_count):
        shifted = jnp.pad(channels, ((offset, 0), (0, 0)))[:length]
        earlier = jnp.pad(segments, (offset, 0), constant_values=-1)[:length]
        result = result + kernel[tap_count - 1 - offset] * jnp.where((earlier == segments)[:, None], shifted, 0.0)
    return result

def scan_sequence(values, step_sizes, decay_rates, input_keys, input_queries, segments, block_size):
    length, head_count, head_width = values.shape
    states = input_keys.shape[1]
    block_count = length // block_size
    log_decay = (step_sizes * decay_rates).reshape(block_count, block_size, head_count)
    cumulative = jnp.cumsum(log_decay, axis=1)
    seg_blocks = segments.reshape(block_count, block_size)
    value_blocks = values.reshape(block_count, block_size, head_count, head_width)
    step_blocks = step_sizes.reshape(block_count, block_size, head_count)
    key_blocks = input_keys.reshape(block_count, block_size, states)
    query_blocks = input_queries.reshape(block_count, block_size, states)
    positions = jnp.arange(block_size)
    causal = positions[:, None] >= positions[None, :]
    allowed = (seg_blocks[:, :, None] == seg_blocks[:, None, :]) & causal[None]
    allowed_heads = allowed[..., None]
    differ = cumulative[:, :, None, :] - cumulative[:, None, :, :]
    decay_matrix = jnp.where(allowed_heads, jnp.exp(jnp.where(allowed_heads, differ, 0.0)), 0.0)
    intersection = jnp.einsum('ctn,csn->cts', query_blocks, key_blocks, precision=highest)
    mixing = decay_matrix * intersection[..., None] * step_blocks[:, None, :, :]
    inside = jnp.einsum('ctsh,cshp->cthp', mixing, value_blocks, precision=highest)
    last_seg = seg_blocks[:, block_size - 1]
    to_end = jnp.exp(cumulative[:, block_size - 1:, :] - cumulative)
    keep_end = (seg_blocks == last_seg[:, None])[..., None]
    weights_end = jnp.where(keep_end, to_end * step_blocks, 0.0)
    local_states = jnp.einsum('csh,cshp,csn->chpn', weights_end, value_blocks, key_blocks, precision=highest)
    whole_decay = jnp.exp(cumulative[:, block_size - 1, :])
    previous_seg = jnp.concatenate([jnp.full((1,), -1, jnp.int32), last_seg[:-1].astype(jnp.int32)])
    linked = last_seg.astype(jnp.int32) == previous_seg

    def carry_step(carried, pieces):
        piece_local, piece_decay, piece_link = pieces
        factor = jnp.where(piece_link, piece_decay, 0.0)
        return (piece_local + factor[:, None, None] * carried, carried)
    start_state = jnp.zeros((head_count, head_width, states), jnp.float32)
    _, entering = lax.scan(carry_step, start_state, (local_states, whole_decay, linked))
    inflow = (seg_blocks.astype(jnp.int32) == previous_seg[:, None])[..., None]
    weights_in = jnp.where(inflow, jnp.exp(cumulative), 0.0)
    outside = jnp.einsum('ctn,chpn->cthp', query_blocks, entering, precision=highest) * weights_in[..., None]
    return (inside + outside).reshape(length, head_count, head_width)

def state_mixer(gate_z, inner_x, state_bc, step_raw, kernel, kernel_bias, step_bias, decay_log, skip_gain, segments):
    seq_count, length = segments.shape
    head_count = step_raw.shape[1]
    inner_width = inner_x.shape[1]
    states = state_bc.shape[1] // 2
    head_width = inner_width // head_count
    channels = jnp.concatenate([inner_x, state_bc], axis=1).reshape(seq_count, length, inner_width + 2 * states)
    convolved = jax.vmap(conv_sequence, in_axes=(0, 0, None, None))(channels, segments, kernel, kernel_bias)
    active = jax.nn.silu(convolved)
    values = active[..., :inner_width].reshape(seq_count, length, head_count, head_width)
    input_keys = active[..., inner_width:inner_width + states]
    input_queries = active[..., inner_width + states:]
    step_sizes = jax.nn.softplus(step_raw.reshape(seq_count, length, head_count) + step_bias)
    decay_rates = -jnp.exp(decay_log)
    scanner = jax.vmap(partial(scan_sequence, block_size=BLOCK_LEN), in_axes=(0, 0, None, 0, 0, 0))
    scanned = scanner(values, step_sizes, decay_rates, input_keys, input_queries, segments)
    mixed_out = scanned + skip_gain[:, None] * values
    return mixed_out.reshape(seq_count * length, inner_width) * jax.nn.silu(gate_z)

def forward(residual, norm_gain, inner_weight, state_weight, step_weight, conv_weight, conv_bias, step_bias, decay_log, skip_gain, gated_gain, out_weight, segment_ids):
    model_width = residual.shape[1]
    inner_width = gated_gain.shape[0]
    blocks = residual.reshape(NSEQ, SEQ_LEN, model_width)
    inner_mat = inner_weight.reshape(model_width, 2 * inner_width)

    def one_sequence(pieces):
        stream, segments = pieces
        scaling = lax.rsqrt(lax.optimization_barrier(jnp.mean(stream * stream, axis=1, keepdims=True)) + epsilon)
        normed = low(stream * scaling * norm_gain)
        projected_zx = low_back(jnp.dot(normed, inner_mat, precision=highest))
        state_bc = low_back(jnp.dot(normed, state_weight, precision=highest))
        step_raw = low_back(jnp.dot(normed, step_weight, precision=highest))
        gated = state_mixer(projected_zx[:, :inner_width], projected_zx[:, inner_width:], state_bc, step_raw, conv_weight, conv_bias, step_bias, decay_log, skip_gain, segments[None])
        scale_g = lax.rsqrt(lax.optimization_barrier(jnp.mean(gated * gated, axis=1, keepdims=True)) + epsilon)
        normed_g = low(gated * scale_g * gated_gain)
        return stream + jnp.dot(normed_g, out_weight, precision=highest)
    result = lax.map(jax.checkpoint(one_sequence), (blocks, segment_ids))
    return result.reshape(NSEQ * SEQ_LEN, model_width)

def reference(residual, segment_ids, norm_gain, inner_weight, state_weight, step_weight, conv_weight, conv_bias, step_bias, decay_log, skip_gain, gated_gain, out_weight, cotangent):
    floats = [argument.astype(jnp.float32) for argument in (residual, norm_gain, inner_weight, state_weight, step_weight, conv_weight, conv_bias, step_bias, decay_log, skip_gain, gated_gain, out_weight)]

    def wrapped(*params):
        return forward(*params, segment_ids)
    result, pullback = jax.vjp(wrapped, *floats)
    gradients = pullback(cotangent.astype(jnp.float32))
    return (result, gradients[0], gradients[1], gradients[2], gradients[3], gradients[4], gradients[5], gradients[6], gradients[7], gradients[8], gradients[9], gradients[10], gradients[11])
```

```python
import functools
import jax
import jax.numpy as jnp
from jax import lax
from jax.experimental import pallas as pl
from jax.experimental.pallas import tpu as pltpu
from jax.sharding import PartitionSpec as P

LANES = 128
BLOCK = 128
WIDTH = 64
VMEM_BYTES = 56 * 1024 * 1024
f32, bf16 = jnp.float32, jnp.bfloat16
ROWS0 = (((0,), (0,)), ((), ()))
COLS1 = (((1,), (1,)), ((), ()))


def mm(a, b):
    return jnp.dot(a, b, preferred_element_type=f32)


def mm_tn(a, b):
    return lax.dot_general(a, b, ROWS0, preferred_element_type=f32)


def mm_nt(a, b):
    return lax.dot_general(a, b, COLS1, preferred_element_type=f32)


def sigmoid(v):
    return 0.5 + 0.5 * jnp.tanh(0.5 * v)


def two_parts(v, low_lanes):
    high = v.astype(bf16)
    return jnp.where(low_lanes, (v - high.astype(f32)).astype(bf16), high)


def head_sums(v, spread):
    high = v.astype(bf16)
    low = (v - high.astype(f32)).astype(bf16)
    return mm_nt(high, spread) + mm_nt(low, spread)


def shifted_masks(seg_ext, seg):
    n = seg.shape[0]
    return [None] + [seg_ext[8 - k : 8 - k + n] == seg for k in (1, 2, 3)]


def convolve(tail, part, masks, taps):
    n = part.shape[0]
    ext = jnp.concatenate([tail, part], axis=0)
    shifts = [part] + [
        jnp.where(masks[k], ext[8 - k : 8 - k + n], 0.0) for k in (1, 2, 3)
    ]
    total = taps[4:5] + taps[3:4] * part
    for k in (1, 2, 3):
        total = total + taps[3 - k : 4 - k] * shifts[k]
    return total, shifts


def wide(v):
    return jnp.concatenate([v, v], axis=1)


def step_state(raw, params, seg, prev_seg, end_seg, n):
    row = lax.broadcasted_iota(jnp.int32, (n, n), 0)
    col = lax.broadcasted_iota(jnp.int32, (n, n), 1)
    v = raw + params[0:1]
    dt = jnp.maximum(v, 0.0) + jnp.log1p(jnp.exp(-jnp.abs(v)))
    a = params[1:2]
    cum = jnp.dot(
        (row >= col).astype(f32), dt * a, precision=lax.Precision.HIGHEST, preferred_element_type=f32
    )
    last = cum[n - 1 : n]
    into = jnp.where(seg == prev_seg, jnp.exp(cum), 0.0)
    onto = jnp.where(seg == end_seg, jnp.exp(last - cum), 0.0)
    through = jnp.where(end_seg == prev_seg, jnp.exp(last), 0.0)
    bias = jnp.where((row >= col) & (seg == jnp.transpose(seg)), 0.0, -1e30)
    return v, dt, a, cum, into, onto, through, bias


def scan_fwd_kernel(
    blocks, x_ref, bc_ref, st_ref, seg_ref, tapx_ref, tapbc_ref, par_ref, spread_ref, skip_ref,
    y_ref, h_ref, state, tail_x, tail_bc, tail_seg,
):
    n = BLOCK
    block = pl.program_id(1)

    @pl.when(block == 0)
    def _():
        state[...] = jnp.zeros_like(state)
        tail_x[...] = jnp.zeros_like(tail_x)
        tail_bc[...] = jnp.zeros_like(tail_bc)
        tail_seg[...] = jnp.full_like(tail_seg, -1)

    seg = seg_ref[...]
    masks = shifted_masks(jnp.concatenate([tail_seg[...], seg], axis=0), seg)
    prev_seg, end_seg = tail_seg[7:8], seg[n - 1 : n]
    v, dt, a, cum, into, onto, through, bias = step_state(
        st_ref[...], par_ref[...], seg, prev_seg, end_seg, n
    )
    cum_t = jnp.transpose(cum)
    low_lanes = lax.broadcasted_iota(jnp.int32, (n, LANES), 1) >= LANES // 2
    spread = spread_ref[...]
    dt_w = mm(two_parts(dt, low_lanes), spread)
    into_w = mm(two_parts(into, low_lanes), spread)
    onto_w = mm(two_parts(onto, low_lanes), spread)
    through_w = mm(two_parts(jnp.broadcast_to(through, (8, LANES)), low_lanes[:8]), spread)[0:1]
    bc_masks = [None] + [wide(m) for m in masks[1:]]
    conv_bc, _ = convolve(tail_bc[...], bc_ref[...], bc_masks, tapbc_ref[...])
    act_bc = conv_bc * sigmoid(conv_bc)
    b, c = act_bc[:, :LANES].astype(bf16), act_bc[:, LANES:].astype(bf16)
    cross = mm_nt(c, b)
    entering = state[...].astype(bf16)
    h_ref[...] = entering
    first_half = lax.broadcasted_iota(jnp.int32, (n, LANES), 1) < WIDTH
    for pair in range(x_ref.shape[1] // LANES):
        sl = slice(pair * LANES, (pair + 1) * LANES)
        conv, _ = convolve(tail_x[:, sl], x_ref[:, sl], masks, tapx_ref[:, sl])
        xs = conv * sigmoid(conv)
        xd = xs * dt_w[:, sl]
        outside = mm(c, entering[:, sl]) * into_w[:, sl]
        mixes = []
        for h in (2 * pair, 2 * pair + 1):
            decay = jnp.exp(cum[:, h : h + 1] - cum_t[h : h + 1, :] + bias)
            mixes.append((decay * cross).astype(bf16))
        stacked = jnp.concatenate(
            [jnp.where(first_half, xd, 0.0), jnp.where(first_half, 0.0, xd)], axis=0
        ).astype(bf16)
        inside = mm(jnp.concatenate(mixes, axis=1), stacked)
        y_ref[:, sl] = inside + outside + skip_ref[0:1, sl] * xs
        local = mm_tn(b, (onto_w[:, sl] * xd).astype(bf16))
        state[:, sl] = through_w[:, sl] * state[:, sl] + local
    tail_x[...] = x_ref[n - 8 :, :]
    tail_bc[...] = bc_ref[n - 8 :, :]
    tail_seg[...] = seg_ref[n - 8 :, :]


def scan_forward(x, bc, st, seg, tapx, tapbc, par, spread, skip, nseq):
    tokens, width = x.shape
    n = BLOCK
    blocks = tokens // nseq // n
    at = lambda s, i: (s * blocks + i, 0)
    whole = lambda s, i: (0, 0)
    states = LANES
    return pl.pallas_call(
        functools.partial(scan_fwd_kernel, blocks),
        grid=(nseq, blocks),
        in_specs=[
            pl.BlockSpec((n, width), at),
            pl.BlockSpec((n, 2 * states), at),
            pl.BlockSpec((n, LANES), at),
            pl.BlockSpec((n, LANES), at),
            pl.BlockSpec(tapx.shape, whole),
            pl.BlockSpec(tapbc.shape, whole),
            pl.BlockSpec(par.shape, whole),
            pl.BlockSpec(spread.shape, whole),
            pl.BlockSpec(skip.shape, whole),
        ],
        out_specs=[pl.BlockSpec((n, width), at), pl.BlockSpec((states, width), at)],
        out_shape=[
            jax.ShapeDtypeStruct((tokens, width), f32),
            jax.ShapeDtypeStruct((tokens // n * states, width), bf16),
        ],
        scratch_shapes=[
            pltpu.VMEM((states, width), f32),
            pltpu.VMEM((8, width), f32),
            pltpu.VMEM((8, 2 * states), f32),
            pltpu.VMEM((8, LANES), jnp.int32),
        ],
        compiler_params=pltpu.CompilerParams(vmem_limit_bytes=VMEM_BYTES),
        cost_estimate=pl.CostEstimate(
            flops=tokens * width * 1000, bytes_accessed=tokens * width * 12, transcendentals=0
        ),
        name="scan_forward",
    )(x, bc, st, seg, tapx, tapbc, par, spread, skip)


def fold(v):
    total = v[0:8]
    for r in range(8, v.shape[0], 8):
        total = total + v[r : r + 8]
    return total


def scan_bwd_kernel(
    blocks, x_ref, xt_ref, bc_ref, bct_ref, st_ref, seg_ref, segt_ref, gy_ref, y_ref, h_ref,
    tapx_ref, tapbc_ref, par_ref, spread_ref, skip_ref,
    gx_ref, gbc_ref, gst_ref, gtapx_ref, gtapbc_ref, gpar_ref,
    gstate, head_x, head_bc, head_seg,
):
    n = BLOCK
    step = pl.program_id(1)
    block = blocks - 1 - step

    @pl.when((step == 0) & (pl.program_id(0) == 0))
    def _():
        gtapx_ref[...] = jnp.zeros_like(gtapx_ref)
        gtapbc_ref[...] = jnp.zeros_like(gtapbc_ref)
        gpar_ref[...] = jnp.zeros_like(gpar_ref)

    @pl.when(step == 0)
    def _():
        gstate[...] = jnp.zeros_like(gstate)
        head_x[...] = jnp.zeros_like(head_x)
        head_bc[...] = jnp.zeros_like(head_bc)
        head_seg[...] = jnp.full_like(head_seg, -1)

    seg = seg_ref[...]
    first = block == 0
    seg_tail = jnp.where(first, -1, segt_ref[...])
    masks = shifted_masks(jnp.concatenate([seg_tail, seg], axis=0), seg)
    seg_next = jnp.concatenate([seg, head_seg[...]], axis=0)
    ahead = [None] + [seg_next[k : k + n] == seg for k in (1, 2, 3)]
    prev_seg, end_seg = seg_tail[7:8], seg[n - 1 : n]
    v, dt, a, cum, into, onto, through, bias = step_state(
        st_ref[...], par_ref[...], seg, prev_seg, end_seg, n
    )
    cum_t = jnp.transpose(cum)
    low_lanes = lax.broadcasted_iota(jnp.int32, (n, LANES), 1) >= LANES // 2
    spread = spread_ref[...]
    dt_w = mm(two_parts(dt, low_lanes), spread)
    into_w = mm(two_parts(into, low_lanes), spread)
    onto_w = mm(two_parts(onto, low_lanes), spread)
    through_w = mm(two_parts(jnp.broadcast_to(through, (8, LANES)), low_lanes[:8]), spread)[0:1]
    bc_masks = [None] + [wide(m) for m in masks[1:]]
    tail_bc = jnp.where(first, 0.0, bct_ref[...])
    conv_bc, shifts_bc = convolve(tail_bc, bc_ref[...], bc_masks, tapbc_ref[...])
    sig_bc = sigmoid(conv_bc)
    act_bc = conv_bc * sig_bc
    b, c = act_bc[:, :LANES].astype(bf16), act_bc[:, LANES:].astype(bf16)
    cross = mm_nt(c, b)
    first_half = lax.broadcasted_iota(jnp.int32, (n, LANES), 1) < WIDTH
    halves = lambda t: jnp.concatenate(
        [jnp.where(first_half, t, 0.0), jnp.where(first_half, 0.0, t)], axis=0
    ).astype(bf16)

    gcross = jnp.zeros((n, n), f32)
    gb = jnp.zeros((n, LANES), f32)
    gc = jnp.zeros((n, LANES), f32)
    sum_q = jnp.zeros((n, LANES), f32)
    sum_state = jnp.zeros((n, LANES), f32)
    sum_dt = jnp.zeros((n, LANES), f32)
    sum_skip = jnp.zeros((8, LANES), f32)
    sum_last = jnp.zeros((8, LANES), f32)
    for pair in range(x_ref.shape[1] // LANES):
        sl = slice(pair * LANES, (pair + 1) * LANES)
        tail_x = jnp.where(first, 0.0, xt_ref[:, sl])
        part = x_ref[:, sl]
        taps = tapx_ref[:, sl]
        conv, shifts = convolve(tail_x, part, masks, taps)
        sig = sigmoid(conv)
        xs = conv * sig
        xd = xs * dt_w[:, sl]
        xd_low = xd.astype(bf16)
        gy = gy_ref[:, sl]
        gy_low = gy.astype(bf16)
        skip = skip_ref[0:1, sl]
        inner = y_ref[:, sl] - skip * xs
        spread_p = spread[:, sl]
        gstate_low = gstate[:, sl].astype(bf16)
        before = h_ref[:, sl]
        gy_into = (gy * into_w[:, sl]).astype(bf16)
        xd_onto = (xd * onto_w[:, sl]).astype(bf16)
        gc = gc + mm_nt(gy_into, before)
        gb = gb + mm_nt(xd_onto, gstate_low)
        g_state = onto_w[:, sl] * mm(b, gstate_low)
        sum_last = sum_last + head_sums(
            fold(gstate[:, sl] * (through_w[:, sl] * before.astype(f32))), spread_p
        )
        gstate[:, sl] = through_w[:, sl] * gstate[:, sl] + mm_tn(c, gy_into)
        gy_halves = halves(gy)
        gmix = mm_nt(gy_halves, xd_low)
        mixes = []
        for i, h in enumerate((2 * pair, 2 * pair + 1)):
            decay = jnp.exp(cum[:, h : h + 1] - cum_t[h : h + 1, :] + bias)
            mixes.append((decay * cross).astype(bf16))
            gcross = gcross + decay * gmix[i * n : (i + 1) * n]
        g_inside = mm_tn(jnp.concatenate(mixes, axis=0), gy_halves)
        gxd = g_inside + g_state
        xd_r, gy_r = xd_low.astype(f32), gy_low.astype(f32)
        sum_q = sum_q + head_sums(gy_r * inner - xd_r * gxd, spread_p)
        sum_state = sum_state + head_sums(xd_r * g_state, spread_p)
        sum_dt = sum_dt + head_sums(xs * gxd, spread_p)
        sum_skip = sum_skip + head_sums(fold(gy * xs), spread_p)
        gxs = dt_w[:, sl] * gxd + skip * gy
        gconv = gxs * (sig * (1.0 + conv * (1.0 - sig)))
        ext = jnp.concatenate([gconv, head_x[:, sl]], axis=0)
        gu = taps[3:4] * gconv
        for k in (1, 2, 3):
            gu = gu + taps[3 - k : 4 - k] * jnp.where(ahead[k], ext[k : k + n], 0.0)
        gx_ref[:, sl] = gu.astype(bf16)
        for k in range(4):
            row = 8 * (3 - k)
            gtapx_ref[row : row + 8, sl] += fold(gconv * shifts[k])
        gtapx_ref[32:40, sl] += fold(gconv)
        head_x[:, sl] = gconv[0:8]
    gcross_low = gcross.astype(bf16)
    gc = gc + mm(gcross_low, b)
    gb = gb + mm_tn(gcross_low, c)
    gconv = jnp.concatenate([gb, gc], axis=1) * (sig_bc * (1.0 + conv_bc * (1.0 - sig_bc)))
    ext = jnp.concatenate([gconv, head_bc[...]], axis=0)
    taps = tapbc_ref[...]
    gu = taps[3:4] * gconv
    for k in (1, 2, 3):
        gu = gu + taps[3 - k : 4 - k] * jnp.where(wide(ahead[k]), ext[k : k + n], 0.0)
    gbc_ref[...] = gu
    for k in range(4):
        row = 8 * (3 - k)
        gtapbc_ref[row : row + 8, :] += fold(gconv * shifts_bc[k])
    gtapbc_ref[32:40, :] += fold(gconv)
    head_bc[...] = gconv[0:8]
    head_seg[...] = seg[0:8]
    rows = lax.broadcasted_iota(jnp.int32, (n, n), 0)
    cols = lax.broadcasted_iota(jnp.int32, (n, n), 1)
    after = jnp.dot(
        (cols >= rows).astype(f32), sum_q, precision=lax.Precision.HIGHEST, preferred_element_type=f32
    )
    edge = jnp.sum(sum_state, axis=0, keepdims=True) + jnp.sum(sum_last, axis=0, keepdims=True)
    glog = after + edge
    gdt = sum_dt + a * glog
    gst = gdt * sigmoid(v)
    gst_ref[...] = gst.astype(bf16)
    gpar_ref[0:8] += fold(gst)
    gpar_ref[8:16] += fold(a * dt * glog)
    gpar_ref[16:24] += sum_skip


def scan_backward(x, bc, st, seg, gy, y, h, tapx, tapbc, par, spread, skip, nseq):
    tokens, width = x.shape
    n = BLOCK
    blocks = tokens // nseq // n
    at = lambda s, i: (s * blocks + blocks - 1 - i, 0)
    tail = lambda s, i: (jnp.maximum((s * blocks + blocks - 1 - i) * (n // 8) - 1, 0), 0)
    whole = lambda s, i: (0, 0)
    states = LANES
    return pl.pallas_call(
        functools.partial(scan_bwd_kernel, blocks),
        grid=(nseq, blocks),
        in_specs=[
            pl.BlockSpec((n, width), at),
            pl.BlockSpec((8, width), tail),
            pl.BlockSpec((n, 2 * states), at),
            pl.BlockSpec((8, 2 * states), tail),
            pl.BlockSpec((n, LANES), at),
            pl.BlockSpec((n, LANES), at),
            pl.BlockSpec((8, LANES), tail),
            pl.BlockSpec((n, width), at),
            pl.BlockSpec((n, width), at),
            pl.BlockSpec((states, width), at),
            pl.BlockSpec(tapx.shape, whole),
            pl.BlockSpec(tapbc.shape, whole),
            pl.BlockSpec(par.shape, whole),
            pl.BlockSpec(spread.shape, whole),
            pl.BlockSpec(skip.shape, whole),
        ],
        out_specs=[
            pl.BlockSpec((n, width), at),
            pl.BlockSpec((n, 2 * states), at),
            pl.BlockSpec((n, LANES), at),
            pl.BlockSpec((40, width), whole),
            pl.BlockSpec((40, 2 * states), whole),
            pl.BlockSpec((24, LANES), whole),
        ],
        out_shape=[
            jax.ShapeDtypeStruct((tokens, width), bf16),
            jax.ShapeDtypeStruct((tokens, 2 * states), f32),
            jax.ShapeDtypeStruct((tokens, LANES), bf16),
            jax.ShapeDtypeStruct((40, width), f32),
            jax.ShapeDtypeStruct((40, 2 * states), f32),
            jax.ShapeDtypeStruct((24, LANES), f32),
        ],
        scratch_shapes=[
            pltpu.VMEM((states, width), f32),
            pltpu.VMEM((8, width), f32),
            pltpu.VMEM((8, 2 * states), f32),
            pltpu.VMEM((8, LANES), jnp.int32),
        ],
        compiler_params=pltpu.CompilerParams(vmem_limit_bytes=VMEM_BYTES),
        cost_estimate=pl.CostEstimate(
            flops=tokens * width * 3000, bytes_accessed=tokens * width * 20, transcendentals=0
        ),
        name="scan_backward",
    )(x, x, bc, bc, st, seg, seg, gy, y, h, tapx, tapbc, par, spread, skip)


def spread_matrix(heads):
    row = lax.broadcasted_iota(jnp.int32, (LANES, heads * WIDTH), 0)
    col = lax.broadcasted_iota(jnp.int32, (LANES, heads * WIDTH), 1)
    return (row % (LANES // 2) == col // WIDTH).astype(bf16)


def on_lanes(v):
    half = jnp.pad(v, [(0, 0)] * (v.ndim - 1) + [(0, LANES // 2 - v.shape[-1])])
    return jnp.concatenate([half, half], axis=-1)


epsilon = 1e-05


def placed_at(whole, piece, offset):
    start = (0,) * (len(whole) - 1) + (offset,)
    return lax.dynamic_update_slice(jnp.zeros(whole, piece.dtype), piece, start)


def per_device(
    residual, segment_ids, norm_gain, inner_weight, state_weight, step_weight, conv_weight,
    conv_bias, step_bias, decay_log, skip_gain, gated_gain, out_weight, cotangent,
):
    rank = lax.axis_index("tensor")
    model_width = residual.shape[1]
    width = inner_weight.shape[2]
    heads = step_weight.shape[1]
    inner_width = gated_gain.shape[0]
    nseq, length = segment_ids.shape
    tokens = nseq * length
    inner_start, head_start = rank * width, rank * heads
    stream = residual.astype(f32)
    scaling = lax.rsqrt(jnp.mean(stream * stream, axis=1, keepdims=True) + epsilon)
    normed = (stream * scaling * norm_gain).astype(bf16)
    normed_all = lax.all_gather(normed, "tensor", axis=0, tiled=True)
    wx = lax.all_gather(
        jnp.concatenate([inner_weight[:, 1], on_lanes(step_weight)], axis=1), "dp", axis=0, tiled=True
    )
    wz = lax.all_gather(inner_weight[:, 0], "dp", axis=0, tiled=True)
    wo = lax.all_gather(out_weight, "dp", axis=1, tiled=True)
    cot_all = lax.all_gather(cotangent, "tensor", axis=0, tiled=True)
    taps = jnp.concatenate([conv_weight, conv_bias[None], jnp.zeros((3, conv_bias.shape[0]), f32)], axis=0)
    tapx = lax.dynamic_slice_in_dim(taps, inner_start, width, 1)
    tapbc = taps[:, inner_width:]
    local = lambda v: lax.dynamic_slice_in_dim(v, head_start, heads, 0)
    rates = -jnp.exp(local(decay_log))
    par = jnp.concatenate(
        [on_lanes(local(step_bias)[None]), on_lanes(rates[None]), jnp.zeros((6, LANES), f32)], axis=0
    )
    skip = jnp.broadcast_to(jnp.repeat(local(skip_gain), WIDTH)[None], (8, width))
    gain = lax.dynamic_slice_in_dim(gated_gain, inner_start, width, 0)
    spread = spread_matrix(heads)
    seg = jnp.broadcast_to(segment_ids.reshape(tokens, 1), (tokens, LANES))

    xst = mm(normed_all, wx)
    bc = mm(normed_all, state_weight)
    x, st = xst[:, :width], xst[:, width:]
    y, h = scan_forward(x, bc, st, seg, tapx, tapbc, par, spread, skip, nseq)
    z = mm(normed_all, wz)
    sig = jax.nn.sigmoid(z)
    silu = z * sig
    gated = y * silu
    gng = mm_nt(cot_all, wo)
    sums = lax.psum(
        jnp.stack([jnp.sum(gated * gated, axis=1), jnp.sum(gng * gain * gated, axis=1)]), "tensor"
    )
    scale_g = lax.rsqrt(sums[0] / inner_width + epsilon)[:, None]
    normed_g = (gated * scale_g * gain).astype(bf16)
    grad_gated = scale_g * gain * gng - gated * (scale_g**3 * sums[1][:, None] / inner_width)
    gain_grad = jnp.sum(gng * gated * scale_g, axis=0)
    gz = (grad_gated * y * (sig * (1.0 + z * (1.0 - sig)))).astype(bf16)
    gy = grad_gated * silu
    scatter = lambda v, axis, dim: lax.psum_scatter(
        v.astype(bf16), axis, scatter_dimension=dim, tiled=True
    ).astype(f32)
    block_out = stream + scatter(mm(normed_g, wo), "tensor", 0)
    out_grad = scatter(mm_tn(normed_g, cot_all), "dp", 1)
    z_grad = scatter(mm_tn(normed_all, gz), "dp", 0)
    gx, gbc, gst, gtapx, gtapbc, gpar = scan_backward(
        x, bc, st, seg, gy, y, h, tapx, tapbc, par, spread, skip, nseq
    )
    gbc = gbc.astype(bf16)
    gxs = jnp.concatenate([gx, gst * (lax.broadcasted_iota(jnp.int32, (1, LANES), 1) < LANES // 2)], axis=1)
    total = mm_nt(gz, wz) + mm_nt(gxs, wx) + mm_nt(gbc, state_weight)
    grad_normed = scatter(total, "tensor", 0)
    x_grad = scatter(mm_tn(normed_all, gxs), "dp", 0)
    state_grad = scatter(mm_tn(normed_all, gbc), ("dp", "tensor"), 0)
    state_grad = lax.all_gather(state_grad, ("dp", "tensor"), axis=0, tiled=True)
    gtapx = gtapx.reshape(5, 8, -1).sum(1)
    gtapbc = gtapbc.reshape(5, 8, -1).sum(1)
    gpar = gpar.reshape(3, 8, -1).sum(1)[:, :heads]
    gtaps = jnp.concatenate(
        [placed_at((5, inner_width), gtapx, inner_start), gtapbc], axis=1
    )
    gpars = placed_at((3, step_bias.shape[0]), gpar, head_start)
    ggain = placed_at((1, inner_width), gain_grad[None], inner_start)
    gtaps, gpars, ggain = lax.psum((gtaps, gpars, ggain), ("dp", "tensor"))
    norm_grad = lax.psum(jnp.sum(grad_normed * stream * scaling, axis=0), ("dp", "tensor"))
    along = jnp.sum(grad_normed * norm_gain * stream, axis=1, keepdims=True)
    residual_grad = (
        cotangent.astype(f32)
        + scaling * norm_gain * grad_normed
        - stream * (scaling**3 * along / model_width)
    )
    inner_grad = jnp.stack([z_grad, x_grad[:, :width]], axis=1)
    return (
        block_out, residual_grad, norm_grad, inner_grad, state_grad,
        x_grad[:, width : width + heads], gtaps[:4], gtaps[4], gpars[0], gpars[1], gpars[2],
        ggain[0], out_grad,
    )


def solution(mesh):
    rows, both = P("dp", "tensor"), P(("dp", "tensor"), None)
    inner, out = P("dp", None, "tensor"), P("tensor", "dp")
    return jax.shard_map(
        per_device,
        mesh=mesh,
        in_specs=(
            both, P("dp", None), P(), inner, P(), rows, P(), P(), P(), P(), P(), P(), out, both,
        ),
        out_specs=(both, both, P(), inner, P(), rows, P(), P(), P(), P(), P(), P(), out),
        check_vma=False,
    )
```

```python
import functools
import jax
import jax.numpy as jnp
from jax import lax
from jax.experimental import pallas as pl
from jax.experimental.pallas import tpu as pltpu
from jax.sharding import PartitionSpec as P

LANES = 128
BLOCK = 128
WIDTH = 64
VMEM_BYTES = 56 * 1024 * 1024
f32, bf16 = jnp.float32, jnp.bfloat16
ROWS0 = (((0,), (0,)), ((), ()))
COLS1 = (((1,), (1,)), ((), ()))


def mm(a, b):
    return jnp.dot(a, b, preferred_element_type=f32)


def mm_tn(a, b):
    return lax.dot_general(a, b, ROWS0, preferred_element_type=f32)


def mm_nt(a, b):
    return lax.dot_general(a, b, COLS1, preferred_element_type=f32)


def sigmoid(v):
    return 0.5 + 0.5 * jnp.tanh(0.5 * v)


def two_parts(v, low_lanes):
    high = v.astype(bf16)
    return jnp.where(low_lanes, (v - high.astype(f32)).astype(bf16), high)


def head_sums(v, spread):
    high = v.astype(bf16)
    low = (v - high.astype(f32)).astype(bf16)
    return mm_nt(high, spread) + mm_nt(low, spread)


def shifted_masks(seg_ext, seg):
    n = seg.shape[0]
    return [None] + [seg_ext[8 - k : 8 - k + n] == seg for k in (1, 2, 3)]


def convolve(tail, part, masks, taps):
    n = part.shape[0]
    ext = jnp.concatenate([tail, part], axis=0)
    shifts = [part] + [
        jnp.where(masks[k], ext[8 - k : 8 - k + n], 0.0) for k in (1, 2, 3)
    ]
    total = taps[4:5] + taps[3:4] * part
    for k in (1, 2, 3):
        total = total + taps[3 - k : 4 - k] * shifts[k]
    return total, shifts


def wide(v):
    return jnp.concatenate([v, v], axis=1)


def step_state(raw, params, seg, prev_seg, end_seg, n):
    row = lax.broadcasted_iota(jnp.int32, (n, n), 0)
    col = lax.broadcasted_iota(jnp.int32, (n, n), 1)
    v = raw + params[0:1]
    dt = jnp.maximum(v, 0.0) + jnp.log1p(jnp.exp(-jnp.abs(v)))
    a = params[1:2]
    cum = jnp.dot(
        (row >= col).astype(f32), dt * a, precision=lax.Precision.HIGHEST, preferred_element_type=f32
    )
    last = cum[n - 1 : n]
    into = jnp.where(seg == prev_seg, jnp.exp(cum), 0.0)
    onto = jnp.where(seg == end_seg, jnp.exp(last - cum), 0.0)
    through = jnp.where(end_seg == prev_seg, jnp.exp(last), 0.0)
    bias = jnp.where((row >= col) & (seg == jnp.transpose(seg)), 0.0, -1e30)
    return v, dt, a, cum, into, onto, through, bias


def scan_fwd_kernel(
    blocks, x_ref, bc_ref, st_ref, seg_ref, tapx_ref, tapbc_ref, par_ref, spread_ref, skip_ref,
    y_ref, h_ref, state, tail_x, tail_bc, tail_seg,
):
    n = BLOCK
    block = pl.program_id(1)

    @pl.when(block == 0)
    def _():
        state[...] = jnp.zeros_like(state)
        tail_x[...] = jnp.zeros_like(tail_x)
        tail_bc[...] = jnp.zeros_like(tail_bc)
        tail_seg[...] = jnp.full_like(tail_seg, -1)

    seg = seg_ref[...]
    masks = shifted_masks(jnp.concatenate([tail_seg[...], seg], axis=0), seg)
    prev_seg, end_seg = tail_seg[7:8], seg[n - 1 : n]
    v, dt, a, cum, into, onto, through, bias = step_state(
        st_ref[...], par_ref[...], seg, prev_seg, end_seg, n
    )
    cum_t = jnp.transpose(cum)
    low_lanes = lax.broadcasted_iota(jnp.int32, (n, LANES), 1) >= LANES // 2
    spread = spread_ref[...]
    dt_w = mm(two_parts(dt, low_lanes), spread)
    into_w = mm(two_parts(into, low_lanes), spread)
    onto_w = mm(two_parts(onto, low_lanes), spread)
    through_w = mm(two_parts(jnp.broadcast_to(through, (8, LANES)), low_lanes[:8]), spread)[0:1]
    bc_masks = [None] + [wide(m) for m in masks[1:]]
    conv_bc, _ = convolve(tail_bc[...], bc_ref[...], bc_masks, tapbc_ref[...])
    act_bc = conv_bc * sigmoid(conv_bc)
    b, c = act_bc[:, :LANES].astype(bf16), act_bc[:, LANES:].astype(bf16)
    cross = mm_nt(c, b)
    entering = state[...].astype(bf16)
    h_ref[...] = entering
    first_half = lax.broadcasted_iota(jnp.int32, (n, LANES), 1) < WIDTH
    for pair in range(x_ref.shape[1] // LANES):
        sl = slice(pair * LANES, (pair + 1) * LANES)
        conv, _ = convolve(tail_x[:, sl], x_ref[:, sl], masks, tapx_ref[:, sl])
        xs = conv * sigmoid(conv)
        xd = xs * dt_w[:, sl]
        outside = mm(c, entering[:, sl]) * into_w[:, sl]
        mixes = []
        for h in (2 * pair, 2 * pair + 1):
            decay = jnp.exp(cum[:, h : h + 1] - cum_t[h : h + 1, :] + bias)
            mixes.append((decay * cross).astype(bf16))
        stacked = jnp.concatenate(
            [jnp.where(first_half, xd, 0.0), jnp.where(first_half, 0.0, xd)], axis=0
        ).astype(bf16)
        inside = mm(jnp.concatenate(mixes, axis=1), stacked)
        y_ref[:, sl] = inside + outside + skip_ref[0:1, sl] * xs
        local = mm_tn(b, (onto_w[:, sl] * xd).astype(bf16))
        state[:, sl] = through_w[:, sl] * state[:, sl] + local
    tail_x[...] = x_ref[n - 8 :, :]
    tail_bc[...] = bc_ref[n - 8 :, :]
    tail_seg[...] = seg_ref[n - 8 :, :]


def scan_forward(x, bc, st, seg, tapx, tapbc, par, spread, skip, nseq):
    tokens, width = x.shape
    n = BLOCK
    blocks = tokens // nseq // n
    at = lambda s, i: (s * blocks + i, 0)
    whole = lambda s, i: (0, 0)
    states = LANES
    return pl.pallas_call(
        functools.partial(scan_fwd_kernel, blocks),
        grid=(nseq, blocks),
        in_specs=[
            pl.BlockSpec((n, width), at),
            pl.BlockSpec((n, 2 * states), at),
            pl.BlockSpec((n, LANES), at),
            pl.BlockSpec((n, LANES), at),
            pl.BlockSpec(tapx.shape, whole),
            pl.BlockSpec(tapbc.shape, whole),
            pl.BlockSpec(par.shape, whole),
            pl.BlockSpec(spread.shape, whole),
            pl.BlockSpec(skip.shape, whole),
        ],
        out_specs=[pl.BlockSpec((n, width), at), pl.BlockSpec((states, width), at)],
        out_shape=[
            jax.ShapeDtypeStruct((tokens, width), f32),
            jax.ShapeDtypeStruct((tokens // n * states, width), bf16),
        ],
        scratch_shapes=[
            pltpu.VMEM((states, width), f32),
            pltpu.VMEM((8, width), f32),
            pltpu.VMEM((8, 2 * states), f32),
            pltpu.VMEM((8, LANES), jnp.int32),
        ],
        compiler_params=pltpu.CompilerParams(vmem_limit_bytes=VMEM_BYTES),
        cost_estimate=pl.CostEstimate(
            flops=tokens * width * 1000, bytes_accessed=tokens * width * 12, transcendentals=0
        ),
        name="scan_forward",
    )(x, bc, st, seg, tapx, tapbc, par, spread, skip)


def fold(v):
    total = v[0:8]
    for r in range(8, v.shape[0], 8):
        total = total + v[r : r + 8]
    return total


def scan_bwd_kernel(
    blocks, x_ref, xt_ref, bc_ref, bct_ref, st_ref, seg_ref, segt_ref, gy_ref, y_ref, h_ref,
    tapx_ref, tapbc_ref, par_ref, spread_ref, skip_ref,
    gx_ref, gbc_ref, gst_ref, gtapx_ref, gtapbc_ref, gpar_ref,
    gstate, head_x, head_bc, head_seg,
):
    n = BLOCK
    step = pl.program_id(1)
    block = blocks - 1 - step

    @pl.when((step == 0) & (pl.program_id(0) == 0))
    def _():
        gtapx_ref[...] = jnp.zeros_like(gtapx_ref)
        gtapbc_ref[...] = jnp.zeros_like(gtapbc_ref)
        gpar_ref[...] = jnp.zeros_like(gpar_ref)

    @pl.when(step == 0)
    def _():
        gstate[...] = jnp.zeros_like(gstate)
        head_x[...] = jnp.zeros_like(head_x)
        head_bc[...] = jnp.zeros_like(head_bc)
        head_seg[...] = jnp.full_like(head_seg, -1)

    seg = seg_ref[...]
    first = block == 0
    seg_tail = jnp.where(first, -1, segt_ref[...])
    masks = shifted_masks(jnp.concatenate([seg_tail, seg], axis=0), seg)
    seg_next = jnp.concatenate([seg, head_seg[...]], axis=0)
    ahead = [None] + [seg_next[k : k + n] == seg for k in (1, 2, 3)]
    prev_seg, end_seg = seg_tail[7:8], seg[n - 1 : n]
    v, dt, a, cum, into, onto, through, bias = step_state(
        st_ref[...], par_ref[...], seg, prev_seg, end_seg, n
    )
    cum_t = jnp.transpose(cum)
    low_lanes = lax.broadcasted_iota(jnp.int32, (n, LANES), 1) >= LANES // 2
    spread = spread_ref[...]
    dt_w = mm(two_parts(dt, low_lanes), spread)
    into_w = mm(two_parts(into, low_lanes), spread)
    onto_w = mm(two_parts(onto, low_lanes), spread)
    through_w = mm(two_parts(jnp.broadcast_to(through, (8, LANES)), low_lanes[:8]), spread)[0:1]
    bc_masks = [None] + [wide(m) for m in masks[1:]]
    tail_bc = jnp.where(first, 0.0, bct_ref[...])
    conv_bc, shifts_bc = convolve(tail_bc, bc_ref[...], bc_masks, tapbc_ref[...])
    sig_bc = sigmoid(conv_bc)
    act_bc = conv_bc * sig_bc
    b, c = act_bc[:, :LANES].astype(bf16), act_bc[:, LANES:].astype(bf16)
    cross = mm_nt(c, b)
    first_half = lax.broadcasted_iota(jnp.int32, (n, LANES), 1) < WIDTH
    halves = lambda t: jnp.concatenate(
        [jnp.where(first_half, t, 0.0), jnp.where(first_half, 0.0, t)], axis=0
    ).astype(bf16)

    gcross = jnp.zeros((n, n), f32)
    gb = jnp.zeros((n, LANES), f32)
    gc = jnp.zeros((n, LANES), f32)
    sum_q = jnp.zeros((n, LANES), f32)
    sum_state = jnp.zeros((n, LANES), f32)
    sum_dt = jnp.zeros((n, LANES), f32)
    sum_skip = jnp.zeros((8, LANES), f32)
    sum_last = jnp.zeros((8, LANES), f32)
    for pair in range(x_ref.shape[1] // LANES):
        sl = slice(pair * LANES, (pair + 1) * LANES)
        tail_x = jnp.where(first, 0.0, xt_ref[:, sl])
        part = x_ref[:, sl]
        taps = tapx_ref[:, sl]
        conv, shifts = convolve(tail_x, part, masks, taps)
        sig = sigmoid(conv)
        xs = conv * sig
        xd = xs * dt_w[:, sl]
        xd_low = xd.astype(bf16)
        gy = gy_ref[:, sl]
        gy_low = gy.astype(bf16)
        skip = skip_ref[0:1, sl]
        inner = y_ref[:, sl] - skip * xs
        spread_p = spread[:, sl]
        gstate_low = gstate[:, sl].astype(bf16)
        before = h_ref[:, sl]
        gy_into = (gy * into_w[:, sl]).astype(bf16)
        xd_onto = (xd * onto_w[:, sl]).astype(bf16)
        gc = gc + mm_nt(gy_into, before)
        gb = gb + mm_nt(xd_onto, gstate_low)
        g_state = onto_w[:, sl] * mm(b, gstate_low)
        sum_last = sum_last + head_sums(
            fold(gstate[:, sl] * (through_w[:, sl] * before.astype(f32))), spread_p
        )
        gstate[:, sl] = through_w[:, sl] * gstate[:, sl] + mm_tn(c, gy_into)
        gy_halves = halves(gy)
        gmix = mm_nt(gy_halves, xd_low)
        mixes = []
        for i, h in enumerate((2 * pair, 2 * pair + 1)):
            decay = jnp.exp(cum[:, h : h + 1] - cum_t[h : h + 1, :] + bias)
            mixes.append((decay * cross).astype(bf16))
            gcross = gcross + decay * gmix[i * n : (i + 1) * n]
        g_inside = mm_tn(jnp.concatenate(mixes, axis=0), gy_halves)
        gxd = g_inside + g_state
        xd_r, gy_r = xd_low.astype(f32), gy_low.astype(f32)
        sum_q = sum_q + head_sums(gy_r * inner - xd_r * gxd, spread_p)
        sum_state = sum_state + head_sums(xd_r * g_state, spread_p)
        sum_dt = sum_dt + head_sums(xs * gxd, spread_p)
        sum_skip = sum_skip + head_sums(fold(gy * xs), spread_p)
        gxs = dt_w[:, sl] * gxd + skip * gy
        gconv = gxs * (sig * (1.0 + conv * (1.0 - sig)))
        ext = jnp.concatenate([gconv, head_x[:, sl]], axis=0)
        gu = taps[3:4] * gconv
        for k in (1, 2, 3):
            gu = gu + taps[3 - k : 4 - k] * jnp.where(ahead[k], ext[k : k + n], 0.0)
        gx_ref[:, sl] = gu.astype(bf16)
        for k in range(4):
            row = 8 * (3 - k)
            gtapx_ref[row : row + 8, sl] += fold(gconv * shifts[k])
        gtapx_ref[32:40, sl] += fold(gconv)
        head_x[:, sl] = gconv[0:8]
    gcross_low = gcross.astype(bf16)
    gc = gc + mm(gcross_low, b)
    gb = gb + mm_tn(gcross_low, c)
    gconv = jnp.concatenate([gb, gc], axis=1) * (sig_bc * (1.0 + conv_bc * (1.0 - sig_bc)))
    ext = jnp.concatenate([gconv, head_bc[...]], axis=0)
    taps = tapbc_ref[...]
    gu = taps[3:4] * gconv
    for k in (1, 2, 3):
        gu = gu + taps[3 - k : 4 - k] * jnp.where(wide(ahead[k]), ext[k : k + n], 0.0)
    gbc_ref[...] = gu
    for k in range(4):
        row = 8 * (3 - k)
        gtapbc_ref[row : row + 8, :] += fold(gconv * shifts_bc[k])
    gtapbc_ref[32:40, :] += fold(gconv)
    head_bc[...] = gconv[0:8]
    head_seg[...] = seg[0:8]
    rows = lax.broadcasted_iota(jnp.int32, (n, n), 0)
    cols = lax.broadcasted_iota(jnp.int32, (n, n), 1)
    after = jnp.dot(
        (cols >= rows).astype(f32), sum_q, precision=lax.Precision.HIGHEST, preferred_element_type=f32
    )
    edge = jnp.sum(sum_state, axis=0, keepdims=True) + jnp.sum(sum_last, axis=0, keepdims=True)
    glog = after + edge
    gdt = sum_dt + a * glog
    gst = gdt * sigmoid(v)
    gst_ref[...] = gst.astype(bf16)
    gpar_ref[0:8] += fold(gst)
    gpar_ref[8:16] += fold(a * dt * glog)
    gpar_ref[16:24] += sum_skip


def scan_backward(x, bc, st, seg, gy, y, h, tapx, tapbc, par, spread, skip, nseq):
    tokens, width = x.shape
    n = BLOCK
    blocks = tokens // nseq // n
    at = lambda s, i: (s * blocks + blocks - 1 - i, 0)
    tail = lambda s, i: (jnp.maximum((s * blocks + blocks - 1 - i) * (n // 8) - 1, 0), 0)
    whole = lambda s, i: (0, 0)
    states = LANES
    return pl.pallas_call(
        functools.partial(scan_bwd_kernel, blocks),
        grid=(nseq, blocks),
        in_specs=[
            pl.BlockSpec((n, width), at),
            pl.BlockSpec((8, width), tail),
            pl.BlockSpec((n, 2 * states), at),
            pl.BlockSpec((8, 2 * states), tail),
            pl.BlockSpec((n, LANES), at),
            pl.BlockSpec((n, LANES), at),
            pl.BlockSpec((8, LANES), tail),
            pl.BlockSpec((n, width), at),
            pl.BlockSpec((n, width), at),
            pl.BlockSpec((states, width), at),
            pl.BlockSpec(tapx.shape, whole),
            pl.BlockSpec(tapbc.shape, whole),
            pl.BlockSpec(par.shape, whole),
            pl.BlockSpec(spread.shape, whole),
            pl.BlockSpec(skip.shape, whole),
        ],
        out_specs=[
            pl.BlockSpec((n, width), at),
            pl.BlockSpec((n, 2 * states), at),
            pl.BlockSpec((n, LANES), at),
            pl.BlockSpec((40, width), whole),
            pl.BlockSpec((40, 2 * states), whole),
            pl.BlockSpec((24, LANES), whole),
        ],
        out_shape=[
            jax.ShapeDtypeStruct((tokens, width), bf16),
            jax.ShapeDtypeStruct((tokens, 2 * states), f32),
            jax.ShapeDtypeStruct((tokens, LANES), bf16),
            jax.ShapeDtypeStruct((40, width), f32),
            jax.ShapeDtypeStruct((40, 2 * states), f32),
            jax.ShapeDtypeStruct((24, LANES), f32),
        ],
        scratch_shapes=[
            pltpu.VMEM((states, width), f32),
            pltpu.VMEM((8, width), f32),
            pltpu.VMEM((8, 2 * states), f32),
            pltpu.VMEM((8, LANES), jnp.int32),
        ],
        compiler_params=pltpu.CompilerParams(vmem_limit_bytes=VMEM_BYTES),
        cost_estimate=pl.CostEstimate(
            flops=tokens * width * 3000, bytes_accessed=tokens * width * 20, transcendentals=0
        ),
        name="scan_backward",
    )(x, x, bc, bc, st, seg, seg, gy, y, h, tapx, tapbc, par, spread, skip)


def spread_matrix(heads):
    row = lax.broadcasted_iota(jnp.int32, (LANES, heads * WIDTH), 0)
    col = lax.broadcasted_iota(jnp.int32, (LANES, heads * WIDTH), 1)
    return (row % (LANES // 2) == col // WIDTH).astype(bf16)


def on_lanes(v):
    half = jnp.pad(v, [(0, 0)] * (v.ndim - 1) + [(0, LANES // 2 - v.shape[-1])])
    return jnp.concatenate([half, half], axis=-1)


MESH = pl.DeviceIdType.MESH


def place():
    dp, rank = lax.axis_index("dp"), lax.axis_index("tensor")
    return dp // 2, dp % 2, rank


def remote(src, dst, send, recv, dp, rank):
    return pltpu.make_async_remote_copy(
        src_ref=src, dst_ref=dst, send_sem=send, recv_sem=recv, device_id=(dp, rank),
        device_id_type=MESH,
    )


def greet(chips, ranks, line=True, tensor=True):
    chip, core, rank = place()
    sem = pltpu.get_barrier_semaphore()
    me = chip * 2 + core

    def signal(dp, r):
        pl.semaphore_signal(sem, inc=1, device_id=(dp, r), device_id_type=MESH)

    if line:
        signal(chip * 2 + 1 - core, rank)
        for step in (1, -1):
            @pl.when((chip + step >= 0) & (chip + step < chips))
            def _():
                signal(me + 2 * step, rank)
    if tensor:
        for k in range(1, ranks):
            signal(me, lax.rem(rank + k, ranks))
    count = ranks - 1 if tensor else 0
    if line:
        count = count + 1 + (chip + chips - 1) // chips + (2 * chips - 2 - chip) // chips
    pl.semaphore_wait(sem, count)


class LineGather:
    sems = 4

    def __init__(self, own, slots, send, recv, local, chips):
        self.own, self.slots, self.send, self.recv, self.local = own, slots, send, recv, local
        self.chips = chips
        self.chip, self.core, self.rank = place()
        self.me = self.chip * 2 + self.core
        self.partner = self.chip * 2 + 1 - self.core
        self.steps = chips

    @staticmethod
    def scratch(chips):
        n = 2 * chips
        return [
            pltpu.SemaphoreType.DMA((3, n)), pltpu.SemaphoreType.DMA((n,)), pltpu.SemaphoreType.DMA,
        ]

    def copy(self, way, origin, src=None):
        target = (self.me + 2, self.me - 2, self.partner)[way]
        slot = self.slots.at[origin]
        return remote(
            slot if src is None else src, slot, self.send.at[way, origin], self.recv.at[origin],
            target, self.rank,
        )

    def pass_on(self, way, origin, src=None, wait=False):
        def go():
            copy = self.copy(way, origin, src)
            copy.wait_send() if wait else copy.start()

        if way == 0:
            pl.when(self.chip + 1 < self.chips)(go)
        elif way == 1:
            pl.when(self.chip > 0)(go)
        else:
            go()

    def step(self, k):
        if k == 0:
            for way in (0, 1, 2):
                self.pass_on(way, self.me, self.own)
            pltpu.make_async_copy(self.own, self.slots.at[self.me], self.local).start()
            return
        for way, origin, there in (
            (0, self.me - 2 * k, self.chip - k >= 0),
            (1, self.me + 2 * k, self.chip + k < self.chips),
        ):
            @pl.when(there)
            def _():
                self.copy(2, origin).wait_recv()
                self.pass_on(way, origin)
                self.pass_on(2, origin)

    def finish(self):
        pltpu.make_async_copy(self.own, self.slots.at[self.me], self.local).wait()
        for way in (0, 1, 2):
            self.pass_on(way, self.me, self.own, wait=True)
        self.copy(2, self.partner).wait_recv()
        for k in range(1, self.chips):
            for way, there, shift in ((0, self.chip - k >= 0, -k), (1, self.chip + k < self.chips, k)):
                @pl.when(there)
                def _():
                    origin = self.me + 2 * shift
                    self.pass_on(way, origin, wait=True)
                    self.pass_on(2, origin, wait=True)
                    self.copy(2, self.partner + 2 * shift).wait_recv()


class TensorGather:
    def __init__(self, own, slots, send, recv, local, ranks):
        self.own, self.slots, self.send, self.recv, self.local = own, slots, send, recv, local
        self.ranks = ranks
        chip, core, self.rank = place()
        self.me = chip * 2 + core
        self.rows = own.shape[0] // 2
        self.steps = 2

    @staticmethod
    def scratch(ranks):
        return [
            pltpu.SemaphoreType.DMA((ranks,)), pltpu.SemaphoreType.DMA((ranks,)), pltpu.SemaphoreType.DMA,
        ]

    def near(self, k, src=None):
        x = self.rank % 2
        y = self.rank // 2
        across = (y * 2 + 1 - x, (1 - y) * 2 + x)
        if k < 2:
            return remote(
                self.own if src is None else src, self.slots.at[self.rank], self.send.at[k],
                self.recv.at[k], self.me, across[k],
            )
        half = self.slots.at[across[k - 2], pl.ds((k - 2) * self.rows, self.rows)]
        return remote(half, half, self.send.at[k], self.recv.at[k], self.me, across[3 - k])

    def direct(self, k):
        return remote(
            self.own, self.slots.at[self.rank], self.send.at[k], self.recv.at[k], self.me,
            lax.rem(self.rank + k, self.ranks),
        )

    def step(self, k):
        if k == 0:
            if self.ranks == 4:
                self.near(0).start()
                self.near(1).start()
            else:
                for j in range(1, self.ranks):
                    self.direct(j).start()
            pltpu.make_async_copy(self.own, self.slots.at[self.rank], self.local).start()
        elif self.ranks == 4:
            for j in (0, 1):
                self.near(j).wait_recv()
                self.near(2 + j).start()

    def finish(self):
        pltpu.make_async_copy(self.own, self.slots.at[self.rank], self.local).wait()
        if self.ranks == 4:
            for j in (0, 1):
                self.near(j).wait_send()
                self.near(2 + j).wait()
        else:
            for j in range(1, self.ranks):
                self.direct(j).wait()


def add_rows(target, others):
    rows = target.shape[0]
    slab = 32 if rows % 32 == 0 else 16

    @pl.loop(0, rows // slab)
    def _(i):
        at = pl.ds(pl.multiple_of(i * slab, slab), slab)
        total = target[at].astype(f32)
        for other in others:
            total = total + other[at].astype(f32)
        target[at] = total.astype(target.dtype)


class LineScatter:
    def __init__(self, parts, out, mine, swap, up, down, send, recv, local, chips):
        self.parts, self.out, self.mine, self.swap, self.up, self.down = parts, out, mine, swap, up, down
        self.send, self.recv, self.local, self.chips = send, recv, local, chips
        self.chip, self.core, self.rank = place()
        self.me = self.chip * 2 + self.core
        self.partner = self.chip * 2 + 1 - self.core
        self.steps = chips

    @staticmethod
    def scratch(chips, shape):
        return [pltpu.VMEM((chips,) + shape, bf16)] * 4 + [
            pltpu.SemaphoreType.DMA((3, chips)), pltpu.SemaphoreType.DMA((3, chips)),
            pltpu.SemaphoreType.DMA((chips,)),
        ]

    def order(self):
        n = self.chips
        return [c for k in range(n // 2) for c in (n - 1 - k, k)]

    def over(self, c):
        return remote(
            self.parts.at[2 * c + 1 - self.core], self.swap.at[c], self.send.at[2, c],
            self.recv.at[2, c], self.partner, self.rank,
        )

    def load(self, c):
        return pltpu.make_async_copy(
            self.parts.at[2 * c + self.core], self.mine.at[c], self.local.at[c]
        )

    def along(self, way, c, first=False):
        buffer = (self.up, self.down)[way]
        src = self.mine.at[c] if first else buffer.at[c]
        return remote(
            src, buffer.at[c], self.send.at[way, c], self.recv.at[way, c],
            self.me + (2, -2)[way], self.rank,
        )

    def step(self, k):
        n, chip = self.chips, self.chip
        if k == 0:
            for c in self.order():
                self.over(c).start()
                self.load(c).start()
            return
        if k == 1:
            for c in self.order():
                self.over(c).wait()
                self.load(c).wait()
                add_rows(self.mine.at[c], [self.swap.at[c]])

                @pl.when((chip == 0) & (c > 0))
                def _():
                    self.along(0, c, True).start()

                @pl.when((chip == n - 1) & (c < n - 1))
                def _():
                    self.along(1, c, True).start()
            return
        t = k - 1
        c = n - 1 - (t - chip)

        @pl.when((chip > 0) & (t >= chip) & (c > chip))
        def _():
            self.along(0, c).wait_recv()
            add_rows(self.up.at[c], [self.mine.at[c]])
            self.along(0, c).start()

        d = t - (n - 1 - chip)

        @pl.when((chip < n - 1) & (d >= 0) & (d < chip))
        def _():
            self.along(1, d).wait_recv()
            add_rows(self.down.at[d], [self.mine.at[d]])
            self.along(1, d).start()

    def finish(self):
        n, chip = self.chips, self.chip
        out, mine, up, down = self.out, self.mine.at[chip], self.up.at[chip], self.down.at[chip]

        @pl.when(chip > 0)
        def _():
            self.along(0, chip).wait_recv()

        @pl.when(chip < n - 1)
        def _():
            self.along(1, chip).wait_recv()

        rows = out.shape[0]
        slab = 16
        has_up, has_down = chip > 0, chip < n - 1

        @pl.when(has_up & has_down)
        def _():
            add_rows(mine, [up])

        @pl.loop(0, rows // slab)
        def _(i):
            at = pl.ds(pl.multiple_of(i * slab, slab), slab)
            out[at] = mine[at].astype(f32)

        other = [(has_down, down), (has_up & jnp.logical_not(has_down), up)]
        for there, buffer in other:
            @pl.when(there)
            def _():
                @pl.loop(0, rows // slab)
                def _(i):
                    at = pl.ds(pl.multiple_of(i * slab, slab), slab)
                    out[at] += buffer[at].astype(f32)

        for c in range(n):
            @pl.when((chip < n - 1) & (c > chip))
            def _():
                self.along(0, c).wait_send()

            @pl.when((chip > 0) & (c < chip))
            def _():
                self.along(1, c).wait_send()


class TensorScatter:
    def __init__(self, parts, out, mine, land, send, recv, local, ranks):
        self.parts, self.out, self.mine, self.land = parts, out, mine, land
        self.send, self.recv, self.local, self.ranks = send, recv, local, ranks
        chip, core, self.rank = place()
        self.me = chip * 2 + core
        self.steps = 1

    @staticmethod
    def scratch(ranks, shape):
        return [
            pltpu.VMEM(shape, bf16), pltpu.VMEM((ranks,) + shape, bf16),
            pltpu.SemaphoreType.DMA((ranks,)), pltpu.SemaphoreType.DMA((ranks,)),
            pltpu.SemaphoreType.DMA,
        ]

    def load(self):
        return pltpu.make_async_copy(self.parts.at[self.rank], self.mine, self.local)

    def copy(self, k):
        to = lax.rem(self.rank + k, self.ranks)
        return remote(
            self.parts.at[to], self.land.at[k], self.send.at[k], self.recv.at[k], self.me, to
        )

    def step(self, k):
        for j in range(1, self.ranks):
            self.copy(j).start()
        self.load().start()

    def finish(self):
        self.load().wait()
        for j in range(1, self.ranks):
            self.copy(j).wait()
        slab = 16

        @pl.loop(0, self.out.shape[0] // slab)
        def _(i):
            at = pl.ds(pl.multiple_of(i * slab, slab), slab)
            total = self.mine[at].astype(f32)
            for j in range(1, self.ranks):
                total = total + self.land[j, at].astype(f32)
            self.out[at] = total


def run_all(jobs):
    for k in range(max(job.steps for job in jobs)):
        for job in jobs:
            if k < job.steps:
                job.step(k)
    for job in jobs:
        job.finish()


def params(number):
    return pltpu.CompilerParams(
        collective_id=number, has_side_effects=True, vmem_limit_bytes=VMEM_BYTES
    )


ANY = pl.BlockSpec(memory_space=pl.ANY)
ONCHIP = pl.BlockSpec(memory_space=pltpu.VMEM)


def gather_kernel(chips, ranks, line, tensor, *refs):
    n = line + tensor
    ins, outs, rest = refs[:n], refs[n : 2 * n], refs[2 * n :]
    greet(chips, ranks)
    jobs = []
    for i in range(n):
        cls, size = (LineGather, chips) if i < line else (TensorGather, ranks)
        jobs.append(cls(ins[i], outs[i], *rest[3 * i : 3 * i + 3], size))
    run_all(jobs)


def gather(number, chips, ranks, line, tensor):
    arrays = list(line) + list(tensor)
    scratch = []
    shapes = []
    for i, v in enumerate(arrays):
        cls, size, count = (
            (LineGather, chips, 2 * chips) if i < len(line) else (TensorGather, ranks, ranks)
        )
        scratch += cls.scratch(size)
        shapes.append(jax.ShapeDtypeStruct((count,) + v.shape, v.dtype))
    return pl.pallas_call(
        functools.partial(gather_kernel, chips, ranks, len(line), len(tensor)),
        in_specs=[ANY] * len(arrays),
        out_specs=[ANY] * len(arrays),
        out_shape=shapes,
        scratch_shapes=scratch,
        compiler_params=params(number),
        name="gather",
    )(*arrays)


def scatter_kernel(chips, ranks, line, tensor, *refs):
    n = line + tensor
    ins, outs, rest = refs[:n], refs[n : 2 * n], list(refs[2 * n :])
    greet(chips, ranks)
    jobs = []
    for i in range(n):
        cls, size, take = (LineScatter, chips, 7) if i < line else (TensorScatter, ranks, 5)
        jobs.append(cls(ins[i], outs[i], *rest[:take], size))
        rest = rest[take:]
    if line:
        jobs[0].steps = chips
    run_all(jobs)


def scatter(number, chips, ranks, line, tensor):
    arrays = list(line) + list(tensor)
    scratch = []
    shapes = []
    for i, v in enumerate(arrays):
        cls, size = (LineScatter, chips) if i < len(line) else (TensorScatter, ranks)
        scratch += cls.scratch(size, v.shape[1:])
        shapes.append(jax.ShapeDtypeStruct(v.shape[1:], f32))
    return pl.pallas_call(
        functools.partial(scatter_kernel, chips, ranks, len(line), len(tensor)),
        in_specs=[ANY] * len(arrays),
        out_specs=[ONCHIP] * len(arrays),
        out_shape=shapes,
        scratch_shapes=scratch,
        compiler_params=params(number),
        name="scatter",
    )(*arrays)


def sum_kernel(chips, ranks, shared, own_ref, out_ref, land, land_r, send, recv, send_r, recv_r):
    chip, core, rank = place()
    me = chip * 2 + core
    devices = 2 * chips
    sem = pltpu.get_barrier_semaphore()
    for k in range(1, devices):
        pl.semaphore_signal(
            sem, inc=1, device_id=(lax.rem(me + k, devices), rank), device_id_type=MESH
        )
    for k in range(1, ranks):
        pl.semaphore_signal(
            sem, inc=1, device_id=(me, lax.rem(rank + k, ranks)), device_id_type=MESH
        )
    pl.semaphore_wait(sem, devices + ranks - 2)
    first = [
        remote(own_ref, land.at[me], send.at[k], recv.at[k], lax.rem(me + k, devices), rank)
        for k in range(1, devices)
    ]
    for copy in first:
        copy.start()
    land[me] = own_ref[...]
    for copy in first:
        copy.wait_recv()
    total = land[0]
    for k in range(1, devices):
        total = total + land[k]
    land_r[rank] = total
    second = [
        remote(
            land_r.at[rank], land_r.at[rank], send_r.at[k], recv_r.at[k], me,
            lax.rem(rank + k, ranks),
        )
        for k in range(1, ranks)
    ]
    for copy in second:
        copy.start()
    for copy in first:
        copy.wait_send()
    for copy in second:
        copy.wait()
    whole = land_r[0, :shared]
    for r in range(1, ranks):
        whole = whole + land_r[r, :shared]
    for r in range(ranks):
        out_ref[r, :shared] = whole
        out_ref[r, shared:] = land_r[r, shared:]


def small_sums(number, chips, ranks, pack, shared):
    shape = pack.shape
    return pl.pallas_call(
        functools.partial(sum_kernel, chips, ranks, shared),
        in_specs=[ONCHIP],
        out_specs=ONCHIP,
        out_shape=jax.ShapeDtypeStruct((ranks,) + shape, f32),
        scratch_shapes=[
            pltpu.VMEM((2 * chips,) + shape, f32),
            pltpu.VMEM((ranks,) + shape, f32),
            pltpu.SemaphoreType.DMA((2 * chips,)),
            pltpu.SemaphoreType.DMA((2 * chips,)),
            pltpu.SemaphoreType.DMA((ranks,)),
            pltpu.SemaphoreType.DMA((ranks,)),
        ],
        compiler_params=params(number),
        name="small_sums",
    )(pack)


def scan_gather_kernel(blocks, total, chips, ranks, line, tensor, *refs):
    n = line + tensor
    own, ins = refs[:9], refs[9 : 9 + n]
    outs, slots = refs[9 + n : 11 + n], refs[11 + n : 11 + 2 * n]
    scratch, rest = refs[11 + 2 * n : 15 + 2 * n], refs[15 + 2 * n :]
    now = pl.program_id(0) * blocks + pl.program_id(1)

    @pl.when(now == 0)
    def _():
        greet(chips, ranks)

    jobs = []
    for i in range(n):
        cls, size = (LineGather, chips) if i < line else (TensorGather, ranks)
        jobs.append(cls(ins[i], slots[i], *rest[3 * i : 3 * i + 3], size))

    @pl.when(now == 0)
    def _():
        for job in jobs:
            job.step(0)

    scan_fwd_kernel(blocks, *own, *outs, *scratch)

    @pl.when(now == total - 1)
    def _():
        most = max(job.steps for job in jobs)
        for k in range(1, most):
            for job in jobs:
                if k < job.steps:
                    job.step(k)
        for job in jobs:
            job.finish()


def scan_forward_gather(
    number, chips, ranks, line, tensor, x, bc, st, seg, tapx, tapbc, par, spread, skip, nseq
):
    tokens, width = x.shape
    n = BLOCK
    blocks = tokens // nseq // n
    at = lambda s, i: (s * blocks + i, 0)
    whole = lambda s, i: (0, 0)
    states = LANES
    arrays = list(line) + list(tensor)
    sems, shapes = [], []
    for i, v in enumerate(arrays):
        cls, size, count = (
            (LineGather, chips, 2 * chips) if i < len(line) else (TensorGather, ranks, ranks)
        )
        sems += cls.scratch(size)
        shapes.append(jax.ShapeDtypeStruct((count,) + v.shape, v.dtype))
    return pl.pallas_call(
        functools.partial(
            scan_gather_kernel, blocks, nseq * blocks, chips, ranks, len(line), len(tensor)
        ),
        grid=(nseq, blocks),
        in_specs=[
            pl.BlockSpec((n, width), at),
            pl.BlockSpec((n, 2 * states), at),
            pl.BlockSpec((n, LANES), at),
            pl.BlockSpec((n, LANES), at),
            pl.BlockSpec(tapx.shape, whole),
            pl.BlockSpec(tapbc.shape, whole),
            pl.BlockSpec(par.shape, whole),
            pl.BlockSpec(spread.shape, whole),
            pl.BlockSpec(skip.shape, whole),
        ]
        + [ANY] * len(arrays),
        out_specs=[pl.BlockSpec((n, width), at), pl.BlockSpec((states, width), at)]
        + [ANY] * len(arrays),
        out_shape=[
            jax.ShapeDtypeStruct((tokens, width), f32),
            jax.ShapeDtypeStruct((tokens // n * states, width), bf16),
        ]
        + shapes,
        scratch_shapes=[
            pltpu.VMEM((states, width), f32),
            pltpu.VMEM((8, width), f32),
            pltpu.VMEM((8, 2 * states), f32),
            pltpu.VMEM((8, LANES), jnp.int32),
        ]
        + sems,
        compiler_params=params(number),
        name="scan_forward",
    )(x, bc, st, seg, tapx, tapbc, par, spread, skip, *arrays)


def scan_scatter_kernel(blocks, total, chips, ranks, line, *refs):
    ins = refs[:15]
    parts, near = refs[15 : 15 + line], refs[15 + line]
    refs = refs[16 + line :]
    outs, refs = refs[:6], refs[6:]
    sums, near_sum, gbc_slots = refs[:line], refs[line], refs[line + 1]
    refs = refs[line + 2 :]
    scratch, gbc_own, refs = refs[:4], refs[4], refs[5:]
    now = pl.program_id(0) * blocks + pl.program_id(1)

    @pl.when(now == 0)
    def _():
        greet(chips, ranks)

    jobs = []
    for i in range(line):
        jobs.append(LineScatter(parts[i], sums[i], *refs[7 * i : 7 * i + 7], chips))
    refs = refs[7 * line :]
    across = TensorScatter(near, near_sum, *refs[:5], ranks)
    around = TensorGather(gbc_own, gbc_slots, *refs[5:], ranks)

    @pl.when(now == 0)
    def _():
        across.step(0)
        for job in jobs:
            job.step(0)

    @pl.when(now == 1)
    def _():
        for job in jobs:
            job.step(1)

    for k in range(2, chips):
        if 2 * k < total - 1:
            @pl.when(now == 2 * k)
            def _():
                jobs[0].step(k)

    scan_bwd_kernel(blocks, *ins, *outs, *scratch)
    row = pl.multiple_of(
        (pl.program_id(0) * blocks + blocks - 1 - pl.program_id(1)) * BLOCK, BLOCK
    )
    gbc_own[pl.ds(row, BLOCK), :] = outs[1][...].astype(bf16)

    @pl.when(now == total - 1)
    def _():
        around.step(0)
        for k in range(2, chips):
            for i, job in enumerate(jobs):
                if i > 0 or 2 * k >= total - 1:
                    job.step(k)
        across.finish()
        around.step(1)
        around.finish()
        for job in jobs:
            job.finish()


def scan_backward_scatter(
    number, chips, ranks, line, near,
    x, bc, st, seg, gy, y, h, tapx, tapbc, par, spread, skip, nseq,
):
    tokens, width = x.shape
    n = BLOCK
    blocks = tokens // nseq // n
    at = lambda s, i: (s * blocks + blocks - 1 - i, 0)
    tail = lambda s, i: (jnp.maximum((s * blocks + blocks - 1 - i) * (n // 8) - 1, 0), 0)
    whole = lambda s, i: (0, 0)
    states = LANES
    sems = []
    for v in line:
        sems += LineScatter.scratch(chips, v.shape[1:])
    sems += TensorScatter.scratch(ranks, near.shape[1:])
    sems += TensorGather.scratch(ranks)
    return pl.pallas_call(
        functools.partial(scan_scatter_kernel, blocks, nseq * blocks, chips, ranks, len(line)),
        grid=(nseq, blocks),
        in_specs=[
            pl.BlockSpec((n, width), at),
            pl.BlockSpec((8, width), tail),
            pl.BlockSpec((n, 2 * states), at),
            pl.BlockSpec((8, 2 * states), tail),
            pl.BlockSpec((n, LANES), at),
            pl.BlockSpec((n, LANES), at),
            pl.BlockSpec((8, LANES), tail),
            pl.BlockSpec((n, width), at),
            pl.BlockSpec((n, width), at),
            pl.BlockSpec((states, width), at),
            pl.BlockSpec(tapx.shape, whole),
            pl.BlockSpec(tapbc.shape, whole),
            pl.BlockSpec(par.shape, whole),
            pl.BlockSpec(spread.shape, whole),
            pl.BlockSpec(skip.shape, whole),
        ]
        + [ANY] * (len(line) + 1),
        out_specs=[
            pl.BlockSpec((n, width), at),
            pl.BlockSpec((n, 2 * states), at),
            pl.BlockSpec((n, LANES), at),
            pl.BlockSpec((40, width), whole),
            pl.BlockSpec((40, 2 * states), whole),
            pl.BlockSpec((24, LANES), whole),
        ]
        + [pl.BlockSpec(v.shape[1:], whole) for v in line]
        + [pl.BlockSpec(near.shape[1:], whole), ANY],
        out_shape=[
            jax.ShapeDtypeStruct((tokens, width), bf16),
            jax.ShapeDtypeStruct((tokens, 2 * states), f32),
            jax.ShapeDtypeStruct((tokens, LANES), bf16),
            jax.ShapeDtypeStruct((40, width), f32),
            jax.ShapeDtypeStruct((40, 2 * states), f32),
            jax.ShapeDtypeStruct((24, LANES), f32),
        ]
        + [jax.ShapeDtypeStruct(v.shape[1:], f32) for v in line]
        + [
            jax.ShapeDtypeStruct(near.shape[1:], f32),
            jax.ShapeDtypeStruct((ranks, tokens, 2 * states), bf16),
        ],
        scratch_shapes=[
            pltpu.VMEM((states, width), f32),
            pltpu.VMEM((8, width), f32),
            pltpu.VMEM((8, 2 * states), f32),
            pltpu.VMEM((8, LANES), jnp.int32),
            pltpu.VMEM((tokens, 2 * states), bf16),
        ]
        + sems,
        compiler_params=params(number),
        name="scan_backward",
    )(x, x, bc, bc, st, seg, seg, gy, y, h, tapx, tapbc, par, spread, skip, *line, near)


epsilon = 1e-05


def per_device(
    residual, segment_ids, norm_gain, inner_weight, state_weight, step_weight, conv_weight,
    conv_bias, step_bias, decay_log, skip_gain, gated_gain, out_weight, cotangent,
):
    rank = lax.axis_index("tensor")
    model_width = residual.shape[1]
    width = inner_weight.shape[2]
    heads = step_weight.shape[1]
    inner_width = gated_gain.shape[0]
    nseq, length = segment_ids.shape
    tokens = nseq * length
    inner_start, head_start = rank * width, rank * heads
    stream = residual.astype(f32)
    scaling = lax.rsqrt(jnp.mean(stream * stream, axis=1, keepdims=True) + epsilon)
    normed = (stream * scaling * norm_gain).astype(bf16)
    chips, ranks = lax.axis_size("dp") // 2, lax.axis_size("tensor")
    wx_own = jnp.concatenate([inner_weight[:, 1], on_lanes(step_weight)], axis=1)
    wx, normed_all = gather(1, chips, ranks, [wx_own], [normed])
    wx, normed_all = wx.reshape(model_width, width + LANES), normed_all.reshape(tokens, model_width)
    taps = jnp.concatenate([conv_weight, conv_bias[None], jnp.zeros((3, conv_bias.shape[0]), f32)], axis=0)
    tapx = lax.dynamic_slice_in_dim(taps, inner_start, width, 1)
    tapbc = taps[:, inner_width:]
    local = lambda v: lax.dynamic_slice_in_dim(v, head_start, heads, 0)
    rates = -jnp.exp(local(decay_log))
    par = jnp.concatenate(
        [on_lanes(local(step_bias)[None]), on_lanes(rates[None]), jnp.zeros((6, LANES), f32)], axis=0
    )
    skip = jnp.broadcast_to(jnp.repeat(local(skip_gain), WIDTH)[None], (8, width))
    gain = lax.dynamic_slice_in_dim(gated_gain, inner_start, width, 0)
    spread = spread_matrix(heads)
    seg = jnp.broadcast_to(segment_ids.reshape(tokens, 1), (tokens, LANES))

    xst = mm(normed_all, wx)
    bc = mm(normed_all, state_weight)
    x, st = xst[:, :width], xst[:, width:]
    y, h, wz, wo, cot_all = scan_forward_gather(
        2, chips, ranks, [inner_weight[:, 0], out_weight.T], [cotangent],
        x, bc, st, seg, tapx, tapbc, par, spread, skip, nseq,
    )
    wz, wo = wz.reshape(model_width, width), wo.reshape(model_width, width)
    cot_all = cot_all.reshape(tokens, model_width)
    z = mm(normed_all, wz)
    sig = jax.nn.sigmoid(z)
    silu = z * sig
    gated = y * silu
    gng = mm(cot_all, wo)
    sums = lax.psum(
        jnp.stack([jnp.sum(gated * gated, axis=1), jnp.sum(gng * gain * gated, axis=1)]), "tensor"
    )
    scale_g = lax.rsqrt(sums[0] / inner_width + epsilon)[:, None]
    normed_g = (gated * scale_g * gain).astype(bf16)
    grad_gated = scale_g * gain * gng - gated * (scale_g**3 * sums[1][:, None] / inner_width)
    gain_grad = jnp.sum(gng * gated * scale_g, axis=0)
    gz = (grad_gated * y * (sig * (1.0 + z * (1.0 - sig)))).astype(bf16)
    gy = grad_gated * silu
    devices = 2 * chips
    parts = lambda v, count: v.astype(bf16).reshape(count, v.shape[0] // count, v.shape[1])
    gx, _, gst, gtapx, gtapbc, gpar, z_grad, out_grad, projected, gbc = scan_backward_scatter(
        3, chips, ranks,
        [parts(mm_tn(normed_all, gz), devices), parts(mm_tn(cot_all, normed_g), devices)],
        parts(mm_nt(normed_g, wo), ranks),
        x, bc, st, seg, gy, y, h, tapx, tapbc, par, spread, skip, nseq,
    )
    block_out = stream + projected
    gbc_own = lax.dynamic_index_in_dim(gbc, rank, 0, keepdims=False)
    gbc = jnp.sum(gbc.astype(f32), axis=0).astype(bf16)
    low = lax.broadcasted_iota(jnp.int32, (1, LANES), 1) < LANES // 2
    gst = jnp.where(low, gst, 0)
    gxs = jnp.concatenate([gx, gst], axis=1)
    depth = model_width // ranks
    rows = lax.dynamic_slice_in_dim(normed_all, rank * depth, depth, 1)
    per = depth * state_weight.shape[1] // model_width
    state_part = jnp.pad(
        mm_tn(rows, gbc).astype(bf16).reshape(model_width, per), ((0, 0), (LANES // 2, LANES // 2 - per))
    )
    grads = mm_tn(normed_all, gxs).astype(bf16)
    grads = jnp.concatenate([grads[:, :width], grads[:, width:] + state_part], axis=1)
    total = mm_nt(gz, wz) + mm_nt(gxs, wx) + mm_nt(gbc_own, state_weight)
    x_grad, grad_normed = scatter(
        4, chips, ranks, [parts(grads, devices)], [parts(total, ranks)]
    )
    own_state = x_grad[:, width + LANES // 2 : width + LANES // 2 + per]
    own_state = own_state.astype(bf16).reshape(depth // devices, state_weight.shape[1])
    state_grad = lax.all_gather(own_state, ("tensor", "dp"), axis=0, tiled=True).astype(f32)
    gtapx = gtapx.reshape(5, 8, -1).sum(1)
    gtapbc = gtapbc.reshape(5, 8, -1).sum(1)
    gpar = gpar.reshape(3, 8, -1).sum(1)[:, :heads]
    norm_grad = jnp.sum(grad_normed * stream * scaling, axis=0)
    flat = lambda v: v.reshape(-1, LANES)
    mine = [gtapx, gain_grad[None], jnp.pad(gpar, ((0, 5), (0, LANES - heads)))]
    ours = [norm_grad[None], gtapbc, jnp.zeros((3, 2 * LANES), f32)]
    shared = sum(v.size for v in ours) // LANES
    sums = small_sums(
        5, chips, ranks, jnp.concatenate([flat(v) for v in ours + mine], axis=0), shared
    )
    ours, mine = sums[0, :shared], sums[:, shared:]
    norm_grad = ours[: model_width // LANES].reshape(-1)
    gtapbc = ours[model_width // LANES :].reshape(8, -1)[:5]
    count = width // LANES
    gtapx = mine[:, : 5 * count].reshape(ranks, 5, width).transpose(1, 0, 2).reshape(5, inner_width)
    gain_grad = mine[:, 5 * count : 6 * count].reshape(inner_width)
    gpars = mine[:, 6 * count : 6 * count + 3, :heads].transpose(1, 0, 2).reshape(3, -1)
    gtaps = jnp.concatenate([gtapx, gtapbc], axis=1)
    along = jnp.sum(grad_normed * norm_gain * stream, axis=1, keepdims=True)
    residual_grad = (
        cotangent.astype(f32)
        + scaling * norm_gain * grad_normed
        - stream * (scaling**3 * along / model_width)
    )
    inner_grad = jnp.stack([z_grad, x_grad[:, :width]], axis=1)
    return (
        block_out, residual_grad, norm_grad, inner_grad, state_grad,
        x_grad[:, width : width + heads], gtaps[:4], gtaps[4], gpars[0], gpars[1], gpars[2],
        gain_grad, out_grad.T,
    )


def solution(mesh):
    rows, both = P("dp", "tensor"), P(("dp", "tensor"), None)
    inner, out = P("dp", None, "tensor"), P("tensor", "dp")
    return jax.shard_map(
        per_device,
        mesh=mesh,
        in_specs=(
            both, P("dp", None), P(), inner, P(), rows, P(), P(), P(), P(), P(), P(), out, both,
        ),
        out_specs=(both, both, P(), inner, P(), rows, P(), P(), P(), P(), P(), P(), out),
        check_vma=False,
    )
```

```python
import functools
import jax
import jax.numpy as jnp
from jax import lax
from jax.experimental import pallas as pl
from jax.experimental.pallas import tpu as pltpu
from jax.sharding import PartitionSpec as P

LANES = 128
BLOCK = 128
WIDTH = 64
VMEM_BYTES = 56 * 1024 * 1024
f32, bf16 = jnp.float32, jnp.bfloat16
ROWS0 = (((0,), (0,)), ((), ()))
COLS1 = (((1,), (1,)), ((), ()))


def mm(a, b):
    return jnp.dot(a, b, preferred_element_type=f32)


def mm_tn(a, b):
    return lax.dot_general(a, b, ROWS0, preferred_element_type=f32)


def mm_nt(a, b):
    return lax.dot_general(a, b, COLS1, preferred_element_type=f32)


def sigmoid(v):
    return 0.5 + 0.5 * jnp.tanh(0.5 * v)


def two_parts(v, low_lanes):
    high = v.astype(bf16)
    return jnp.where(low_lanes, (v - high.astype(f32)).astype(bf16), high)


def head_sums(v, spread):
    high = v.astype(bf16)
    low = (v - high.astype(f32)).astype(bf16)
    return mm_nt(high, spread) + mm_nt(low, spread)


def shifted_masks(seg_ext, seg):
    n = seg.shape[0]
    return [None] + [seg_ext[8 - k : 8 - k + n] == seg for k in (1, 2, 3)]


def convolve(tail, part, masks, taps):
    n = part.shape[0]
    ext = jnp.concatenate([tail, part], axis=0)
    shifts = [part] + [
        jnp.where(masks[k], ext[8 - k : 8 - k + n], 0.0) for k in (1, 2, 3)
    ]
    total = taps[4:5] + taps[3:4] * part
    for k in (1, 2, 3):
        total = total + taps[3 - k : 4 - k] * shifts[k]
    return total, shifts


def wide(v):
    return jnp.concatenate([v, v], axis=1)


def step_state(raw, params, seg, prev_seg, end_seg, n):
    row = lax.broadcasted_iota(jnp.int32, (n, n), 0)
    col = lax.broadcasted_iota(jnp.int32, (n, n), 1)
    v = raw + params[0:1]
    dt = jnp.maximum(v, 0.0) + jnp.log1p(jnp.exp(-jnp.abs(v)))
    a = params[1:2]
    cum = jnp.dot(
        (row >= col).astype(f32), dt * a, precision=lax.Precision.HIGHEST, preferred_element_type=f32
    )
    last = cum[n - 1 : n]
    into = jnp.where(seg == prev_seg, jnp.exp(cum), 0.0)
    onto = jnp.where(seg == end_seg, jnp.exp(last - cum), 0.0)
    through = jnp.where(end_seg == prev_seg, jnp.exp(last), 0.0)
    bias = jnp.where((row >= col) & (seg == jnp.transpose(seg)), 0.0, -1e30)
    return v, dt, a, cum, into, onto, through, bias


def scan_fwd_kernel(
    blocks, x_ref, bc_ref, st_ref, seg_ref, tapx_ref, tapbc_ref, par_ref, spread_ref, skip_ref,
    y_ref, h_ref, state, tail_x, tail_bc, tail_seg,
):
    n = BLOCK
    block = pl.program_id(1)

    @pl.when(block == 0)
    def _():
        state[...] = jnp.zeros_like(state)
        tail_x[...] = jnp.zeros_like(tail_x)
        tail_bc[...] = jnp.zeros_like(tail_bc)
        tail_seg[...] = jnp.full_like(tail_seg, -1)

    seg = seg_ref[...]
    masks = shifted_masks(jnp.concatenate([tail_seg[...], seg], axis=0), seg)
    prev_seg, end_seg = tail_seg[7:8], seg[n - 1 : n]
    v, dt, a, cum, into, onto, through, bias = step_state(
        st_ref[...], par_ref[...], seg, prev_seg, end_seg, n
    )
    cum_t = jnp.transpose(cum)
    low_lanes = lax.broadcasted_iota(jnp.int32, (n, LANES), 1) >= LANES // 2
    spread = spread_ref[...]
    dt_w = mm(two_parts(dt, low_lanes), spread)
    into_w = mm(two_parts(into, low_lanes), spread)
    onto_w = mm(two_parts(onto, low_lanes), spread)
    through_w = mm(two_parts(jnp.broadcast_to(through, (8, LANES)), low_lanes[:8]), spread)[0:1]
    bc_masks = [None] + [wide(m) for m in masks[1:]]
    conv_bc, _ = convolve(tail_bc[...], bc_ref[...], bc_masks, tapbc_ref[...])
    act_bc = conv_bc * sigmoid(conv_bc)
    b, c = act_bc[:, :LANES].astype(bf16), act_bc[:, LANES:].astype(bf16)
    cross = mm_nt(c, b)
    entering = state[...].astype(bf16)
    h_ref[...] = entering
    first_half = lax.broadcasted_iota(jnp.int32, (n, LANES), 1) < WIDTH
    for pair in range(x_ref.shape[1] // LANES):
        sl = slice(pair * LANES, (pair + 1) * LANES)
        conv, _ = convolve(tail_x[:, sl], x_ref[:, sl], masks, tapx_ref[:, sl])
        xs = conv * sigmoid(conv)
        xd = xs * dt_w[:, sl]
        outside = mm(c, entering[:, sl]) * into_w[:, sl]
        mixes = []
        for h in (2 * pair, 2 * pair + 1):
            decay = jnp.exp(cum[:, h : h + 1] - cum_t[h : h + 1, :] + bias)
            mixes.append((decay * cross).astype(bf16))
        stacked = jnp.concatenate(
            [jnp.where(first_half, xd, 0.0), jnp.where(first_half, 0.0, xd)], axis=0
        ).astype(bf16)
        inside = mm(jnp.concatenate(mixes, axis=1), stacked)
        y_ref[:, sl] = inside + outside + skip_ref[0:1, sl] * xs
        local = mm_tn(b, (onto_w[:, sl] * xd).astype(bf16))
        state[:, sl] = through_w[:, sl] * state[:, sl] + local
    tail_x[...] = x_ref[n - 8 :, :]
    tail_bc[...] = bc_ref[n - 8 :, :]
    tail_seg[...] = seg_ref[n - 8 :, :]


def fold(v):
    total = v[0:8]
    for r in range(8, v.shape[0], 8):
        total = total + v[r : r + 8]
    return total


def scan_bwd_kernel(
    blocks, x_ref, xt_ref, bc_ref, bct_ref, st_ref, seg_ref, segt_ref, gy_ref, y_ref, h_ref,
    tapx_ref, tapbc_ref, par_ref, spread_ref, skip_ref,
    gx_ref, gbc_ref, gst_ref, gtapx_ref, gtapbc_ref, gpar_ref,
    gstate, head_x, head_bc, head_seg,
):
    n = BLOCK
    step = pl.program_id(1)
    block = blocks - 1 - step

    @pl.when((step == 0) & (pl.program_id(0) == 0))
    def _():
        gtapx_ref[...] = jnp.zeros_like(gtapx_ref)
        gtapbc_ref[...] = jnp.zeros_like(gtapbc_ref)
        gpar_ref[...] = jnp.zeros_like(gpar_ref)

    @pl.when(step == 0)
    def _():
        gstate[...] = jnp.zeros_like(gstate)
        head_x[...] = jnp.zeros_like(head_x)
        head_bc[...] = jnp.zeros_like(head_bc)
        head_seg[...] = jnp.full_like(head_seg, -1)

    seg = seg_ref[...]
    first = block == 0
    seg_tail = jnp.where(first, -1, segt_ref[...])
    masks = shifted_masks(jnp.concatenate([seg_tail, seg], axis=0), seg)
    seg_next = jnp.concatenate([seg, head_seg[...]], axis=0)
    ahead = [None] + [seg_next[k : k + n] == seg for k in (1, 2, 3)]
    prev_seg, end_seg = seg_tail[7:8], seg[n - 1 : n]
    v, dt, a, cum, into, onto, through, bias = step_state(
        st_ref[...], par_ref[...], seg, prev_seg, end_seg, n
    )
    cum_t = jnp.transpose(cum)
    low_lanes = lax.broadcasted_iota(jnp.int32, (n, LANES), 1) >= LANES // 2
    spread = spread_ref[...]
    dt_w = mm(two_parts(dt, low_lanes), spread)
    into_w = mm(two_parts(into, low_lanes), spread)
    onto_w = mm(two_parts(onto, low_lanes), spread)
    through_w = mm(two_parts(jnp.broadcast_to(through, (8, LANES)), low_lanes[:8]), spread)[0:1]
    bc_masks = [None] + [wide(m) for m in masks[1:]]
    tail_bc = jnp.where(first, 0.0, bct_ref[...])
    conv_bc, shifts_bc = convolve(tail_bc, bc_ref[...], bc_masks, tapbc_ref[...])
    sig_bc = sigmoid(conv_bc)
    act_bc = conv_bc * sig_bc
    b, c = act_bc[:, :LANES].astype(bf16), act_bc[:, LANES:].astype(bf16)
    cross = mm_nt(c, b)
    first_half = lax.broadcasted_iota(jnp.int32, (n, LANES), 1) < WIDTH
    halves = lambda t: jnp.concatenate(
        [jnp.where(first_half, t, 0.0), jnp.where(first_half, 0.0, t)], axis=0
    ).astype(bf16)

    gcross = jnp.zeros((n, n), f32)
    gb = jnp.zeros((n, LANES), f32)
    gc = jnp.zeros((n, LANES), f32)
    sum_q = jnp.zeros((n, LANES), f32)
    sum_state = jnp.zeros((n, LANES), f32)
    sum_dt = jnp.zeros((n, LANES), f32)
    sum_skip = jnp.zeros((8, LANES), f32)
    sum_last = jnp.zeros((8, LANES), f32)
    for pair in range(x_ref.shape[1] // LANES):
        sl = slice(pair * LANES, (pair + 1) * LANES)
        tail_x = jnp.where(first, 0.0, xt_ref[:, sl])
        part = x_ref[:, sl]
        taps = tapx_ref[:, sl]
        conv, shifts = convolve(tail_x, part, masks, taps)
        sig = sigmoid(conv)
        xs = conv * sig
        xd = xs * dt_w[:, sl]
        xd_low = xd.astype(bf16)
        gy = gy_ref[:, sl]
        gy_low = gy.astype(bf16)
        skip = skip_ref[0:1, sl]
        inner = y_ref[:, sl] - skip * xs
        spread_p = spread[:, sl]
        gstate_low = gstate[:, sl].astype(bf16)
        before = h_ref[:, sl]
        gy_into = (gy * into_w[:, sl]).astype(bf16)
        xd_onto = (xd * onto_w[:, sl]).astype(bf16)
        gc = gc + mm_nt(gy_into, before)
        gb = gb + mm_nt(xd_onto, gstate_low)
        g_state = onto_w[:, sl] * mm(b, gstate_low)
        sum_last = sum_last + head_sums(
            fold(gstate[:, sl] * (through_w[:, sl] * before.astype(f32))), spread_p
        )
        gstate[:, sl] = through_w[:, sl] * gstate[:, sl] + mm_tn(c, gy_into)
        gy_halves = halves(gy)
        gmix = mm_nt(gy_halves, xd_low)
        mixes = []
        for i, h in enumerate((2 * pair, 2 * pair + 1)):
            decay = jnp.exp(cum[:, h : h + 1] - cum_t[h : h + 1, :] + bias)
            mixes.append((decay * cross).astype(bf16))
            gcross = gcross + decay * gmix[i * n : (i + 1) * n]
        g_inside = mm_tn(jnp.concatenate(mixes, axis=0), gy_halves)
        gxd = g_inside + g_state
        xd_r, gy_r = xd_low.astype(f32), gy_low.astype(f32)
        sum_q = sum_q + head_sums(gy_r * inner - xd_r * gxd, spread_p)
        sum_state = sum_state + head_sums(xd_r * g_state, spread_p)
        sum_dt = sum_dt + head_sums(xs * gxd, spread_p)
        sum_skip = sum_skip + head_sums(fold(gy * xs), spread_p)
        gxs = dt_w[:, sl] * gxd + skip * gy
        gconv = gxs * (sig * (1.0 + conv * (1.0 - sig)))
        ext = jnp.concatenate([gconv, head_x[:, sl]], axis=0)
        gu = taps[3:4] * gconv
        for k in (1, 2, 3):
            gu = gu + taps[3 - k : 4 - k] * jnp.where(ahead[k], ext[k : k + n], 0.0)
        gx_ref[:, sl] = gu.astype(bf16)
        for k in range(4):
            row = 8 * (3 - k)
            gtapx_ref[row : row + 8, sl] += fold(gconv * shifts[k])
        gtapx_ref[32:40, sl] += fold(gconv)
        head_x[:, sl] = gconv[0:8]
    gcross_low = gcross.astype(bf16)
    gc = gc + mm(gcross_low, b)
    gb = gb + mm_tn(gcross_low, c)
    gconv = jnp.concatenate([gb, gc], axis=1) * (sig_bc * (1.0 + conv_bc * (1.0 - sig_bc)))
    ext = jnp.concatenate([gconv, head_bc[...]], axis=0)
    taps = tapbc_ref[...]
    gu = taps[3:4] * gconv
    for k in (1, 2, 3):
        gu = gu + taps[3 - k : 4 - k] * jnp.where(wide(ahead[k]), ext[k : k + n], 0.0)
    gbc_ref[...] = gu.astype(gbc_ref.dtype)
    for k in range(4):
        row = 8 * (3 - k)
        gtapbc_ref[row : row + 8, :] += fold(gconv * shifts_bc[k])
    gtapbc_ref[32:40, :] += fold(gconv)
    head_bc[...] = gconv[0:8]
    head_seg[...] = seg[0:8]
    rows = lax.broadcasted_iota(jnp.int32, (n, n), 0)
    cols = lax.broadcasted_iota(jnp.int32, (n, n), 1)
    after = jnp.dot(
        (cols >= rows).astype(f32), sum_q, precision=lax.Precision.HIGHEST, preferred_element_type=f32
    )
    edge = jnp.sum(sum_state, axis=0, keepdims=True) + jnp.sum(sum_last, axis=0, keepdims=True)
    glog = after + edge
    gdt = sum_dt + a * glog
    gst = gdt * sigmoid(v)
    gst_ref[...] = jnp.where(low_lanes, 0.0, gst).astype(bf16)
    gpar_ref[0:8] += fold(gst)
    gpar_ref[8:16] += fold(a * dt * glog)
    gpar_ref[16:24] += sum_skip


def spread_matrix(heads):
    row = lax.broadcasted_iota(jnp.int32, (LANES, heads * WIDTH), 0)
    col = lax.broadcasted_iota(jnp.int32, (LANES, heads * WIDTH), 1)
    return (row % (LANES // 2) == col // WIDTH).astype(bf16)


def on_lanes(v):
    half = jnp.pad(v, [(0, 0)] * (v.ndim - 1) + [(0, LANES // 2 - v.shape[-1])])
    return jnp.concatenate([half, half], axis=-1)


MESH = pl.DeviceIdType.MESH


def place():
    dp, rank = lax.axis_index("dp"), lax.axis_index("tensor")
    return dp // 2, dp % 2, rank


def remote(src, dst, send, recv, dp, rank):
    return pltpu.make_async_remote_copy(
        src_ref=src, dst_ref=dst, send_sem=send, recv_sem=recv, device_id=(dp, rank),
        device_id_type=MESH,
    )


def greet(chips, ranks):
    chip, core, rank = place()
    sem = pltpu.get_barrier_semaphore()
    me = chip * 2 + core

    def signal(dp, r):
        pl.semaphore_signal(sem, inc=1, device_id=(dp, r), device_id_type=MESH)

    signal(chip * 2 + 1 - core, rank)
    for step in (1, -1):
        @pl.when((chip + step >= 0) & (chip + step < chips))
        def _():
            signal(me + 2 * step, rank)
    for k in range(1, ranks):
        signal(me, lax.rem(rank + k, ranks))
    pl.semaphore_wait(sem, ranks + (chip + chips - 1) // chips + (2 * chips - 2 - chip) // chips)


def greet_all(chips, ranks):
    chip, core, rank = place()
    sem = pltpu.get_barrier_semaphore()
    me, devices = chip * 2 + core, 2 * chips
    for k in range(1, devices):
        pl.semaphore_signal(
            sem, inc=1, device_id=(lax.rem(me + k, devices), rank), device_id_type=MESH
        )
    for k in range(1, ranks):
        pl.semaphore_signal(
            sem, inc=1, device_id=(me, lax.rem(rank + k, ranks)), device_id_type=MESH
        )
    pl.semaphore_wait(sem, devices + ranks - 2)


def slab(ref, index, rows):
    return ref.at[pl.ds(pl.multiple_of(index * rows, rows), rows)]


class LineGather:
    def __init__(self, own, slots, send, recv, local, chips):
        self.own, self.slots, self.send, self.recv, self.local = own, slots, send, recv, local
        self.chips, self.rows = chips, own.shape[0]
        self.chip, self.core, self.rank = place()
        self.me = self.chip * 2 + self.core
        self.partner = self.chip * 2 + 1 - self.core
        self.steps = chips

    @staticmethod
    def scratch(chips):
        n = 2 * chips
        return [
            pltpu.SemaphoreType.DMA((3, n)), pltpu.SemaphoreType.DMA((n,)), pltpu.SemaphoreType.DMA,
        ]

    def copy(self, way, origin, src=None):
        target = (self.me + 2, self.me - 2, self.partner)[way]
        slot = slab(self.slots, origin, self.rows)
        return remote(
            slot if src is None else src, slot, self.send.at[way, origin], self.recv.at[origin],
            target, self.rank,
        )

    def pass_on(self, way, origin, src=None, wait=False):
        def go():
            copy = self.copy(way, origin, src)
            copy.wait_send() if wait else copy.start()

        if way == 0:
            pl.when(self.chip + 1 < self.chips)(go)
        elif way == 1:
            pl.when(self.chip > 0)(go)
        else:
            go()

    def keep(self):
        return pltpu.make_async_copy(self.own, slab(self.slots, self.me, self.rows), self.local)

    def sides(self, k):
        return ((0, self.chip - k >= 0, -k), (1, self.chip + k < self.chips, k))

    def step(self, k):
        if k == 0:
            for way in (0, 1, 2):
                self.pass_on(way, self.me, self.own)
            self.keep().start()
            return
        for way, there, shift in self.sides(k):
            @pl.when(there)
            def _():
                origin = self.me + 2 * shift
                self.copy(2, origin).wait_recv()
                self.pass_on(way, origin)
                self.pass_on(2, origin)

    def arrive(self, k, use=None):
        if k == 0:
            self.keep().wait()
            self.copy(2, self.partner).wait_recv()
            if use is not None:
                use(self.chip)
            return
        for way, there, shift in self.sides(k):
            @pl.when(there)
            def _():
                self.copy(2, self.partner + 2 * shift).wait_recv()
                if use is not None:
                    use(self.chip + shift)

    def sent(self):
        for way in (0, 1, 2):
            self.pass_on(way, self.me, self.own, wait=True)
        for k in range(1, self.chips):
            for way, there, shift in self.sides(k):
                @pl.when(there)
                def _():
                    origin = self.me + 2 * shift
                    self.pass_on(way, origin, wait=True)
                    self.pass_on(2, origin, wait=True)

    def finish(self):
        for k in range(self.chips):
            self.arrive(k)
        self.sent()


class TensorGather:
    def __init__(self, own, slots, send, recv, local, ranks):
        self.own, self.slots, self.send, self.recv, self.local = own, slots, send, recv, local
        self.ranks, self.rows = ranks, own.shape[0]
        chip, core, self.rank = place()
        self.me = chip * 2 + core
        self.steps = 2

    @staticmethod
    def scratch(ranks):
        return [
            pltpu.SemaphoreType.DMA((ranks,)), pltpu.SemaphoreType.DMA((ranks,)), pltpu.SemaphoreType.DMA,
        ]

    def near(self, k):
        x = self.rank % 2
        y = self.rank // 2
        across = (y * 2 + 1 - x, (1 - y) * 2 + x)
        if k < 2:
            return remote(
                self.own, slab(self.slots, self.rank, self.rows), self.send.at[k], self.recv.at[k],
                self.me, across[k],
            )
        half = slab(self.slots, across[k - 2] * 2 + (k - 2), self.rows // 2)
        return remote(half, half, self.send.at[k], self.recv.at[k], self.me, across[3 - k])

    def direct(self, k):
        return remote(
            self.own, slab(self.slots, self.rank, self.rows), self.send.at[k], self.recv.at[k],
            self.me, lax.rem(self.rank + k, self.ranks),
        )

    def keep(self):
        return pltpu.make_async_copy(self.own, slab(self.slots, self.rank, self.rows), self.local)

    def step(self, k):
        if k == 0:
            if self.ranks == 4:
                self.near(0).start()
                self.near(1).start()
            else:
                for j in range(1, self.ranks):
                    self.direct(j).start()
            self.keep().start()
        elif self.ranks == 4:
            for j in (0, 1):
                self.near(j).wait_recv()
                self.near(2 + j).start()

    def finish(self):
        self.keep().wait()
        if self.ranks == 4:
            for j in (0, 1):
                self.near(j).wait_send()
                self.near(2 + j).wait()
        else:
            for j in range(1, self.ranks):
                self.direct(j).wait()


def add_rows(target, others, out=None):
    out = target if out is None else out
    rows = target.shape[0]
    some = 32 if rows % 32 == 0 else 16 if rows % 16 == 0 else 8

    @pl.loop(0, rows // some)
    def _(i):
        at = pl.ds(pl.multiple_of(i * some, some), some)
        total = target[at].astype(f32)
        for other in others:
            total = total + other[at].astype(f32)
        out[at] = total.astype(out.dtype)


class LineScatter:
    def __init__(self, parts, out, mine, swap, up, down, send, recv, local, chips):
        self.parts, self.out, self.mine, self.swap, self.up, self.down = parts, out, mine, swap, up, down
        self.send, self.recv, self.local, self.chips = send, recv, local, chips
        self.rows = parts.shape[0] // (2 * chips)
        self.chip, self.core, self.rank = place()
        self.me = self.chip * 2 + self.core
        self.partner = self.chip * 2 + 1 - self.core
        self.steps = chips

    @staticmethod
    def scratch(chips, shape, dtype=bf16):
        block = (chips, shape[0] // (2 * chips)) + tuple(shape[1:])
        return [pltpu.VMEM(block, dtype)] * 4 + [
            pltpu.SemaphoreType.DMA((3, chips)), pltpu.SemaphoreType.DMA((3, chips)),
            pltpu.SemaphoreType.DMA((chips,)),
        ]

    def order(self):
        n = self.chips
        return [c for k in range(n // 2) for c in (n - 1 - k, k)]

    def over(self, c):
        return remote(
            slab(self.parts, 2 * c + 1 - self.core, self.rows), self.swap.at[c], self.send.at[2, c],
            self.recv.at[2, c], self.partner, self.rank,
        )

    def load(self, c):
        return pltpu.make_async_copy(
            slab(self.parts, 2 * c + self.core, self.rows), self.mine.at[c], self.local.at[c]
        )

    def along(self, way, c, first=False):
        buffer = (self.up, self.down)[way]
        src = self.mine.at[c] if first else buffer.at[c]
        return remote(
            src, buffer.at[c], self.send.at[way, c], self.recv.at[way, c],
            self.me + (2, -2)[way], self.rank,
        )

    def step(self, k):
        n, chip = self.chips, self.chip
        if k == 0:
            for c in self.order():
                self.over(c).start()
                self.load(c).start()
            return
        if k == 1:
            for c in self.order():
                self.over(c).wait()
                self.load(c).wait()
                add_rows(self.mine.at[c], [self.swap.at[c]])

                @pl.when((chip == 0) & (c > 0))
                def _():
                    self.along(0, c, True).start()

                @pl.when((chip == n - 1) & (c < n - 1))
                def _():
                    self.along(1, c, True).start()
            return
        t = k - 1
        c = n - 1 - (t - chip)

        @pl.when((chip > 0) & (t >= chip) & (c > chip))
        def _():
            self.along(0, c).wait_recv()
            add_rows(self.up.at[c], [self.mine.at[c]])
            self.along(0, c).start()

        d = t - (n - 1 - chip)

        @pl.when((chip < n - 1) & (d >= 0) & (d < chip))
        def _():
            self.along(1, d).wait_recv()
            add_rows(self.down.at[d], [self.mine.at[d]])
            self.along(1, d).start()

    def finish(self):
        n, chip = self.chips, self.chip
        out, mine, up, down = self.out, self.mine.at[chip], self.up.at[chip], self.down.at[chip]

        @pl.when(chip == 0)
        def _():
            self.along(1, chip).wait_recv()
            add_rows(mine, [down], out)

        @pl.when(chip == n - 1)
        def _():
            self.along(0, chip).wait_recv()
            add_rows(mine, [up], out)

        @pl.when((chip > 0) & (chip < n - 1))
        def _():
            self.along(0, chip).wait_recv()
            self.along(1, chip).wait_recv()
            add_rows(mine, [up, down], out)

        for c in range(n):
            @pl.when((chip < n - 1) & (c > chip))
            def _():
                self.along(0, c).wait_send()

            @pl.when((chip > 0) & (c < chip))
            def _():
                self.along(1, c).wait_send()


class TensorScatter:
    def __init__(self, parts, land, send, recv, local, ranks):
        self.parts, self.land = parts, land
        self.send, self.recv, self.local, self.ranks = send, recv, local, ranks
        self.rows = parts.shape[0] // ranks
        chip, core, self.rank = place()
        self.me = chip * 2 + core
        self.steps = 1

    @staticmethod
    def scratch(ranks, shape):
        return [
            pltpu.VMEM((ranks, shape[0] // ranks, shape[1]), bf16),
            pltpu.SemaphoreType.DMA((ranks,)), pltpu.SemaphoreType.DMA((ranks,)),
            pltpu.SemaphoreType.DMA,
        ]

    def load(self):
        return pltpu.make_async_copy(
            slab(self.parts, self.rank, self.rows), self.land.at[0], self.local
        )

    def copy(self, k):
        to = lax.rem(self.rank + k, self.ranks)
        return remote(
            slab(self.parts, to, self.rows), self.land.at[k], self.send.at[k], self.recv.at[k],
            self.me, to,
        )

    def step(self, k):
        for j in range(1, self.ranks):
            self.copy(j).start()
        self.load().start()

    def arrive(self):
        self.load().wait()
        for j in range(1, self.ranks):
            self.copy(j).wait()

    def total(self, at):
        total = self.land[0, at].astype(f32)
        for j in range(1, self.ranks):
            total = total + self.land[j, at].astype(f32)
        return total


def row_loop(rows, some, body):
    @pl.loop(0, rows // some)
    def _(i):
        body(pl.ds(pl.multiple_of(i * some, some), some))


def params(number):
    return pltpu.CompilerParams(
        collective_id=number, has_side_effects=True, vmem_limit_bytes=VMEM_BYTES
    )


ANY = pl.BlockSpec(memory_space=pl.ANY)
ONCHIP = pl.BlockSpec(memory_space=pltpu.VMEM)


epsilon = 1e-05
CHUNK = 256


def shaped(shape, dtype):
    return jax.ShapeDtypeStruct(shape, dtype)


def dma(count=None):
    return pltpu.SemaphoreType.DMA if count is None else pltpu.SemaphoreType.DMA((count,))


def project_kernel(
    chips, ranks, res_ref, gain_ref, ws_ref, wx_own, x_ref, st_ref, bc_ref, normed_out, wx_out,
    own, normed, wx, *sems
):
    greet(chips, ranks)
    line = LineGather(wx_own, wx, *sems[:3], chips)
    tensor = TensorGather(own, normed, *sems[3:6], ranks)
    line.step(0)
    gain = gain_ref[...]

    def norm(at):
        v = res_ref[at].astype(f32)
        scaling = lax.rsqrt(jnp.mean(v * v, axis=1, keepdims=True) + epsilon)
        own[at] = (v * scaling * gain).astype(bf16)

    row_loop(own.shape[0], 32, norm)
    tensor.step(0)
    line.step(1)
    tensor.step(1)
    if chips > 2:
        line.step(2)
    tensor.finish()
    keep_normed = pltpu.make_async_copy(normed, normed_out, sems[6])
    keep_normed.start()
    tokens, width = x_ref.shape
    deep = 2 * line.rows

    def states(at):
        bc_ref[at] = mm(normed[at], ws_ref[...])

    row_loop(tokens, CHUNK, states)

    def use(first, chip):
        ks = pl.ds(pl.multiple_of(chip * deep, deep), deep)

        def rows(at):
            left = normed[at, ks]
            x, st = mm(left, wx[ks, :width]), mm(left, wx[ks, width:])
            if first:
                x_ref[at], st_ref[at] = x, st
            else:
                x_ref[at] += x
                st_ref[at] += st

        row_loop(tokens, CHUNK, rows)

    line.arrive(0, functools.partial(use, True))
    line.arrive(1, functools.partial(use, False))
    for k in range(2, chips):
        if k + 1 < chips:
            line.step(k + 1)
        line.arrive(k, functools.partial(use, False))
    keep_wx = pltpu.make_async_copy(wx, wx_out, sems[7])
    keep_wx.start()
    line.sent()
    keep_normed.wait()
    keep_wx.wait()


def project(number, chips, ranks, residual, norm_gain, ws, wx_own):
    rows, model = residual.shape
    tokens, width = rows * ranks, wx_own.shape[1]
    return pl.pallas_call(
        functools.partial(project_kernel, chips, ranks),
        in_specs=[ONCHIP, ONCHIP, ONCHIP, ANY],
        out_specs=[ONCHIP, ONCHIP, ONCHIP, ANY, ANY],
        out_shape=[
            shaped((tokens, width - LANES), f32), shaped((tokens, LANES), f32),
            shaped((tokens, ws.shape[1]), f32), shaped((tokens, model), bf16),
            shaped((model, width), bf16),
        ],
        scratch_shapes=[
            pltpu.VMEM((rows, model), bf16), pltpu.VMEM((tokens, model), bf16),
            pltpu.VMEM((model, width), bf16),
            *LineGather.scratch(chips), *TensorGather.scratch(ranks), dma(), dma(),
        ],
        compiler_params=params(number),
        name="project",
    )(residual, norm_gain, ws, wx_own)


def scan_gather_kernel(blocks, total, chips, ranks, *refs):
    own, (wz_own, cot_own) = refs[:9], refs[9:11]
    outs, (wz_out, cot_out) = refs[11:13], refs[13:15]
    scratch, sems = refs[15:19], refs[19:]
    now = pl.program_id(0) * blocks + pl.program_id(1)
    line = LineGather(wz_own, wz_out, *sems[:3], chips)
    tensor = TensorGather(cot_own, cot_out, *sems[3:], ranks)

    @pl.when(now == 0)
    def _():
        greet(chips, ranks)
        line.step(0)
        tensor.step(0)

    @pl.when(now == total - 2)
    def _():
        line.step(1)

    scan_fwd_kernel(blocks, *own, *outs, *scratch)

    @pl.when(now == total - 1)
    def _():
        tensor.step(1)
        for k in range(2, chips):
            line.step(k)
        line.finish()
        tensor.finish()


def scan_forward_gather(
    number, chips, ranks, wz_own, cot_own, x, bc, st, seg, tapx, tapbc, par, spread, skip, nseq
):
    tokens, width = x.shape
    n = BLOCK
    blocks = tokens // nseq // n
    at = lambda s, i: (s * blocks + i, 0)
    whole = lambda s, i: (0, 0)
    states = LANES
    return pl.pallas_call(
        functools.partial(scan_gather_kernel, blocks, nseq * blocks, chips, ranks),
        grid=(nseq, blocks),
        in_specs=[
            pl.BlockSpec((n, width), at),
            pl.BlockSpec((n, 2 * states), at),
            pl.BlockSpec((n, LANES), at),
            pl.BlockSpec((n, LANES), at),
            pl.BlockSpec(tapx.shape, whole),
            pl.BlockSpec(tapbc.shape, whole),
            pl.BlockSpec(par.shape, whole),
            pl.BlockSpec(spread.shape, whole),
            pl.BlockSpec(skip.shape, whole),
            ANY,
            ANY,
        ],
        out_specs=[
            pl.BlockSpec((n, width), at), pl.BlockSpec((states, width), at), ANY, ANY,
        ],
        out_shape=[
            shaped((tokens, width), f32),
            shaped((tokens // n * states, width), bf16),
            shaped((wz_own.shape[0] * 2 * chips, width), bf16),
            shaped((tokens, cot_own.shape[1]), bf16),
        ],
        scratch_shapes=[
            pltpu.VMEM((states, width), f32),
            pltpu.VMEM((8, width), f32),
            pltpu.VMEM((8, 2 * states), f32),
            pltpu.VMEM((8, LANES), jnp.int32),
            *LineGather.scratch(chips), *TensorGather.scratch(ranks),
        ],
        compiler_params=params(number),
        name="scan_forward",
    )(x, bc, st, seg, tapx, tapbc, par, spread, skip, wz_own, cot_own)


def lane_sums(v):
    total = v[:, :LANES]
    for i in range(LANES, v.shape[1], LANES):
        total = total + v[:, i : i + LANES]
    return total


def row_sums(picks, v):
    high = v.astype(bf16)
    low = (v - high.astype(f32)).astype(bf16)
    return mm_nt(picks, high) + mm_nt(picks, low)


def gate_kernel(
    chips, ranks, gain_ref, wo_own, normed_in, wz_in, y_in, cot_in,
    gz_ref, gy_ref, ng_ref, ggain_ref, wo_out,
    wo, normed, wz, y, cot, z, gng, squares, dots, columns, land, send, recv, loads, *sems
):
    line = LineGather(wo_own, wo, *sems[:3], chips)
    tokens, width = y.shape
    inner = width * ranks
    rank = line.rank
    load = [
        pltpu.make_async_copy(src, dst, loads.at[i])
        for i, (src, dst) in enumerate(((normed_in, normed), (wz_in, wz), (y_in, y), (cot_in, cot)))
    ]
    greet(chips, ranks)
    line.step(0)
    for copy in load:
        copy.start()
    load[0].wait()
    load[1].wait()

    def gate(at):
        z[at] = mm(normed[at], wz[...])

    row_loop(tokens, CHUNK, gate)
    load[2].wait()
    load[3].wait()
    deep = 2 * line.rows

    def use(first, chip):
        ks = pl.ds(pl.multiple_of(chip * deep, deep), deep)

        def rows(at):
            v = mm(cot[at, ks], wo[ks])
            if first:
                gng[at] = v
            else:
                gng[at] += v

        row_loop(tokens, CHUNK, rows)

    line.arrive(0, functools.partial(use, True))
    for k in range(1, chips):
        line.step(k)
        line.arrive(k, functools.partial(use, False))
    keep = pltpu.make_async_copy(wo, wo_out, loads.at[4])
    keep.start()
    gain = gain_ref[0:1]

    def sums(at):
        zz = z[at]
        gated = y[at] * (zz * sigmoid(zz))
        squares[at] = lane_sums(gated * gated)
        dots[at] = lane_sums(gng[at] * gain * gated)

    row_loop(tokens, 16, sums)
    half = lax.broadcasted_iota(jnp.int32, (8, LANES), 0) < 4
    one, other = half.astype(bf16), jnp.logical_not(half).astype(bf16)
    for r in range(0, tokens, CHUNK):
        at = slice(r, r + CHUNK)
        land[rank, :, at] = row_sums(one, squares[at]) + row_sums(other, dots[at])
    copies = [
        remote(
            land.at[rank], land.at[rank], send.at[k], recv.at[k], line.me, lax.rem(rank + k, ranks)
        )
        for k in range(1, ranks)
    ]
    for copy in copies:
        copy.start()
    line.sent()
    for copy in copies:
        copy.wait()
    for r in range(0, tokens, LANES):
        at = slice(r, r + LANES)
        total = land[0, :, at]
        for k in range(1, ranks):
            total = total + land[k, :, at]
        columns[at] = jnp.transpose(jnp.concatenate([total] * (LANES // 8), axis=0))
    ggain_ref[...] = jnp.zeros_like(ggain_ref)

    def grads(at):
        zz, yy, gg = z[at], y[at], gng[at]
        sig = sigmoid(zz)
        silu = zz * sig
        gated = yy * silu
        scale = lax.rsqrt(columns[at, 0:1] / inner + epsilon)
        ng_ref[at] = (gated * scale * gain).astype(bf16)
        weight = scale * scale * scale * columns[at, 4:5] / inner
        ggain_ref[...] += fold(gg * gated * scale)
        grad = scale * gain * gg - gated * weight
        gz_ref[at] = (grad * yy * (sig * (1.0 + zz * (1.0 - sig)))).astype(bf16)
        gy_ref[at] = grad * silu

    row_loop(tokens, 16, grads)
    keep.wait()


def gate(number, chips, ranks, gain, wo_own, normed, wz, y, cot):
    tokens, width = y.shape
    model = normed.shape[1]
    return pl.pallas_call(
        functools.partial(gate_kernel, chips, ranks),
        in_specs=[ONCHIP] + [ANY] * 5,
        out_specs=[ONCHIP] * 4 + [ANY],
        out_shape=[
            shaped((tokens, width), bf16), shaped((tokens, width), f32), shaped((tokens, width), bf16),
            shaped((8, width), f32), shaped((model, width), bf16),
        ],
        scratch_shapes=[
            pltpu.VMEM((model, width), bf16), pltpu.VMEM((tokens, model), bf16),
            pltpu.VMEM((model, width), bf16), pltpu.VMEM((tokens, width), f32),
            pltpu.VMEM((tokens, model), bf16), pltpu.VMEM((tokens, width), f32),
            pltpu.VMEM((tokens, width), f32), pltpu.VMEM((tokens, LANES), f32),
            pltpu.VMEM((tokens, LANES), f32), pltpu.VMEM((tokens, LANES), f32),
            pltpu.VMEM((ranks, 8, tokens), f32), dma(ranks), dma(ranks), dma(5),
            *LineGather.scratch(chips),
        ],
        compiler_params=params(number),
        name="gate",
    )(gain, wo_own, normed, wz, y, cot)


def stream_grads(src, grad, parts, wide, cbuf, stage, csem, ssem):
    count = src.shape[1] // CHUNK

    def load(j):
        slot = lax.rem(j, 2)
        columns = pl.ds(pl.multiple_of(j * CHUNK, CHUNK), CHUNK)
        return pltpu.make_async_copy(src.at[:, columns], cbuf.at[slot], csem.at[slot])

    def store(j):
        slot = lax.rem(j, 2)
        return pltpu.make_async_copy(
            stage.at[slot, :, pl.ds(0, wide)], slab(parts, j, CHUNK), ssem.at[slot]
        )

    load(0).start()

    @pl.loop(0, count)
    def _(j):
        slot = lax.rem(j, 2)

        @pl.when(j + 1 < count)
        def _():
            load(j + 1).start()

        load(j).wait()

        @pl.when(j >= 2)
        def _():
            store(j - 2).wait()

        stage[slot, :, :wide] = mm_tn(cbuf[slot], grad[...]).astype(bf16)
        store(j).start()

    for j in (count - 2, count - 1):
        store(j).wait()


def stream_back(terms, kept, parts, stage, ssem):
    tokens, model = parts.shape
    count = model // CHUNK

    def loads(j):
        slot = lax.rem(j, 2)
        return [
            pltpu.make_async_copy(slab(right, j, CHUNK), buffer.at[slot], sem.at[slot])
            for _, right, buffer, sem in terms
        ]

    def store(j):
        slot = lax.rem(j, 2)
        columns = pl.ds(pl.multiple_of(j * CHUNK, CHUNK), CHUNK)
        return pltpu.make_async_copy(stage.at[slot], parts.at[:, columns], ssem.at[slot])

    for copy in loads(0):
        copy.start()

    @pl.loop(0, count)
    def _(j):
        slot = lax.rem(j, 2)

        @pl.when(j + 1 < count)
        def _():
            for copy in loads(j + 1):
                copy.start()

        for copy in loads(j):
            copy.wait()

        @pl.when(j >= 2)
        def _():
            store(j - 2).wait()

        for r in range(0, tokens, CHUNK):
            at = slice(r, r + CHUNK)
            total = jnp.zeros((CHUNK, CHUNK), f32)
            for left, _, buffer, _ in terms:
                total = total + mm_nt(left[at], buffer[slot])
            for left, right in kept:
                total = total + mm_nt(left[at], right[pl.ds(pl.multiple_of(j * CHUNK, CHUNK), CHUNK)])
            stage[slot, at] = total.astype(bf16)
        store(j).start()

    for j in (count - 2, count - 1):
        store(j).wait()


def backward_kernel(blocks, total, chips, ranks, *refs):
    ins, refs = refs[:15], refs[15:]
    (res_ref, ws_ref, ggain_ref, gz_in, ng_in, normed_in, cot_in, wo_in, wz_in, wx_in), refs = refs[:10], refs[10:]
    (z_sum, o_sum, block_out, pack_ref, xparts, tparts, sparts, zparts, oparts, pparts, gbc_slots), refs = refs[:11], refs[11:]
    scratch, refs = refs[:4], refs[4:]
    (gxs, gbc_own, gtapx, gtapbc, gpar, gz, ng, cbuf, stage, back, wbuf, xbuf, gbc_sum, state_stage), refs = refs[:14], refs[14:]
    (loads, csem, ssem, bsem, wsem, xsem), refs = refs[:6], refs[6:]
    job0 = LineScatter(zparts, z_sum, *refs[:7], chips)
    job1 = LineScatter(oparts, o_sum, *refs[7:14], chips)
    across = TensorScatter(pparts, *refs[14:18], ranks)
    around = TensorGather(gbc_own, gbc_slots, *refs[18:], ranks)
    now = pl.program_id(0) * blocks + pl.program_id(1)
    tokens, width = gz.shape
    rank = across.rank

    @pl.when(now == 0)
    def _():
        fetch = [
            pltpu.make_async_copy(gz_in, gz, loads.at[0]),
            pltpu.make_async_copy(ng_in, ng, loads.at[1]),
        ]
        for copy in fetch:
            copy.start()
        greet(chips, ranks)
        fetch[0].wait()
        stream_grads(normed_in, gz, zparts, width, cbuf, stage, csem, ssem)
        job0.step(0)
        fetch[1].wait()
        stream_back([(ng, wo_in, wbuf, wsem)], [], pparts, back, bsem)
        across.step(0)
        job0.step(1)
        stream_grads(cot_in, ng, oparts, width, cbuf, stage, csem, ssem)
        job1.step(0)

    early = [k for k in range(2, chips) if 2 * k - 3 < total - 1]

    @pl.when(now == 1)
    def _():
        job1.step(1)

    for k in early:
        @pl.when(now == 2 * k - 3)
        def _():
            job0.step(k)

    @pl.when(now == total - 1)
    def _():
        if chips > 2:
            job1.step(2)

    row = pl.multiple_of(
        (pl.program_id(0) * blocks + blocks - 1 - pl.program_id(1)) * BLOCK, BLOCK
    )
    here = pl.ds(row, BLOCK)
    outs = (
        gxs.at[here, pl.ds(0, width)], gbc_own.at[here], gxs.at[here, pl.ds(width, LANES)],
        gtapx, gtapbc, gpar,
    )
    scan_bwd_kernel(blocks, *ins, *outs, *scratch)

    @pl.when(now == total - 1)
    def _():
        around.step(0)
        stream_grads(normed_in, gxs, xparts, width + LANES, cbuf, stage, csem, ssem)
        around.step(1)
        for k in range(2, chips):
            if k not in early:
                job0.step(k)
        for k in range(3, chips):
            job1.step(k)
        stream_back(
            [(gz, wz_in, wbuf, wsem), (gxs, wx_in, xbuf, xsem)], [(gbc_own, ws_ref)], tparts, back, bsem
        )
        around.finish()
        for r in range(ranks):
            copy = pltpu.make_async_copy(slab(gbc_slots, r, tokens), cbuf.at[r % 2], csem.at[r % 2])
            copy.start()
            copy.wait()

            def add(at):
                v = cbuf[r % 2, at].astype(f32)
                gbc_sum[at] = v if r == 0 else gbc_sum[at] + v

            row_loop(tokens, 64, add)

        def rounded(at):
            gbc_own[at] = gbc_sum[at].astype(bf16)

        row_loop(tokens, 64, rounded)
        depth = sparts.shape[0]
        for i in range(depth // CHUNK):
            columns = pl.ds(pl.multiple_of(rank * depth + i * CHUNK, CHUNK), CHUNK)
            copy = pltpu.make_async_copy(normed_in.at[:, columns], cbuf.at[0], csem.at[0])
            copy.start()
            copy.wait()
            state_stage[...] = mm_tn(cbuf[0], gbc_own[...])
            copy = pltpu.make_async_copy(state_stage, sparts.at[pl.ds(i * CHUNK, CHUNK)], csem.at[1])
            copy.start()
            copy.wait()
        pack_ref[...] = jnp.zeros_like(pack_ref)
        for k in range(5):
            rows = slice(8 * k, 8 * k + 8)
            pack_ref[k : k + 1, :width] = jnp.sum(gtapx[rows], axis=0, keepdims=True)
            pack_ref[k : k + 1, width:] = jnp.sum(gtapbc[rows], axis=0, keepdims=True)
        pack_ref[5:6, :width] = jnp.sum(ggain_ref[...], axis=0, keepdims=True)
        for k in range(3):
            pack_ref[6:7, k * LANES : (k + 1) * LANES] = jnp.sum(
                gpar[8 * k : 8 * k + 8], axis=0, keepdims=True
            )
        across.arrive()

        def residual(at):
            block_out[at] = res_ref[at].astype(f32) + across.total(at)

        row_loop(across.rows, 16, residual)
        job0.finish()
        job1.finish()


def backward(
    number, chips, ranks, residual, ws, ggain, gz, ng, normed, cot, wo, wz, wx,
    x, bc, st, seg, gy, y, h, tapx, tapbc, par, spread, skip, nseq,
):
    tokens, width = x.shape
    model = normed.shape[1]
    n = BLOCK
    blocks = tokens // nseq // n
    at = lambda s, i: (s * blocks + blocks - 1 - i, 0)
    tail = lambda s, i: (jnp.maximum((s * blocks + blocks - 1 - i) * (n // 8) - 1, 0), 0)
    whole = lambda s, i: (0, 0)
    states = LANES
    full = lambda v: pl.BlockSpec(v.shape, whole)
    once = lambda shape: pl.BlockSpec(shape, whole)
    own = model // (2 * chips)
    depth = model // ranks
    return pl.pallas_call(
        functools.partial(backward_kernel, blocks, nseq * blocks, chips, ranks),
        grid=(nseq, blocks),
        in_specs=[
            pl.BlockSpec((n, width), at),
            pl.BlockSpec((8, width), tail),
            pl.BlockSpec((n, 2 * states), at),
            pl.BlockSpec((8, 2 * states), tail),
            pl.BlockSpec((n, LANES), at),
            pl.BlockSpec((n, LANES), at),
            pl.BlockSpec((8, LANES), tail),
            pl.BlockSpec((n, width), at),
            pl.BlockSpec((n, width), at),
            pl.BlockSpec((states, width), at),
            full(tapx), full(tapbc), full(par), full(spread), full(skip),
            full(residual), full(ws), full(ggain),
        ]
        + [ANY] * 7,
        out_specs=[
            once((own, width)), once((own, width)), once(residual.shape), once((8, width + 2 * states)),
        ]
        + [ANY] * 7,
        out_shape=[
            shaped((own, width), f32), shaped((own, width), f32), shaped(residual.shape, f32),
            shaped((8, width + 2 * states), f32),
            shaped((model, width + LANES), bf16), shaped((tokens, model), bf16),
            shaped((depth, 2 * states), f32),
            shaped((model, width), bf16), shaped((model, width), bf16), shaped((tokens, model), bf16),
            shaped((ranks * tokens, 2 * states), bf16),
        ],
        scratch_shapes=[
            pltpu.VMEM((states, width), f32),
            pltpu.VMEM((8, width), f32),
            pltpu.VMEM((8, 2 * states), f32),
            pltpu.VMEM((8, LANES), jnp.int32),
            pltpu.VMEM((tokens, width + LANES), bf16),
            pltpu.VMEM((tokens, 2 * states), bf16),
            pltpu.VMEM((40, width), f32),
            pltpu.VMEM((40, 2 * states), f32),
            pltpu.VMEM((24, LANES), f32),
            pltpu.VMEM((tokens, width), bf16),
            pltpu.VMEM((tokens, width), bf16),
            pltpu.VMEM((2, tokens, CHUNK), bf16),
            pltpu.VMEM((2, CHUNK, width + LANES), bf16),
            pltpu.VMEM((2, tokens, CHUNK), bf16),
            pltpu.VMEM((2, CHUNK, width), bf16),
            pltpu.VMEM((2, CHUNK, width + LANES), bf16),
            pltpu.VMEM((tokens, 2 * states), f32),
            pltpu.VMEM((CHUNK, 2 * states), f32),
            *[dma(2)] * 6,
            *LineScatter.scratch(chips, (model, width)),
            *LineScatter.scratch(chips, (model, width)),
            *TensorScatter.scratch(ranks, (tokens, model)),
            *TensorGather.scratch(ranks),
        ],
        compiler_params=params(number),
        name="backward",
    )(
        x, x, bc, bc, st, seg, seg, gy, y, h, tapx, tapbc, par, spread, skip,
        residual, ws, ggain, gz, ng, normed, cot, wo, wz, wx,
    )


def everyone(buffer, mine, count, send, recv, device):
    row = buffer.at[mine]
    return [
        remote(row, row, send.at[k], recv.at[k], *device(lax.rem(mine + k, count)))
        for k in range(1, count)
    ]


def added(buffer, count):
    total = buffer[0]
    for k in range(1, count):
        total = total + buffer[k]
    return total


def finish_kernel(chips, ranks, *refs):
    (pack_ref, res_ref, cot_ref, gain_ref, xparts, tparts, sparts), refs = refs[:7], refs[7:]
    (x_ref, out_ref, state_ref, sums_ref, norm_ref), refs = refs[:5], refs[5:]
    (state_own, state_line, state_low, state_all, land_dp, land_rank, norm_rank, norm_dp, norm_acc), refs = refs[:9], refs[9:]
    (psend, precv, qsend, qrecv, nsend, nrecv, msend, mrecv), refs = refs[:8], refs[8:]
    x_job = LineScatter(xparts, x_ref, *refs[:7], chips)
    s_job = LineScatter(sparts, state_own, *refs[7:14], chips)
    across = TensorScatter(tparts, *refs[14:18], ranks)
    s_line = LineGather(state_own, state_line, *refs[18:21], chips)
    s_rank = TensorGather(state_low, state_all, *refs[21:24], ranks)
    me, rank, devices = x_job.me, x_job.rank, 2 * chips
    over_dp = lambda d: (d, rank)
    over_rank = lambda r: (me, r)
    width = x_ref.shape[1] - LANES
    greet_all(chips, ranks)
    s_job.step(0)
    x_job.step(0)
    across.step(0)
    land_dp[me] = pack_ref[...]
    first = everyone(land_dp, me, devices, psend, precv, over_dp)
    for copy in first:
        copy.start()
    s_job.step(1)
    x_job.step(1)
    for copy in first:
        copy.wait()
    land_rank[rank] = added(land_dp, devices)
    second = everyone(land_rank, rank, ranks, qsend, qrecv, over_rank)
    for copy in second:
        copy.start()
    for k in range(2, chips):
        s_job.step(k)
        x_job.step(k)
    s_job.finish()
    for k in range(chips):
        s_line.step(k)
    s_line.finish()

    def lower(at):
        state_low[at] = state_line[at].astype(bf16)

    row_loop(state_low.shape[0], 64, lower)
    s_rank.step(0)
    for copy in second:
        copy.wait()
    shared = land_rank[0, :, width:]
    for r in range(1, ranks):
        shared = shared + land_rank[r, :, width:]
    for r in range(ranks):
        sums_ref[:, r * width : (r + 1) * width] = land_rank[r, :, :width]
    sums_ref[:, ranks * width :] = shared
    across.arrive()
    norm_acc[...] = jnp.zeros_like(norm_acc)
    gain = gain_ref[...]
    model = gain.shape[1]

    def last(at):
        grad = across.total(at)
        v = res_ref[at].astype(f32)
        scaling = lax.rsqrt(jnp.mean(v * v, axis=1, keepdims=True) + epsilon)
        norm_acc[...] += fold(grad * v * scaling)
        grad = grad * gain
        along = jnp.sum(grad * v, axis=1, keepdims=True)
        weight = scaling * scaling * scaling * along / model
        out_ref[at] = cot_ref[at].astype(f32) + scaling * grad - v * weight

    row_loop(across.rows, 16, last)
    row = jnp.sum(norm_acc[...], axis=0, keepdims=True)
    eighth = model // 8
    for i in range(8):
        norm_rank[rank, i : i + 1, :] = row[:, i * eighth : (i + 1) * eighth]
    third = everyone(norm_rank, rank, ranks, nsend, nrecv, over_rank)
    for copy in third:
        copy.start()
    s_rank.step(1)
    for copy in third:
        copy.wait()
    norm_dp[me] = added(norm_rank, ranks)
    fourth = everyone(norm_dp, me, devices, msend, mrecv, over_dp)
    for copy in fourth:
        copy.start()
    x_job.finish()
    s_rank.finish()

    def state(at):
        state_ref[at] = state_all[at].astype(f32)

    row_loop(state_ref.shape[0], 64, state)
    for copy in fourth:
        copy.wait()
    norm_ref[...] = added(norm_dp, devices)


def finish(number, chips, ranks, pack, residual, cot, norm_gain, xparts, tparts, sparts):
    rows, model = residual.shape
    devices = 2 * chips
    own = model // devices
    depth, states = sparts.shape
    wide = pack.shape[1]
    width = wide - states
    return pl.pallas_call(
        functools.partial(finish_kernel, chips, ranks),
        in_specs=[ONCHIP] * 4 + [ANY] * 3,
        out_specs=[ONCHIP] * 5,
        out_shape=[
            shaped((own, xparts.shape[1]), f32), shaped((rows, model), f32), shaped((model, states), f32),
            shaped((8, width * ranks + states), f32), shaped((8, model // 8), f32),
        ],
        scratch_shapes=[
            pltpu.VMEM((depth // devices, states), f32), pltpu.VMEM((depth, states), f32),
            pltpu.VMEM((depth, states), bf16), pltpu.VMEM((model, states), bf16),
            pltpu.VMEM((devices, 8, wide), f32), pltpu.VMEM((ranks, 8, wide), f32),
            pltpu.VMEM((ranks, 8, model // 8), f32), pltpu.VMEM((devices, 8, model // 8), f32),
            pltpu.VMEM((8, model), f32),
            dma(devices), dma(devices), dma(ranks), dma(ranks),
            dma(ranks), dma(ranks), dma(devices), dma(devices),
            *LineScatter.scratch(chips, xparts.shape),
            *LineScatter.scratch(chips, sparts.shape, f32),
            *TensorScatter.scratch(ranks, tparts.shape),
            *LineGather.scratch(chips), *TensorGather.scratch(ranks),
        ],
        compiler_params=params(number),
        name="finish",
    )(pack, residual, cot, norm_gain, xparts, tparts, sparts)


def per_device(
    residual, segment_ids, norm_gain, inner_weight, state_weight, step_weight, conv_weight,
    conv_bias, step_bias, decay_log, skip_gain, gated_gain, out_weight, cotangent,
):
    rank = lax.axis_index("tensor")
    chips, ranks = lax.axis_size("dp") // 2, lax.axis_size("tensor")
    width = inner_weight.shape[2]
    heads = step_weight.shape[1]
    inner_width = gated_gain.shape[0]
    nseq, length = segment_ids.shape
    tokens = nseq * length
    inner_start, head_start = rank * width, rank * heads
    taps = jnp.concatenate([conv_weight, conv_bias[None], jnp.zeros((3, conv_bias.shape[0]), f32)], axis=0)
    tapx = lax.dynamic_slice_in_dim(taps, inner_start, width, 1)
    tapbc = taps[:, inner_width:]
    local = lambda v: lax.dynamic_slice_in_dim(v, head_start, heads, 0)
    rates = -jnp.exp(local(decay_log))
    par = jnp.concatenate(
        [on_lanes(local(step_bias)[None]), on_lanes(rates[None]), jnp.zeros((6, LANES), f32)], axis=0
    )
    skip = jnp.broadcast_to(jnp.repeat(local(skip_gain), WIDTH)[None], (8, width))
    gain = jnp.broadcast_to(
        lax.dynamic_slice_in_dim(gated_gain, inner_start, width, 0)[None], (8, width)
    )
    spread = spread_matrix(heads)
    seg = jnp.broadcast_to(segment_ids.reshape(tokens, 1), (tokens, LANES))

    wx_own = jnp.concatenate([inner_weight[:, 1], on_lanes(step_weight)], axis=1)
    x, st, bc, normed, wx = project(
        1, chips, ranks, residual, norm_gain[None], state_weight, wx_own
    )
    y, h, wz, cot = scan_forward_gather(
        2, chips, ranks, inner_weight[:, 0], cotangent,
        x, bc, st, seg, tapx, tapbc, par, spread, skip, nseq,
    )
    gz, gy, ng, ggain, wo = gate(3, chips, ranks, gain, out_weight.T, normed, wz, y, cot)
    z_grad, out_grad, block_out, pack, xparts, tparts, sparts, *_ = backward(
        4, chips, ranks, residual, state_weight, ggain, gz, ng, normed, cot, wo, wz, wx,
        x, bc, st, seg, gy, y, h, tapx, tapbc, par, spread, skip, nseq,
    )
    x_grad, residual_grad, state_grad, sums, norm_grad = finish(
        5, chips, ranks, pack, residual, cotangent, norm_gain[None], xparts, tparts, sparts
    )
    inner_grad = jnp.stack([z_grad, x_grad[:, :width]], axis=1)
    by_head = sums[6, :inner_width].reshape(ranks, width)
    by_head = [by_head[:, k * LANES : k * LANES + heads].reshape(-1) for k in range(3)]
    return (
        block_out, residual_grad, norm_grad.reshape(-1), inner_grad, state_grad,
        x_grad[:, width : width + heads], sums[:4], sums[4], *by_head,
        sums[5, :inner_width], out_grad.T,
    )


def solution(mesh):
    rows, both = P("dp", "tensor"), P(("dp", "tensor"), None)
    inner, out = P("dp", None, "tensor"), P("tensor", "dp")
    return jax.shard_map(
        per_device,
        mesh=mesh,
        in_specs=(
            both, P("dp", None), P(), inner, P(), rows, P(), P(), P(), P(), P(), P(), out, both,
        ),
        out_specs=(both, both, P(), inner, P(), rows, P(), P(), P(), P(), P(), P(), out),
        check_vma=False,
    )
```

```python
import functools
import jax
import jax.numpy as jnp
from jax import lax
from jax.experimental import pallas as pl
from jax.experimental.pallas import tpu as pltpu
from jax.sharding import PartitionSpec as P

LANES = 128
BLOCK = 128
WIDTH = 64
VMEM_BYTES = 60 * 1024 * 1024
f32, bf16 = jnp.float32, jnp.bfloat16
ROWS0 = (((0,), (0,)), ((), ()))
COLS1 = (((1,), (1,)), ((), ()))


def mm(a, b):
    return jnp.dot(a, b, preferred_element_type=f32)


def mm_tn(a, b):
    return lax.dot_general(a, b, ROWS0, preferred_element_type=f32)


def mm_nt(a, b):
    return lax.dot_general(a, b, COLS1, preferred_element_type=f32)


def sigmoid(v):
    return 0.5 + 0.5 * jnp.tanh(0.5 * v)


def two_parts(v, low_lanes):
    high = v.astype(bf16)
    return jnp.where(low_lanes, (v - high.astype(f32)).astype(bf16), high)


def head_sums(v, spread):
    high = v.astype(bf16)
    low = (v - high.astype(f32)).astype(bf16)
    return mm_nt(high, spread) + mm_nt(low, spread)


def shifted_masks(seg_ext, seg):
    n = seg.shape[0]
    return [None] + [seg_ext[8 - k : 8 - k + n] == seg for k in (1, 2, 3)]


def convolve(tail, part, masks, taps):
    n = part.shape[0]
    ext = jnp.concatenate([tail, part], axis=0)
    total = taps[4:5] + taps[3:4] * part
    for k in (1, 2, 3):
        total = total + taps[3 - k : 4 - k] * jnp.where(masks[k], ext[8 - k : 8 - k + n], 0.0)
    return total


def wide(v):
    return jnp.concatenate([v, v], axis=1)


def step_state(raw, params, seg, prev_seg, end_seg, n):
    row = lax.broadcasted_iota(jnp.int32, (n, n), 0)
    col = lax.broadcasted_iota(jnp.int32, (n, n), 1)
    v = raw + params[0:1]
    dt = jnp.maximum(v, 0.0) + jnp.log1p(jnp.exp(-jnp.abs(v)))
    a = params[1:2]
    cum = jnp.dot(
        (row >= col).astype(f32), dt * a, precision=lax.Precision.HIGHEST, preferred_element_type=f32
    )
    last = cum[n - 1 : n]
    into = jnp.where(seg == prev_seg, jnp.exp(cum), 0.0)
    onto = jnp.where(seg == end_seg, jnp.exp(last - cum), 0.0)
    through = jnp.where(end_seg == prev_seg, jnp.exp(last), 0.0)
    bias = jnp.where((row >= col) & (seg == jnp.transpose(seg)), 0.0, -1e30)
    return v, dt, a, cum, into, onto, through, bias


def scan_fwd_kernel(
    blocks, x_ref, bc_ref, st_ref, seg_ref, tapx_ref, tapbc_ref, par_ref, spread_ref, skip_ref,
    y_ref, h_ref, conv_ref, convbc_ref, state, tail_x, tail_bc, tail_seg,
):
    n = BLOCK
    block = pl.program_id(1)

    @pl.when(block == 0)
    def _():
        state[...] = jnp.zeros_like(state)
        tail_x[...] = jnp.zeros_like(tail_x)
        tail_bc[...] = jnp.zeros_like(tail_bc)
        tail_seg[...] = jnp.full_like(tail_seg, -1)

    seg = seg_ref[...]
    masks = shifted_masks(jnp.concatenate([tail_seg[...], seg], axis=0), seg)
    prev_seg, end_seg = tail_seg[7:8], seg[n - 1 : n]
    v, dt, a, cum, into, onto, through, bias = step_state(
        st_ref[...], par_ref[...], seg, prev_seg, end_seg, n
    )
    cum_t = jnp.transpose(cum)
    low_lanes = lax.broadcasted_iota(jnp.int32, (n, LANES), 1) >= LANES // 2
    spread = spread_ref[...]
    dt_w = mm(two_parts(dt, low_lanes), spread)
    into_w = mm(two_parts(into, low_lanes), spread)
    onto_w = mm(two_parts(onto, low_lanes), spread)
    through_w = mm(two_parts(jnp.broadcast_to(through, (8, LANES)), low_lanes[:8]), spread)[0:1]
    bc_masks = [None] + [wide(m) for m in masks[1:]]
    conv_bc = convolve(tail_bc[...], bc_ref[...], bc_masks, tapbc_ref[...])
    convbc_ref[...] = conv_bc
    act_bc = conv_bc * sigmoid(conv_bc)
    b, c = act_bc[:, :LANES].astype(bf16), act_bc[:, LANES:].astype(bf16)
    cross = mm_nt(c, b)
    entering = state[...].astype(bf16)
    h_ref[...] = entering
    first_half = lax.broadcasted_iota(jnp.int32, (n, LANES), 1) < WIDTH
    for pair in range(x_ref.shape[1] // LANES):
        sl = slice(pair * LANES, (pair + 1) * LANES)
        conv = convolve(tail_x[:, sl], x_ref[:, sl], masks, tapx_ref[:, sl])
        conv_ref[:, sl] = conv
        xs = conv * sigmoid(conv)
        xd = xs * dt_w[:, sl]
        outside = mm(c, entering[:, sl]) * into_w[:, sl]
        mixes = []
        for h in (2 * pair, 2 * pair + 1):
            decay = jnp.exp(cum[:, h : h + 1] - cum_t[h : h + 1, :] + bias)
            mixes.append((decay * cross).astype(bf16))
        stacked = jnp.concatenate(
            [jnp.where(first_half, xd, 0.0), jnp.where(first_half, 0.0, xd)], axis=0
        ).astype(bf16)
        inside = mm(jnp.concatenate(mixes, axis=1), stacked)
        y_ref[:, sl] = inside + outside + skip_ref[0:1, sl] * xs
        local = mm_tn(b, (onto_w[:, sl] * xd).astype(bf16))
        state[:, sl] = through_w[:, sl] * state[:, sl] + local
    tail_x[...] = x_ref[n - 8 :, :]
    tail_bc[...] = bc_ref[n - 8 :, :]
    tail_seg[...] = seg_ref[n - 8 :, :]


def fold(v):
    total = v[0:8]
    for r in range(8, v.shape[0], 8):
        total = total + v[r : r + 8]
    return total


def scan_bwd_kernel(
    blocks, x_ref, conv_ref, bc_ref, convbc_ref, st_ref, seg_ref, segt_ref, gy_ref, y_ref, h_ref,
    tapx_ref, tapbc_ref, par_ref, spread_ref, skip_ref,
    gx_ref, gbc_ref, gst_ref, gtapx_ref, gtapbc_ref, gpar_ref,
    gstate, head_x, head_bc, head_seg, xs_s, slope_s, back_s, dt_s, onto_s, xd_s, into_s, onto_low, sums_s,
):
    n = BLOCK
    step = pl.program_id(1)
    block = blocks - 1 - step

    @pl.when((step == 0) & (pl.program_id(0) == 0))
    def _():
        gtapx_ref[...] = jnp.zeros_like(gtapx_ref)
        gtapbc_ref[...] = jnp.zeros_like(gtapbc_ref)
        gpar_ref[...] = jnp.zeros_like(gpar_ref)

    @pl.when(step == 0)
    def _():
        gstate[...] = jnp.zeros_like(gstate)
        head_x[...] = jnp.zeros_like(head_x)
        head_bc[...] = jnp.zeros_like(head_bc)
        head_seg[...] = jnp.full_like(head_seg, -1)

    seg = seg_ref[...]
    first = block == 0
    seg_next = jnp.concatenate([seg, head_seg[...]], axis=0)
    ahead = [None] + [seg_next[k : k + n] == seg for k in (1, 2, 3)]
    prev_seg = jnp.where(first, -1, segt_ref[7:8])
    end_seg = seg[n - 1 : n]
    v, dt, a, cum, into, onto, through, bias = step_state(
        st_ref[...], par_ref[...], seg, prev_seg, end_seg, n
    )
    cum_t = jnp.transpose(cum)
    low_lanes = lax.broadcasted_iota(jnp.int32, (n, LANES), 1) >= LANES // 2
    spread = spread_ref[...]
    dt_s[...] = mm(two_parts(dt, low_lanes), spread)
    into_w = mm(two_parts(into, low_lanes), spread)
    onto_s[...] = mm(two_parts(onto, low_lanes), spread)
    through_w = mm(two_parts(jnp.broadcast_to(through, (8, LANES)), low_lanes[:8]), spread)[0:1]
    conv_bc = convbc_ref[...]
    sig_bc = sigmoid(conv_bc)
    act_bc = conv_bc * sig_bc
    b, c = act_bc[:, :LANES].astype(bf16), act_bc[:, LANES:].astype(bf16)
    cross = mm_nt(c, b)
    first_half = lax.broadcasted_iota(jnp.int32, (n, LANES), 1) < WIDTH
    halves = lambda t: jnp.concatenate(
        [jnp.where(first_half, t, 0.0), jnp.where(first_half, 0.0, t)], axis=0
    ).astype(bf16)
    pairs = [slice(i, i + LANES) for i in range(0, x_ref.shape[1], LANES)]

    for sl in pairs:
        conv = conv_ref[:, sl]
        sig = sigmoid(conv)
        xs = conv * sig
        xs_s[:, sl] = xs
        slope_s[:, sl] = sig + xs * (1.0 - sig)
        xd = xs * dt_s[:, sl]
        xd_s[:, sl] = xd.astype(bf16)
        onto_low[:, sl] = (xd * onto_s[:, sl]).astype(bf16)
        into_s[:, sl] = (gy_ref[:, sl] * into_w[:, sl]).astype(bf16)
    before = h_ref[...]
    gstate_low = gstate[...].astype(bf16)
    gy_into = into_s[...]
    gc = mm_nt(gy_into, before)
    gb = mm_nt(onto_low[...], gstate_low)
    back_s[...] = mm(b, gstate_low)
    edges = 5 * n
    for sl in pairs:
        old = through_w[:, sl] * gstate[:, sl]
        last = fold(old * before[:, sl].astype(f32))
        skips = fold(gy_ref[:, sl] * xs_s[:, sl])
        both = jnp.concatenate([last, skips], axis=0)
        high = both.astype(bf16)
        sums_s[edges : edges + 16, sl] = high
        sums_s[edges + 16 : edges + 32, sl] = (both - high.astype(f32)).astype(bf16)
        gstate[:, sl] = old + mm_tn(c, gy_into[:, sl])
    gcross = jnp.zeros((n, n), f32)
    for pair, sl in enumerate(pairs):
        xs = xs_s[:, sl]
        xd_low = xd_s[:, sl]
        gy = gy_ref[:, sl]
        skip = skip_ref[0:1, sl]
        inner = y_ref[:, sl] - skip * xs
        g_state = onto_s[:, sl] * back_s[:, sl]
        gy_halves = halves(gy)
        gmix = mm_nt(gy_halves, xd_low)
        mixes = []
        for i, h in enumerate((2 * pair, 2 * pair + 1)):
            decay = jnp.exp(cum[:, h : h + 1] - cum_t[h : h + 1, :] + bias)
            mixes.append((decay * cross).astype(bf16))
            gcross = gcross + decay * gmix[i * n : (i + 1) * n]
        gxd = mm_tn(jnp.concatenate(mixes, axis=0), gy_halves) + g_state
        xd_r, gy_r = xd_low.astype(f32), gy.astype(bf16).astype(f32)
        q = gy_r * inner - xd_r * gxd
        high = q.astype(bf16)
        sums_s[0:n, sl] = high
        sums_s[n : 2 * n, sl] = (q - high.astype(f32)).astype(bf16)
        q = xd_r * g_state
        high = q.astype(bf16)
        sums_s[2 * n : 3 * n, sl] = high
        sums_s[3 * n : 4 * n, sl] = (q - high.astype(f32)).astype(bf16)
        sums_s[4 * n : 5 * n, sl] = (xs * gxd).astype(bf16)
        gconv = (dt_s[:, sl] * gxd + skip * gy) * slope_s[:, sl]
        taps = tapx_ref[:, sl]
        part = x_ref[:, sl]
        ext = jnp.concatenate([gconv, head_x[:, sl]], axis=0)
        gu = taps[3:4] * gconv
        gtapx_ref[24:32, sl] += fold(gconv * part)
        for k in (1, 2, 3):
            later = jnp.where(ahead[k], ext[k : k + n], 0.0)
            gu = gu + taps[3 - k : 4 - k] * later
            gtapx_ref[8 * (3 - k) : 8 * (4 - k), sl] += fold(later * part)
        gx_ref[:, sl] = gu.astype(bf16)
        gtapx_ref[32:40, sl] += fold(gconv)
        head_x[:, sl] = gconv[0:8]
    sums = mm_nt(sums_s[...], spread)
    sum_q = sums[0:n] + sums[n : 2 * n]
    sum_state = sums[2 * n : 3 * n] + sums[3 * n : 4 * n]
    sum_dt = sums[4 * n : 5 * n]
    sum_last = sums[edges : edges + 8] + sums[edges + 16 : edges + 24]
    sum_skip = sums[edges + 8 : edges + 16] + sums[edges + 24 : edges + 32]
    gcross_low = gcross.astype(bf16)
    gc = gc + mm(gcross_low, b)
    gb = gb + mm_tn(gcross_low, c)
    gconv = jnp.concatenate([gb, gc], axis=1) * (sig_bc + act_bc * (1.0 - sig_bc))
    ext = jnp.concatenate([gconv, head_bc[...]], axis=0)
    taps = tapbc_ref[...]
    part = bc_ref[...]
    gu = taps[3:4] * gconv
    gtapbc_ref[24:32, :] += fold(gconv * part)
    for k in (1, 2, 3):
        later = jnp.where(wide(ahead[k]), ext[k : k + n], 0.0)
        gu = gu + taps[3 - k : 4 - k] * later
        gtapbc_ref[8 * (3 - k) : 8 * (4 - k), :] += fold(later * part)
    gbc_ref[...] = gu.astype(gbc_ref.dtype)
    gtapbc_ref[32:40, :] += fold(gconv)
    head_bc[...] = gconv[0:8]
    head_seg[...] = seg[0:8]
    rows = lax.broadcasted_iota(jnp.int32, (n, n), 0)
    cols = lax.broadcasted_iota(jnp.int32, (n, n), 1)
    after = jnp.dot(
        (cols >= rows).astype(f32), sum_q, precision=lax.Precision.HIGHEST, preferred_element_type=f32
    )
    edge = jnp.sum(sum_state, axis=0, keepdims=True) + jnp.sum(sum_last, axis=0, keepdims=True)
    glog = after + edge
    gdt = sum_dt + a * glog
    gst = gdt * sigmoid(v)
    gst_ref[...] = jnp.where(low_lanes, 0.0, gst).astype(bf16)
    gpar_ref[0:8] += fold(gst)
    gpar_ref[8:16] += fold(a * dt * glog)
    gpar_ref[16:24] += sum_skip


def scan_bwd_scratch(width, states):
    n = BLOCK
    return [
        pltpu.VMEM((states, width), f32),
        pltpu.VMEM((8, width), f32),
        pltpu.VMEM((8, 2 * states), f32),
        pltpu.VMEM((8, LANES), jnp.int32),
        *[pltpu.VMEM((n, width), f32)] * 5,
        *[pltpu.VMEM((n, width), bf16)] * 3,
        pltpu.VMEM((5 * n + 32, width), bf16),
    ]


def spread_matrix(heads):
    row = lax.broadcasted_iota(jnp.int32, (LANES, heads * WIDTH), 0)
    col = lax.broadcasted_iota(jnp.int32, (LANES, heads * WIDTH), 1)
    return (row % (LANES // 2) == col // WIDTH).astype(bf16)


def on_lanes(v):
    half = jnp.pad(v, [(0, 0)] * (v.ndim - 1) + [(0, LANES // 2 - v.shape[-1])])
    return jnp.concatenate([half, half], axis=-1)


MESH = pl.DeviceIdType.MESH


def place():
    dp, rank = lax.axis_index("dp"), lax.axis_index("tensor")
    return dp // 2, dp % 2, rank


def remote(src, dst, send, recv, dp, rank):
    return pltpu.make_async_remote_copy(
        src_ref=src, dst_ref=dst, send_sem=send, recv_sem=recv, device_id=(dp, rank),
        device_id_type=MESH,
    )


def greet(chips, ranks):
    chip, core, rank = place()
    sem = pltpu.get_barrier_semaphore()
    me = chip * 2 + core

    def signal(dp, r):
        pl.semaphore_signal(sem, inc=1, device_id=(dp, r), device_id_type=MESH)

    signal(chip * 2 + 1 - core, rank)
    for step in (1, -1):
        @pl.when((chip + step >= 0) & (chip + step < chips))
        def _():
            signal(me + 2 * step, rank)
    for k in range(1, ranks):
        signal(me, lax.rem(rank + k, ranks))
    pl.semaphore_wait(sem, ranks + (chip + chips - 1) // chips + (2 * chips - 2 - chip) // chips)


def greet_all(chips, ranks):
    chip, core, rank = place()
    sem = pltpu.get_barrier_semaphore()
    me, devices = chip * 2 + core, 2 * chips
    for k in range(1, devices):
        pl.semaphore_signal(
            sem, inc=1, device_id=(lax.rem(me + k, devices), rank), device_id_type=MESH
        )
    for k in range(1, ranks):
        pl.semaphore_signal(
            sem, inc=1, device_id=(me, lax.rem(rank + k, ranks)), device_id_type=MESH
        )
    pl.semaphore_wait(sem, devices + ranks - 2)


def slab(ref, index, rows):
    return ref.at[pl.ds(pl.multiple_of(index * rows, rows), rows)]


class LineGather:
    def __init__(self, own, slots, send, recv, local, chips):
        self.own, self.slots, self.send, self.recv, self.local = own, slots, send, recv, local
        self.chips, self.rows = chips, own.shape[0]
        self.chip, self.core, self.rank = place()
        self.me = self.chip * 2 + self.core
        self.partner = self.chip * 2 + 1 - self.core
        self.steps = chips

    @staticmethod
    def scratch(chips):
        n = 2 * chips
        return [
            pltpu.SemaphoreType.DMA((3, n)), pltpu.SemaphoreType.DMA((n,)), pltpu.SemaphoreType.DMA,
        ]

    def copy(self, way, origin, src=None):
        target = (self.me + 2, self.me - 2, self.partner)[way]
        slot = slab(self.slots, origin, self.rows)
        return remote(
            slot if src is None else src, slot, self.send.at[way, origin], self.recv.at[origin],
            target, self.rank,
        )

    def pass_on(self, way, origin, src=None, wait=False):
        def go():
            copy = self.copy(way, origin, src)
            copy.wait_send() if wait else copy.start()

        if way == 0:
            pl.when(self.chip + 1 < self.chips)(go)
        elif way == 1:
            pl.when(self.chip > 0)(go)
        else:
            go()

    def keep(self):
        return pltpu.make_async_copy(self.own, slab(self.slots, self.me, self.rows), self.local)

    def sides(self, k):
        return ((0, self.chip - k >= 0, -k), (1, self.chip + k < self.chips, k))

    def step(self, k):
        if k == 0:
            for way in (0, 1, 2):
                self.pass_on(way, self.me, self.own)
            self.keep().start()
            return
        for way, there, shift in self.sides(k):
            @pl.when(there)
            def _():
                origin = self.me + 2 * shift
                self.copy(2, origin).wait_recv()
                self.pass_on(way, origin)
                self.pass_on(2, origin)

    def arrive(self, k, use=None):
        if k == 0:
            self.keep().wait()
            self.copy(2, self.partner).wait_recv()
            if use is not None:
                use(self.chip)
            return
        for way, there, shift in self.sides(k):
            @pl.when(there)
            def _():
                self.copy(2, self.partner + 2 * shift).wait_recv()
                if use is not None:
                    use(self.chip + shift)

    def sent(self):
        for way in (0, 1, 2):
            self.pass_on(way, self.me, self.own, wait=True)
        for k in range(1, self.chips):
            for way, there, shift in self.sides(k):
                @pl.when(there)
                def _():
                    origin = self.me + 2 * shift
                    self.pass_on(way, origin, wait=True)
                    self.pass_on(2, origin, wait=True)

    def finish(self):
        for k in range(self.chips):
            self.arrive(k)
        self.sent()


class TensorGather:
    def __init__(self, own, slots, send, recv, local, ranks):
        self.own, self.slots, self.send, self.recv, self.local = own, slots, send, recv, local
        self.ranks, self.rows = ranks, own.shape[0]
        chip, core, self.rank = place()
        self.me = chip * 2 + core
        self.steps = 2

    @staticmethod
    def scratch(ranks):
        return [
            pltpu.SemaphoreType.DMA((ranks,)), pltpu.SemaphoreType.DMA((ranks,)), pltpu.SemaphoreType.DMA,
        ]

    def near(self, k):
        x = self.rank % 2
        y = self.rank // 2
        across = (y * 2 + 1 - x, (1 - y) * 2 + x)
        if k < 2:
            return remote(
                self.own, slab(self.slots, self.rank, self.rows), self.send.at[k], self.recv.at[k],
                self.me, across[k],
            )
        half = slab(self.slots, across[k - 2] * 2 + (k - 2), self.rows // 2)
        return remote(half, half, self.send.at[k], self.recv.at[k], self.me, across[3 - k])

    def direct(self, k):
        return remote(
            self.own, slab(self.slots, self.rank, self.rows), self.send.at[k], self.recv.at[k],
            self.me, lax.rem(self.rank + k, self.ranks),
        )

    def keep(self):
        return pltpu.make_async_copy(self.own, slab(self.slots, self.rank, self.rows), self.local)

    def step(self, k):
        if k == 0:
            if self.ranks == 4:
                self.near(0).start()
                self.near(1).start()
            else:
                for j in range(1, self.ranks):
                    self.direct(j).start()
            self.keep().start()
        elif self.ranks == 4:
            for j in (0, 1):
                self.near(j).wait_recv()
                self.near(2 + j).start()

    def finish(self):
        self.keep().wait()
        if self.ranks == 4:
            for j in (0, 1):
                self.near(j).wait_send()
                self.near(2 + j).wait()
        else:
            for j in range(1, self.ranks):
                self.direct(j).wait()


def add_rows(target, others, out=None):
    out = target if out is None else out
    rows = target.shape[0]
    some = 32 if rows % 32 == 0 else 16 if rows % 16 == 0 else 8

    @pl.loop(0, rows // some)
    def _(i):
        at = pl.ds(pl.multiple_of(i * some, some), some)
        total = target[at].astype(f32)
        for other in others:
            total = total + other[at].astype(f32)
        out[at] = total.astype(out.dtype)


class LineScatter:
    def __init__(self, parts, swap, flow, send, recv, temp, tsem, chips):
        self.parts, self.swap, self.flow = parts, swap, flow
        self.send, self.recv, self.temp, self.tsem, self.chips = send, recv, temp, tsem, chips
        self.rows, self.wide = parts.shape[0] // (2 * chips), parts.shape[1]
        self.chip, self.core, self.rank = place()
        self.me = self.chip * 2 + self.core
        self.partner = self.chip * 2 + 1 - self.core

    @staticmethod
    def scratch(chips, shape, dtype=bf16):
        block = (shape[0] // (2 * chips),) + tuple(shape[1:])
        return [
            pltpu.VMEM((chips,) + block, dtype), pltpu.VMEM((chips + 1,) + block, dtype),
            pltpu.SemaphoreType.DMA((3, chips)), pltpu.SemaphoreType.DMA((3, chips)),
        ]

    def order(self):
        n = self.chips
        return [c for k in range(n // 2) for c in (n - 1 - k, k)]

    def over(self, c):
        return remote(
            slab(self.parts, 2 * c + 1 - self.core, self.rows), self.swap.at[c], self.send.at[2, c],
            self.recv.at[2, c], self.partner, self.rank,
        )

    def load(self, i):
        c = self.order()[i]
        return pltpu.make_async_copy(
            slab(self.parts, 2 * c + self.core, self.rows), self.held(i), self.tsem.at[i % 2]
        )

    def held(self, i):
        return self.temp.at[i % 2, pl.ds(0, self.rows), pl.ds(0, self.wide)]

    def along(self, way, c, first=False):
        if way == 0:
            here = there = c
        else:
            here, there = c, jnp.where(c == self.chip - 1, self.chips, c)
        src = self.swap.at[c] if first else self.flow.at[here]
        return remote(
            src, self.flow.at[there], self.send.at[way, c], self.recv.at[way, c],
            self.me + (2, -2)[way], self.rank,
        )

    def step(self, k):
        n, chip = self.chips, self.chip
        if k == 0:
            for c in self.order():
                self.over(c).start()
            return
        if k == 1:
            self.load(0).start()
            self.load(1).start()
            for i, c in enumerate(self.order()):
                self.over(c).wait()
                self.load(i).wait()
                add_rows(self.swap.at[c], [self.held(i)])
                if i + 2 < n:
                    self.load(i + 2).start()

                @pl.when((chip == 0) & (c > 0))
                def _():
                    self.along(0, c, True).start()

                @pl.when((chip == n - 1) & (c < n - 1))
                def _():
                    self.along(1, c, True).start()
            return
        t = k - 1
        c = n - 1 - (t - chip)

        @pl.when((chip > 0) & (t >= chip) & (c > chip))
        def _():
            self.along(0, c).wait_recv()
            add_rows(self.flow.at[c], [self.swap.at[c]])
            self.along(0, c).start()

        d = t - (n - 1 - chip)

        @pl.when((chip < n - 1) & (d >= 0) & (d < chip))
        def _():
            self.along(1, d).wait_recv()
            add_rows(self.flow.at[d], [self.swap.at[d]])
            self.along(1, d).start()

    def finish(self, out):
        n, chip = self.chips, self.chip
        mine, up, down = self.swap.at[chip], self.flow.at[chip], self.flow.at[n]

        @pl.when(chip == 0)
        def _():
            self.along(1, chip).wait_recv()
            add_rows(mine, [down], out)

        @pl.when(chip == n - 1)
        def _():
            self.along(0, chip).wait_recv()
            add_rows(mine, [up], out)

        @pl.when((chip > 0) & (chip < n - 1))
        def _():
            self.along(0, chip).wait_recv()
            self.along(1, chip).wait_recv()
            add_rows(mine, [up, down], out)

        for c in range(n):
            @pl.when((chip < n - 1) & (c > chip))
            def _():
                self.along(0, c).wait_send()

            @pl.when((chip > 0) & (c < chip))
            def _():
                self.along(1, c).wait_send()


class TensorScatter:
    def __init__(self, parts, land, send, recv, local, ranks):
        self.parts, self.land = parts, land
        self.send, self.recv, self.local, self.ranks = send, recv, local, ranks
        self.rows = parts.shape[0] // ranks
        chip, core, self.rank = place()
        self.me = chip * 2 + core
        self.steps = 1

    @staticmethod
    def scratch(ranks):
        return [
            pltpu.SemaphoreType.DMA((ranks,)), pltpu.SemaphoreType.DMA((ranks,)),
            pltpu.SemaphoreType.DMA,
        ]

    def load(self):
        return pltpu.make_async_copy(
            slab(self.parts, self.rank, self.rows), self.land.at[0], self.local
        )

    def copy(self, k):
        to = lax.rem(self.rank + k, self.ranks)
        return remote(
            slab(self.parts, to, self.rows), self.land.at[k], self.send.at[k], self.recv.at[k],
            self.me, to,
        )

    def step(self, k):
        for j in range(1, self.ranks):
            self.copy(j).start()

    def arrive(self):
        for j in range(1, self.ranks):
            self.copy(j).wait()

    def total(self, at):
        total = self.land[0, at].astype(f32)
        for j in range(1, self.ranks):
            total = total + self.land[j, at].astype(f32)
        return total


def row_loop(rows, some, body):
    @pl.loop(0, rows // some)
    def _(i):
        body(pl.ds(pl.multiple_of(i * some, some), some))


def params(number):
    return pltpu.CompilerParams(
        collective_id=number, has_side_effects=True, vmem_limit_bytes=VMEM_BYTES
    )


ANY = pl.BlockSpec(memory_space=pl.ANY)
ONCHIP = pl.BlockSpec(memory_space=pltpu.VMEM)


epsilon = 1e-05
CHUNK = 256


def shaped(shape, dtype):
    return jax.ShapeDtypeStruct(shape, dtype)


def dma(count=None):
    return pltpu.SemaphoreType.DMA if count is None else pltpu.SemaphoreType.DMA((count,))


def project_kernel(
    chips, ranks, res_ref, gain_ref, ws_ref, wx_own, x_ref, st_ref, bc_ref, normed_out, wx_out,
    own, normed, wx, *sems
):
    greet(chips, ranks)
    line = LineGather(wx_own, wx, *sems[:3], chips)
    tensor = TensorGather(own, normed, *sems[3:6], ranks)
    line.step(0)
    gain = gain_ref[...]

    def norm(at):
        v = res_ref[at].astype(f32)
        scaling = lax.rsqrt(jnp.mean(v * v, axis=1, keepdims=True) + epsilon)
        own[at] = (v * scaling * gain).astype(bf16)

    row_loop(own.shape[0], 32, norm)
    tensor.step(0)
    line.step(1)
    tensor.step(1)
    if chips > 2:
        line.step(2)
    tensor.finish()
    keep_normed = pltpu.make_async_copy(normed, normed_out, sems[6])
    keep_normed.start()
    tokens, width = x_ref.shape
    deep = 2 * line.rows

    def states(at):
        bc_ref[at] = mm(normed[at], ws_ref[...])

    row_loop(tokens, CHUNK, states)

    def use(first, chip):
        ks = pl.ds(pl.multiple_of(chip * deep, deep), deep)

        def rows(at):
            left = normed[at, ks]
            x, st = mm(left, wx[ks, :width]), mm(left, wx[ks, width:])
            if first:
                x_ref[at], st_ref[at] = x, st
            else:
                x_ref[at] += x
                st_ref[at] += st

        row_loop(tokens, CHUNK, rows)

    line.arrive(0, functools.partial(use, True))
    line.arrive(1, functools.partial(use, False))
    for k in range(2, chips):
        if k + 1 < chips:
            line.step(k + 1)
        line.arrive(k, functools.partial(use, False))
    keep_wx = pltpu.make_async_copy(wx, wx_out, sems[7])
    keep_wx.start()
    line.sent()
    keep_normed.wait()
    keep_wx.wait()


def project(number, chips, ranks, residual, norm_gain, ws, wx_own):
    rows, model = residual.shape
    tokens, width = rows * ranks, wx_own.shape[1]
    return pl.pallas_call(
        functools.partial(project_kernel, chips, ranks),
        in_specs=[ONCHIP, ONCHIP, ONCHIP, ANY],
        out_specs=[ONCHIP, ONCHIP, ONCHIP, ANY, ANY],
        out_shape=[
            shaped((tokens, width - LANES), f32), shaped((tokens, LANES), f32),
            shaped((tokens, ws.shape[1]), f32), shaped((tokens, model), bf16),
            shaped((model, width), bf16),
        ],
        scratch_shapes=[
            pltpu.VMEM((rows, model), bf16), pltpu.VMEM((tokens, model), bf16),
            pltpu.VMEM((model, width), bf16),
            *LineGather.scratch(chips), *TensorGather.scratch(ranks), dma(), dma(),
        ],
        compiler_params=params(number),
        name="project",
    )(residual, norm_gain, ws, wx_own)


def scan_gather_kernel(blocks, total, chips, ranks, *refs):
    own, (wz_own, cot_own) = refs[:9], refs[9:11]
    outs, (wz_out, cot_out) = refs[11:15], refs[15:17]
    scratch, sems = refs[17:21], refs[21:]
    now = pl.program_id(0) * blocks + pl.program_id(1)
    line = LineGather(wz_own, wz_out, *sems[:3], chips)
    tensor = TensorGather(cot_own, cot_out, *sems[3:], ranks)

    @pl.when(now == 0)
    def _():
        greet(chips, ranks)
        line.step(0)
        tensor.step(0)

    @pl.when(now == total - 2)
    def _():
        line.step(1)

    scan_fwd_kernel(blocks, *own, *outs, *scratch)

    @pl.when(now == total - 1)
    def _():
        tensor.step(1)
        for k in range(2, chips):
            line.step(k)
        line.finish()
        tensor.finish()


def scan_forward_gather(
    number, chips, ranks, wz_own, cot_own, x, bc, st, seg, tapx, tapbc, par, spread, skip, nseq
):
    tokens, width = x.shape
    n = BLOCK
    blocks = tokens // nseq // n
    at = lambda s, i: (s * blocks + i, 0)
    whole = lambda s, i: (0, 0)
    states = LANES
    return pl.pallas_call(
        functools.partial(scan_gather_kernel, blocks, nseq * blocks, chips, ranks),
        grid=(nseq, blocks),
        in_specs=[
            pl.BlockSpec((n, width), at),
            pl.BlockSpec((n, 2 * states), at),
            pl.BlockSpec((n, LANES), at),
            pl.BlockSpec((n, LANES), at),
            pl.BlockSpec(tapx.shape, whole),
            pl.BlockSpec(tapbc.shape, whole),
            pl.BlockSpec(par.shape, whole),
            pl.BlockSpec(spread.shape, whole),
            pl.BlockSpec(skip.shape, whole),
            pl.BlockSpec(wz_own.shape, whole),
            pl.BlockSpec(cot_own.shape, whole),
        ],
        out_specs=[
            pl.BlockSpec((n, width), at), pl.BlockSpec((states, width), at),
            pl.BlockSpec((n, width), at), pl.BlockSpec((n, 2 * states), at), ANY, ANY,
        ],
        out_shape=[
            shaped((tokens, width), f32),
            shaped((tokens // n * states, width), bf16),
            shaped((tokens, width), f32),
            shaped((tokens, 2 * states), f32),
            shaped((wz_own.shape[0] * 2 * chips, width), bf16),
            shaped((tokens, cot_own.shape[1]), bf16),
        ],
        scratch_shapes=[
            pltpu.VMEM((states, width), f32),
            pltpu.VMEM((8, width), f32),
            pltpu.VMEM((8, 2 * states), f32),
            pltpu.VMEM((8, LANES), jnp.int32),
            *LineGather.scratch(chips), *TensorGather.scratch(ranks),
        ],
        compiler_params=params(number),
        name="scan_forward",
    )(x, bc, st, seg, tapx, tapbc, par, spread, skip, wz_own, cot_own)


def lane_sums(v):
    total = v[:, :LANES]
    for i in range(LANES, v.shape[1], LANES):
        total = total + v[:, i : i + LANES]
    return total


def row_sums(picks, v):
    high = v.astype(bf16)
    low = (v - high.astype(f32)).astype(bf16)
    return mm_nt(picks, high) + mm_nt(picks, low)


def gate_kernel(
    chips, ranks, gain_ref, wo_own, normed_in, wz_in, y_in, cot_in,
    gz_ref, gy_ref, ng_ref, ggain_ref, wo_out,
    wo, normed, wz, y, cot, z, gng, squares, dots, columns, land, send, recv, loads, *sems
):
    line = LineGather(wo_own, wo, *sems[:3], chips)
    tokens, width = y.shape
    inner = width * ranks
    rank = line.rank
    load = [
        pltpu.make_async_copy(src, dst, loads.at[i])
        for i, (src, dst) in enumerate(((normed_in, normed), (wz_in, wz), (y_in, y), (cot_in, cot)))
    ]
    greet(chips, ranks)
    line.step(0)
    for copy in load:
        copy.start()
    load[0].wait()
    load[1].wait()

    def gate(at):
        z[at] = mm(normed[at], wz[...])

    row_loop(tokens, CHUNK, gate)
    load[2].wait()
    load[3].wait()
    deep = 2 * line.rows

    def use(first, chip):
        ks = pl.ds(pl.multiple_of(chip * deep, deep), deep)

        def rows(at):
            v = mm(cot[at, ks], wo[ks])
            if first:
                gng[at] = v
            else:
                gng[at] += v

        row_loop(tokens, CHUNK, rows)

    line.arrive(0, functools.partial(use, True))
    for k in range(1, chips):
        line.step(k)
        line.arrive(k, functools.partial(use, False))
    keep = pltpu.make_async_copy(wo, wo_out, loads.at[4])
    keep.start()
    gain = gain_ref[0:1]

    def sums(at):
        zz = z[at]
        gated = y[at] * (zz * sigmoid(zz))
        squares[at] = lane_sums(gated * gated)
        dots[at] = lane_sums(gng[at] * gain * gated)

    row_loop(tokens, 16, sums)
    half = lax.broadcasted_iota(jnp.int32, (8, LANES), 0) < 4
    one, other = half.astype(bf16), jnp.logical_not(half).astype(bf16)
    for r in range(0, tokens, CHUNK):
        at = slice(r, r + CHUNK)
        land[rank, :, at] = row_sums(one, squares[at]) + row_sums(other, dots[at])
    copies = [
        remote(
            land.at[rank], land.at[rank], send.at[k], recv.at[k], line.me, lax.rem(rank + k, ranks)
        )
        for k in range(1, ranks)
    ]
    for copy in copies:
        copy.start()
    line.sent()
    for copy in copies:
        copy.wait()
    for r in range(0, tokens, LANES):
        at = slice(r, r + LANES)
        total = land[0, :, at]
        for k in range(1, ranks):
            total = total + land[k, :, at]
        columns[at] = jnp.transpose(jnp.concatenate([total] * (LANES // 8), axis=0))
    ggain_ref[...] = jnp.zeros_like(ggain_ref)

    def grads(at):
        zz, yy, gg = z[at], y[at], gng[at]
        sig = sigmoid(zz)
        silu = zz * sig
        gated = yy * silu
        scale = lax.rsqrt(columns[at, 0:1] / inner + epsilon)
        ng_ref[at] = (gated * scale * gain).astype(bf16)
        weight = scale * scale * scale * columns[at, 4:5] / inner
        ggain_ref[...] += fold(gg * gated * scale)
        grad = scale * gain * gg - gated * weight
        gz_ref[at] = (grad * yy * (sig * (1.0 + zz * (1.0 - sig)))).astype(bf16)
        gy_ref[at] = grad * silu

    row_loop(tokens, 16, grads)
    keep.wait()


def gate(number, chips, ranks, gain, wo_own, normed, wz, y, cot):
    tokens, width = y.shape
    model = normed.shape[1]
    return pl.pallas_call(
        functools.partial(gate_kernel, chips, ranks),
        in_specs=[ONCHIP] + [ANY] * 5,
        out_specs=[ONCHIP] * 4 + [ANY],
        out_shape=[
            shaped((tokens, width), bf16), shaped((tokens, width), f32), shaped((tokens, width), bf16),
            shaped((8, width), f32), shaped((model, width), bf16),
        ],
        scratch_shapes=[
            pltpu.VMEM((model, width), bf16), pltpu.VMEM((tokens, model), bf16),
            pltpu.VMEM((model, width), bf16), pltpu.VMEM((tokens, width), f32),
            pltpu.VMEM((tokens, model), bf16), pltpu.VMEM((tokens, width), f32),
            pltpu.VMEM((tokens, width), f32), pltpu.VMEM((tokens, LANES), f32),
            pltpu.VMEM((tokens, LANES), f32), pltpu.VMEM((tokens, LANES), f32),
            pltpu.VMEM((ranks, 8, tokens), f32), dma(ranks), dma(ranks), dma(5),
            *LineGather.scratch(chips),
        ],
        compiler_params=params(number),
        name="gate",
    )(gain, wo_own, normed, wz, y, cot)


def stream_grads(src, grad, parts, wide, cbuf, stage, csem, ssem):
    count = src.shape[1] // CHUNK

    def load(j):
        slot = lax.rem(j, 2)
        columns = pl.ds(pl.multiple_of(j * CHUNK, CHUNK), CHUNK)
        return pltpu.make_async_copy(src.at[:, columns], cbuf.at[slot], csem.at[slot])

    def store(j):
        slot = lax.rem(j, 2)
        return pltpu.make_async_copy(
            stage.at[slot, :, pl.ds(0, wide)], slab(parts, j, CHUNK), ssem.at[slot]
        )

    load(0).start()

    @pl.loop(0, count)
    def _(j):
        slot = lax.rem(j, 2)

        @pl.when(j + 1 < count)
        def _():
            load(j + 1).start()

        load(j).wait()

        @pl.when(j >= 2)
        def _():
            store(j - 2).wait()

        stage[slot, :, :wide] = mm_tn(cbuf[slot], grad[...]).astype(bf16)
        store(j).start()

    for j in (count - 2, count - 1):
        store(j).wait()


def stream_back(terms, kept, parts, stage, ssem, begin=0, end=1):
    tokens, model = parts.shape
    base, count = int(model // CHUNK * begin), int(model // CHUNK * (end - begin))

    def loads(j):
        slot = lax.rem(j, 2)
        return [
            pltpu.make_async_copy(slab(right, base + j, CHUNK), buffer.at[slot], sem.at[slot])
            for _, right, buffer, sem in terms
        ]

    def store(j):
        slot = lax.rem(j, 2)
        columns = pl.ds(pl.multiple_of((base + j) * CHUNK, CHUNK), CHUNK)
        return pltpu.make_async_copy(stage.at[slot], parts.at[:, columns], ssem.at[slot])

    for copy in loads(0):
        copy.start()

    @pl.loop(0, count)
    def _(j):
        slot = lax.rem(j, 2)

        @pl.when(j + 1 < count)
        def _():
            for copy in loads(j + 1):
                copy.start()

        for copy in loads(j):
            copy.wait()

        @pl.when(j >= 2)
        def _():
            store(j - 2).wait()

        for r in range(0, tokens, CHUNK):
            at = slice(r, r + CHUNK)
            total = jnp.zeros((CHUNK, CHUNK), f32)
            for left, _, buffer, _ in terms:
                total = total + mm_nt(left[at], buffer[slot])
            for left, right in kept:
                total = total + mm_nt(
                    left[at], right[pl.ds(pl.multiple_of((base + j) * CHUNK, CHUNK), CHUNK)]
                )
            stage[slot, at] = total.astype(bf16)
        store(j).start()

    for j in (count - 2, count - 1):
        store(j).wait()


def everyone(buffer, mine, count, send, recv, device):
    row = buffer.at[mine]
    return [
        remote(row, row, send.at[k], recv.at[k], *device(lax.rem(mine + k, count)))
        for k in range(1, count)
    ]


def added(buffer, count):
    total = buffer[0]
    for k in range(1, count):
        total = total + buffer[k]
    return total


def backward_kernel(blocks, total, chips, ranks, *refs):
    ins, refs = refs[:15], refs[15:]
    (ggain_ref, gain_ref), refs = refs[:2], refs[2:]
    (res_in, cot_own_in, ws_in, gz_in, ng_in, normed_in, cot_in, wo_in, wz_in, wx_in), refs = refs[:10], refs[10:]
    (sums_ref, norm_ref, state_ref), refs = refs[:3], refs[3:]
    (z_sum, o_sum, x_sum, block_out, res_grad), refs = refs[:5], refs[5:]
    (xparts, tparts, sparts, zparts, oparts, pparts, gbc_slots, pland), refs = refs[:8], refs[8:]
    scratch, refs = refs[:13], refs[13:]
    (gxs, gbc_own, gtapx, gtapbc, gpar, gz, ng, cbuf, stage, back, wbuf, xbuf), refs = refs[:12], refs[12:]
    (gbc_sum, ws, res, other, wide_out, line_out, tland, state_stage), refs = refs[:8], refs[8:]
    (state_own, state_line, state_low, state_all, pack, packs, land_rank), refs = refs[:7], refs[7:]
    (norm_rank, norm_dp, norm_acc), refs = refs[:3], refs[3:]
    (loads, csem, ssem, bsem, wsem, xsem, osem), refs = refs[:7], refs[7:]
    (qsend, qrecv, nsend, nrecv, msend, mrecv), refs = refs[:6], refs[6:]
    z_job = LineScatter(zparts, *refs[:4], stage, ssem, chips)
    o_job = LineScatter(oparts, *refs[4:8], stage, ssem, chips)
    x_job = LineScatter(xparts, *refs[8:12], stage, ssem, chips)
    s_job = LineScatter(sparts, *refs[12:16], state_stage, csem, chips)
    refs = refs[16:]
    first = TensorScatter(pparts, pland, *refs[:3], ranks)
    second = TensorScatter(tparts, tland, *refs[3:6], ranks)
    around = TensorGather(gbc_own, gbc_slots, *refs[6:9], ranks)
    s_line = LineGather(state_own, state_line, *refs[9:12], chips)
    s_rank = TensorGather(state_low, state_all, *refs[12:15], ranks)
    p_line = LineGather(pack, packs, *refs[15:18], chips)
    now = pl.program_id(0) * blocks + pl.program_id(1)
    tokens, width = gz.shape
    model = normed_in.shape[1]
    rank, me, devices = first.rank, first.me, 2 * chips
    over_dp = lambda d: (d, rank)
    over_rank = lambda r: (me, r)
    fetch = [
        pltpu.make_async_copy(src, dst, loads.at[i])
        for i, (src, dst) in enumerate(((gz_in, gz), (ng_in, ng), (ws_in, ws), (res_in, res)))
    ]

    def once(src, dst, sem):
        copy = pltpu.make_async_copy(src, dst, sem)
        copy.start()
        copy.wait()

    @pl.when(now == 0)
    def _():
        for copy in fetch:
            copy.start()
        greet_all(chips, ranks)
        fetch[0].wait()
        stream_grads(normed_in, gz, zparts, width, cbuf, stage, csem, ssem)
        z_job.step(0)
        fetch[1].wait()
        stream_back([(ng, wo_in, wbuf, wsem)], [], pparts, back, bsem)
        first.step(0)
        z_job.step(1)
        stream_grads(cot_in, ng, oparts, width, cbuf, stage, csem, ssem)
        o_job.step(0)

    early = [k for k in range(2, chips) if 3 * k - 4 < total - 1]

    @pl.when(now == 2)
    def _():
        o_job.step(1)

    for k in early:
        @pl.when(now == 3 * k - 4)
        def _():
            z_job.step(k)

    row = pl.multiple_of(
        (pl.program_id(0) * blocks + blocks - 1 - pl.program_id(1)) * BLOCK, BLOCK
    )
    here = pl.ds(row, BLOCK)
    outs = (
        gxs.at[here, pl.ds(0, width)], gbc_own.at[here], gxs.at[here, pl.ds(width, LANES)],
        gtapx, gtapbc, gpar,
    )
    scan_bwd_kernel(blocks, *ins, *outs, *scratch)

    @pl.when(now == total - 1)
    def _():
        around.step(0)
        fetch[2].wait()
        fetch[3].wait()
        stream_grads(normed_in, gxs, xparts, width + LANES, cbuf, stage, csem, ssem)
        x_job.step(0)
        pack[...] = jnp.zeros_like(pack)
        for k in range(5):
            rows = slice(8 * k, 8 * k + 8)
            pack[k : k + 1, :width] = jnp.sum(gtapx[rows], axis=0, keepdims=True)
            pack[k : k + 1, width:] = jnp.sum(gtapbc[rows], axis=0, keepdims=True)
        pack[5:6, :width] = jnp.sum(ggain_ref[...], axis=0, keepdims=True)
        for k in range(3):
            pack[6:7, k * LANES : (k + 1) * LANES] = jnp.sum(
                gpar[8 * k : 8 * k + 8], axis=0, keepdims=True
            )
        p_line.step(0)
        for k in range(2, chips):
            if k not in early:
                z_job.step(k)
        around.step(1)
        if chips > 2:
            o_job.step(2)
        terms = [(gz, wz_in, wbuf, wsem), (gxs, wx_in, xbuf, xsem)]
        stream_back(terms, [(gbc_own, ws)], tparts, back, bsem, 0, 0.5)
        x_job.step(1)
        for k in range(3, chips):
            o_job.step(k)
        stream_back(terms, [(gbc_own, ws)], tparts, back, bsem, 0.5, 1)
        second.step(0)
        for k in range(1, chips):
            p_line.step(k)
        around.finish()
        for r in range(ranks):
            once(slab(gbc_slots, r, tokens), cbuf.at[r % 2], csem.at[r % 2])

            def add(at):
                v = cbuf[r % 2, at].astype(f32)
                gbc_sum[at] = v if r == 0 else gbc_sum[at] + v

            row_loop(tokens, 64, add)

        def rounded(at):
            gbc_own[at] = gbc_sum[at].astype(bf16)

        row_loop(tokens, 64, rounded)
        depth = sparts.shape[0]
        for i in range(depth // CHUNK):
            columns = pl.ds(pl.multiple_of(rank * depth + i * CHUNK, CHUNK), CHUNK)
            once(normed_in.at[:, columns], cbuf.at[0], csem.at[0])
            state_stage[0] = mm_tn(cbuf[0], gbc_own[...])
            once(state_stage.at[0], sparts.at[pl.ds(i * CHUNK, CHUNK)], csem.at[1])
        s_job.step(0)
        z_job.finish(line_out.at[:, pl.ds(0, width)])
        once(line_out.at[:, pl.ds(0, width)], z_sum, osem.at[0])
        s_job.step(1)
        p_line.finish()
        total_pack = packs[0:8]
        for k in range(1, devices):
            total_pack = total_pack + packs[8 * k : 8 * k + 8]
        land_rank[rank] = total_pack
        packed = everyone(land_rank, rank, ranks, qsend, qrecv, over_rank)
        for copy in packed:
            copy.start()
        first.arrive()
        for r in range(ranks):
            if r == 0:
                once(slab(pparts, rank, first.rows), other, osem.at[1])
            else:
                once(pland.at[r], other, osem.at[1])

            def add(at):
                wide_out[at] = (res[at] if r == 0 else wide_out[at]).astype(f32) + other[at].astype(f32)

            row_loop(first.rows, 16, add)
        keep = pltpu.make_async_copy(wide_out, block_out, osem.at[2])
        keep.start()
        o_job.finish(line_out.at[:, pl.ds(0, width)])
        once(line_out.at[:, pl.ds(0, width)], o_sum, osem.at[0])
        for k in range(2, chips):
            s_job.step(k)
            x_job.step(k)
        for copy in packed:
            copy.wait()
        shared = land_rank[0, :, width:]
        for r in range(1, ranks):
            shared = shared + land_rank[r, :, width:]
        for r in range(ranks):
            sums_ref[:, r * width : (r + 1) * width] = land_rank[r, :, :width]
        sums_ref[:, ranks * width :] = shared
        s_job.finish(state_own)
        for k in range(chips):
            s_line.step(k)
        keep.wait()
        once(cot_own_in, other, osem.at[1])
        once(slab(tparts, rank, second.rows), tland.at[0], osem.at[2])
        second.arrive()
        norm_acc[...] = jnp.zeros_like(norm_acc)
        gain = gain_ref[...]

        def last(at):
            grad = second.total(at)
            v = res[at].astype(f32)
            scaling = lax.rsqrt(jnp.mean(v * v, axis=1, keepdims=True) + epsilon)
            norm_acc[...] += fold(grad * v * scaling)
            grad = grad * gain
            along = jnp.sum(grad * v, axis=1, keepdims=True)
            weight = scaling * scaling * scaling * along / model
            wide_out[at] = other[at].astype(f32) + scaling * grad - v * weight

        row_loop(second.rows, 16, last)
        keep_grad = pltpu.make_async_copy(wide_out, res_grad, osem.at[2])
        keep_grad.start()
        line = jnp.sum(norm_acc[...], axis=0, keepdims=True)
        eighth = model // 8
        for i in range(8):
            norm_rank[rank, i : i + 1, :] = line[:, i * eighth : (i + 1) * eighth]
        across = everyone(norm_rank, rank, ranks, nsend, nrecv, over_rank)
        for copy in across:
            copy.start()
        s_line.finish()

        def lower(at):
            state_low[at] = state_line[at].astype(bf16)

        row_loop(state_low.shape[0], 64, lower)
        s_rank.step(0)
        for copy in across:
            copy.wait()
        norm_dp[me] = added(norm_rank, ranks)
        along_dp = everyone(norm_dp, me, devices, msend, mrecv, over_dp)
        for copy in along_dp:
            copy.start()
        s_rank.step(1)
        x_job.finish(line_out)
        once(line_out, x_sum, osem.at[0])
        s_rank.finish()

        def state(at):
            state_ref[at] = state_all[at].astype(f32)

        row_loop(state_ref.shape[0], 64, state)
        for copy in along_dp:
            copy.wait()
        norm_ref[...] = added(norm_dp, devices)
        keep_grad.wait()


def backward(
    number, chips, ranks, ggain, norm_gain, residual, cot_own, ws, gz, ng, normed, cot, wo, wz, wx,
    x, conv, bc, convbc, st, seg, gy, y, h, tapx, tapbc, par, spread, skip, nseq,
):
    tokens, width = x.shape
    rows, model = residual.shape
    n = BLOCK
    blocks = tokens // nseq // n
    at = lambda s, i: (s * blocks + blocks - 1 - i, 0)
    tail = lambda s, i: (jnp.maximum((s * blocks + blocks - 1 - i) * (n // 8) - 1, 0), 0)
    whole = lambda s, i: (0, 0)
    states = LANES
    full = lambda v: pl.BlockSpec(v.shape, whole)
    once = lambda shape: pl.BlockSpec(shape, whole)
    devices = 2 * chips
    own, depth, wide = model // devices, model // ranks, width + 2 * states
    return pl.pallas_call(
        functools.partial(backward_kernel, blocks, nseq * blocks, chips, ranks),
        grid=(nseq, blocks),
        in_specs=[
            pl.BlockSpec((n, width), at),
            pl.BlockSpec((n, width), at),
            pl.BlockSpec((n, 2 * states), at),
            pl.BlockSpec((n, 2 * states), at),
            pl.BlockSpec((n, LANES), at),
            pl.BlockSpec((n, LANES), at),
            pl.BlockSpec((8, LANES), tail),
            pl.BlockSpec((n, width), at),
            pl.BlockSpec((n, width), at),
            pl.BlockSpec((states, width), at),
            full(tapx), full(tapbc), full(par), full(spread), full(skip), full(ggain), full(norm_gain),
        ]
        + [ANY] * 10,
        out_specs=[
            once((8, width * ranks + 2 * states)), once((8, model // 8)), once((model, 2 * states)),
        ]
        + [ANY] * 13,
        out_shape=[
            shaped((8, width * ranks + 2 * states), f32), shaped((8, model // 8), f32),
            shaped((model, 2 * states), f32),
            shaped((own, width), f32), shaped((own, width), f32), shaped((own, width + LANES), f32),
            shaped((rows, model), f32), shaped((rows, model), f32),
            shaped((model, width + LANES), bf16), shaped((tokens, model), bf16),
            shaped((depth, 2 * states), f32),
            shaped((model, width), bf16), shaped((model, width), bf16), shaped((tokens, model), bf16),
            shaped((ranks * tokens, 2 * states), bf16), shaped((ranks, rows, model), bf16),
        ],
        scratch_shapes=[
            *scan_bwd_scratch(width, states),
            pltpu.VMEM((tokens, width + LANES), bf16),
            pltpu.VMEM((tokens, 2 * states), bf16),
            pltpu.VMEM((40, width), f32),
            pltpu.VMEM((40, 2 * states), f32),
            pltpu.VMEM((24, LANES), f32),
            pltpu.VMEM((tokens, width), bf16),
            pltpu.VMEM((tokens, width), bf16),
            pltpu.VMEM((2, tokens, CHUNK), bf16),
            pltpu.VMEM((2, CHUNK, width + LANES), bf16),
            pltpu.VMEM((2, tokens, CHUNK), bf16),
            pltpu.VMEM((2, CHUNK, width), bf16),
            pltpu.VMEM((2, CHUNK, width + LANES), bf16),
            pltpu.VMEM((tokens, 2 * states), f32),
            pltpu.VMEM((model, 2 * states), bf16),
            pltpu.VMEM((rows, model), bf16),
            pltpu.VMEM((rows, model), bf16),
            pltpu.VMEM((rows, model), f32),
            pltpu.VMEM((own, width + LANES), f32),
            pltpu.VMEM((ranks, rows, model), bf16),
            pltpu.VMEM((2, CHUNK, 2 * states), f32),
            pltpu.VMEM((depth // devices, 2 * states), f32),
            pltpu.VMEM((depth, 2 * states), f32),
            pltpu.VMEM((depth, 2 * states), bf16),
            pltpu.VMEM((model, 2 * states), bf16),
            pltpu.VMEM((8, wide), f32),
            pltpu.VMEM((8 * devices, wide), f32),
            pltpu.VMEM((ranks, 8, wide), f32),
            pltpu.VMEM((ranks, 8, model // 8), f32),
            pltpu.VMEM((devices, 8, model // 8), f32),
            pltpu.VMEM((8, model), f32),
            dma(4), *[dma(2)] * 5, dma(3),
            *[dma(ranks)] * 4, *[dma(devices)] * 2,
            *LineScatter.scratch(chips, (model, width)),
            *LineScatter.scratch(chips, (model, width)),
            *LineScatter.scratch(chips, (model, width + LANES)),
            *LineScatter.scratch(chips, (depth, 2 * states), f32),
            *TensorScatter.scratch(ranks), *TensorScatter.scratch(ranks),
            *TensorGather.scratch(ranks), *LineGather.scratch(chips),
            *TensorGather.scratch(ranks), *LineGather.scratch(chips),
        ],
        compiler_params=params(number),
        name="backward",
    )(
        x, conv, bc, convbc, st, seg, seg, gy, y, h, tapx, tapbc, par, spread, skip, ggain, norm_gain,
        residual, cot_own, ws, gz, ng, normed, cot, wo, wz, wx,
    )


def per_device(
    residual, segment_ids, norm_gain, inner_weight, state_weight, step_weight, conv_weight,
    conv_bias, step_bias, decay_log, skip_gain, gated_gain, out_weight, cotangent,
):
    rank = lax.axis_index("tensor")
    chips, ranks = lax.axis_size("dp") // 2, lax.axis_size("tensor")
    width = inner_weight.shape[2]
    heads = step_weight.shape[1]
    inner_width = gated_gain.shape[0]
    nseq, length = segment_ids.shape
    tokens = nseq * length
    inner_start, head_start = rank * width, rank * heads
    taps = jnp.concatenate([conv_weight, conv_bias[None], jnp.zeros((3, conv_bias.shape[0]), f32)], axis=0)
    tapx = lax.dynamic_slice_in_dim(taps, inner_start, width, 1)
    tapbc = taps[:, inner_width:]
    local = lambda v: lax.dynamic_slice_in_dim(v, head_start, heads, 0)
    rates = -jnp.exp(local(decay_log))
    par = jnp.concatenate(
        [on_lanes(local(step_bias)[None]), on_lanes(rates[None]), jnp.zeros((6, LANES), f32)], axis=0
    )
    skip = jnp.broadcast_to(jnp.repeat(local(skip_gain), WIDTH)[None], (8, width))
    gain = jnp.broadcast_to(
        lax.dynamic_slice_in_dim(gated_gain, inner_start, width, 0)[None], (8, width)
    )
    spread = spread_matrix(heads)
    seg = jnp.broadcast_to(segment_ids.reshape(tokens, 1), (tokens, LANES))

    wx_own = jnp.concatenate([inner_weight[:, 1], on_lanes(step_weight)], axis=1)
    x, st, bc, normed, wx = project(
        1, chips, ranks, residual, norm_gain[None], state_weight, wx_own
    )
    y, h, conv, convbc, wz, cot = scan_forward_gather(
        2, chips, ranks, inner_weight[:, 0], cotangent,
        x, bc, st, seg, tapx, tapbc, par, spread, skip, nseq,
    )
    gz, gy, ng, ggain, wo = gate(3, chips, ranks, gain, out_weight.T, normed, wz, y, cot)
    sums, norm_grad, state_grad, z_grad, out_grad, x_grad, block_out, residual_grad, *_ = backward(
        4, chips, ranks, ggain, norm_gain[None], residual, cotangent, state_weight,
        gz, ng, normed, cot, wo, wz, wx,
        x, conv, bc, convbc, st, seg, gy, y, h, tapx, tapbc, par, spread, skip, nseq,
    )
    inner_grad = jnp.stack([z_grad, x_grad[:, :width]], axis=1)
    by_head = sums[6, :inner_width].reshape(ranks, width)
    by_head = [by_head[:, k * LANES : k * LANES + heads].reshape(-1) for k in range(3)]
    return (
        block_out, residual_grad, norm_grad.reshape(-1), inner_grad, state_grad,
        x_grad[:, width : width + heads], sums[:4], sums[4], *by_head,
        sums[5, :inner_width], out_grad.T,
    )


def solution(mesh):
    rows, both = P("dp", "tensor"), P(("dp", "tensor"), None)
    inner, out = P("dp", None, "tensor"), P("tensor", "dp")
    return jax.shard_map(
        per_device,
        mesh=mesh,
        in_specs=(
            both, P("dp", None), P(), inner, P(), rows, P(), P(), P(), P(), P(), P(), out, both,
        ),
        out_specs=(both, both, P(), inner, P(), rows, P(), P(), P(), P(), P(), P(), out),
        check_vma=False,
    )
```

```python
import functools
import jax
import jax.numpy as jnp
from jax import lax
from jax.experimental import pallas as pl
from jax.experimental.pallas import tpu as pltpu
from jax.sharding import PartitionSpec as P

LANES = 128
BLOCK = 128
WIDTH = 64
VMEM_BYTES = 60 * 1024 * 1024
f32, bf16 = jnp.float32, jnp.bfloat16
ROWS0 = (((0,), (0,)), ((), ()))
COLS1 = (((1,), (1,)), ((), ()))


def mm(a, b):
    return jnp.dot(a, b, preferred_element_type=f32)


def mm_tn(a, b):
    return lax.dot_general(a, b, ROWS0, preferred_element_type=f32)


def mm_nt(a, b):
    return lax.dot_general(a, b, COLS1, preferred_element_type=f32)


def sigmoid(v):
    return 0.5 + 0.5 * jnp.tanh(0.5 * v)


def two_parts(v, low_lanes):
    high = v.astype(bf16)
    return jnp.where(low_lanes, (v - high.astype(f32)).astype(bf16), high)


def head_sums(v, spread):
    high = v.astype(bf16)
    low = (v - high.astype(f32)).astype(bf16)
    return mm_nt(high, spread) + mm_nt(low, spread)


def shifted_masks(seg_ext, seg):
    n = seg.shape[0]
    return [None] + [seg_ext[8 - k : 8 - k + n] == seg for k in (1, 2, 3)]


def convolve(tail, part, masks, taps):
    n = part.shape[0]
    ext = jnp.concatenate([tail, part], axis=0)
    total = taps[4:5] + taps[3:4] * part
    for k in (1, 2, 3):
        total = total + taps[3 - k : 4 - k] * jnp.where(masks[k], ext[8 - k : 8 - k + n], 0.0)
    return total


def wide(v):
    return jnp.concatenate([v, v], axis=1)


def step_state(raw, params, seg, prev_seg, end_seg, n):
    row = lax.broadcasted_iota(jnp.int32, (n, n), 0)
    col = lax.broadcasted_iota(jnp.int32, (n, n), 1)
    v = raw + params[0:1]
    dt = jnp.maximum(v, 0.0) + jnp.log1p(jnp.exp(-jnp.abs(v)))
    a = params[1:2]
    cum = jnp.dot(
        (row >= col).astype(f32), dt * a, precision=lax.Precision.HIGHEST, preferred_element_type=f32
    )
    last = cum[n - 1 : n]
    into = jnp.where(seg == prev_seg, jnp.exp(cum), 0.0)
    onto = jnp.where(seg == end_seg, jnp.exp(last - cum), 0.0)
    through = jnp.where(end_seg == prev_seg, jnp.exp(last), 0.0)
    bias = jnp.where((row >= col) & (seg == jnp.transpose(seg)), 0.0, -1e30)
    return v, dt, a, cum, into, onto, through, bias


def scan_fwd_kernel(
    blocks, x_ref, bc_ref, st_ref, seg_ref, tapx_ref, tapbc_ref, par_ref, spread_ref, skip_ref,
    y_ref, h_ref, conv_ref, convbc_ref, state, tail_x, tail_bc, tail_seg,
):
    n = BLOCK
    block = pl.program_id(1)

    @pl.when(block == 0)
    def _():
        state[...] = jnp.zeros_like(state)
        tail_x[...] = jnp.zeros_like(tail_x)
        tail_bc[...] = jnp.zeros_like(tail_bc)
        tail_seg[...] = jnp.full_like(tail_seg, -1)

    seg = seg_ref[...]
    masks = shifted_masks(jnp.concatenate([tail_seg[...], seg], axis=0), seg)
    prev_seg, end_seg = tail_seg[7:8], seg[n - 1 : n]
    v, dt, a, cum, into, onto, through, bias = step_state(
        st_ref[...], par_ref[...], seg, prev_seg, end_seg, n
    )
    cum_t = jnp.transpose(cum)
    low_lanes = lax.broadcasted_iota(jnp.int32, (n, LANES), 1) >= LANES // 2
    spread = spread_ref[...]
    dt_w = mm(two_parts(dt, low_lanes), spread)
    into_w = mm(two_parts(into, low_lanes), spread)
    onto_w = mm(two_parts(onto, low_lanes), spread)
    through_w = mm(two_parts(jnp.broadcast_to(through, (8, LANES)), low_lanes[:8]), spread)[0:1]
    bc_masks = [None] + [wide(m) for m in masks[1:]]
    conv_bc = convolve(tail_bc[...], bc_ref[...], bc_masks, tapbc_ref[...])
    convbc_ref[...] = conv_bc
    act_bc = conv_bc * sigmoid(conv_bc)
    b, c = act_bc[:, :LANES].astype(bf16), act_bc[:, LANES:].astype(bf16)
    cross = mm_nt(c, b)
    entering = state[...].astype(bf16)
    h_ref[...] = entering
    first_half = lax.broadcasted_iota(jnp.int32, (n, LANES), 1) < WIDTH
    for pair in range(x_ref.shape[1] // LANES):
        sl = slice(pair * LANES, (pair + 1) * LANES)
        conv = convolve(tail_x[:, sl], x_ref[:, sl], masks, tapx_ref[:, sl])
        conv_ref[:, sl] = conv
        xs = conv * sigmoid(conv)
        xd = xs * dt_w[:, sl]
        outside = mm(c, entering[:, sl]) * into_w[:, sl]
        mixes = []
        for h in (2 * pair, 2 * pair + 1):
            decay = jnp.exp(cum[:, h : h + 1] - cum_t[h : h + 1, :] + bias)
            mixes.append((decay * cross).astype(bf16))
        stacked = jnp.concatenate(
            [jnp.where(first_half, xd, 0.0), jnp.where(first_half, 0.0, xd)], axis=0
        ).astype(bf16)
        inside = mm(jnp.concatenate(mixes, axis=1), stacked)
        y_ref[:, sl] = inside + outside + skip_ref[0:1, sl] * xs
        local = mm_tn(b, (onto_w[:, sl] * xd).astype(bf16))
        state[:, sl] = through_w[:, sl] * state[:, sl] + local
    tail_x[...] = x_ref[n - 8 :, :]
    tail_bc[...] = bc_ref[n - 8 :, :]
    tail_seg[...] = seg_ref[n - 8 :, :]


def fold(v):
    total = v[0:8]
    for r in range(8, v.shape[0], 8):
        total = total + v[r : r + 8]
    return total


def scan_bwd_kernel(
    blocks, x_ref, conv_ref, bc_ref, convbc_ref, st_ref, seg_ref, segt_ref, gy_ref, y_ref, h_ref,
    tapx_ref, tapbc_ref, par_ref, spread_ref, skip_ref,
    gx_ref, gbc_ref, gst_ref, gtapx_ref, gtapbc_ref, gpar_ref,
    gstate, head_x, head_bc, head_seg, xs_s, slope_s, back_s, dt_s, onto_s, xd_s, sums_s,
):
    n = BLOCK
    step = pl.program_id(1)
    block = blocks - 1 - step

    @pl.when((step == 0) & (pl.program_id(0) == 0))
    def _():
        gtapx_ref[...] = jnp.zeros_like(gtapx_ref)
        gtapbc_ref[...] = jnp.zeros_like(gtapbc_ref)
        gpar_ref[...] = jnp.zeros_like(gpar_ref)

    @pl.when(step == 0)
    def _():
        gstate[...] = jnp.zeros_like(gstate)
        head_x[...] = jnp.zeros_like(head_x)
        head_bc[...] = jnp.zeros_like(head_bc)
        head_seg[...] = jnp.full_like(head_seg, -1)

    seg = seg_ref[...]
    first = block == 0
    seg_next = jnp.concatenate([seg, head_seg[...]], axis=0)
    ahead = [None] + [seg_next[k : k + n] == seg for k in (1, 2, 3)]
    prev_seg = jnp.where(first, -1, segt_ref[7:8])
    end_seg = seg[n - 1 : n]
    v, dt, a, cum, into, onto, through, bias = step_state(
        st_ref[...], par_ref[...], seg, prev_seg, end_seg, n
    )
    cum_t = jnp.transpose(cum)
    low_lanes = lax.broadcasted_iota(jnp.int32, (n, LANES), 1) >= LANES // 2
    spread = spread_ref[...]
    dt_s[...] = mm(two_parts(dt, low_lanes), spread)
    into_w = mm(two_parts(into, low_lanes), spread)
    onto_s[...] = mm(two_parts(onto, low_lanes), spread)
    through_w = mm(two_parts(jnp.broadcast_to(through, (8, LANES)), low_lanes[:8]), spread)[0:1]
    conv_bc = convbc_ref[...]
    sig_bc = sigmoid(conv_bc)
    act_bc = conv_bc * sig_bc
    b, c = act_bc[:, :LANES].astype(bf16), act_bc[:, LANES:].astype(bf16)
    cross = mm_nt(c, b)
    first_half = lax.broadcasted_iota(jnp.int32, (n, LANES), 1) < WIDTH
    halves = lambda t: jnp.concatenate(
        [jnp.where(first_half, t, 0.0), jnp.where(first_half, 0.0, t)], axis=0
    ).astype(bf16)
    into_s, onto_low = sums_s.at[0:n], sums_s.at[n : 2 * n]
    pairs = [slice(i, i + LANES) for i in range(0, x_ref.shape[1], LANES)]

    for sl in pairs:
        conv = conv_ref[:, sl]
        sig = sigmoid(conv)
        xs = conv * sig
        xs_s[:, sl] = xs
        slope_s[:, sl] = sig + xs * (1.0 - sig)
        xd = xs * dt_s[:, sl]
        xd_s[:, sl] = xd.astype(bf16)
        onto_low[:, sl] = (xd * onto_s[:, sl]).astype(bf16)
        into_s[:, sl] = (gy_ref[:, sl] * into_w[:, sl]).astype(bf16)
    before = h_ref[...]
    gstate_low = gstate[...].astype(bf16)
    gy_into = into_s[...]
    gc = mm_nt(gy_into, before)
    gb = mm_nt(onto_low[...], gstate_low)
    back_s[...] = mm(b, gstate_low)
    edges = 5 * n
    for sl in pairs:
        old = through_w[:, sl] * gstate[:, sl]
        last = fold(old * before[:, sl].astype(f32))
        skips = fold(gy_ref[:, sl] * xs_s[:, sl])
        both = jnp.concatenate([last, skips], axis=0)
        high = both.astype(bf16)
        sums_s[edges : edges + 16, sl] = high
        sums_s[edges + 16 : edges + 32, sl] = (both - high.astype(f32)).astype(bf16)
        gstate[:, sl] = old + mm_tn(c, gy_into[:, sl])
    gcross = jnp.zeros((n, n), f32)
    for pair, sl in enumerate(pairs):
        xs = xs_s[:, sl]
        xd_low = xd_s[:, sl]
        gy = gy_ref[:, sl]
        skip = skip_ref[0:1, sl]
        inner = y_ref[:, sl] - skip * xs
        g_state = onto_s[:, sl] * back_s[:, sl]
        gy_halves = halves(gy)
        gmix = mm_nt(gy_halves, xd_low)
        mixes = []
        for i, h in enumerate((2 * pair, 2 * pair + 1)):
            decay = jnp.exp(cum[:, h : h + 1] - cum_t[h : h + 1, :] + bias)
            mixes.append((decay * cross).astype(bf16))
            gcross = gcross + decay * gmix[i * n : (i + 1) * n]
        gxd = mm_tn(jnp.concatenate(mixes, axis=0), gy_halves) + g_state
        xd_r, gy_r = xd_low.astype(f32), gy.astype(bf16).astype(f32)
        q = gy_r * inner - xd_r * gxd
        high = q.astype(bf16)
        sums_s[0:n, sl] = high
        sums_s[n : 2 * n, sl] = (q - high.astype(f32)).astype(bf16)
        q = xd_r * g_state
        high = q.astype(bf16)
        sums_s[2 * n : 3 * n, sl] = high
        sums_s[3 * n : 4 * n, sl] = (q - high.astype(f32)).astype(bf16)
        sums_s[4 * n : 5 * n, sl] = (xs * gxd).astype(bf16)
        gconv = (dt_s[:, sl] * gxd + skip * gy) * slope_s[:, sl]
        taps = tapx_ref[:, sl]
        part = x_ref[:, sl]
        ext = jnp.concatenate([gconv, head_x[:, sl]], axis=0)
        gu = taps[3:4] * gconv
        gtapx_ref[24:32, sl] += fold(gconv * part)
        for k in (1, 2, 3):
            later = jnp.where(ahead[k], ext[k : k + n], 0.0)
            gu = gu + taps[3 - k : 4 - k] * later
            gtapx_ref[8 * (3 - k) : 8 * (4 - k), sl] += fold(later * part)
        gx_ref[:, sl] = gu.astype(bf16)
        gtapx_ref[32:40, sl] += fold(gconv)
        head_x[:, sl] = gconv[0:8]
    sums = mm_nt(sums_s[...], spread)
    sum_q = sums[0:n] + sums[n : 2 * n]
    sum_state = sums[2 * n : 3 * n] + sums[3 * n : 4 * n]
    sum_dt = sums[4 * n : 5 * n]
    sum_last = sums[edges : edges + 8] + sums[edges + 16 : edges + 24]
    sum_skip = sums[edges + 8 : edges + 16] + sums[edges + 24 : edges + 32]
    gcross_low = gcross.astype(bf16)
    gc = gc + mm(gcross_low, b)
    gb = gb + mm_tn(gcross_low, c)
    gconv = jnp.concatenate([gb, gc], axis=1) * (sig_bc + act_bc * (1.0 - sig_bc))
    ext = jnp.concatenate([gconv, head_bc[...]], axis=0)
    taps = tapbc_ref[...]
    part = bc_ref[...]
    gu = taps[3:4] * gconv
    gtapbc_ref[24:32, :] += fold(gconv * part)
    for k in (1, 2, 3):
        later = jnp.where(wide(ahead[k]), ext[k : k + n], 0.0)
        gu = gu + taps[3 - k : 4 - k] * later
        gtapbc_ref[8 * (3 - k) : 8 * (4 - k), :] += fold(later * part)
    gbc_ref[...] = gu.astype(gbc_ref.dtype)
    gtapbc_ref[32:40, :] += fold(gconv)
    head_bc[...] = gconv[0:8]
    head_seg[...] = seg[0:8]
    rows = lax.broadcasted_iota(jnp.int32, (n, n), 0)
    cols = lax.broadcasted_iota(jnp.int32, (n, n), 1)
    after = jnp.dot(
        (cols >= rows).astype(f32), sum_q, precision=lax.Precision.HIGHEST, preferred_element_type=f32
    )
    edge = jnp.sum(sum_state, axis=0, keepdims=True) + jnp.sum(sum_last, axis=0, keepdims=True)
    glog = after + edge
    gdt = sum_dt + a * glog
    gst = gdt * sigmoid(v)
    gst_ref[...] = jnp.where(low_lanes, 0.0, gst).astype(bf16)
    gpar_ref[0:8] += fold(gst)
    gpar_ref[8:16] += fold(a * dt * glog)
    gpar_ref[16:24] += sum_skip


def scan_bwd_scratch(width, states):
    n = BLOCK
    return [
        pltpu.VMEM((states, width), f32),
        pltpu.VMEM((8, width), f32),
        pltpu.VMEM((8, 2 * states), f32),
        pltpu.VMEM((8, LANES), jnp.int32),
        *[pltpu.VMEM((n, width), f32)] * 5,
        pltpu.VMEM((n, width), bf16),
        pltpu.VMEM((5 * n + 32, width), bf16),
    ]


def spread_matrix(heads):
    row = lax.broadcasted_iota(jnp.int32, (LANES, heads * WIDTH), 0)
    col = lax.broadcasted_iota(jnp.int32, (LANES, heads * WIDTH), 1)
    return (row % (LANES // 2) == col // WIDTH).astype(bf16)


def on_lanes(v):
    half = jnp.pad(v, [(0, 0)] * (v.ndim - 1) + [(0, LANES // 2 - v.shape[-1])])
    return jnp.concatenate([half, half], axis=-1)


MESH = pl.DeviceIdType.MESH


def place():
    dp, rank = lax.axis_index("dp"), lax.axis_index("tensor")
    return dp // 2, dp % 2, rank


def remote(src, dst, send, recv, dp, rank):
    return pltpu.make_async_remote_copy(
        src_ref=src, dst_ref=dst, send_sem=send, recv_sem=recv, device_id=(dp, rank),
        device_id_type=MESH,
    )


def greet(chips, ranks):
    chip, core, rank = place()
    sem = pltpu.get_barrier_semaphore()
    me = chip * 2 + core

    def signal(dp, r):
        pl.semaphore_signal(sem, inc=1, device_id=(dp, r), device_id_type=MESH)

    signal(chip * 2 + 1 - core, rank)
    for step in (1, -1):
        @pl.when((chip + step >= 0) & (chip + step < chips))
        def _():
            signal(me + 2 * step, rank)
    for k in range(1, ranks):
        signal(me, lax.rem(rank + k, ranks))
    pl.semaphore_wait(sem, ranks + (chip + chips - 1) // chips + (2 * chips - 2 - chip) // chips)


def greet_all(chips, ranks):
    chip, core, rank = place()
    sem = pltpu.get_barrier_semaphore()
    me, devices = chip * 2 + core, 2 * chips
    for k in range(1, devices):
        pl.semaphore_signal(
            sem, inc=1, device_id=(lax.rem(me + k, devices), rank), device_id_type=MESH
        )
    for k in range(1, ranks):
        pl.semaphore_signal(
            sem, inc=1, device_id=(me, lax.rem(rank + k, ranks)), device_id_type=MESH
        )
    pl.semaphore_wait(sem, devices + ranks - 2)


def slab(ref, index, rows):
    return ref.at[pl.ds(pl.multiple_of(index * rows, rows), rows)]


class LineGather:
    def __init__(self, own, slots, send, recv, local, chips):
        self.own, self.slots, self.send, self.recv, self.local = own, slots, send, recv, local
        self.chips, self.rows = chips, own.shape[0]
        self.chip, self.core, self.rank = place()
        self.me = self.chip * 2 + self.core
        self.partner = self.chip * 2 + 1 - self.core
        self.steps = chips

    @staticmethod
    def scratch(chips):
        n = 2 * chips
        return [
            pltpu.SemaphoreType.DMA((3, n)), pltpu.SemaphoreType.DMA((n,)), pltpu.SemaphoreType.DMA,
        ]

    def copy(self, way, origin, src=None):
        target = (self.me + 2, self.me - 2, self.partner)[way]
        slot = slab(self.slots, origin, self.rows)
        return remote(
            slot if src is None else src, slot, self.send.at[way, origin], self.recv.at[origin],
            target, self.rank,
        )

    def pass_on(self, way, origin, src=None, wait=False):
        def go():
            copy = self.copy(way, origin, src)
            copy.wait_send() if wait else copy.start()

        if way == 0:
            pl.when(self.chip + 1 < self.chips)(go)
        elif way == 1:
            pl.when(self.chip > 0)(go)
        else:
            go()

    def keep(self):
        return pltpu.make_async_copy(self.own, slab(self.slots, self.me, self.rows), self.local)

    def sides(self, k):
        return ((0, self.chip - k >= 0, -k), (1, self.chip + k < self.chips, k))

    def step(self, k):
        if k == 0:
            for way in (0, 1, 2):
                self.pass_on(way, self.me, self.own)
            self.keep().start()
            return
        for way, there, shift in self.sides(k):
            @pl.when(there)
            def _():
                origin = self.me + 2 * shift
                self.copy(2, origin).wait_recv()
                self.pass_on(way, origin)
                self.pass_on(2, origin)

    def arrive(self, k, use=None):
        if k == 0:
            self.keep().wait()
            self.copy(2, self.partner).wait_recv()
            if use is not None:
                use(self.chip)
            return
        for way, there, shift in self.sides(k):
            @pl.when(there)
            def _():
                self.copy(2, self.partner + 2 * shift).wait_recv()
                if use is not None:
                    use(self.chip + shift)

    def sent(self):
        for way in (0, 1, 2):
            self.pass_on(way, self.me, self.own, wait=True)
        for k in range(1, self.chips):
            for way, there, shift in self.sides(k):
                @pl.when(there)
                def _():
                    origin = self.me + 2 * shift
                    self.pass_on(way, origin, wait=True)
                    self.pass_on(2, origin, wait=True)

    def finish(self):
        for k in range(self.chips):
            self.arrive(k)
        self.sent()


class TensorGather:
    def __init__(self, own, slots, send, recv, local, ranks):
        self.own, self.slots, self.send, self.recv, self.local = own, slots, send, recv, local
        self.ranks, self.rows = ranks, own.shape[0]
        chip, core, self.rank = place()
        self.me = chip * 2 + core
        self.steps = 2

    @staticmethod
    def scratch(ranks):
        return [
            pltpu.SemaphoreType.DMA((ranks,)), pltpu.SemaphoreType.DMA((ranks,)), pltpu.SemaphoreType.DMA,
        ]

    def near(self, k):
        x = self.rank % 2
        y = self.rank // 2
        across = (y * 2 + 1 - x, (1 - y) * 2 + x)
        if k < 2:
            return remote(
                self.own, slab(self.slots, self.rank, self.rows), self.send.at[k], self.recv.at[k],
                self.me, across[k],
            )
        half = slab(self.slots, across[k - 2] * 2 + (k - 2), self.rows // 2)
        return remote(half, half, self.send.at[k], self.recv.at[k], self.me, across[3 - k])

    def direct(self, k):
        return remote(
            self.own, slab(self.slots, self.rank, self.rows), self.send.at[k], self.recv.at[k],
            self.me, lax.rem(self.rank + k, self.ranks),
        )

    def keep(self):
        return pltpu.make_async_copy(self.own, slab(self.slots, self.rank, self.rows), self.local)

    def step(self, k):
        if k == 0:
            if self.ranks == 4:
                self.near(0).start()
                self.near(1).start()
            else:
                for j in range(1, self.ranks):
                    self.direct(j).start()
            self.keep().start()
        elif self.ranks == 4:
            for j in (0, 1):
                self.near(j).wait_recv()
                self.near(2 + j).start()

    def finish(self):
        self.keep().wait()
        if self.ranks == 4:
            for j in (0, 1):
                self.near(j).wait_send()
                self.near(2 + j).wait()
        else:
            for j in range(1, self.ranks):
                self.direct(j).wait()


def add_rows(target, others, out=None):
    out = target if out is None else out
    rows = target.shape[0]
    some = 64 if rows % 64 == 0 else rows
    kind = out.dtype if len(others) == 1 else f32

    def add(at):
        total = target[at].astype(kind)
        for other in others:
            total = total + other[at].astype(kind)
        out[at] = total.astype(out.dtype)

    row_loop(rows, some, add)


class LineScatter:
    def __init__(self, parts, swap, flow, send, recv, chips):
        self.parts, self.swap, self.flow = parts, swap, flow
        self.send, self.recv, self.chips = send, recv, chips
        self.rows = parts.shape[0] // (2 * chips)
        self.chip, self.core, self.rank = place()
        self.me = self.chip * 2 + self.core
        self.partner = self.chip * 2 + 1 - self.core

    @staticmethod
    def scratch(chips, shape, dtype=bf16):
        block = (shape[0] // (2 * chips),) + tuple(shape[1:])
        return [
            pltpu.VMEM((chips,) + block, dtype), pltpu.VMEM((chips + 1,) + block, dtype),
            pltpu.SemaphoreType.DMA((3, chips)), pltpu.SemaphoreType.DMA((3, chips)),
        ]

    def order(self):
        n = self.chips
        return [c for k in range(n // 2) for c in (n - 1 - k, k)]

    def over(self, c):
        return remote(
            slab(self.parts, 2 * c + 1 - self.core, self.rows), self.swap.at[c], self.send.at[2, c],
            self.recv.at[2, c], self.partner, self.rank,
        )

    def along(self, way, c, first=False):
        if way == 0:
            here = there = c
        else:
            here, there = c, jnp.where(c == self.chip - 1, self.chips, c)
        src = self.swap.at[c] if first else self.flow.at[here]
        return remote(
            src, self.flow.at[there], self.send.at[way, c], self.recv.at[way, c],
            self.me + (2, -2)[way], self.rank,
        )

    def send_off(self, c):
        n, chip = self.chips, self.chip

        @pl.when((chip == 0) & (c > 0))
        def _():
            self.along(0, c, True).start()

        @pl.when((chip == n - 1) & (c < n - 1))
        def _():
            self.along(1, c, True).start()

    def send_rest(self):
        for c in self.order()[2:]:
            self.send_off(c)

    def step(self, k, hold=False):
        n, chip = self.chips, self.chip
        if k == 0:
            for c in self.order():
                self.over(c).start()
            return
        if k == 1:
            for i, c in enumerate(self.order()):
                self.over(c).wait()
                add_rows(self.swap.at[c], [slab(self.parts, 2 * c + self.core, self.rows)])
                if i < 2 or not hold:
                    self.send_off(c)
            return
        t = k - 1
        c = n - 1 - (t - chip)

        @pl.when((chip > 0) & (t >= chip) & (c > chip))
        def _():
            self.along(0, c).wait_recv()
            add_rows(self.flow.at[c], [self.swap.at[c]])
            self.along(0, c).start()

        d = t - (n - 1 - chip)

        @pl.when((chip < n - 1) & (d >= 0) & (d < chip))
        def _():
            self.along(1, d).wait_recv()
            add_rows(self.flow.at[d], [self.swap.at[d]])
            self.along(1, d).start()

    def finish(self, out):
        n, chip = self.chips, self.chip
        mine, up, down = self.swap.at[chip], self.flow.at[chip], self.flow.at[n]

        @pl.when(chip == 0)
        def _():
            self.along(1, chip).wait_recv()
            add_rows(mine, [down], out)

        @pl.when(chip == n - 1)
        def _():
            self.along(0, chip).wait_recv()
            add_rows(mine, [up], out)

        @pl.when((chip > 0) & (chip < n - 1))
        def _():
            self.along(0, chip).wait_recv()
            self.along(1, chip).wait_recv()
            add_rows(mine, [up, down], out)

        for c in range(n):
            @pl.when((chip < n - 1) & (c > chip))
            def _():
                self.along(0, c).wait_send()

            @pl.when((chip > 0) & (c < chip))
            def _():
                self.along(1, c).wait_send()


class DirectScatter:
    def __init__(self, parts, land, temp, send, recv, tsem, ranks):
        self.parts, self.land, self.temp = parts, land, temp
        self.send, self.recv, self.tsem, self.ranks = send, recv, tsem, ranks
        self.rows = parts.shape[0] // ranks
        chip, core, self.rank = place()
        self.me = chip * 2 + core

    @staticmethod
    def scratch(ranks):
        return [dma(ranks), dma(ranks), dma(2)]

    def copy(self, k):
        to = lax.rem(self.rank + k, self.ranks)
        return remote(
            slab(self.parts, to, self.rows), self.land.at[k], self.send.at[k], self.recv.at[k],
            self.me, to,
        )

    def step(self, k, g):
        if k == 0 and g == 1:
            for j in range(1, self.ranks):
                self.copy(j).start()

    def arrive(self):
        for j in range(1, self.ranks):
            self.copy(j).wait()

    def totals(self, some, body):
        @pl.loop(0, self.rows // some)
        def _(i):
            at = pl.ds(pl.multiple_of(i * some, some), some)
            total = None
            for j in range(self.ranks):
                src = slab(self.parts, self.rank * (self.rows // some) + i, some) if j == 0 else self.land.at[j, at]
                copy = pltpu.make_async_copy(src, self.temp.at[j % 2, pl.ds(0, some)], self.tsem.at[j % 2])
                copy.start()
                copy.wait()
                v = self.temp[j % 2, pl.ds(0, some)].astype(f32)
                total = v if total is None else total + v
            body(at, total)


class SmallScatter:
    def __init__(self, parts, swap, land, send, recv, chips):
        self.parts, self.swap, self.land, self.send, self.recv = parts, swap, land, send, recv
        self.chips, self.rows = chips, parts.shape[0] // (2 * chips)
        self.chip, self.core, self.rank = place()

    @staticmethod
    def scratch(chips, shape, dtype):
        block = pltpu.VMEM((chips, shape[0] // (2 * chips), shape[1]), dtype)
        return [
            block, block, pltpu.SemaphoreType.DMA((2, chips)), pltpu.SemaphoreType.DMA((2, chips)),
        ]

    def over(self, c):
        return remote(
            slab(self.parts, 2 * c + 1 - self.core, self.rows), self.swap.at[c], self.send.at[0, c],
            self.recv.at[0, c], self.chip * 2 + 1 - self.core, self.rank,
        )

    def straight(self, k):
        to = lax.rem(self.chip + k, self.chips)
        return remote(
            self.swap.at[to], self.land.at[self.chip], self.send.at[1, k], self.recv.at[1, k],
            2 * to + self.core, self.rank,
        )

    def step(self, k):
        if k == 0:
            for c in range(self.chips):
                self.over(c).start()
            return
        for c in range(self.chips):
            self.over(c).wait()
            add_rows(self.swap.at[c], [slab(self.parts, 2 * c + self.core, self.rows)])
        for j in range(1, self.chips):
            self.straight(j).start()

    def finish(self, out):
        for j in range(1, self.chips):
            self.straight(j).wait()
        total = self.swap[self.chip].astype(f32)
        for j in range(1, self.chips):
            total = total + self.land[lax.rem(self.chip + j, self.chips)].astype(f32)
        out[...] = total.astype(out.dtype)


class SmallGather:
    def __init__(self, own, slots, send, recv, chips):
        self.own, self.slots, self.send, self.recv = own, slots, send, recv
        self.chips, self.rows = chips, own.shape[0]
        self.chip, self.core, self.rank = place()
        self.me = self.chip * 2 + self.core

    @staticmethod
    def scratch(chips):
        return [pltpu.SemaphoreType.DMA((2, chips)), pltpu.SemaphoreType.DMA((2, chips))]

    def straight(self, k):
        slot = slab(self.slots, self.me, self.rows)
        return remote(
            self.own, slot, self.send.at[0, k], self.recv.at[0, k],
            2 * lax.rem(self.chip + k, self.chips) + self.core, self.rank,
        )

    def over(self, k):
        slot = slab(
            self.slots, 2 * lax.rem(self.chip + self.chips - k, self.chips) + self.core, self.rows
        )
        return remote(
            self.own if k == 0 else slot, slot, self.send.at[1, k], self.recv.at[1, k],
            self.chip * 2 + 1 - self.core, self.rank,
        )

    def step(self, k):
        if k == 0:
            for j in range(1, self.chips):
                self.straight(j).start()
            self.over(0).start()
            self.slots[pl.ds(pl.multiple_of(self.me * self.rows, self.rows), self.rows)] = self.own[...]
            return
        for j in range(1, self.chips):
            self.straight(j).wait_recv()
            self.over(j).start()

    def finish(self):
        for j in range(1, self.chips):
            self.straight(j).wait_send()
        for j in range(self.chips):
            self.over(j).wait()


class HalvesScatter:
    def __init__(self, parts, land, temp, send, recv, tsem):
        self.parts, self.land, self.temp, self.send, self.recv, self.tsem = parts, land, temp, send, recv, tsem
        chip, core, self.rank = place()
        self.me = chip * 2 + core
        self.rows = parts.shape[0] // 4
        self.half, self.wide = self.rows // 2, parts.shape[1] // 2
        x, y = self.rank % 2, self.rank // 2
        self.across = (y * 2 + 1 - x, (1 - y) * 2 + x)
        self.far = (1 - y) * 2 + 1 - x

    @staticmethod
    def scratch(shape):
        return [
            pltpu.VMEM((2, 6, shape[0] // 8, shape[1] // 2), bf16),
            *[pltpu.SemaphoreType.DMA((2, n)) for n in (6, 6, 2)],
        ]

    @staticmethod
    def temp(shape):
        return pltpu.VMEM((2, 2, shape[0] // 8, shape[1] // 2), bf16)

    def part(self, g, owner, way):
        return slab(self.parts.at[:, pl.ds(g * self.wide, self.wide)], owner * 2 + way, self.half)

    def copy(self, g, i):
        if i < 4:
            way = i // 2
            src = self.part(g, self.across[way] if i % 2 == 0 else self.far, way)
            to = self.across[way]
        else:
            way = i - 4
            src, to = self.land.at[g, 2 * way + 1], self.across[1 - way]
        return remote(
            src, self.land.at[g, i], self.send.at[g, i], self.recv.at[g, i], self.me, to
        )

    def fetch(self, g, owner, way):
        return pltpu.make_async_copy(
            self.part(g, owner, way), self.temp.at[g, way], self.tsem.at[g, way]
        )

    def step(self, k, g):
        if k == 0:
            for i in (1, 3, 0, 2):
                self.copy(g, i).start()
            return
        for way in (0, 1):
            self.fetch(g, self.across[1 - way], way).start()
        for way in (0, 1):
            self.copy(g, 2 * way + 1).wait_recv()
            self.fetch(g, self.across[1 - way], way).wait()
            add_rows(self.land.at[g, 2 * way + 1], [self.temp.at[g, way]])
            self.copy(g, 4 + way).start()
        for way in (0, 1):
            self.fetch(g, self.rank, way).start()

    def arrive(self):
        for g in (0, 1):
            for way in (0, 1):
                self.copy(g, 2 * way + 1).wait_send()
                self.copy(g, 2 * way).wait()
                self.copy(g, 4 + way).wait()
                self.fetch(g, self.rank, way).wait()

    def totals(self, some, body):
        for way in (0, 1):
            def add(i):
                at = pl.ds(pl.multiple_of(i * some, some), some)
                total = jnp.concatenate(
                    [
                        self.temp[g, way, at].astype(f32)
                        + self.land[g, 2 * way, at].astype(f32)
                        + self.land[g, 4 + way, at].astype(f32)
                        for g in (0, 1)
                    ],
                    axis=1,
                )
                body(pl.ds(pl.multiple_of(way * self.half + i * some, some), some), total)

            pl.loop(0, self.half // some)(add)


def row_loop(rows, some, body):
    @pl.loop(0, rows // some)
    def _(i):
        body(pl.ds(pl.multiple_of(i * some, some), some))


def params(number):
    return pltpu.CompilerParams(
        collective_id=number, has_side_effects=True, vmem_limit_bytes=VMEM_BYTES
    )


ANY = pl.BlockSpec(memory_space=pl.ANY)
ONCHIP = pl.BlockSpec(memory_space=pltpu.VMEM)


epsilon = 1e-05
CHUNK = 256


def shaped(shape, dtype):
    return jax.ShapeDtypeStruct(shape, dtype)


def dma(count=None):
    return pltpu.SemaphoreType.DMA if count is None else pltpu.SemaphoreType.DMA((count,))


def project_kernel(
    chips, ranks, res_ref, gain_ref, ws_ref, wx_own, x_ref, st_ref, bc_ref, normed_out, wx_out,
    own, normed, wx, *sems
):
    greet(chips, ranks)
    line = LineGather(wx_own, wx, *sems[:3], chips)
    tensor = TensorGather(own, normed, *sems[3:6], ranks)
    line.step(0)
    gain = gain_ref[...]

    def norm(at):
        v = res_ref[at].astype(f32)
        scaling = lax.rsqrt(jnp.mean(v * v, axis=1, keepdims=True) + epsilon)
        own[at] = (v * scaling * gain).astype(bf16)

    row_loop(own.shape[0], 32, norm)
    tensor.step(0)
    line.step(1)
    tensor.step(1)
    if chips > 2:
        line.step(2)
    tensor.finish()
    keep_normed = pltpu.make_async_copy(normed, normed_out, sems[6])
    keep_normed.start()
    tokens, width = x_ref.shape
    deep = 2 * line.rows

    def states(at):
        bc_ref[at] = mm(normed[at], ws_ref[...])

    row_loop(tokens, CHUNK, states)

    def use(first, chip):
        ks = pl.ds(pl.multiple_of(chip * deep, deep), deep)

        def rows(at):
            left = normed[at, ks]
            x, st = mm(left, wx[ks, :width]), mm(left, wx[ks, width:])
            if first:
                x_ref[at], st_ref[at] = x, st
            else:
                x_ref[at] += x
                st_ref[at] += st

        row_loop(tokens, CHUNK, rows)

    line.arrive(0, functools.partial(use, True))
    line.arrive(1, functools.partial(use, False))
    for k in range(2, chips):
        if k + 1 < chips:
            line.step(k + 1)
        line.arrive(k, functools.partial(use, False))
    keep_wx = pltpu.make_async_copy(wx, wx_out, sems[7])
    keep_wx.start()
    line.sent()
    keep_normed.wait()
    keep_wx.wait()


def project(number, chips, ranks, residual, norm_gain, ws, wx_own):
    rows, model = residual.shape
    tokens, width = rows * ranks, wx_own.shape[1]
    return pl.pallas_call(
        functools.partial(project_kernel, chips, ranks),
        in_specs=[ONCHIP, ONCHIP, ONCHIP, ANY],
        out_specs=[ONCHIP, ONCHIP, ONCHIP, ANY, ANY],
        out_shape=[
            shaped((tokens, width - LANES), f32), shaped((tokens, LANES), f32),
            shaped((tokens, ws.shape[1]), f32), shaped((tokens, model), bf16),
            shaped((model, width), bf16),
        ],
        scratch_shapes=[
            pltpu.VMEM((rows, model), bf16), pltpu.VMEM((tokens, model), bf16),
            pltpu.VMEM((model, width), bf16),
            *LineGather.scratch(chips), *TensorGather.scratch(ranks), dma(), dma(),
        ],
        compiler_params=params(number),
        name="project",
    )(residual, norm_gain, ws, wx_own)


def scan_gather_kernel(blocks, total, chips, ranks, *refs):
    own, (wz_own, cot_own) = refs[:9], refs[9:11]
    outs, (wz_out, cot_out) = refs[11:15], refs[15:17]
    scratch, sems = refs[17:21], refs[21:]
    now = pl.program_id(0) * blocks + pl.program_id(1)
    line = LineGather(wz_own, wz_out, *sems[:3], chips)
    tensor = TensorGather(cot_own, cot_out, *sems[3:], ranks)

    @pl.when(now == 0)
    def _():
        greet(chips, ranks)
        line.step(0)
        tensor.step(0)

    @pl.when(now == total - 2)
    def _():
        line.step(1)

    scan_fwd_kernel(blocks, *own, *outs, *scratch)

    @pl.when(now == total - 1)
    def _():
        tensor.step(1)
        for k in range(2, chips):
            line.step(k)
        line.finish()
        tensor.finish()


def scan_forward_gather(
    number, chips, ranks, wz_own, cot_own, x, bc, st, seg, tapx, tapbc, par, spread, skip, nseq
):
    tokens, width = x.shape
    n = BLOCK
    blocks = tokens // nseq // n
    at = lambda s, i: (s * blocks + i, 0)
    whole = lambda s, i: (0, 0)
    states = LANES
    return pl.pallas_call(
        functools.partial(scan_gather_kernel, blocks, nseq * blocks, chips, ranks),
        grid=(nseq, blocks),
        in_specs=[
            pl.BlockSpec((n, width), at),
            pl.BlockSpec((n, 2 * states), at),
            pl.BlockSpec((n, LANES), at),
            pl.BlockSpec((n, LANES), at),
            pl.BlockSpec(tapx.shape, whole),
            pl.BlockSpec(tapbc.shape, whole),
            pl.BlockSpec(par.shape, whole),
            pl.BlockSpec(spread.shape, whole),
            pl.BlockSpec(skip.shape, whole),
            pl.BlockSpec(wz_own.shape, whole),
            pl.BlockSpec(cot_own.shape, whole),
        ],
        out_specs=[
            pl.BlockSpec((n, width), at), pl.BlockSpec((states, width), at),
            pl.BlockSpec((n, width), at), pl.BlockSpec((n, 2 * states), at), ANY, ANY,
        ],
        out_shape=[
            shaped((tokens, width), f32),
            shaped((tokens // n * states, width), bf16),
            shaped((tokens, width), f32),
            shaped((tokens, 2 * states), f32),
            shaped((wz_own.shape[0] * 2 * chips, width), bf16),
            shaped((tokens, cot_own.shape[1]), bf16),
        ],
        scratch_shapes=[
            pltpu.VMEM((states, width), f32),
            pltpu.VMEM((8, width), f32),
            pltpu.VMEM((8, 2 * states), f32),
            pltpu.VMEM((8, LANES), jnp.int32),
            *LineGather.scratch(chips), *TensorGather.scratch(ranks),
        ],
        compiler_params=params(number),
        name="scan_forward",
    )(x, bc, st, seg, tapx, tapbc, par, spread, skip, wz_own, cot_own)


def lane_sums(v):
    total = v[:, :LANES]
    for i in range(LANES, v.shape[1], LANES):
        total = total + v[:, i : i + LANES]
    return total


def row_sums(picks, v):
    high = v.astype(bf16)
    low = (v - high.astype(f32)).astype(bf16)
    return mm_nt(picks, high) + mm_nt(picks, low)


def gate_kernel(
    chips, ranks, gain_ref, wo_own, normed_in, wz_in, y_in, cot_in,
    gz_ref, gy_ref, ng_ref, ggain_ref, wo_out,
    wo, normed, wz, y, cot, z, gng, squares, dots, columns, land, send, recv, loads, *sems
):
    line = LineGather(wo_own, wo, *sems[:3], chips)
    tokens, width = y.shape
    inner = width * ranks
    rank = line.rank
    load = [
        pltpu.make_async_copy(src, dst, loads.at[i])
        for i, (src, dst) in enumerate(((normed_in, normed), (wz_in, wz), (y_in, y), (cot_in, cot)))
    ]
    greet(chips, ranks)
    line.step(0)
    for copy in load:
        copy.start()
    load[0].wait()
    load[1].wait()

    def gate(at):
        z[at] = mm(normed[at], wz[...])

    row_loop(tokens, CHUNK, gate)
    load[2].wait()
    load[3].wait()
    deep = 2 * line.rows

    def use(first, chip):
        ks = pl.ds(pl.multiple_of(chip * deep, deep), deep)

        def rows(at):
            v = mm(cot[at, ks], wo[ks])
            if first:
                gng[at] = v
            else:
                gng[at] += v

        row_loop(tokens, CHUNK, rows)

    line.arrive(0, functools.partial(use, True))
    for k in range(1, chips):
        line.step(k)
        line.arrive(k, functools.partial(use, False))
    keep = pltpu.make_async_copy(wo, wo_out, loads.at[4])
    keep.start()
    gain = gain_ref[0:1]

    def sums(at):
        zz = z[at]
        gated = y[at] * (zz * sigmoid(zz))
        squares[at] = lane_sums(gated * gated)
        dots[at] = lane_sums(gng[at] * gain * gated)

    row_loop(tokens, 16, sums)
    half = lax.broadcasted_iota(jnp.int32, (8, LANES), 0) < 4
    one, other = half.astype(bf16), jnp.logical_not(half).astype(bf16)
    for r in range(0, tokens, CHUNK):
        at = slice(r, r + CHUNK)
        land[rank, :, at] = row_sums(one, squares[at]) + row_sums(other, dots[at])
    copies = [
        remote(
            land.at[rank], land.at[rank], send.at[k], recv.at[k], line.me, lax.rem(rank + k, ranks)
        )
        for k in range(1, ranks)
    ]
    for copy in copies:
        copy.start()
    line.sent()
    for copy in copies:
        copy.wait()
    for r in range(0, tokens, LANES):
        at = slice(r, r + LANES)
        total = land[0, :, at]
        for k in range(1, ranks):
            total = total + land[k, :, at]
        columns[at] = jnp.transpose(jnp.concatenate([total] * (LANES // 8), axis=0))
    ggain_ref[...] = jnp.zeros_like(ggain_ref)

    def grads(at):
        zz, yy, gg = z[at], y[at], gng[at]
        sig = sigmoid(zz)
        silu = zz * sig
        gated = yy * silu
        scale = lax.rsqrt(columns[at, 0:1] / inner + epsilon)
        ng_ref[at] = (gated * scale * gain).astype(bf16)
        weight = scale * scale * scale * columns[at, 4:5] / inner
        ggain_ref[...] += fold(gg * gated * scale)
        grad = scale * gain * gg - gated * weight
        gz_ref[at] = (grad * yy * (sig * (1.0 + zz * (1.0 - sig)))).astype(bf16)
        gy_ref[at] = grad * silu

    row_loop(tokens, 16, grads)
    keep.wait()


def gate(number, chips, ranks, gain, wo_own, normed, wz, y, cot):
    tokens, width = y.shape
    model = normed.shape[1]
    return pl.pallas_call(
        functools.partial(gate_kernel, chips, ranks),
        in_specs=[ONCHIP] + [ANY] * 5,
        out_specs=[ONCHIP] * 4 + [ANY],
        out_shape=[
            shaped((tokens, width), bf16), shaped((tokens, width), f32), shaped((tokens, width), bf16),
            shaped((8, width), f32), shaped((model, width), bf16),
        ],
        scratch_shapes=[
            pltpu.VMEM((model, width), bf16), pltpu.VMEM((tokens, model), bf16),
            pltpu.VMEM((model, width), bf16), pltpu.VMEM((tokens, width), f32),
            pltpu.VMEM((tokens, model), bf16), pltpu.VMEM((tokens, width), f32),
            pltpu.VMEM((tokens, width), f32), pltpu.VMEM((tokens, LANES), f32),
            pltpu.VMEM((tokens, LANES), f32), pltpu.VMEM((tokens, LANES), f32),
            pltpu.VMEM((ranks, 8, tokens), f32), dma(ranks), dma(ranks), dma(5),
            *LineGather.scratch(chips),
        ],
        compiler_params=params(number),
        name="gate",
    )(gain, wo_own, normed, wz, y, cot)


class Grads:
    def __init__(self, src, grad, parts, cbuf, csem):
        self.src, self.grad, self.parts, self.cbuf, self.csem = src, grad, parts, cbuf, csem
        self.count = src.shape[1] // CHUNK

    def load(self, j):
        slot = lax.rem(j, 2)
        columns = pl.ds(pl.multiple_of(j * CHUNK, CHUNK), CHUNK)
        return pltpu.make_async_copy(
            self.src.at[:, columns], self.cbuf.at[slot], self.csem.at[slot]
        )

    def begin(self):
        self.load(0).start()

    def run(self):
        @pl.loop(0, self.count)
        def _(j):
            @pl.when(j + 1 < self.count)
            def _():
                self.load(j + 1).start()

            self.load(j).wait()
            at = pl.ds(pl.multiple_of(j * CHUNK, CHUNK), CHUNK)
            self.parts[at] = mm_tn(self.cbuf[lax.rem(j, 2)], self.grad[...]).astype(bf16)


class Back:
    def __init__(self, terms, parts, stage, ssem):
        self.terms, self.parts, self.stage, self.ssem = terms, parts, stage, ssem
        self.count = parts.shape[1] // CHUNK

    def loads(self, j):
        slot = lax.rem(j, 2)
        return [
            pltpu.make_async_copy(slab(right, j, CHUNK), buffer.at[slot], sem.at[slot])
            for _, right, buffer, sem in self.terms
        ]

    def store(self, j):
        slot = lax.rem(j, 2)
        columns = pl.ds(pl.multiple_of(j * CHUNK, CHUNK), CHUNK)
        return pltpu.make_async_copy(
            self.stage.at[slot], self.parts.at[:, columns], self.ssem.at[slot]
        )

    def begin(self):
        for copy in self.loads(0):
            copy.start()

    def run(self, between=None):
        count = self.count

        @pl.loop(0, count)
        def _(j):
            slot = lax.rem(j, 2)

            @pl.when(j + 1 < count)
            def _():
                for copy in self.loads(j + 1):
                    copy.start()

            for copy in self.loads(j):
                copy.wait()

            @pl.when(j >= 2)
            def _():
                self.store(j - 2).wait()

            if between is not None:
                pl.when(j == count // 2 + 1)(between)

            for r in range(0, self.parts.shape[0], CHUNK):
                at = slice(r, r + CHUNK)
                total = jnp.zeros((CHUNK, CHUNK), f32)
                for left, _, buffer, _ in self.terms:
                    total = total + mm_nt(left[at], buffer[slot])
                self.stage[slot, at] = total.astype(bf16)
            self.store(j).start()

        for j in (count - 2, count - 1):
            self.store(j).wait()


def everyone(buffer, mine, count, send, recv, device):
    row = buffer.at[mine]
    return [
        remote(row, row, send.at[k], recv.at[k], *device(lax.rem(mine + k, count)))
        for k in range(1, count)
    ]


def added(buffer, count):
    total = buffer[0]
    for k in range(1, count):
        total = total + buffer[k]
    return total


def backward_kernel(blocks, total, chips, ranks, *refs):
    ins, refs = refs[:15], refs[15:]
    (ggain_ref, gain_ref), refs = refs[:2], refs[2:]
    (res_in, cot_own_in, ws_in, gz_in, ng_in, normed_in, cot_in, wo_in, wz_in, wx_in), refs = refs[:10], refs[10:]
    (sums_ref, norm_ref), refs = refs[:2], refs[2:]
    (z_sum, o_sum, x_sum, block_out, res_grad, state_out), refs = refs[:6], refs[6:]
    (tparts, pparts, pland, tland), refs = refs[:4], refs[4:]
    scratch, refs = refs[:11], refs[11:]
    (gxs, gbc_own, gtapx, gtapbc, gpar, gz, ng, cbuf, parts, back, wbuf, xbuf), refs = refs[:12], refs[12:]
    (gbc_slots, sbuf, wide_out, line_out, sparts, state_f, state_g), refs = refs[:7], refs[7:]
    (state_own, state_line, state_low, land_core, land_chip, land_rank), refs = refs[:6], refs[6:]
    (norm_rank, norm_dp, norm_acc), refs = refs[:3], refs[3:]
    (loads, csem, bsem, wsem, xsem, ysem, osem, fsem), refs = refs[:8], refs[8:]
    (psem, qsem, rsem, nsem, msem), refs = refs[:5], refs[5:]
    half_parts = parts.at[:, pl.ds(0, gz.shape[1])]
    z_job = LineScatter(half_parts, *refs[:4], chips)
    o_job = LineScatter(half_parts, *refs[4:8], chips)
    x_job = LineScatter(parts, *refs[8:12], chips)
    s_job = SmallScatter(sparts, *refs[12:16], chips)
    refs = refs[16:]
    around = TensorGather(gbc_own, gbc_slots, *refs[:3], ranks)
    s_line = SmallGather(state_own, state_line, *refs[3:5], chips)
    state_all = gbc_slots.at[pl.ds(gz.shape[0], normed_in.shape[1])]
    s_rank = TensorGather(state_low, state_all, *refs[5:8], ranks)
    temp, refs = refs[8], refs[9:]
    if ranks == 4:
        first = HalvesScatter(pparts, refs[0], temp, *refs[1:4])
        second = HalvesScatter(tparts, refs[4], temp, *refs[5:8])
    else:
        first = DirectScatter(pparts, pland, temp, *refs[:3], ranks)
        second = DirectScatter(tparts, tland, temp, *refs[3:6], ranks)
    now = pl.program_id(0) * blocks + pl.program_id(1)
    tokens, width = gz.shape
    model = normed_in.shape[1]
    rank, me, devices = first.rank, first.me, 2 * chips
    chip, core = z_job.chip, z_job.core
    over_dp = lambda d: (d, rank)
    over_rank = lambda r: (me, r)
    by_core = everyone(land_core, core, 2, psem.at[0], psem.at[1], lambda c: (chip * 2 + c, rank))
    by_chip = everyone(land_chip, chip, chips, qsem.at[0], qsem.at[1], lambda c: (c * 2 + core, rank))
    by_rank = everyone(land_rank, rank, ranks, rsem.at[0], rsem.at[1], over_rank)
    norm_by_rank = everyone(norm_rank, rank, ranks, nsem.at[0], nsem.at[1], over_rank)
    norm_by_dp = everyone(norm_dp, me, devices, msem.at[0], msem.at[1], over_dp)

    def begin(copies):
        for copy in copies:
            copy.start()

    def end(copies):
        for copy in copies:
            copy.wait()
    fetch = [
        pltpu.make_async_copy(src, dst, loads.at[i])
        for i, (src, dst) in enumerate(((gz_in, gz), (ng_in, ng)))
    ]
    pieces = model // width
    own_rows = first.rows

    def piece(ref, p, at):
        return ref[pl.ds(pl.multiple_of(at.start + p * own_rows, 16), at.size)]

    def pieced(ref, at):
        return jnp.concatenate([piece(ref, p, at) for p in range(pieces)], axis=1).astype(f32)

    def own_copies(src, ref, sems):
        return [
            pltpu.make_async_copy(
                src.at[:, pl.ds(p * width, width)], ref.at[pl.ds(p * own_rows, own_rows)], sems.at[p]
            )
            for p in range(pieces)
        ]

    own_res = own_copies(res_in, gz, fsem.at[0])
    own_cot = own_copies(cot_own_in, ng, fsem.at[1])
    half_out = line_out.at[:, pl.ds(0, width)]
    keep_z = pltpu.make_async_copy(half_out, z_sum, osem.at[0])
    keep_o = pltpu.make_async_copy(half_out, o_sum, osem.at[0])
    keep_x = pltpu.make_async_copy(line_out, x_sum, osem.at[0])
    keep_block = pltpu.make_async_copy(wide_out, block_out, osem.at[2])
    keep_grad = pltpu.make_async_copy(wide_out, res_grad, osem.at[2])

    z_part = Grads(normed_in, gz, half_parts, cbuf, csem)
    o_part = Grads(cot_in, ng, half_parts, cbuf, csem)
    x_part = Grads(normed_in, gxs, parts, cbuf, csem)
    out_part = Back([(ng, wo_in, wbuf, wsem)], pparts, back, bsem)
    in_part = Back(
        [(gz, wz_in, wbuf, wsem), (gxs, wx_in, xbuf, xsem), (gbc_own, ws_in, sbuf, ysem)],
        tparts, back, bsem,
    )

    @pl.when(now == 0)
    def _():
        z_part.begin()
        for copy in fetch:
            copy.start()
        out_part.begin()
        greet_all(chips, ranks)
        fetch[0].wait()
        z_part.run()
        z_job.step(0)
        fetch[1].wait()
        o_part.begin()
        out_part.run(lambda: z_job.step(1))
        first.step(0, 0)
        first.step(0, 1)

    early = [k for k in range(2, chips) if 2 * k - 2 < total - 1]

    @pl.when(now == 1)
    def _():
        o_part.run()
        o_job.step(0)

    for k in early:
        @pl.when(now == 2 * k - 2)
        def _():
            z_job.step(k)

    @pl.when(now == 3)
    def _():
        o_job.step(1)

    @pl.when(now == 5)
    def _():
        first.step(1, 0)
        first.step(1, 1)

    @pl.when(now == total - 1)
    def _():
        x_part.begin()
        in_part.begin()

    row = pl.multiple_of(
        (pl.program_id(0) * blocks + blocks - 1 - pl.program_id(1)) * BLOCK, BLOCK
    )
    here = pl.ds(row, BLOCK)
    outs = (
        gxs.at[here, pl.ds(0, width)], gbc_own.at[here], gxs.at[here, pl.ds(width, LANES)],
        gtapx, gtapbc, gpar,
    )
    scan_bwd_kernel(blocks, *ins, *outs, *scratch)

    @pl.when(now == total - 1)
    def _():
        around.step(0)
        begin(own_cot)
        pack = land_core.at[core]
        pack[...] = jnp.zeros(land_core.shape[1:], f32)
        for k in range(5):
            rows = slice(8 * k, 8 * k + 8)
            pack[k : k + 1, :width] = jnp.sum(gtapx[rows], axis=0, keepdims=True)
            pack[k : k + 1, width:] = jnp.sum(gtapbc[rows], axis=0, keepdims=True)
        pack[5:6, :width] = jnp.sum(ggain_ref[...], axis=0, keepdims=True)
        for k in range(3):
            pack[6:7, k * LANES : (k + 1) * LANES] = jnp.sum(
                gpar[8 * k : 8 * k + 8], axis=0, keepdims=True
            )
        begin(by_core)
        x_part.run()
        x_job.step(0)
        end(by_core)
        land_chip[chip] = added(land_core, 2)
        begin(by_chip)
        depth = sparts.shape[0]

        def own_columns(i):
            columns = pl.ds(pl.multiple_of(rank * depth + i * CHUNK, CHUNK), CHUNK)
            return pltpu.make_async_copy(normed_in.at[:, columns], cbuf.at[i], csem.at[i])

        for i in range(depth // CHUNK):
            own_columns(i).start()
        for k in range(2, chips):
            if k not in early:
                z_job.step(k)
        if chips > 2:
            o_job.step(2)
        around.step(1)

        def between():
            second.step(0, 0)
            around.finish()

            def add(at):
                total = gbc_slots[at].astype(f32)
                for r in range(1, ranks):
                    there = pl.ds(pl.multiple_of(at.start + r * tokens, 128), at.size)
                    total = total + gbc_slots[there].astype(f32)
                gbc_slots[at] = total.astype(bf16)

            row_loop(tokens, 128, add)
            for i in range(depth // CHUNK):
                own_columns(i).wait()
                sparts[i * CHUNK : (i + 1) * CHUNK] = mm_tn(cbuf[i], gbc_slots[:tokens]).astype(
                    sparts.dtype
                )
            s_job.step(0)
            for k in range(3, chips):
                o_job.step(k)
            s_job.step(1)
            x_job.step(1, True)

        in_part.run(between)
        second.step(0, 1)
        begin(own_res)
        s_job.finish(state_own)
        s_line.step(0)
        x_job.send_rest()
        z_job.finish(half_out)
        keep_z.start()
        first.arrive()
        end(own_res)

        def plus(at, total):
            wide_out[at] = pieced(gz, at) + total

        first.totals(32, plus)
        keep_block.start()
        second.step(1, 0)
        end(by_chip)
        land_rank[rank] = added(land_chip, chips)
        begin(by_rank)
        keep_z.wait()
        o_job.finish(half_out)
        keep_o.start()
        s_line.step(1)
        s_line.finish()

        def lower(at):
            state_low[at] = state_line[at].astype(bf16)

        row_loop(depth, 64, lower)
        end(by_rank)
        s_rank.step(0)
        shared = land_rank[0, :, width:]
        for r in range(1, ranks):
            shared = shared + land_rank[r, :, width:]
        for r in range(ranks):
            sums_ref[:, r * width : (r + 1) * width] = land_rank[r, :, :width]
        sums_ref[:, ranks * width :] = shared
        if chips > 2:
            x_job.step(2)
        second.step(1, 1)
        s_rank.step(1)
        for k in range(3, chips):
            x_job.step(k)
        keep_block.wait()
        end(own_cot)
        second.arrive()
        norm_acc[...] = jnp.zeros_like(norm_acc)
        gain = gain_ref[...]

        def last(at, grad):
            v = pieced(gz, at)
            scaling = lax.rsqrt(jnp.mean(v * v, axis=1, keepdims=True) + epsilon)
            norm_acc[...] += fold(grad * v * scaling)
            grad = grad * gain
            along = jnp.sum(grad * v, axis=1, keepdims=True)
            weight = scaling * scaling * scaling * along / model
            wide_out[at] = pieced(ng, at) + scaling * grad - v * weight

        second.totals(32, last)
        keep_grad.start()
        line = jnp.sum(norm_acc[...], axis=0, keepdims=True)
        eighth = model // 8
        for i in range(8):
            norm_rank[rank, i : i + 1, :] = line[:, i * eighth : (i + 1) * eighth]
        begin(norm_by_rank)
        s_rank.finish()
        buffers = (state_f, state_g)
        stored = []
        some = depth // 2
        for r in range(2 * ranks):
            if r >= 2:
                stored[r - 2].wait()

            def state(at):
                low = pl.ds(pl.multiple_of(at.start + r * some, 64), at.size)
                buffers[r % 2][at] = state_all[low].astype(f32)

            row_loop(some, 64, state)
            copy = pltpu.make_async_copy(
                buffers[r % 2], state_out.at[pl.ds(r * some, some)], osem.at[1 + r % 2 * 2]
            )
            copy.start()
            stored.append(copy)
        end(norm_by_rank)
        norm_dp[me] = added(norm_rank, ranks)
        begin(norm_by_dp)
        keep_o.wait()
        x_job.finish(line_out)
        keep_x.start()
        end(stored[-2:])
        end(norm_by_dp)
        norm_ref[...] = added(norm_dp, devices)
        keep_x.wait()
        keep_grad.wait()


def backward(
    number, chips, ranks, ggain, norm_gain, residual, cot_own, ws, gz, ng, normed, cot, wo, wz, wx,
    x, conv, bc, convbc, st, seg, gy, y, h, tapx, tapbc, par, spread, skip, nseq,
):
    tokens, width = x.shape
    rows, model = residual.shape
    n = BLOCK
    blocks = tokens // nseq // n
    at = lambda s, i: (s * blocks + blocks - 1 - i, 0)
    tail = lambda s, i: (jnp.maximum((s * blocks + blocks - 1 - i) * (n // 8) - 1, 0), 0)
    whole = lambda s, i: (0, 0)
    states = LANES
    full = lambda v: pl.BlockSpec(v.shape, whole)
    once = lambda shape: pl.BlockSpec(shape, whole)
    devices = 2 * chips
    own, depth, wide = model // devices, model // ranks, width + 2 * states
    kind = bf16 if depth // devices % 16 == 0 else f32
    return pl.pallas_call(
        functools.partial(backward_kernel, blocks, nseq * blocks, chips, ranks),
        grid=(nseq, blocks),
        in_specs=[
            pl.BlockSpec((n, width), at),
            pl.BlockSpec((n, width), at),
            pl.BlockSpec((n, 2 * states), at),
            pl.BlockSpec((n, 2 * states), at),
            pl.BlockSpec((n, LANES), at),
            pl.BlockSpec((n, LANES), at),
            pl.BlockSpec((8, LANES), tail),
            pl.BlockSpec((n, width), at),
            pl.BlockSpec((n, width), at),
            pl.BlockSpec((states, width), at),
            full(tapx), full(tapbc), full(par), full(spread), full(skip), full(ggain), full(norm_gain),
        ]
        + [ANY] * 10,
        out_specs=[
            once((8, width * ranks + 2 * states)), once((8, model // 8)),
        ]
        + [ANY] * 10,
        out_shape=[
            shaped((8, width * ranks + 2 * states), f32), shaped((8, model // 8), f32),
            shaped((own, width), f32), shaped((own, width), f32), shaped((own, width + LANES), f32),
            shaped((rows, model), f32), shaped((rows, model), f32), shaped((model, 2 * states), f32),
            shaped((tokens, model), bf16), shaped((tokens, model), bf16),
            *[shaped((ranks, rows, model) if ranks != 4 else (8, LANES), bf16)] * 2,
        ],
        scratch_shapes=[
            *scan_bwd_scratch(width, states),
            pltpu.VMEM((tokens, width + LANES), bf16),
            pltpu.VMEM((tokens, 2 * states), bf16),
            pltpu.VMEM((40, width), f32),
            pltpu.VMEM((40, 2 * states), f32),
            pltpu.VMEM((24, LANES), f32),
            pltpu.VMEM((tokens, width), bf16),
            pltpu.VMEM((tokens, width), bf16),
            pltpu.VMEM((2, tokens, CHUNK), bf16),
            pltpu.VMEM((model, width + LANES), bf16),
            pltpu.VMEM((2, tokens, CHUNK), bf16),
            pltpu.VMEM((2, CHUNK, width), bf16),
            pltpu.VMEM((2, CHUNK, width + LANES), bf16),
            pltpu.VMEM((ranks * tokens, 2 * states), bf16),
            pltpu.VMEM((2, CHUNK, 2 * states), bf16),
            pltpu.VMEM((rows, model), f32),
            pltpu.VMEM((own, width + LANES), f32),
            pltpu.VMEM((depth, 2 * states), kind),
            pltpu.VMEM((depth // 2, 2 * states), f32),
            pltpu.VMEM((depth // 2, 2 * states), f32),
            pltpu.VMEM((depth // devices, 2 * states), kind),
            pltpu.VMEM((depth, 2 * states), kind),
            pltpu.VMEM((depth, 2 * states), bf16),
            pltpu.VMEM((2, 8, wide), f32),
            pltpu.VMEM((chips, 8, wide), f32),
            pltpu.VMEM((ranks, 8, wide), f32),
            pltpu.VMEM((ranks, 8, model // 8), f32),
            pltpu.VMEM((devices, 8, model // 8), f32),
            pltpu.VMEM((8, model), f32),
            dma(2), *[dma(2)] * 5, dma(4), pltpu.SemaphoreType.DMA((2, model // width)),
            *[pltpu.SemaphoreType.DMA((2, n)) for n in (2, chips, ranks, ranks, devices)],
            *LineScatter.scratch(chips, (model, width)),
            *LineScatter.scratch(chips, (model, width)),
            *LineScatter.scratch(chips, (model, width + LANES)),
            *SmallScatter.scratch(chips, (depth, 2 * states), kind),
            *TensorGather.scratch(ranks), *SmallGather.scratch(chips), *TensorGather.scratch(ranks),
            HalvesScatter.temp((tokens, model)) if ranks == 4 else pltpu.VMEM((2, rows // 2, model), bf16),
            *(HalvesScatter.scratch((tokens, model)) if ranks == 4 else DirectScatter.scratch(ranks)) * 2,
        ],
        compiler_params=params(number),
        name="backward",
    )(
        x, conv, bc, convbc, st, seg, seg, gy, y, h, tapx, tapbc, par, spread, skip, ggain, norm_gain,
        residual, cot_own, ws, gz, ng, normed, cot, wo, wz, wx,
    )


def per_device(
    residual, segment_ids, norm_gain, inner_weight, state_weight, step_weight, conv_weight,
    conv_bias, step_bias, decay_log, skip_gain, gated_gain, out_weight, cotangent,
):
    rank = lax.axis_index("tensor")
    chips, ranks = lax.axis_size("dp") // 2, lax.axis_size("tensor")
    width = inner_weight.shape[2]
    heads = step_weight.shape[1]
    inner_width = gated_gain.shape[0]
    nseq, length = segment_ids.shape
    tokens = nseq * length
    inner_start, head_start = rank * width, rank * heads
    taps = jnp.concatenate([conv_weight, conv_bias[None], jnp.zeros((3, conv_bias.shape[0]), f32)], axis=0)
    tapx = lax.dynamic_slice_in_dim(taps, inner_start, width, 1)
    tapbc = taps[:, inner_width:]
    local = lambda v: lax.dynamic_slice_in_dim(v, head_start, heads, 0)
    rates = -jnp.exp(local(decay_log))
    par = jnp.concatenate(
        [on_lanes(local(step_bias)[None]), on_lanes(rates[None]), jnp.zeros((6, LANES), f32)], axis=0
    )
    skip = jnp.broadcast_to(jnp.repeat(local(skip_gain), WIDTH)[None], (8, width))
    gain = jnp.broadcast_to(
        lax.dynamic_slice_in_dim(gated_gain, inner_start, width, 0)[None], (8, width)
    )
    spread = spread_matrix(heads)
    seg = jnp.broadcast_to(segment_ids.reshape(tokens, 1), (tokens, LANES))

    wx_own = jnp.concatenate([inner_weight[:, 1], on_lanes(step_weight)], axis=1)
    x, st, bc, normed, wx = project(
        1, chips, ranks, residual, norm_gain[None], state_weight, wx_own
    )
    y, h, conv, convbc, wz, cot = scan_forward_gather(
        2, chips, ranks, inner_weight[:, 0], cotangent,
        x, bc, st, seg, tapx, tapbc, par, spread, skip, nseq,
    )
    gz, gy, ng, ggain, wo = gate(3, chips, ranks, gain, out_weight.T, normed, wz, y, cot)
    sums, norm_grad, z_grad, out_grad, x_grad, block_out, residual_grad, state_grad, *_ = backward(
        4, chips, ranks, ggain, norm_gain[None], residual, cotangent, state_weight,
        gz, ng, normed, cot, wo, wz, wx,
        x, conv, bc, convbc, st, seg, gy, y, h, tapx, tapbc, par, spread, skip, nseq,
    )
    inner_grad = jnp.stack([z_grad, x_grad[:, :width]], axis=1)
    by_head = sums[6, :inner_width].reshape(ranks, width)
    by_head = [by_head[:, k * LANES : k * LANES + heads].reshape(-1) for k in range(3)]
    return (
        block_out, residual_grad, norm_grad.reshape(-1), inner_grad, state_grad,
        x_grad[:, width : width + heads], sums[:4], sums[4], *by_head,
        sums[5, :inner_width], out_grad.T,
    )


def solution(mesh):
    rows, both = P("dp", "tensor"), P(("dp", "tensor"), None)
    inner, out = P("dp", None, "tensor"), P("tensor", "dp")
    return jax.shard_map(
        per_device,
        mesh=mesh,
        in_specs=(
            both, P("dp", None), P(), inner, P(), rows, P(), P(), P(), P(), P(), P(), out, both,
        ),
        out_specs=(both, both, P(), inner, P(), rows, P(), P(), P(), P(), P(), P(), out),
        check_vma=False,
    )
```

```python
import functools
import jax
import jax.numpy as jnp
from jax import lax
from jax.experimental import pallas as pl
from jax.experimental.pallas import tpu as pltpu
from jax.sharding import PartitionSpec as P

LANES = 128
BLOCK = 128
WIDTH = 64
VMEM_BYTES = 60 * 1024 * 1024
f32, bf16 = jnp.float32, jnp.bfloat16
ROWS0 = (((0,), (0,)), ((), ()))
COLS1 = (((1,), (1,)), ((), ()))


def mm(a, b):
    return jnp.dot(a, b, preferred_element_type=f32)


def mm_tn(a, b):
    return lax.dot_general(a, b, ROWS0, preferred_element_type=f32)


def mm_nt(a, b):
    return lax.dot_general(a, b, COLS1, preferred_element_type=f32)


def sigmoid(v):
    return 0.5 + 0.5 * jnp.tanh(0.5 * v)


def two_parts(v, low_lanes):
    high = v.astype(bf16)
    return jnp.where(low_lanes, (v - high.astype(f32)).astype(bf16), high)


def head_sums(v, spread):
    high = v.astype(bf16)
    low = (v - high.astype(f32)).astype(bf16)
    return mm_nt(high, spread) + mm_nt(low, spread)


def shifted_masks(seg_ext, seg):
    n = seg.shape[0]
    return [None] + [seg_ext[8 - k : 8 - k + n] == seg for k in (1, 2, 3)]


def convolve(tail, part, masks, taps):
    n = part.shape[0]
    ext = jnp.concatenate([tail, part], axis=0)
    total = taps[4:5] + taps[3:4] * part
    for k in (1, 2, 3):
        total = total + taps[3 - k : 4 - k] * jnp.where(masks[k], ext[8 - k : 8 - k + n], 0.0)
    return total


def wide(v):
    return jnp.concatenate([v, v], axis=1)


def step_state(raw, params, seg, prev_seg, end_seg, n):
    row = lax.broadcasted_iota(jnp.int32, (n, n), 0)
    col = lax.broadcasted_iota(jnp.int32, (n, n), 1)
    v = raw + params[0:1]
    dt = jnp.maximum(v, 0.0) + jnp.log1p(jnp.exp(-jnp.abs(v)))
    a = params[1:2]
    cum = jnp.dot(
        (row >= col).astype(f32), dt * a, precision=lax.Precision.HIGHEST, preferred_element_type=f32
    )
    last = cum[n - 1 : n]
    into = jnp.where(seg == prev_seg, jnp.exp(cum), 0.0)
    onto = jnp.where(seg == end_seg, jnp.exp(last - cum), 0.0)
    through = jnp.where(end_seg == prev_seg, jnp.exp(last), 0.0)
    bias = jnp.where((row >= col) & (seg == jnp.transpose(seg)), 0.0, -1e30)
    return v, dt, a, cum, into, onto, through, bias


def scan_fwd_kernel(
    blocks, x_ref, bc_ref, st_ref, seg_ref, tapx_ref, tapbc_ref, par_ref, spread_ref, skip_ref,
    y_ref, h_ref, conv_ref, convbc_ref, state, tail_x, tail_bc, tail_seg,
):
    n = BLOCK
    block = pl.program_id(1)

    @pl.when(block == 0)
    def _():
        state[...] = jnp.zeros_like(state)
        tail_x[...] = jnp.zeros_like(tail_x)
        tail_bc[...] = jnp.zeros_like(tail_bc)
        tail_seg[...] = jnp.full_like(tail_seg, -1)

    seg = seg_ref[...]
    masks = shifted_masks(jnp.concatenate([tail_seg[...], seg], axis=0), seg)
    prev_seg, end_seg = tail_seg[7:8], seg[n - 1 : n]
    v, dt, a, cum, into, onto, through, bias = step_state(
        st_ref[...], par_ref[...], seg, prev_seg, end_seg, n
    )
    cum_t = jnp.transpose(cum)
    low_lanes = lax.broadcasted_iota(jnp.int32, (n, LANES), 1) >= LANES // 2
    spread = spread_ref[...]
    dt_w = mm(two_parts(dt, low_lanes), spread)
    into_w = mm(two_parts(into, low_lanes), spread)
    onto_w = mm(two_parts(onto, low_lanes), spread)
    through_w = mm(two_parts(jnp.broadcast_to(through, (8, LANES)), low_lanes[:8]), spread)[0:1]
    bc_masks = [None] + [wide(m) for m in masks[1:]]
    conv_bc = convolve(tail_bc[...], bc_ref[...], bc_masks, tapbc_ref[...])
    convbc_ref[...] = conv_bc
    act_bc = conv_bc * sigmoid(conv_bc)
    b, c = act_bc[:, :LANES].astype(bf16), act_bc[:, LANES:].astype(bf16)
    cross = mm_nt(c, b)
    entering = state[...].astype(bf16)
    h_ref[...] = entering
    first_half = lax.broadcasted_iota(jnp.int32, (n, LANES), 1) < WIDTH
    for pair in range(x_ref.shape[1] // LANES):
        sl = slice(pair * LANES, (pair + 1) * LANES)
        conv = convolve(tail_x[:, sl], x_ref[:, sl], masks, tapx_ref[:, sl])
        conv_ref[:, sl] = conv
        xs = conv * sigmoid(conv)
        xd = xs * dt_w[:, sl]
        outside = mm(c, entering[:, sl]) * into_w[:, sl]
        mixes = []
        for h in (2 * pair, 2 * pair + 1):
            decay = jnp.exp(cum[:, h : h + 1] - cum_t[h : h + 1, :] + bias)
            mixes.append((decay * cross).astype(bf16))
        stacked = jnp.concatenate(
            [jnp.where(first_half, xd, 0.0), jnp.where(first_half, 0.0, xd)], axis=0
        ).astype(bf16)
        inside = mm(jnp.concatenate(mixes, axis=1), stacked)
        y_ref[:, sl] = inside + outside + skip_ref[0:1, sl] * xs
        local = mm_tn(b, (onto_w[:, sl] * xd).astype(bf16))
        state[:, sl] = through_w[:, sl] * state[:, sl] + local
    tail_x[...] = x_ref[n - 8 :, :]
    tail_bc[...] = bc_ref[n - 8 :, :]
    tail_seg[...] = seg_ref[n - 8 :, :]


def fold(v):
    total = v[0:8]
    for r in range(8, v.shape[0], 8):
        total = total + v[r : r + 8]
    return total


def scan_bwd_kernel(
    blocks, x_ref, conv_ref, bc_ref, convbc_ref, st_ref, seg_ref, segt_ref, gy_ref, y_ref, h_ref,
    tapx_ref, tapbc_ref, par_ref, spread_ref, skip_ref,
    gx_ref, gbc_ref, gst_ref, gtapx_ref, gtapbc_ref, gpar_ref,
    gstate, head_x, head_bc, head_seg, xs_s, slope_s, back_s, dt_s, onto_s, xd_s, sums_s,
):
    n = BLOCK
    step = pl.program_id(1)
    block = blocks - 1 - step

    @pl.when((step == 0) & (pl.program_id(0) == 0))
    def _():
        gtapx_ref[...] = jnp.zeros_like(gtapx_ref)
        gtapbc_ref[...] = jnp.zeros_like(gtapbc_ref)
        gpar_ref[...] = jnp.zeros_like(gpar_ref)

    @pl.when(step == 0)
    def _():
        gstate[...] = jnp.zeros_like(gstate)
        head_x[...] = jnp.zeros_like(head_x)
        head_bc[...] = jnp.zeros_like(head_bc)
        head_seg[...] = jnp.full_like(head_seg, -1)

    seg = seg_ref[...]
    first = block == 0
    seg_next = jnp.concatenate([seg, head_seg[...]], axis=0)
    ahead = [None] + [seg_next[k : k + n] == seg for k in (1, 2, 3)]
    prev_seg = jnp.where(first, -1, segt_ref[7:8])
    end_seg = seg[n - 1 : n]
    v, dt, a, cum, into, onto, through, bias = step_state(
        st_ref[...], par_ref[...], seg, prev_seg, end_seg, n
    )
    cum_t = jnp.transpose(cum)
    low_lanes = lax.broadcasted_iota(jnp.int32, (n, LANES), 1) >= LANES // 2
    spread = spread_ref[...]
    dt_s[...] = mm(two_parts(dt, low_lanes), spread)
    into_w = mm(two_parts(into, low_lanes), spread)
    onto_s[...] = mm(two_parts(onto, low_lanes), spread)
    through_w = mm(two_parts(jnp.broadcast_to(through, (8, LANES)), low_lanes[:8]), spread)[0:1]
    conv_bc = convbc_ref[...]
    sig_bc = sigmoid(conv_bc)
    act_bc = conv_bc * sig_bc
    b, c = act_bc[:, :LANES].astype(bf16), act_bc[:, LANES:].astype(bf16)
    cross = mm_nt(c, b)
    first_half = lax.broadcasted_iota(jnp.int32, (n, LANES), 1) < WIDTH
    halves = lambda t: jnp.concatenate(
        [jnp.where(first_half, t, 0.0), jnp.where(first_half, 0.0, t)], axis=0
    ).astype(bf16)
    into_s, onto_low = sums_s.at[0:n], sums_s.at[n : 2 * n]
    pairs = [slice(i, i + LANES) for i in range(0, x_ref.shape[1], LANES)]

    for sl in pairs:
        conv = conv_ref[:, sl]
        sig = sigmoid(conv)
        xs = conv * sig
        xs_s[:, sl] = xs
        slope_s[:, sl] = sig + xs * (1.0 - sig)
        xd = xs * dt_s[:, sl]
        xd_s[:, sl] = xd.astype(bf16)
        onto_low[:, sl] = (xd * onto_s[:, sl]).astype(bf16)
        into_s[:, sl] = (gy_ref[:, sl] * into_w[:, sl]).astype(bf16)
    before = h_ref[...]
    gstate_low = gstate[...].astype(bf16)
    gy_into = into_s[...]
    gc = mm_nt(gy_into, before)
    gb = mm_nt(onto_low[...], gstate_low)
    back_s[...] = mm(b, gstate_low)
    edges = 5 * n
    for sl in pairs:
        old = through_w[:, sl] * gstate[:, sl]
        last = fold(old * before[:, sl].astype(f32))
        skips = fold(gy_ref[:, sl] * xs_s[:, sl])
        both = jnp.concatenate([last, skips], axis=0)
        high = both.astype(bf16)
        sums_s[edges : edges + 16, sl] = high
        sums_s[edges + 16 : edges + 32, sl] = (both - high.astype(f32)).astype(bf16)
        gstate[:, sl] = old + mm_tn(c, gy_into[:, sl])
    gcross = jnp.zeros((n, n), f32)
    for pair, sl in enumerate(pairs):
        xs = xs_s[:, sl]
        xd_low = xd_s[:, sl]
        gy = gy_ref[:, sl]
        skip = skip_ref[0:1, sl]
        inner = y_ref[:, sl] - skip * xs
        g_state = onto_s[:, sl] * back_s[:, sl]
        gy_halves = halves(gy)
        gmix = mm_nt(gy_halves, xd_low)
        mixes = []
        for i, h in enumerate((2 * pair, 2 * pair + 1)):
            decay = jnp.exp(cum[:, h : h + 1] - cum_t[h : h + 1, :] + bias)
            mixes.append((decay * cross).astype(bf16))
            gcross = gcross + decay * gmix[i * n : (i + 1) * n]
        gxd = mm_tn(jnp.concatenate(mixes, axis=0), gy_halves) + g_state
        xd_r, gy_r = xd_low.astype(f32), gy.astype(bf16).astype(f32)
        q = gy_r * inner - xd_r * gxd
        high = q.astype(bf16)
        sums_s[0:n, sl] = high
        sums_s[n : 2 * n, sl] = (q - high.astype(f32)).astype(bf16)
        q = xd_r * g_state
        high = q.astype(bf16)
        sums_s[2 * n : 3 * n, sl] = high
        sums_s[3 * n : 4 * n, sl] = (q - high.astype(f32)).astype(bf16)
        sums_s[4 * n : 5 * n, sl] = (xs * gxd).astype(bf16)
        gconv = (dt_s[:, sl] * gxd + skip * gy) * slope_s[:, sl]
        taps = tapx_ref[:, sl]
        part = x_ref[:, sl]
        ext = jnp.concatenate([gconv, head_x[:, sl]], axis=0)
        gu = taps[3:4] * gconv
        gtapx_ref[24:32, sl] += fold(gconv * part)
        for k in (1, 2, 3):
            later = jnp.where(ahead[k], ext[k : k + n], 0.0)
            gu = gu + taps[3 - k : 4 - k] * later
            gtapx_ref[8 * (3 - k) : 8 * (4 - k), sl] += fold(later * part)
        gx_ref[:, sl] = gu.astype(bf16)
        gtapx_ref[32:40, sl] += fold(gconv)
        head_x[:, sl] = gconv[0:8]
    sums = mm_nt(sums_s[...], spread)
    sum_q = sums[0:n] + sums[n : 2 * n]
    sum_state = sums[2 * n : 3 * n] + sums[3 * n : 4 * n]
    sum_dt = sums[4 * n : 5 * n]
    sum_last = sums[edges : edges + 8] + sums[edges + 16 : edges + 24]
    sum_skip = sums[edges + 8 : edges + 16] + sums[edges + 24 : edges + 32]
    gcross_low = gcross.astype(bf16)
    gc = gc + mm(gcross_low, b)
    gb = gb + mm_tn(gcross_low, c)
    gconv = jnp.concatenate([gb, gc], axis=1) * (sig_bc + act_bc * (1.0 - sig_bc))
    ext = jnp.concatenate([gconv, head_bc[...]], axis=0)
    taps = tapbc_ref[...]
    part = bc_ref[...]
    gu = taps[3:4] * gconv
    gtapbc_ref[24:32, :] += fold(gconv * part)
    for k in (1, 2, 3):
        later = jnp.where(wide(ahead[k]), ext[k : k + n], 0.0)
        gu = gu + taps[3 - k : 4 - k] * later
        gtapbc_ref[8 * (3 - k) : 8 * (4 - k), :] += fold(later * part)
    gbc_ref[...] = gu.astype(gbc_ref.dtype)
    gtapbc_ref[32:40, :] += fold(gconv)
    head_bc[...] = gconv[0:8]
    head_seg[...] = seg[0:8]
    rows = lax.broadcasted_iota(jnp.int32, (n, n), 0)
    cols = lax.broadcasted_iota(jnp.int32, (n, n), 1)
    after = jnp.dot(
        (cols >= rows).astype(f32), sum_q, precision=lax.Precision.HIGHEST, preferred_element_type=f32
    )
    edge = jnp.sum(sum_state, axis=0, keepdims=True) + jnp.sum(sum_last, axis=0, keepdims=True)
    glog = after + edge
    gdt = sum_dt + a * glog
    gst = gdt * sigmoid(v)
    gst_ref[...] = jnp.where(low_lanes, 0.0, gst).astype(bf16)
    gpar_ref[0:8] += fold(gst)
    gpar_ref[8:16] += fold(a * dt * glog)
    gpar_ref[16:24] += sum_skip


def scan_bwd_scratch(width, states):
    n = BLOCK
    return [
        pltpu.VMEM((states, width), f32),
        pltpu.VMEM((8, width), f32),
        pltpu.VMEM((8, 2 * states), f32),
        pltpu.VMEM((8, LANES), jnp.int32),
        *[pltpu.VMEM((n, width), f32)] * 5,
        pltpu.VMEM((n, width), bf16),
        pltpu.VMEM((5 * n + 32, width), bf16),
    ]


def on_lanes(v):
    half = jnp.pad(v, [(0, 0)] * (v.ndim - 1) + [(0, LANES // 2 - v.shape[-1])])
    return jnp.concatenate([half, half], axis=-1)


MESH = pl.DeviceIdType.MESH


def place():
    dp, rank = lax.axis_index("dp"), lax.axis_index("tensor")
    return dp // 2, dp % 2, rank


def remote(src, dst, send, recv, dp, rank):
    return pltpu.make_async_remote_copy(
        src_ref=src, dst_ref=dst, send_sem=send, recv_sem=recv, device_id=(dp, rank),
        device_id_type=MESH,
    )


def greet(chips, ranks):
    chip, core, rank = place()
    sem = pltpu.get_barrier_semaphore()
    me = chip * 2 + core

    def signal(dp, r):
        pl.semaphore_signal(sem, inc=1, device_id=(dp, r), device_id_type=MESH)

    signal(chip * 2 + 1 - core, rank)
    for step in (1, -1):
        @pl.when((chip + step >= 0) & (chip + step < chips))
        def _():
            signal(me + 2 * step, rank)
    for k in range(1, ranks):
        signal(me, lax.rem(rank + k, ranks))
    pl.semaphore_wait(sem, ranks + (chip + chips - 1) // chips + (2 * chips - 2 - chip) // chips)


def greet_all(chips, ranks):
    chip, core, rank = place()
    sem = pltpu.get_barrier_semaphore()
    me, devices = chip * 2 + core, 2 * chips
    for k in range(1, devices):
        pl.semaphore_signal(
            sem, inc=1, device_id=(lax.rem(me + k, devices), rank), device_id_type=MESH
        )
    for k in range(1, ranks):
        pl.semaphore_signal(
            sem, inc=1, device_id=(me, lax.rem(rank + k, ranks)), device_id_type=MESH
        )
    pl.semaphore_wait(sem, devices + ranks - 2)


def slab(ref, index, rows):
    return ref.at[pl.ds(pl.multiple_of(index * rows, rows), rows)]


class LineGather:
    def __init__(self, own, slots, send, recv, local, chips):
        self.own, self.slots, self.send, self.recv, self.local = own, slots, send, recv, local
        self.chips, self.rows = chips, own.shape[0]
        self.chip, self.core, self.rank = place()
        self.me = self.chip * 2 + self.core
        self.partner = self.chip * 2 + 1 - self.core
        self.steps = chips

    @staticmethod
    def scratch(chips):
        n = 2 * chips
        return [
            pltpu.SemaphoreType.DMA((3, n)), pltpu.SemaphoreType.DMA((n,)), pltpu.SemaphoreType.DMA,
        ]

    def copy(self, way, origin, src=None):
        target = (self.me + 2, self.me - 2, self.partner)[way]
        slot = slab(self.slots, origin, self.rows)
        return remote(
            slot if src is None else src, slot, self.send.at[way, origin], self.recv.at[origin],
            target, self.rank,
        )

    def pass_on(self, way, origin, src=None, wait=False):
        def go():
            copy = self.copy(way, origin, src)
            copy.wait_send() if wait else copy.start()

        if way == 0:
            pl.when(self.chip + 1 < self.chips)(go)
        elif way == 1:
            pl.when(self.chip > 0)(go)
        else:
            go()

    def keep(self):
        return pltpu.make_async_copy(self.own, slab(self.slots, self.me, self.rows), self.local)

    def sides(self, k):
        return ((0, self.chip - k >= 0, -k), (1, self.chip + k < self.chips, k))

    def step(self, k):
        if k == 0:
            for way in (0, 1, 2):
                self.pass_on(way, self.me, self.own)
            self.keep().start()
            return
        for way, there, shift in self.sides(k):
            @pl.when(there)
            def _():
                origin = self.me + 2 * shift
                self.copy(2, origin).wait_recv()
                self.pass_on(way, origin)
                self.pass_on(2, origin)

    def arrive(self, k, use=None):
        if k == 0:
            self.keep().wait()
            self.copy(2, self.partner).wait_recv()
            if use is not None:
                use(self.chip)
            return
        for way, there, shift in self.sides(k):
            @pl.when(there)
            def _():
                self.copy(2, self.partner + 2 * shift).wait_recv()
                if use is not None:
                    use(self.chip + shift)

    def each(self, k, use):
        if k == 0:
            use(self.chip)
            return
        for way, there, shift in self.sides(k):
            @pl.when(there)
            def _():
                use(self.chip + shift)

    def sent(self):
        for way in (0, 1, 2):
            self.pass_on(way, self.me, self.own, wait=True)
        for k in range(1, self.chips):
            for way, there, shift in self.sides(k):
                @pl.when(there)
                def _():
                    origin = self.me + 2 * shift
                    self.pass_on(way, origin, wait=True)
                    self.pass_on(2, origin, wait=True)

    def finish(self):
        for k in range(self.chips):
            self.arrive(k)
        self.sent()


class TensorGather:
    def __init__(self, own, slots, send, recv, local, ranks):
        self.own, self.slots, self.send, self.recv, self.local = own, slots, send, recv, local
        self.ranks, self.rows = ranks, own.shape[0]
        chip, core, self.rank = place()
        self.me = chip * 2 + core
        self.kept = False

    @staticmethod
    def scratch(ranks):
        return [
            pltpu.SemaphoreType.DMA((ranks,)), pltpu.SemaphoreType.DMA((ranks,)), pltpu.SemaphoreType.DMA,
        ]

    def near(self, k):
        x = self.rank % 2
        y = self.rank // 2
        across = (y * 2 + 1 - x, (1 - y) * 2 + x)
        if k < 2:
            return remote(
                self.own, slab(self.slots, self.rank, self.rows), self.send.at[k], self.recv.at[k],
                self.me, across[k],
            )
        half = slab(self.slots, across[k - 2] * 2 + (k - 2), self.rows // 2)
        return remote(half, half, self.send.at[k], self.recv.at[k], self.me, across[3 - k])

    def direct(self, k):
        return remote(
            self.own, slab(self.slots, self.rank, self.rows), self.send.at[k], self.recv.at[k],
            self.me, lax.rem(self.rank + k, self.ranks),
        )

    def keep(self):
        return pltpu.make_async_copy(self.own, slab(self.slots, self.rank, self.rows), self.local)

    def step(self, k):
        if k == 0:
            if self.ranks == 4:
                self.near(0).start()
                self.near(1).start()
            else:
                for j in range(1, self.ranks):
                    self.direct(j).start()
            self.keep().start()
        elif self.ranks == 4:
            for j in (0, 1):
                self.near(j).wait_recv()
                self.near(2 + j).start()

    def near_rows(self):
        self.keep().wait()
        self.kept = True
        x, y = self.rank % 2, self.rank // 2
        return [self.rank, y * 2 + 1 - x, (1 - y) * 2 + x], [(1 - y) * 2 + 1 - x]

    def finish(self):
        if not self.kept:
            self.keep().wait()
        if self.ranks == 4:
            for j in (0, 1):
                self.near(j).wait_send()
                self.near(2 + j).wait()
        else:
            for j in range(1, self.ranks):
                self.direct(j).wait()


def add_rows(target, others, out=None):
    out = target if out is None else out
    rows = target.shape[0]
    some = 64 if rows % 64 == 0 else rows
    kind = out.dtype if len(others) == 1 else f32

    def add(at):
        total = target[at].astype(kind)
        for other in others:
            total = total + other[at].astype(kind)
        out[at] = total.astype(out.dtype)

    row_loop(rows, some, add)


class LineScatter:
    def __init__(self, parts, swap, flow, send, recv, chips):
        self.parts, self.swap, self.flow = parts, swap, flow
        self.send, self.recv, self.chips = send, recv, chips
        self.rows = parts.shape[0] // (2 * chips)
        self.chip, self.core, self.rank = place()
        self.me = self.chip * 2 + self.core
        self.partner = self.chip * 2 + 1 - self.core

    @staticmethod
    def scratch(chips, shape, dtype=bf16):
        block = (shape[0] // (2 * chips),) + tuple(shape[1:])
        return [
            pltpu.VMEM((chips,) + block, dtype), pltpu.VMEM((chips + 1,) + block, dtype),
            pltpu.SemaphoreType.DMA((3, chips)), pltpu.SemaphoreType.DMA((3, chips)),
        ]

    def order(self):
        n = self.chips
        return [c for k in range(n // 2) for c in (n - 1 - k, k)]

    def over(self, c):
        return remote(
            slab(self.parts, 2 * c + 1 - self.core, self.rows), self.swap.at[c], self.send.at[2, c],
            self.recv.at[2, c], self.partner, self.rank,
        )

    def along(self, way, c, first=False):
        if way == 0:
            here = there = c
        else:
            here, there = c, jnp.where(c == self.chip - 1, self.chips, c)
        src = self.swap.at[c] if first else self.flow.at[here]
        return remote(
            src, self.flow.at[there], self.send.at[way, c], self.recv.at[way, c],
            self.me + (2, -2)[way], self.rank,
        )

    def send_off(self, c):
        n, chip = self.chips, self.chip

        @pl.when((chip == 0) & (c > 0))
        def _():
            self.along(0, c, True).start()

        @pl.when((chip == n - 1) & (c < n - 1))
        def _():
            self.along(1, c, True).start()

    def send_rest(self):
        for c in self.order()[2:]:
            self.send_off(c)

    def step(self, k, hold=False):
        n, chip = self.chips, self.chip
        if k == 0:
            for c in self.order():
                self.over(c).start()
            return
        if k == 1:
            for i, c in enumerate(self.order()):
                self.over(c).wait()
                add_rows(self.swap.at[c], [slab(self.parts, 2 * c + self.core, self.rows)])
                if i < 2 or not hold:
                    self.send_off(c)
            return
        t = k - 1
        c = n - 1 - (t - chip)

        @pl.when((chip > 0) & (t >= chip) & (c > chip))
        def _():
            self.along(0, c).wait_recv()
            add_rows(self.flow.at[c], [self.swap.at[c]])
            self.along(0, c).start()

        d = t - (n - 1 - chip)

        @pl.when((chip < n - 1) & (d >= 0) & (d < chip))
        def _():
            self.along(1, d).wait_recv()
            add_rows(self.flow.at[d], [self.swap.at[d]])
            self.along(1, d).start()

    def finish(self, out):
        n, chip = self.chips, self.chip
        mine, up, down = self.swap.at[chip], self.flow.at[chip], self.flow.at[n]

        @pl.when(chip == 0)
        def _():
            self.along(1, chip).wait_recv()
            add_rows(mine, [down], out)

        @pl.when(chip == n - 1)
        def _():
            self.along(0, chip).wait_recv()
            add_rows(mine, [up], out)

        @pl.when((chip > 0) & (chip < n - 1))
        def _():
            self.along(0, chip).wait_recv()
            self.along(1, chip).wait_recv()
            add_rows(mine, [up, down], out)

        for c in range(n):
            @pl.when((chip < n - 1) & (c > chip))
            def _():
                self.along(0, c).wait_send()

            @pl.when((chip > 0) & (c < chip))
            def _():
                self.along(1, c).wait_send()


class DirectScatter:
    def __init__(self, parts, land, temp, send, recv, tsem, ranks):
        self.parts, self.land, self.temp = parts, land, temp
        self.send, self.recv, self.tsem, self.ranks = send, recv, tsem, ranks
        self.rows = parts.shape[0] // ranks
        chip, core, self.rank = place()
        self.me = chip * 2 + core

    @staticmethod
    def scratch(ranks):
        return [dma(ranks), dma(ranks), dma(2)]

    def copy(self, k):
        to = lax.rem(self.rank + k, self.ranks)
        return remote(
            slab(self.parts, to, self.rows), self.land.at[k], self.send.at[k], self.recv.at[k],
            self.me, to,
        )

    def step(self, k, g):
        if k == 0 and g == 1:
            for j in range(1, self.ranks):
                self.copy(j).start()

    def arrive(self):
        for j in range(1, self.ranks):
            self.copy(j).wait()

    def totals(self, some, body):
        @pl.loop(0, self.rows // some)
        def _(i):
            at = pl.ds(pl.multiple_of(i * some, some), some)
            total = None
            for j in range(self.ranks):
                src = slab(self.parts, self.rank * (self.rows // some) + i, some) if j == 0 else self.land.at[j, at]
                copy = pltpu.make_async_copy(src, self.temp.at[j % 2, pl.ds(0, some)], self.tsem.at[j % 2])
                copy.start()
                copy.wait()
                v = self.temp[j % 2, pl.ds(0, some)].astype(f32)
                total = v if total is None else total + v
            body(at, total)


class SmallScatter:
    def __init__(self, parts, swap, land, send, recv, chips):
        self.parts, self.swap, self.land, self.send, self.recv = parts, swap, land, send, recv
        self.chips, self.rows = chips, parts.shape[0] // (2 * chips)
        self.chip, self.core, self.rank = place()

    @staticmethod
    def scratch(chips, shape, dtype):
        block = pltpu.VMEM((chips, shape[0] // (2 * chips), shape[1]), dtype)
        return [
            block, block, pltpu.SemaphoreType.DMA((2, chips)), pltpu.SemaphoreType.DMA((2, chips)),
        ]

    def over(self, c):
        return remote(
            slab(self.parts, 2 * c + 1 - self.core, self.rows), self.swap.at[c], self.send.at[0, c],
            self.recv.at[0, c], self.chip * 2 + 1 - self.core, self.rank,
        )

    def straight(self, k):
        to = lax.rem(self.chip + k, self.chips)
        return remote(
            self.swap.at[to], self.land.at[self.chip], self.send.at[1, k], self.recv.at[1, k],
            2 * to + self.core, self.rank,
        )

    def step(self, k):
        if k == 0:
            for c in range(self.chips):
                self.over(c).start()
            return
        for c in range(self.chips):
            self.over(c).wait()
            add_rows(self.swap.at[c], [slab(self.parts, 2 * c + self.core, self.rows)])
        for j in range(1, self.chips):
            self.straight(j).start()

    def finish(self, out):
        for j in range(1, self.chips):
            self.straight(j).wait()
        total = self.swap[self.chip].astype(f32)
        for j in range(1, self.chips):
            total = total + self.land[lax.rem(self.chip + j, self.chips)].astype(f32)
        out[...] = total.astype(out.dtype)


class SmallGather:
    def __init__(self, own, slots, send, recv, chips):
        self.own, self.slots, self.send, self.recv = own, slots, send, recv
        self.chips, self.rows = chips, own.shape[0]
        self.chip, self.core, self.rank = place()
        self.me = self.chip * 2 + self.core

    @staticmethod
    def scratch(chips):
        return [pltpu.SemaphoreType.DMA((2, chips)), pltpu.SemaphoreType.DMA((2, chips))]

    def straight(self, k):
        slot = slab(self.slots, self.me, self.rows)
        return remote(
            self.own, slot, self.send.at[0, k], self.recv.at[0, k],
            2 * lax.rem(self.chip + k, self.chips) + self.core, self.rank,
        )

    def over(self, k):
        slot = slab(
            self.slots, 2 * lax.rem(self.chip + self.chips - k, self.chips) + self.core, self.rows
        )
        return remote(
            self.own if k == 0 else slot, slot, self.send.at[1, k], self.recv.at[1, k],
            self.chip * 2 + 1 - self.core, self.rank,
        )

    def step(self, k):
        if k == 0:
            for j in range(1, self.chips):
                self.straight(j).start()
            self.over(0).start()
            self.slots[pl.ds(pl.multiple_of(self.me * self.rows, self.rows), self.rows)] = self.own[...]
            return
        for j in range(1, self.chips):
            self.straight(j).wait_recv()
            self.over(j).start()

    def finish(self):
        for j in range(1, self.chips):
            self.straight(j).wait_send()
        for j in range(self.chips):
            self.over(j).wait()


class HalvesScatter:
    def __init__(self, parts, land, temp, send, recv, tsem):
        self.parts, self.land, self.temp, self.send, self.recv, self.tsem = parts, land, temp, send, recv, tsem
        chip, core, self.rank = place()
        self.me = chip * 2 + core
        self.rows = parts.shape[0] // 4
        self.half, self.wide = self.rows // 2, parts.shape[1] // 2
        x, y = self.rank % 2, self.rank // 2
        self.across = (y * 2 + 1 - x, (1 - y) * 2 + x)
        self.far = (1 - y) * 2 + 1 - x

    @staticmethod
    def scratch(shape):
        return [
            pltpu.VMEM((2, 6, shape[0] // 8, shape[1] // 2), bf16),
            *[pltpu.SemaphoreType.DMA((2, n)) for n in (6, 6, 2)],
        ]

    @staticmethod
    def temp(shape):
        return pltpu.VMEM((2, 2, shape[0] // 8, shape[1] // 2), bf16)

    def part(self, g, owner, way):
        return slab(self.parts.at[:, pl.ds(g * self.wide, self.wide)], owner * 2 + way, self.half)

    def copy(self, g, i):
        if i < 4:
            way = i // 2
            src = self.part(g, self.across[way] if i % 2 == 0 else self.far, way)
            to = self.across[way]
        else:
            way = i - 4
            src, to = self.land.at[g, 2 * way + 1], self.across[1 - way]
        return remote(
            src, self.land.at[g, i], self.send.at[g, i], self.recv.at[g, i], self.me, to
        )

    def fetch(self, g, owner, way):
        return pltpu.make_async_copy(
            self.part(g, owner, way), self.temp.at[g, way], self.tsem.at[g, way]
        )

    def step(self, k, g):
        if k == 0:
            for i in (1, 3, 0, 2):
                self.copy(g, i).start()
            return
        for way in (0, 1):
            self.fetch(g, self.across[1 - way], way).start()
        for way in (0, 1):
            self.copy(g, 2 * way + 1).wait_recv()
            self.fetch(g, self.across[1 - way], way).wait()
            add_rows(self.land.at[g, 2 * way + 1], [self.temp.at[g, way]])
            self.copy(g, 4 + way).start()
        for way in (0, 1):
            self.fetch(g, self.rank, way).start()

    def arrive(self):
        for g in (0, 1):
            for way in (0, 1):
                self.copy(g, 2 * way + 1).wait_send()
                self.copy(g, 2 * way).wait()
                self.copy(g, 4 + way).wait()
                self.fetch(g, self.rank, way).wait()

    def totals(self, some, body):
        for way in (0, 1):
            def add(i):
                at = pl.ds(pl.multiple_of(i * some, some), some)
                total = jnp.concatenate(
                    [
                        self.temp[g, way, at].astype(f32)
                        + self.land[g, 2 * way, at].astype(f32)
                        + self.land[g, 4 + way, at].astype(f32)
                        for g in (0, 1)
                    ],
                    axis=1,
                )
                body(pl.ds(pl.multiple_of(way * self.half + i * some, some), some), total)

            pl.loop(0, self.half // some)(add)


def row_loop(rows, some, body):
    @pl.loop(0, rows // some)
    def _(i):
        body(pl.ds(pl.multiple_of(i * some, some), some))


def params(number):
    return pltpu.CompilerParams(
        collective_id=number, has_side_effects=True, vmem_limit_bytes=VMEM_BYTES
    )


ANY = pl.BlockSpec(memory_space=pl.ANY)
ONCHIP = pl.BlockSpec(memory_space=pltpu.VMEM)


epsilon = 1e-05
CHUNK = 256


def shaped(shape, dtype):
    return jax.ShapeDtypeStruct(shape, dtype)


def dma(count=None):
    return pltpu.SemaphoreType.DMA if count is None else pltpu.SemaphoreType.DMA((count,))


def exact_mm(v, picks):
    high = v.astype(bf16)
    rest = v - high.astype(f32)
    middle = rest.astype(bf16)
    low = (rest - middle.astype(f32)).astype(bf16)
    return mm(high, picks) + mm(middle, picks) + mm(low, picks)


def prepare(
    rank, heads, seg_in, taps_in, bias_in, heads_in, gain_in,
    seg_out, tapx_out, tapbc_out, par_out, skip_out, gain_out, spread_out,
):
    width, inner = tapx_out.shape[1], gain_in.shape[1]
    length = seg_in.shape[1]
    for s in range(seg_in.shape[0]):
        for r in range(0, length, LANES):
            row = jnp.broadcast_to(seg_in[s : s + 1, r : r + LANES], (LANES, LANES))
            at = s * length + r
            seg_out[at : at + LANES] = jnp.transpose(row.astype(f32)).astype(jnp.int32)
    own = pl.ds(pl.multiple_of(rank * width, LANES), width)
    tapx_out[...] = jnp.zeros_like(tapx_out)
    tapbc_out[...] = jnp.zeros_like(tapbc_out)
    tapx_out[0:4], tapx_out[4:5] = taps_in[:, own], bias_in[:, own]
    tapbc_out[0:4], tapbc_out[4:5] = taps_in[:, inner:], bias_in[:, inner:]
    gain_out[...] = jnp.broadcast_to(gain_in[:, own], gain_out.shape)
    row = lax.broadcasted_iota(jnp.int32, spread_out.shape, 0)
    col = lax.broadcasted_iota(jnp.int32, spread_out.shape, 1)
    half = LANES // 2
    folded = jnp.where(row >= half, row - half, row)
    start = folded * WIDTH
    spread_out[...] = ((col >= start) & (col < start + WIDTH)).astype(bf16)
    row = lax.broadcasted_iota(jnp.int32, (LANES, LANES), 0)
    col = lax.broadcasted_iota(jnp.int32, (LANES, LANES), 1)
    lane = jnp.where(col >= half, col - half, col)
    picked = exact_mm(
        heads_in[...], ((row == rank * heads + lane) & (lane < heads)).astype(bf16)
    )
    lane = lax.broadcasted_iota(jnp.int32, (1, LANES), 1)
    there = jnp.where(lane >= half, lane - half, lane) < heads
    par_out[...] = jnp.zeros_like(par_out)
    par_out[0:1] = picked[0:1]
    par_out[1:2] = jnp.where(there, -jnp.exp(picked[1:2]), 0.0)
    skip = jnp.where(lane < half, picked[2:3], 0.0)
    skip_out[...] = exact_mm(jnp.broadcast_to(skip, (8, LANES)), spread_out[...])


def project_kernel(
    chips, ranks, heads, res_ref, gain_ref, ws_ref, seg_in, taps_in, bias_in, heads_in, gated_in, wx_own,
    x_ref, st_ref, bc_ref, seg_out, tapx_out, tapbc_out, par_out, skip_out, gain_out, spread_out,
    normed_out, wx_out, own, normed, wx, *sems
):
    greet(chips, ranks)
    line = LineGather(wx_own, wx, *sems[:3], chips)
    tensor = TensorGather(own, normed, *sems[3:6], ranks)
    line.step(0)
    gain = gain_ref[...]

    def norm(at):
        v = res_ref[at].astype(f32)
        scaling = lax.rsqrt(jnp.mean(v * v, axis=1, keepdims=True) + epsilon)
        own[at] = (v * scaling * gain).astype(bf16)

    row_loop(own.shape[0], 32, norm)
    tensor.step(0)
    prepare(
        line.rank, heads, seg_in, taps_in, bias_in, heads_in, gated_in,
        seg_out, tapx_out, tapbc_out, par_out, skip_out, gain_out, spread_out,
    )
    line.step(1)
    tensor.step(1)
    if chips > 2:
        line.step(2)
    tokens, width = x_ref.shape
    deep, some = 2 * line.rows, own.shape[0]

    def states(blocks):
        for r in blocks:
            at = pl.ds(pl.multiple_of(r * some, some), some)
            bc_ref[at] = mm(normed[at], ws_ref[...])

    def use(first, blocks, chip):
        ks = pl.ds(pl.multiple_of(chip * deep, deep), deep)
        for r in blocks:
            at = pl.ds(pl.multiple_of(r * some, some), some)
            left = normed[at, ks]
            x, st = mm(left, wx[ks, :width]), mm(left, wx[ks, width:])
            if first:
                x_ref[at], st_ref[at] = x, st
            else:
                x_ref[at] += x
                st_ref[at] += st

    every = list(range(ranks))
    early, late = tensor.near_rows() if ranks == 4 else ([], every)
    for k in (0, 1):
        line.arrive(k, functools.partial(use, k == 0, early))
    states(early)
    tensor.finish()
    keep_normed = pltpu.make_async_copy(normed, normed_out, sems[6])
    keep_normed.start()
    for k in (0, 1):
        line.each(k, functools.partial(use, k == 0, late))
    states(late)
    for k in range(2, chips):
        if k + 1 < chips:
            line.step(k + 1)
        line.arrive(k, functools.partial(use, False, every))
    keep_wx = pltpu.make_async_copy(wx, wx_out, sems[7])
    keep_wx.start()
    line.sent()
    keep_normed.wait()
    keep_wx.wait()


def project(
    number, chips, ranks, heads, residual, norm_gain, ws, segments, taps, bias, by_head, gated_gain, wx_own
):
    rows, model = residual.shape
    tokens, width = rows * ranks, wx_own.shape[1]
    inner = width - LANES
    return pl.pallas_call(
        functools.partial(project_kernel, chips, ranks, heads),
        in_specs=[ONCHIP] * 8 + [ANY],
        out_specs=[ONCHIP] * 10 + [ANY, ANY],
        out_shape=[
            shaped((tokens, inner), f32), shaped((tokens, LANES), f32),
            shaped((tokens, ws.shape[1]), f32),
            shaped((tokens, LANES), jnp.int32), shaped((8, inner), f32), shaped((8, ws.shape[1]), f32),
            shaped((8, LANES), f32), shaped((8, inner), f32), shaped((8, inner), f32),
            shaped((LANES, inner), bf16),
            shaped((tokens, model), bf16), shaped((model, width), bf16),
        ],
        scratch_shapes=[
            pltpu.VMEM((rows, model), bf16), pltpu.VMEM((tokens, model), bf16),
            pltpu.VMEM((model, width), bf16),
            *LineGather.scratch(chips), *TensorGather.scratch(ranks), dma(), dma(),
        ],
        compiler_params=params(number),
        name="project",
    )(residual, norm_gain, ws, segments, taps, bias, by_head, gated_gain, wx_own)


def scan_gather_kernel(blocks, total, chips, ranks, *refs):
    own, (wz_own, cot_own) = refs[:9], refs[9:11]
    outs, (wz_out, cot_out) = refs[11:15], refs[15:17]
    scratch, sems = refs[17:21], refs[21:]
    now = pl.program_id(0) * blocks + pl.program_id(1)
    line = LineGather(wz_own, wz_out, *sems[:3], chips)
    tensor = TensorGather(cot_own, cot_out, *sems[3:], ranks)

    @pl.when(now == 0)
    def _():
        greet(chips, ranks)
        line.step(0)
        tensor.step(0)

    @pl.when(now == total - 2)
    def _():
        line.step(1)

    scan_fwd_kernel(blocks, *own, *outs, *scratch)

    @pl.when(now == total - 1)
    def _():
        tensor.step(1)
        for k in range(2, chips):
            line.step(k)
        line.finish()
        tensor.finish()


def scan_forward_gather(
    number, chips, ranks, wz_own, cot_own, x, bc, st, seg, tapx, tapbc, par, spread, skip, nseq
):
    tokens, width = x.shape
    n = BLOCK
    blocks = tokens // nseq // n
    at = lambda s, i: (s * blocks + i, 0)
    whole = lambda s, i: (0, 0)
    states = LANES
    return pl.pallas_call(
        functools.partial(scan_gather_kernel, blocks, nseq * blocks, chips, ranks),
        grid=(nseq, blocks),
        in_specs=[
            pl.BlockSpec((n, width), at),
            pl.BlockSpec((n, 2 * states), at),
            pl.BlockSpec((n, LANES), at),
            pl.BlockSpec((n, LANES), at),
            pl.BlockSpec(tapx.shape, whole),
            pl.BlockSpec(tapbc.shape, whole),
            pl.BlockSpec(par.shape, whole),
            pl.BlockSpec(spread.shape, whole),
            pl.BlockSpec(skip.shape, whole),
            pl.BlockSpec(wz_own.shape, whole),
            pl.BlockSpec(cot_own.shape, whole),
        ],
        out_specs=[
            pl.BlockSpec((n, width), at), pl.BlockSpec((states, width), at),
            pl.BlockSpec((n, width), at), pl.BlockSpec((n, 2 * states), at), ANY, ANY,
        ],
        out_shape=[
            shaped((tokens, width), f32),
            shaped((tokens // n * states, width), bf16),
            shaped((tokens, width), f32),
            shaped((tokens, 2 * states), f32),
            shaped((wz_own.shape[0] * 2 * chips, width), bf16),
            shaped((tokens, cot_own.shape[1]), bf16),
        ],
        scratch_shapes=[
            pltpu.VMEM((states, width), f32),
            pltpu.VMEM((8, width), f32),
            pltpu.VMEM((8, 2 * states), f32),
            pltpu.VMEM((8, LANES), jnp.int32),
            *LineGather.scratch(chips), *TensorGather.scratch(ranks),
        ],
        compiler_params=params(number),
        name="scan_forward",
    )(x, bc, st, seg, tapx, tapbc, par, spread, skip, wz_own, cot_own)


def lane_sums(v):
    total = v[:, :LANES]
    for i in range(LANES, v.shape[1], LANES):
        total = total + v[:, i : i + LANES]
    return total


def row_sums(picks, v):
    high = v.astype(bf16)
    low = (v - high.astype(f32)).astype(bf16)
    return mm_nt(picks, high) + mm_nt(picks, low)


def gate_kernel(
    chips, ranks, gain_ref, wo_own, normed_in, wz_in, y_in, cot_in,
    gz_ref, gy_ref, ng_ref, ggain_ref, wo_out,
    wo, normed, wz, y, cot, z, gng, squares, dots, columns, land, send, recv, loads, *sems
):
    line = LineGather(wo_own, wo, *sems[:3], chips)
    tokens, width = y.shape
    inner = width * ranks
    rank = line.rank
    load = [
        pltpu.make_async_copy(src, dst, loads.at[i])
        for i, (src, dst) in enumerate(((normed_in, normed), (wz_in, wz), (y_in, y), (cot_in, cot)))
    ]
    greet(chips, ranks)
    line.step(0)
    for copy in load:
        copy.start()
    load[0].wait()
    load[1].wait()

    def gate(at):
        z[at] = mm(normed[at], wz[...])

    row_loop(tokens, CHUNK, gate)
    load[2].wait()

    def square(at):
        zz = z[at]
        gated = y[at] * (zz * sigmoid(zz))
        squares[at] = lane_sums(gated * gated)

    row_loop(tokens, 32, square)
    load[3].wait()
    deep = 2 * line.rows

    def use(first, chip):
        ks = pl.ds(pl.multiple_of(chip * deep, deep), deep)

        def rows(at):
            v = mm(cot[at, ks], wo[ks])
            if first:
                gng[at] = v
            else:
                gng[at] += v

        row_loop(tokens, CHUNK, rows)

    line.arrive(0, functools.partial(use, True))
    for k in range(1, chips):
        line.step(k)
        line.arrive(k, functools.partial(use, False))
    keep = pltpu.make_async_copy(wo, wo_out, loads.at[4])
    keep.start()
    gain = gain_ref[0:1]

    def sums(at):
        zz = z[at]
        dots[at] = lane_sums(gng[at] * gain * (y[at] * (zz * sigmoid(zz))))

    row_loop(tokens, 32, sums)
    half = lax.broadcasted_iota(jnp.int32, (8, LANES), 0) < 4
    one, other = half.astype(bf16), jnp.logical_not(half).astype(bf16)
    for r in range(0, tokens, CHUNK):
        at = slice(r, r + CHUNK)
        land[rank, :, at] = row_sums(one, squares[at]) + row_sums(other, dots[at])
    copies = [
        remote(
            land.at[rank], land.at[rank], send.at[k], recv.at[k], line.me, lax.rem(rank + k, ranks)
        )
        for k in range(1, ranks)
    ]
    for copy in copies:
        copy.start()
    line.sent()
    for copy in copies:
        copy.wait()
    for r in range(0, tokens, LANES):
        at = slice(r, r + LANES)
        total = land[0, :, at]
        for k in range(1, ranks):
            total = total + land[k, :, at]
        columns[at] = jnp.transpose(jnp.concatenate([total] * (LANES // 8), axis=0))
    ggain_ref[...] = jnp.zeros_like(ggain_ref)

    def grads(at):
        zz, yy, gg = z[at], y[at], gng[at]
        sig = sigmoid(zz)
        silu = zz * sig
        gated = yy * silu
        scale = lax.rsqrt(columns[at, 0:1] / inner + epsilon)
        ng_ref[at] = (gated * scale * gain).astype(bf16)
        weight = scale * scale * scale * columns[at, 4:5] / inner
        ggain_ref[...] += fold(gg * gated * scale)
        grad = scale * gain * gg - gated * weight
        gz_ref[at] = (grad * yy * (sig * (1.0 + zz * (1.0 - sig)))).astype(bf16)
        gy_ref[at] = grad * silu

    row_loop(tokens, 32, grads)
    keep.wait()


def gate(number, chips, ranks, gain, wo_own, normed, wz, y, cot):
    tokens, width = y.shape
    model = normed.shape[1]
    return pl.pallas_call(
        functools.partial(gate_kernel, chips, ranks),
        in_specs=[ONCHIP] + [ANY] * 5,
        out_specs=[ONCHIP] * 4 + [ANY],
        out_shape=[
            shaped((tokens, width), bf16), shaped((tokens, width), f32), shaped((tokens, width), bf16),
            shaped((8, width), f32), shaped((model, width), bf16),
        ],
        scratch_shapes=[
            pltpu.VMEM((model, width), bf16), pltpu.VMEM((tokens, model), bf16),
            pltpu.VMEM((model, width), bf16), pltpu.VMEM((tokens, width), f32),
            pltpu.VMEM((tokens, model), bf16), pltpu.VMEM((tokens, width), f32),
            pltpu.VMEM((tokens, width), f32), pltpu.VMEM((tokens, LANES), f32),
            pltpu.VMEM((tokens, LANES), f32), pltpu.VMEM((tokens, LANES), f32),
            pltpu.VMEM((ranks, 8, tokens), f32), dma(ranks), dma(ranks), dma(5),
            *LineGather.scratch(chips),
        ],
        compiler_params=params(number),
        name="gate",
    )(gain, wo_own, normed, wz, y, cot)


class Grads:
    def __init__(self, src, grad, parts, cbuf, csem):
        self.src, self.grad, self.parts, self.cbuf, self.csem = src, grad, parts, cbuf, csem
        self.count = src.shape[1] // CHUNK

    def load(self, j):
        slot = lax.rem(j, 2)
        columns = pl.ds(pl.multiple_of(j * CHUNK, CHUNK), CHUNK)
        return pltpu.make_async_copy(
            self.src.at[:, columns], self.cbuf.at[slot], self.csem.at[slot]
        )

    def begin(self):
        self.load(0).start()

    def run(self):
        @pl.loop(0, self.count)
        def _(j):
            @pl.when(j + 1 < self.count)
            def _():
                self.load(j + 1).start()

            self.load(j).wait()
            at = pl.ds(pl.multiple_of(j * CHUNK, CHUNK), CHUNK)
            self.parts[at] = mm_tn(self.cbuf[lax.rem(j, 2)], self.grad[...]).astype(bf16)


class Back:
    def __init__(self, terms, parts, stage, ssem):
        self.terms, self.parts, self.stage, self.ssem = terms, parts, stage, ssem
        self.count = parts.shape[1] // CHUNK

    def loads(self, j):
        slot = lax.rem(j, 2)
        return [
            pltpu.make_async_copy(slab(right, j, CHUNK), buffer.at[slot], sem.at[slot])
            for _, right, buffer, sem in self.terms
        ]

    def store(self, j):
        slot = lax.rem(j, 2)
        columns = pl.ds(pl.multiple_of(j * CHUNK, CHUNK), CHUNK)
        return pltpu.make_async_copy(
            self.stage.at[slot], self.parts.at[:, columns], self.ssem.at[slot]
        )

    def begin(self):
        for copy in self.loads(0):
            copy.start()

    def run(self, between=None):
        count = self.count

        @pl.loop(0, count)
        def _(j):
            slot = lax.rem(j, 2)

            @pl.when(j + 1 < count)
            def _():
                for copy in self.loads(j + 1):
                    copy.start()

            for copy in self.loads(j):
                copy.wait()

            @pl.when(j >= 2)
            def _():
                self.store(j - 2).wait()

            if between is not None:
                pl.when(j == count // 2 + 1)(between)

            for r in range(0, self.parts.shape[0], CHUNK):
                at = slice(r, r + CHUNK)
                total = jnp.zeros((CHUNK, CHUNK), f32)
                for left, _, buffer, _ in self.terms:
                    total = total + mm_nt(left[at], buffer[slot])
                self.stage[slot, at] = total.astype(bf16)
            self.store(j).start()

        for j in (count - 2, count - 1):
            self.store(j).wait()


def everyone(buffer, mine, count, send, recv, device):
    row = buffer.at[mine]
    return [
        remote(row, row, send.at[k], recv.at[k], *device(lax.rem(mine + k, count)))
        for k in range(1, count)
    ]


def added(buffer, count):
    total = buffer[0]
    for k in range(1, count):
        total = total + buffer[k]
    return total


def backward_kernel(blocks, total, chips, ranks, *refs):
    ins, refs = refs[:15], refs[15:]
    (ggain_ref, gain_ref), refs = refs[:2], refs[2:]
    (res_in, cot_own_in, ws_in, gz_in, ng_in, normed_in, cot_in, wo_in, wz_in, wx_in), refs = refs[:10], refs[10:]
    (sums_ref, norm_ref), refs = refs[:2], refs[2:]
    (z_sum, o_sum, x_sum, block_out, res_grad, state_out), refs = refs[:6], refs[6:]
    (tparts, pparts, pland, tland), refs = refs[:4], refs[4:]
    scratch, refs = refs[:11], refs[11:]
    (gxs, gbc_own, gtapx, gtapbc, gpar, gz, ng, cbuf, parts, back, wbuf, xbuf), refs = refs[:12], refs[12:]
    (gbc_slots, sbuf, wide_out, line_out, sparts, state_f, state_g), refs = refs[:7], refs[7:]
    (state_own, state_line, state_low, land_core, land_chip, land_rank), refs = refs[:6], refs[6:]
    (norm_rank, norm_dp, norm_acc), refs = refs[:3], refs[3:]
    (loads, csem, bsem, wsem, xsem, ysem, osem, fsem), refs = refs[:8], refs[8:]
    (psem, qsem, rsem, nsem, msem), refs = refs[:5], refs[5:]
    half_parts = parts.at[:, pl.ds(0, gz.shape[1])]
    z_job = LineScatter(half_parts, *refs[:4], chips)
    o_job = LineScatter(half_parts, *refs[4:8], chips)
    x_job = LineScatter(parts, *refs[8:12], chips)
    s_job = SmallScatter(sparts, *refs[12:16], chips)
    refs = refs[16:]
    around = TensorGather(gbc_own, gbc_slots, *refs[:3], ranks)
    s_line = SmallGather(state_own, state_line, *refs[3:5], chips)
    state_all = gbc_slots.at[pl.ds(gz.shape[0], normed_in.shape[1])]
    s_rank = TensorGather(state_low, state_all, *refs[5:8], ranks)
    temp, refs = refs[8], refs[9:]
    if ranks == 4:
        first = HalvesScatter(pparts, refs[0], temp, *refs[1:4])
        second = HalvesScatter(tparts, refs[4], temp, *refs[5:8])
    else:
        first = DirectScatter(pparts, pland, temp, *refs[:3], ranks)
        second = DirectScatter(tparts, tland, temp, *refs[3:6], ranks)
    now = pl.program_id(0) * blocks + pl.program_id(1)
    tokens, width = gz.shape
    model = normed_in.shape[1]
    rank, me, devices = first.rank, first.me, 2 * chips
    chip, core = z_job.chip, z_job.core
    over_dp = lambda d: (d, rank)
    over_rank = lambda r: (me, r)
    by_core = everyone(land_core, core, 2, psem.at[0], psem.at[1], lambda c: (chip * 2 + c, rank))
    by_chip = everyone(land_chip, chip, chips, qsem.at[0], qsem.at[1], lambda c: (c * 2 + core, rank))
    by_rank = everyone(land_rank, rank, ranks, rsem.at[0], rsem.at[1], over_rank)
    norm_by_rank = everyone(norm_rank, rank, ranks, nsem.at[0], nsem.at[1], over_rank)
    norm_by_dp = everyone(norm_dp, me, devices, msem.at[0], msem.at[1], over_dp)

    def begin(copies):
        for copy in copies:
            copy.start()

    def end(copies):
        for copy in copies:
            copy.wait()
    fetch = [
        pltpu.make_async_copy(src, dst, loads.at[i])
        for i, (src, dst) in enumerate(((gz_in, gz), (ng_in, ng)))
    ]
    pieces = model // width
    own_rows = first.rows

    def piece(ref, p, at):
        return ref[pl.ds(pl.multiple_of(at.start + p * own_rows, 16), at.size)]

    def pieced(ref, at):
        return jnp.concatenate([piece(ref, p, at) for p in range(pieces)], axis=1).astype(f32)

    def own_copies(src, ref, sems):
        return [
            pltpu.make_async_copy(
                src.at[:, pl.ds(p * width, width)], ref.at[pl.ds(p * own_rows, own_rows)], sems.at[p]
            )
            for p in range(pieces)
        ]

    own_res = own_copies(res_in, gz, fsem.at[0])
    own_cot = own_copies(cot_own_in, ng, fsem.at[1])
    half_out = line_out.at[:, pl.ds(0, width)]
    keep_z = pltpu.make_async_copy(half_out, z_sum, osem.at[0])
    keep_o = pltpu.make_async_copy(half_out, o_sum, osem.at[0])
    keep_x = pltpu.make_async_copy(line_out, x_sum, osem.at[0])
    keep_block = pltpu.make_async_copy(wide_out, block_out, osem.at[2])
    keep_grad = pltpu.make_async_copy(wide_out, res_grad, osem.at[2])

    z_part = Grads(normed_in, gz, half_parts, cbuf, csem)
    o_part = Grads(cot_in, ng, half_parts, cbuf, csem)
    x_part = Grads(normed_in, gxs, parts, cbuf, csem)
    out_part = Back([(ng, wo_in, wbuf, wsem)], pparts, back, bsem)
    in_part = Back(
        [(gz, wz_in, wbuf, wsem), (gxs, wx_in, xbuf, xsem), (gbc_own, ws_in, sbuf, ysem)],
        tparts, back, bsem,
    )

    @pl.when(now == 0)
    def _():
        z_part.begin()
        for copy in fetch:
            copy.start()
        out_part.begin()
        greet_all(chips, ranks)
        fetch[0].wait()
        z_part.run()
        z_job.step(0)
        fetch[1].wait()
        o_part.begin()
        out_part.run(lambda: z_job.step(1))
        first.step(0, 0)
        first.step(0, 1)

    early = [k for k in range(2, chips) if 2 * k - 2 < total - 1]

    @pl.when(now == 1)
    def _():
        o_part.run()
        o_job.step(0)

    for k in early:
        @pl.when(now == 2 * k - 2)
        def _():
            z_job.step(k)

    @pl.when(now == 3)
    def _():
        o_job.step(1)

    @pl.when(now == 5)
    def _():
        first.step(1, 0)
        first.step(1, 1)

    @pl.when(now == total - 1)
    def _():
        x_part.begin()
        in_part.begin()

    row = pl.multiple_of(
        (pl.program_id(0) * blocks + blocks - 1 - pl.program_id(1)) * BLOCK, BLOCK
    )
    here = pl.ds(row, BLOCK)
    outs = (
        gxs.at[here, pl.ds(0, width)], gbc_own.at[here], gxs.at[here, pl.ds(width, LANES)],
        gtapx, gtapbc, gpar,
    )
    scan_bwd_kernel(blocks, *ins, *outs, *scratch)

    @pl.when(now == total - 1)
    def _():
        around.step(0)
        begin(own_cot)
        pack = land_core.at[core]
        pack[...] = jnp.zeros(land_core.shape[1:], f32)
        for k in range(5):
            rows = slice(8 * k, 8 * k + 8)
            pack[k : k + 1, :width] = jnp.sum(gtapx[rows], axis=0, keepdims=True)
            pack[k : k + 1, width:] = jnp.sum(gtapbc[rows], axis=0, keepdims=True)
        pack[5:6, :width] = jnp.sum(ggain_ref[...], axis=0, keepdims=True)
        for k in range(3):
            pack[6:7, k * LANES : (k + 1) * LANES] = jnp.sum(
                gpar[8 * k : 8 * k + 8], axis=0, keepdims=True
            )
        begin(by_core)
        x_part.run()
        x_job.step(0)
        end(by_core)
        land_chip[chip] = added(land_core, 2)
        begin(by_chip)
        depth = sparts.shape[0]

        def own_columns(i):
            columns = pl.ds(pl.multiple_of(rank * depth + i * CHUNK, CHUNK), CHUNK)
            return pltpu.make_async_copy(normed_in.at[:, columns], cbuf.at[i], csem.at[i])

        for i in range(depth // CHUNK):
            own_columns(i).start()
        for k in range(2, chips):
            if k not in early:
                z_job.step(k)
        if chips > 2:
            o_job.step(2)
        around.step(1)

        def between():
            second.step(0, 0)
            around.finish()

            def add(at):
                total = gbc_slots[at].astype(f32)
                for r in range(1, ranks):
                    there = pl.ds(pl.multiple_of(at.start + r * tokens, 128), at.size)
                    total = total + gbc_slots[there].astype(f32)
                gbc_slots[at] = total.astype(bf16)

            row_loop(tokens, 128, add)
            for i in range(depth // CHUNK):
                own_columns(i).wait()
                sparts[i * CHUNK : (i + 1) * CHUNK] = mm_tn(cbuf[i], gbc_slots[:tokens]).astype(
                    sparts.dtype
                )
            s_job.step(0)
            for k in range(3, chips):
                o_job.step(k)
            s_job.step(1)
            x_job.step(1, True)

        in_part.run(between)
        second.step(0, 1)
        begin(own_res)
        s_job.finish(state_own)
        s_line.step(0)
        x_job.send_rest()
        z_job.finish(half_out)
        keep_z.start()
        first.arrive()
        end(own_res)

        def plus(at, total):
            wide_out[at] = pieced(gz, at) + total

        first.totals(32, plus)
        keep_block.start()
        second.step(1, 0)
        end(by_chip)
        land_rank[rank] = added(land_chip, chips)
        begin(by_rank)
        keep_z.wait()
        o_job.finish(half_out)
        keep_o.start()
        s_line.step(1)
        s_line.finish()

        def lower(at):
            state_low[at] = state_line[at].astype(bf16)

        row_loop(depth, 64, lower)
        end(by_rank)
        s_rank.step(0)
        shared = land_rank[0, :, width:]
        for r in range(1, ranks):
            shared = shared + land_rank[r, :, width:]
        for r in range(ranks):
            sums_ref[:, r * width : (r + 1) * width] = land_rank[r, :, :width]
        sums_ref[:, ranks * width :] = shared
        if chips > 2:
            x_job.step(2)
        second.step(1, 1)
        s_rank.step(1)
        for k in range(3, chips):
            x_job.step(k)
        keep_block.wait()
        end(own_cot)
        second.arrive()
        norm_acc[...] = jnp.zeros_like(norm_acc)
        gain = gain_ref[...]

        def last(at, grad):
            v = pieced(gz, at)
            scaling = lax.rsqrt(jnp.mean(v * v, axis=1, keepdims=True) + epsilon)
            norm_acc[...] += fold(grad * v * scaling)
            grad = grad * gain
            along = jnp.sum(grad * v, axis=1, keepdims=True)
            weight = scaling * scaling * scaling * along / model
            wide_out[at] = pieced(ng, at) + scaling * grad - v * weight

        second.totals(32, last)
        keep_grad.start()
        line = jnp.sum(norm_acc[...], axis=0, keepdims=True)
        eighth = model // 8
        for i in range(8):
            norm_rank[rank, i : i + 1, :] = line[:, i * eighth : (i + 1) * eighth]
        begin(norm_by_rank)
        s_rank.finish()
        buffers = (state_f, state_g)
        stored = []
        some = depth // 2
        for r in range(2 * ranks):
            if r >= 2:
                stored[r - 2].wait()

            def state(at):
                low = pl.ds(pl.multiple_of(at.start + r * some, 64), at.size)
                buffers[r % 2][at] = state_all[low].astype(f32)

            row_loop(some, 64, state)
            copy = pltpu.make_async_copy(
                buffers[r % 2], state_out.at[pl.ds(r * some, some)], osem.at[1 + r % 2 * 2]
            )
            copy.start()
            stored.append(copy)
        end(norm_by_rank)
        norm_dp[me] = added(norm_rank, ranks)
        begin(norm_by_dp)
        keep_o.wait()
        x_job.finish(line_out)
        keep_x.start()
        end(stored[-2:])
        end(norm_by_dp)
        norm_ref[...] = added(norm_dp, devices)
        keep_x.wait()
        keep_grad.wait()


def backward(
    number, chips, ranks, ggain, norm_gain, residual, cot_own, ws, gz, ng, normed, cot, wo, wz, wx,
    x, conv, bc, convbc, st, seg, gy, y, h, tapx, tapbc, par, spread, skip, nseq,
):
    tokens, width = x.shape
    rows, model = residual.shape
    n = BLOCK
    blocks = tokens // nseq // n
    at = lambda s, i: (s * blocks + blocks - 1 - i, 0)
    tail = lambda s, i: (jnp.maximum((s * blocks + blocks - 1 - i) * (n // 8) - 1, 0), 0)
    whole = lambda s, i: (0, 0)
    states = LANES
    full = lambda v: pl.BlockSpec(v.shape, whole)
    once = lambda shape: pl.BlockSpec(shape, whole)
    devices = 2 * chips
    own, depth, wide = model // devices, model // ranks, width + 2 * states
    kind = bf16 if depth // devices % 16 == 0 else f32
    return pl.pallas_call(
        functools.partial(backward_kernel, blocks, nseq * blocks, chips, ranks),
        grid=(nseq, blocks),
        in_specs=[
            pl.BlockSpec((n, width), at),
            pl.BlockSpec((n, width), at),
            pl.BlockSpec((n, 2 * states), at),
            pl.BlockSpec((n, 2 * states), at),
            pl.BlockSpec((n, LANES), at),
            pl.BlockSpec((n, LANES), at),
            pl.BlockSpec((8, LANES), tail),
            pl.BlockSpec((n, width), at),
            pl.BlockSpec((n, width), at),
            pl.BlockSpec((states, width), at),
            full(tapx), full(tapbc), full(par), full(spread), full(skip), full(ggain), full(norm_gain),
        ]
        + [ANY] * 10,
        out_specs=[
            once((8, width * ranks + 2 * states)), once((8, model // 8)),
        ]
        + [ANY] * 10,
        out_shape=[
            shaped((8, width * ranks + 2 * states), f32), shaped((8, model // 8), f32),
            shaped((own, width), f32), shaped((own, width), f32), shaped((own, width + LANES), f32),
            shaped((rows, model), f32), shaped((rows, model), f32), shaped((model, 2 * states), f32),
            shaped((tokens, model), bf16), shaped((tokens, model), bf16),
            *[shaped((ranks, rows, model) if ranks != 4 else (8, LANES), bf16)] * 2,
        ],
        scratch_shapes=[
            *scan_bwd_scratch(width, states),
            pltpu.VMEM((tokens, width + LANES), bf16),
            pltpu.VMEM((tokens, 2 * states), bf16),
            pltpu.VMEM((40, width), f32),
            pltpu.VMEM((40, 2 * states), f32),
            pltpu.VMEM((24, LANES), f32),
            pltpu.VMEM((tokens, width), bf16),
            pltpu.VMEM((tokens, width), bf16),
            pltpu.VMEM((2, tokens, CHUNK), bf16),
            pltpu.VMEM((model, width + LANES), bf16),
            pltpu.VMEM((2, tokens, CHUNK), bf16),
            pltpu.VMEM((2, CHUNK, width), bf16),
            pltpu.VMEM((2, CHUNK, width + LANES), bf16),
            pltpu.VMEM((ranks * tokens, 2 * states), bf16),
            pltpu.VMEM((2, CHUNK, 2 * states), bf16),
            pltpu.VMEM((rows, model), f32),
            pltpu.VMEM((own, width + LANES), f32),
            pltpu.VMEM((depth, 2 * states), kind),
            pltpu.VMEM((depth // 2, 2 * states), f32),
            pltpu.VMEM((depth // 2, 2 * states), f32),
            pltpu.VMEM((depth // devices, 2 * states), kind),
            pltpu.VMEM((depth, 2 * states), kind),
            pltpu.VMEM((depth, 2 * states), bf16),
            pltpu.VMEM((2, 8, wide), f32),
            pltpu.VMEM((chips, 8, wide), f32),
            pltpu.VMEM((ranks, 8, wide), f32),
            pltpu.VMEM((ranks, 8, model // 8), f32),
            pltpu.VMEM((devices, 8, model // 8), f32),
            pltpu.VMEM((8, model), f32),
            dma(2), *[dma(2)] * 5, dma(4), pltpu.SemaphoreType.DMA((2, model // width)),
            *[pltpu.SemaphoreType.DMA((2, n)) for n in (2, chips, ranks, ranks, devices)],
            *LineScatter.scratch(chips, (model, width)),
            *LineScatter.scratch(chips, (model, width)),
            *LineScatter.scratch(chips, (model, width + LANES)),
            *SmallScatter.scratch(chips, (depth, 2 * states), kind),
            *TensorGather.scratch(ranks), *SmallGather.scratch(chips), *TensorGather.scratch(ranks),
            HalvesScatter.temp((tokens, model)) if ranks == 4 else pltpu.VMEM((2, rows // 2, model), bf16),
            *(HalvesScatter.scratch((tokens, model)) if ranks == 4 else DirectScatter.scratch(ranks)) * 2,
        ],
        compiler_params=params(number),
        name="backward",
    )(
        x, conv, bc, convbc, st, seg, seg, gy, y, h, tapx, tapbc, par, spread, skip, ggain, norm_gain,
        residual, cot_own, ws, gz, ng, normed, cot, wo, wz, wx,
    )


def per_device(
    residual, segment_ids, norm_gain, inner_weight, state_weight, step_weight, conv_weight,
    conv_bias, step_bias, decay_log, skip_gain, gated_gain, out_weight, cotangent,
):
    chips, ranks = lax.axis_size("dp") // 2, lax.axis_size("tensor")
    width = inner_weight.shape[2]
    heads = step_weight.shape[1]
    inner_width = gated_gain.shape[0]
    nseq = segment_ids.shape[0]
    wx_own = jnp.concatenate([inner_weight[:, 1], on_lanes(step_weight)], axis=1)
    by_head = jnp.stack([step_bias, decay_log, skip_gain])
    by_head = jnp.pad(by_head, ((0, 5), (0, LANES - by_head.shape[1])))
    x, st, bc, seg, tapx, tapbc, par, skip, gain, spread, normed, wx = project(
        1, chips, ranks, heads, residual, norm_gain[None], state_weight, segment_ids,
        conv_weight, conv_bias[None], by_head, gated_gain[None], wx_own,
    )
    y, h, conv, convbc, wz, cot = scan_forward_gather(
        2, chips, ranks, inner_weight[:, 0], cotangent,
        x, bc, st, seg, tapx, tapbc, par, spread, skip, nseq,
    )
    gz, gy, ng, ggain, wo = gate(3, chips, ranks, gain, out_weight.T, normed, wz, y, cot)
    sums, norm_grad, z_grad, out_grad, x_grad, block_out, residual_grad, state_grad, *_ = backward(
        4, chips, ranks, ggain, norm_gain[None], residual, cotangent, state_weight,
        gz, ng, normed, cot, wo, wz, wx,
        x, conv, bc, convbc, st, seg, gy, y, h, tapx, tapbc, par, spread, skip, nseq,
    )
    inner_grad = jnp.stack([z_grad, x_grad[:, :width]], axis=1)
    by_head = sums[6, :inner_width].reshape(ranks, width)
    by_head = [by_head[:, k * LANES : k * LANES + heads].reshape(-1) for k in range(3)]
    return (
        block_out, residual_grad, norm_grad.reshape(-1), inner_grad, state_grad,
        x_grad[:, width : width + heads], sums[:4], sums[4], *by_head,
        sums[5, :inner_width], out_grad.T,
    )


def solution(mesh):
    rows, both = P("dp", "tensor"), P(("dp", "tensor"), None)
    inner, out = P("dp", None, "tensor"), P("tensor", "dp")
    return jax.shard_map(
        per_device,
        mesh=mesh,
        in_specs=(
            both, P("dp", None), P(), inner, P(), rows, P(), P(), P(), P(), P(), P(), out, both,
        ),
        out_specs=(both, both, P(), inner, P(), rows, P(), P(), P(), P(), P(), P(), out),
        check_vma=False,
    )
```

```python
import functools
import jax
import jax.numpy as jnp
from jax import lax
from jax.experimental import pallas as pl
from jax.experimental.pallas import tpu as pltpu
from jax.sharding import PartitionSpec as P

LANES = 128
BLOCK = 128
WIDTH = 64
VMEM_BYTES = 60 * 1024 * 1024
f32, bf16 = jnp.float32, jnp.bfloat16
ROWS0 = (((0,), (0,)), ((), ()))
COLS1 = (((1,), (1,)), ((), ()))


def mm(a, b):
    return jnp.dot(a, b, preferred_element_type=f32)


def mm_tn(a, b):
    return lax.dot_general(a, b, ROWS0, preferred_element_type=f32)


def mm_nt(a, b):
    return lax.dot_general(a, b, COLS1, preferred_element_type=f32)


def sigmoid(v):
    return 0.5 + 0.5 * jnp.tanh(0.5 * v)


def two_parts(v, low_lanes):
    high = v.astype(bf16)
    return jnp.where(low_lanes, (v - high.astype(f32)).astype(bf16), high)


def head_sums(v, spread):
    high = v.astype(bf16)
    low = (v - high.astype(f32)).astype(bf16)
    return mm_nt(high, spread) + mm_nt(low, spread)


def shifted_masks(seg_ext, seg):
    n = seg.shape[0]
    return [None] + [seg_ext[8 - k : 8 - k + n] == seg for k in (1, 2, 3)]


def convolve(tail, part, masks, taps):
    n = part.shape[0]
    ext = jnp.concatenate([tail, part], axis=0)
    total = taps[4:5] + taps[3:4] * part
    for k in (1, 2, 3):
        total = total + taps[3 - k : 4 - k] * jnp.where(masks[k], ext[8 - k : 8 - k + n], 0.0)
    return total


def wide(v):
    return jnp.concatenate([v, v], axis=1)


def step_state(raw, params, seg, prev_seg, end_seg, n):
    row = lax.broadcasted_iota(jnp.int32, (n, n), 0)
    col = lax.broadcasted_iota(jnp.int32, (n, n), 1)
    v = raw + params[0:1]
    dt = jnp.maximum(v, 0.0) + jnp.log1p(jnp.exp(-jnp.abs(v)))
    a = params[1:2]
    cum = jnp.dot(
        (row >= col).astype(f32), dt * a, precision=lax.Precision.HIGHEST, preferred_element_type=f32
    )
    last = cum[n - 1 : n]
    into = jnp.where(seg == prev_seg, jnp.exp(cum), 0.0)
    onto = jnp.where(seg == end_seg, jnp.exp(last - cum), 0.0)
    through = jnp.where(end_seg == prev_seg, jnp.exp(last), 0.0)
    bias = jnp.where((row >= col) & (seg == jnp.transpose(seg)), 0.0, -1e30)
    return v, dt, a, cum, into, onto, through, bias


def scan_fwd_kernel(
    blocks, x_ref, bc_ref, st_ref, seg_ref, tapx_ref, tapbc_ref, par_ref, spread_ref, skip_ref,
    y_ref, h_ref, conv_ref, convbc_ref, state, tail_x, tail_bc, tail_seg,
):
    n = BLOCK
    block = pl.program_id(1)

    @pl.when(block == 0)
    def _():
        state[...] = jnp.zeros_like(state)
        tail_x[...] = jnp.zeros_like(tail_x)
        tail_bc[...] = jnp.zeros_like(tail_bc)
        tail_seg[...] = jnp.full_like(tail_seg, -1)

    seg = seg_ref[...]
    masks = shifted_masks(jnp.concatenate([tail_seg[...], seg], axis=0), seg)
    prev_seg, end_seg = tail_seg[7:8], seg[n - 1 : n]
    v, dt, a, cum, into, onto, through, bias = step_state(
        st_ref[...], par_ref[...], seg, prev_seg, end_seg, n
    )
    cum_t = jnp.transpose(cum)
    low_lanes = lax.broadcasted_iota(jnp.int32, (n, LANES), 1) >= LANES // 2
    spread = spread_ref[...]
    dt_w = mm(two_parts(dt, low_lanes), spread)
    into_w = mm(two_parts(into, low_lanes), spread)
    onto_w = mm(two_parts(onto, low_lanes), spread)
    through_w = mm(two_parts(jnp.broadcast_to(through, (8, LANES)), low_lanes[:8]), spread)[0:1]
    bc_masks = [None] + [wide(m) for m in masks[1:]]
    conv_bc = convolve(tail_bc[...], bc_ref[...], bc_masks, tapbc_ref[...])
    convbc_ref[...] = conv_bc
    act_bc = conv_bc * sigmoid(conv_bc)
    b, c = act_bc[:, :LANES].astype(bf16), act_bc[:, LANES:].astype(bf16)
    cross = mm_nt(c, b)
    entering = state[...].astype(bf16)
    h_ref[...] = entering
    first_half = lax.broadcasted_iota(jnp.int32, (n, LANES), 1) < WIDTH
    for pair in range(x_ref.shape[1] // LANES):
        sl = slice(pair * LANES, (pair + 1) * LANES)
        conv = convolve(tail_x[:, sl], x_ref[:, sl], masks, tapx_ref[:, sl])
        conv_ref[:, sl] = conv
        xs = conv * sigmoid(conv)
        xd = xs * dt_w[:, sl]
        outside = mm(c, entering[:, sl]) * into_w[:, sl]
        mixes = []
        for h in (2 * pair, 2 * pair + 1):
            decay = jnp.exp(cum[:, h : h + 1] - cum_t[h : h + 1, :] + bias)
            mixes.append((decay * cross).astype(bf16))
        stacked = jnp.concatenate(
            [jnp.where(first_half, xd, 0.0), jnp.where(first_half, 0.0, xd)], axis=0
        ).astype(bf16)
        inside = mm(jnp.concatenate(mixes, axis=1), stacked)
        y_ref[:, sl] = inside + outside + skip_ref[0:1, sl] * xs
        local = mm_tn(b, (onto_w[:, sl] * xd).astype(bf16))
        state[:, sl] = through_w[:, sl] * state[:, sl] + local
    tail_x[...] = x_ref[n - 8 :, :]
    tail_bc[...] = bc_ref[n - 8 :, :]
    tail_seg[...] = seg_ref[n - 8 :, :]


def fold(v):
    total = v[0:8]
    for r in range(8, v.shape[0], 8):
        total = total + v[r : r + 8]
    return total


def scan_bwd_kernel(
    blocks, x_ref, conv_ref, bc_ref, convbc_ref, st_ref, seg_ref, segt_ref, gy_ref, y_ref, h_ref,
    tapx_ref, tapbc_ref, par_ref, spread_ref, skip_ref,
    gx_ref, gbc_ref, gst_ref, gtapx_ref, gtapbc_ref, gpar_ref,
    gstate, head_x, head_bc, head_seg, xs_s, slope_s, back_s, dt_s, onto_s, xd_s, sums_s,
):
    n = BLOCK
    step = pl.program_id(1)
    block = blocks - 1 - step

    @pl.when((step == 0) & (pl.program_id(0) == 0))
    def _():
        gtapx_ref[...] = jnp.zeros_like(gtapx_ref)
        gtapbc_ref[...] = jnp.zeros_like(gtapbc_ref)
        gpar_ref[...] = jnp.zeros_like(gpar_ref)

    @pl.when(step == 0)
    def _():
        gstate[...] = jnp.zeros_like(gstate)
        head_x[...] = jnp.zeros_like(head_x)
        head_bc[...] = jnp.zeros_like(head_bc)
        head_seg[...] = jnp.full_like(head_seg, -1)

    seg = seg_ref[...]
    first = block == 0
    seg_next = jnp.concatenate([seg, head_seg[...]], axis=0)
    ahead = [None] + [seg_next[k : k + n] == seg for k in (1, 2, 3)]
    prev_seg = jnp.where(first, -1, segt_ref[7:8])
    end_seg = seg[n - 1 : n]
    v, dt, a, cum, into, onto, through, bias = step_state(
        st_ref[...], par_ref[...], seg, prev_seg, end_seg, n
    )
    cum_t = jnp.transpose(cum)
    low_lanes = lax.broadcasted_iota(jnp.int32, (n, LANES), 1) >= LANES // 2
    spread = spread_ref[...]
    dt_s[...] = mm(two_parts(dt, low_lanes), spread)
    into_w = mm(two_parts(into, low_lanes), spread)
    onto_s[...] = mm(two_parts(onto, low_lanes), spread)
    through_w = mm(two_parts(jnp.broadcast_to(through, (8, LANES)), low_lanes[:8]), spread)[0:1]
    conv_bc = convbc_ref[...]
    sig_bc = sigmoid(conv_bc)
    act_bc = conv_bc * sig_bc
    b, c = act_bc[:, :LANES].astype(bf16), act_bc[:, LANES:].astype(bf16)
    cross = mm_nt(c, b)
    first_half = lax.broadcasted_iota(jnp.int32, (n, LANES), 1) < WIDTH
    halves = lambda t: jnp.concatenate(
        [jnp.where(first_half, t, 0.0), jnp.where(first_half, 0.0, t)], axis=0
    ).astype(bf16)
    into_s, onto_low = sums_s.at[0:n], sums_s.at[n : 2 * n]
    pairs = [slice(i, i + LANES) for i in range(0, x_ref.shape[1], LANES)]

    for sl in pairs:
        conv = conv_ref[:, sl]
        sig = sigmoid(conv)
        xs = conv * sig
        xs_s[:, sl] = xs
        slope_s[:, sl] = sig + xs * (1.0 - sig)
        xd = xs * dt_s[:, sl]
        xd_s[:, sl] = xd.astype(bf16)
        onto_low[:, sl] = (xd * onto_s[:, sl]).astype(bf16)
        into_s[:, sl] = (gy_ref[:, sl] * into_w[:, sl]).astype(bf16)
    before = h_ref[...]
    gstate_low = gstate[...].astype(bf16)
    gy_into = into_s[...]
    gc = mm_nt(gy_into, before)
    gb = mm_nt(onto_low[...], gstate_low)
    back_s[...] = mm(b, gstate_low)
    edges = 5 * n
    for sl in pairs:
        old = through_w[:, sl] * gstate[:, sl]
        last = fold(old * before[:, sl].astype(f32))
        skips = fold(gy_ref[:, sl] * xs_s[:, sl])
        both = jnp.concatenate([last, skips], axis=0)
        high = both.astype(bf16)
        sums_s[edges : edges + 16, sl] = high
        sums_s[edges + 16 : edges + 32, sl] = (both - high.astype(f32)).astype(bf16)
        gstate[:, sl] = old + mm_tn(c, gy_into[:, sl])
    gcross = jnp.zeros((n, n), f32)
    for pair, sl in enumerate(pairs):
        xs = xs_s[:, sl]
        xd_low = xd_s[:, sl]
        gy = gy_ref[:, sl]
        skip = skip_ref[0:1, sl]
        inner = y_ref[:, sl] - skip * xs
        g_state = onto_s[:, sl] * back_s[:, sl]
        gy_halves = halves(gy)
        gmix = mm_nt(gy_halves, xd_low)
        mixes = []
        for i, h in enumerate((2 * pair, 2 * pair + 1)):
            decay = jnp.exp(cum[:, h : h + 1] - cum_t[h : h + 1, :] + bias)
            mixes.append((decay * cross).astype(bf16))
            gcross = gcross + decay * gmix[i * n : (i + 1) * n]
        gxd = mm_tn(jnp.concatenate(mixes, axis=0), gy_halves) + g_state
        xd_r, gy_r = xd_low.astype(f32), gy.astype(bf16).astype(f32)
        q = gy_r * inner - xd_r * gxd
        high = q.astype(bf16)
        sums_s[0:n, sl] = high
        sums_s[n : 2 * n, sl] = (q - high.astype(f32)).astype(bf16)
        q = xd_r * g_state
        high = q.astype(bf16)
        sums_s[2 * n : 3 * n, sl] = high
        sums_s[3 * n : 4 * n, sl] = (q - high.astype(f32)).astype(bf16)
        sums_s[4 * n : 5 * n, sl] = (xs * gxd).astype(bf16)
        gconv = (dt_s[:, sl] * gxd + skip * gy) * slope_s[:, sl]
        taps = tapx_ref[:, sl]
        part = x_ref[:, sl]
        ext = jnp.concatenate([gconv, head_x[:, sl]], axis=0)
        gu = taps[3:4] * gconv
        gtapx_ref[24:32, sl] += fold(gconv * part)
        for k in (1, 2, 3):
            later = jnp.where(ahead[k], ext[k : k + n], 0.0)
            gu = gu + taps[3 - k : 4 - k] * later
            gtapx_ref[8 * (3 - k) : 8 * (4 - k), sl] += fold(later * part)
        gx_ref[:, sl] = gu.astype(bf16)
        gtapx_ref[32:40, sl] += fold(gconv)
        head_x[:, sl] = gconv[0:8]
    sums = mm_nt(sums_s[...], spread)
    sum_q = sums[0:n] + sums[n : 2 * n]
    sum_state = sums[2 * n : 3 * n] + sums[3 * n : 4 * n]
    sum_dt = sums[4 * n : 5 * n]
    sum_last = sums[edges : edges + 8] + sums[edges + 16 : edges + 24]
    sum_skip = sums[edges + 8 : edges + 16] + sums[edges + 24 : edges + 32]
    gcross_low = gcross.astype(bf16)
    gc = gc + mm(gcross_low, b)
    gb = gb + mm_tn(gcross_low, c)
    gconv = jnp.concatenate([gb, gc], axis=1) * (sig_bc + act_bc * (1.0 - sig_bc))
    ext = jnp.concatenate([gconv, head_bc[...]], axis=0)
    taps = tapbc_ref[...]
    part = bc_ref[...]
    gu = taps[3:4] * gconv
    gtapbc_ref[24:32, :] += fold(gconv * part)
    for k in (1, 2, 3):
        later = jnp.where(wide(ahead[k]), ext[k : k + n], 0.0)
        gu = gu + taps[3 - k : 4 - k] * later
        gtapbc_ref[8 * (3 - k) : 8 * (4 - k), :] += fold(later * part)
    gbc_ref[...] = gu.astype(gbc_ref.dtype)
    gtapbc_ref[32:40, :] += fold(gconv)
    head_bc[...] = gconv[0:8]
    head_seg[...] = seg[0:8]
    rows = lax.broadcasted_iota(jnp.int32, (n, n), 0)
    cols = lax.broadcasted_iota(jnp.int32, (n, n), 1)
    after = jnp.dot(
        (cols >= rows).astype(f32), sum_q, precision=lax.Precision.HIGHEST, preferred_element_type=f32
    )
    edge = jnp.sum(sum_state, axis=0, keepdims=True) + jnp.sum(sum_last, axis=0, keepdims=True)
    glog = after + edge
    gdt = sum_dt + a * glog
    gst = gdt * sigmoid(v)
    gst_ref[...] = jnp.where(low_lanes, 0.0, gst).astype(bf16)
    gpar_ref[0:8] += fold(gst)
    gpar_ref[8:16] += fold(a * dt * glog)
    gpar_ref[16:24] += sum_skip


def scan_bwd_scratch(width, states):
    n = BLOCK
    return [
        pltpu.VMEM((states, width), f32),
        pltpu.VMEM((8, width), f32),
        pltpu.VMEM((8, 2 * states), f32),
        pltpu.VMEM((8, LANES), jnp.int32),
        *[pltpu.VMEM((n, width), f32)] * 5,
        pltpu.VMEM((n, width), bf16),
        pltpu.VMEM((5 * n + 32, width), bf16),
    ]


def on_lanes(v):
    half = jnp.pad(v, [(0, 0)] * (v.ndim - 1) + [(0, LANES // 2 - v.shape[-1])])
    return jnp.concatenate([half, half], axis=-1)


MESH = pl.DeviceIdType.MESH


def place():
    dp, rank = lax.axis_index("dp"), lax.axis_index("tensor")
    return dp // 2, dp % 2, rank


def remote(src, dst, send, recv, dp, rank):
    return pltpu.make_async_remote_copy(
        src_ref=src, dst_ref=dst, send_sem=send, recv_sem=recv, device_id=(dp, rank),
        device_id_type=MESH,
    )


def greet(chips, ranks):
    chip, core, rank = place()
    sem = pltpu.get_barrier_semaphore()
    me = chip * 2 + core

    def signal(dp, r):
        pl.semaphore_signal(sem, inc=1, device_id=(dp, r), device_id_type=MESH)

    signal(chip * 2 + 1 - core, rank)
    for step in (1, -1):
        @pl.when((chip + step >= 0) & (chip + step < chips))
        def _():
            signal(me + 2 * step, rank)
    for k in range(1, ranks):
        signal(me, lax.rem(rank + k, ranks))
    pl.semaphore_wait(sem, ranks + (chip + chips - 1) // chips + (2 * chips - 2 - chip) // chips)


def greet_all(chips, ranks):
    chip, core, rank = place()
    sem = pltpu.get_barrier_semaphore()
    me, devices = chip * 2 + core, 2 * chips
    for k in range(1, devices):
        pl.semaphore_signal(
            sem, inc=1, device_id=(lax.rem(me + k, devices), rank), device_id_type=MESH
        )
    for k in range(1, ranks):
        pl.semaphore_signal(
            sem, inc=1, device_id=(me, lax.rem(rank + k, ranks)), device_id_type=MESH
        )
    pl.semaphore_wait(sem, devices + ranks - 2)


def slab(ref, index, rows):
    return ref.at[pl.ds(pl.multiple_of(index * rows, rows), rows)]


class LineGather:
    def __init__(self, own, slots, send, recv, local, chips):
        self.own, self.slots, self.send, self.recv, self.local = own, slots, send, recv, local
        self.chips, self.rows = chips, own.shape[0]
        self.chip, self.core, self.rank = place()
        self.me = self.chip * 2 + self.core
        self.partner = self.chip * 2 + 1 - self.core
        self.steps = chips

    @staticmethod
    def scratch(chips):
        n = 2 * chips
        return [
            pltpu.SemaphoreType.DMA((3, n)), pltpu.SemaphoreType.DMA((n,)), pltpu.SemaphoreType.DMA,
        ]

    def copy(self, way, origin, src=None):
        target = (self.me + 2, self.me - 2, self.partner)[way]
        slot = slab(self.slots, origin, self.rows)
        return remote(
            slot if src is None else src, slot, self.send.at[way, origin], self.recv.at[origin],
            target, self.rank,
        )

    def pass_on(self, way, origin, src=None, wait=False):
        def go():
            copy = self.copy(way, origin, src)
            copy.wait_send() if wait else copy.start()

        if way == 0:
            pl.when(self.chip + 1 < self.chips)(go)
        elif way == 1:
            pl.when(self.chip > 0)(go)
        else:
            go()

    def keep(self):
        return pltpu.make_async_copy(self.own, slab(self.slots, self.me, self.rows), self.local)

    def sides(self, k):
        return ((0, self.chip - k >= 0, -k), (1, self.chip + k < self.chips, k))

    def step(self, k):
        if k == 0:
            for way in (0, 1, 2):
                self.pass_on(way, self.me, self.own)
            self.keep().start()
            return
        for way, there, shift in self.sides(k):
            @pl.when(there)
            def _():
                origin = self.me + 2 * shift
                self.copy(2, origin).wait_recv()
                self.pass_on(way, origin)
                self.pass_on(2, origin)

    def arrive(self, k, use=None):
        if k == 0:
            self.keep().wait()
            self.copy(2, self.partner).wait_recv()
            if use is not None:
                use(self.chip)
            return
        for way, there, shift in self.sides(k):
            @pl.when(there)
            def _():
                self.copy(2, self.partner + 2 * shift).wait_recv()
                if use is not None:
                    use(self.chip + shift)

    def each(self, k, use):
        if k == 0:
            use(self.chip)
            return
        for way, there, shift in self.sides(k):
            @pl.when(there)
            def _():
                use(self.chip + shift)

    def sent(self):
        for way in (0, 1, 2):
            self.pass_on(way, self.me, self.own, wait=True)
        for k in range(1, self.chips):
            for way, there, shift in self.sides(k):
                @pl.when(there)
                def _():
                    origin = self.me + 2 * shift
                    self.pass_on(way, origin, wait=True)
                    self.pass_on(2, origin, wait=True)

    def finish(self):
        for k in range(self.chips):
            self.arrive(k)
        self.sent()


class TensorGather:
    def __init__(self, own, slots, send, recv, local, ranks):
        self.own, self.slots, self.send, self.recv, self.local = own, slots, send, recv, local
        self.ranks, self.rows = ranks, own.shape[0]
        chip, core, self.rank = place()
        self.me = chip * 2 + core
        self.kept = False

    @staticmethod
    def scratch(ranks):
        return [
            pltpu.SemaphoreType.DMA((ranks,)), pltpu.SemaphoreType.DMA((ranks,)), pltpu.SemaphoreType.DMA,
        ]

    def near(self, k):
        x = self.rank % 2
        y = self.rank // 2
        across = (y * 2 + 1 - x, (1 - y) * 2 + x)
        if k < 2:
            return remote(
                self.own, slab(self.slots, self.rank, self.rows), self.send.at[k], self.recv.at[k],
                self.me, across[k],
            )
        half = slab(self.slots, across[k - 2] * 2 + (k - 2), self.rows // 2)
        return remote(half, half, self.send.at[k], self.recv.at[k], self.me, across[3 - k])

    def direct(self, k):
        return remote(
            self.own, slab(self.slots, self.rank, self.rows), self.send.at[k], self.recv.at[k],
            self.me, lax.rem(self.rank + k, self.ranks),
        )

    def keep(self):
        return pltpu.make_async_copy(self.own, slab(self.slots, self.rank, self.rows), self.local)

    def step(self, k):
        if k == 0:
            if self.ranks == 4:
                self.near(0).start()
                self.near(1).start()
            else:
                for j in range(1, self.ranks):
                    self.direct(j).start()
            self.keep().start()
        elif self.ranks == 4:
            for j in (0, 1):
                self.near(j).wait_recv()
                self.near(2 + j).start()

    def near_rows(self):
        self.keep().wait()
        self.kept = True
        x, y = self.rank % 2, self.rank // 2
        return [self.rank, y * 2 + 1 - x, (1 - y) * 2 + x], [(1 - y) * 2 + 1 - x]

    def finish(self):
        if not self.kept:
            self.keep().wait()
        if self.ranks == 4:
            for j in (0, 1):
                self.near(j).wait_send()
                self.near(2 + j).wait()
        else:
            for j in range(1, self.ranks):
                self.direct(j).wait()


def add_rows(target, others, out=None):
    out = target if out is None else out
    rows = target.shape[0]
    some = 64 if rows % 64 == 0 else rows
    kind = out.dtype if len(others) == 1 else f32

    def add(at):
        total = target[at].astype(kind)
        for other in others:
            total = total + other[at].astype(kind)
        out[at] = total.astype(out.dtype)

    row_loop(rows, some, add)


class LineScatter:
    def __init__(self, parts, swap, flow, send, recv, chips):
        self.parts, self.swap, self.flow = parts, swap, flow
        self.send, self.recv, self.chips = send, recv, chips
        self.rows = parts.shape[0] // (2 * chips)
        self.chip, self.core, self.rank = place()
        self.me = self.chip * 2 + self.core
        self.partner = self.chip * 2 + 1 - self.core

    @staticmethod
    def scratch(chips, shape, dtype=bf16):
        block = (shape[0] // (2 * chips),) + tuple(shape[1:])
        return [
            pltpu.VMEM((chips,) + block, dtype), pltpu.VMEM((chips + 1,) + block, dtype),
            pltpu.SemaphoreType.DMA((3, chips)), pltpu.SemaphoreType.DMA((3, chips)),
        ]

    def order(self):
        n = self.chips
        return [c for k in range(n // 2) for c in (n - 1 - k, k)]

    def over(self, c):
        return remote(
            slab(self.parts, 2 * c + 1 - self.core, self.rows), self.swap.at[c], self.send.at[2, c],
            self.recv.at[2, c], self.partner, self.rank,
        )

    def along(self, way, c, first=False):
        if way == 0:
            here = there = c
        else:
            here, there = c, jnp.where(c == self.chip - 1, self.chips, c)
        src = self.swap.at[c] if first else self.flow.at[here]
        return remote(
            src, self.flow.at[there], self.send.at[way, c], self.recv.at[way, c],
            self.me + (2, -2)[way], self.rank,
        )

    def send_off(self, c):
        n, chip = self.chips, self.chip

        @pl.when((chip == 0) & (c > 0))
        def _():
            self.along(0, c, True).start()

        @pl.when((chip == n - 1) & (c < n - 1))
        def _():
            self.along(1, c, True).start()

    def send_rest(self):
        for c in self.order()[2:]:
            self.send_off(c)

    def step(self, k, hold=False):
        n, chip = self.chips, self.chip
        if k == 0:
            for c in self.order():
                self.over(c).start()
            return
        if k == 1:
            for i, c in enumerate(self.order()):
                self.over(c).wait()
                add_rows(self.swap.at[c], [slab(self.parts, 2 * c + self.core, self.rows)])
                if i < 2 or not hold:
                    self.send_off(c)
            return
        t = k - 1
        c = n - 1 - (t - chip)

        @pl.when((chip > 0) & (t >= chip) & (c > chip))
        def _():
            self.along(0, c).wait_recv()
            add_rows(self.flow.at[c], [self.swap.at[c]])
            self.along(0, c).start()

        d = t - (n - 1 - chip)

        @pl.when((chip < n - 1) & (d >= 0) & (d < chip))
        def _():
            self.along(1, d).wait_recv()
            add_rows(self.flow.at[d], [self.swap.at[d]])
            self.along(1, d).start()

    def finish(self, out):
        n, chip = self.chips, self.chip
        mine, up, down = self.swap.at[chip], self.flow.at[chip], self.flow.at[n]

        @pl.when(chip == 0)
        def _():
            self.along(1, chip).wait_recv()
            add_rows(mine, [down], out)

        @pl.when(chip == n - 1)
        def _():
            self.along(0, chip).wait_recv()
            add_rows(mine, [up], out)

        @pl.when((chip > 0) & (chip < n - 1))
        def _():
            self.along(0, chip).wait_recv()
            self.along(1, chip).wait_recv()
            add_rows(mine, [up, down], out)

        for c in range(n):
            @pl.when((chip < n - 1) & (c > chip))
            def _():
                self.along(0, c).wait_send()

            @pl.when((chip > 0) & (c < chip))
            def _():
                self.along(1, c).wait_send()


class DirectScatter:
    def __init__(self, parts, land, temp, send, recv, tsem, ranks):
        self.parts, self.land, self.temp = parts, land, temp
        self.send, self.recv, self.tsem, self.ranks = send, recv, tsem, ranks
        self.rows = parts.shape[0] // ranks
        chip, core, self.rank = place()
        self.me = chip * 2 + core

    @staticmethod
    def scratch(ranks):
        return [dma(ranks), dma(ranks), dma(2)]

    def copy(self, k):
        to = lax.rem(self.rank + k, self.ranks)
        return remote(
            slab(self.parts, to, self.rows), self.land.at[k], self.send.at[k], self.recv.at[k],
            self.me, to,
        )

    def step(self, k, g):
        if k == 0 and g == 1:
            for j in range(1, self.ranks):
                self.copy(j).start()

    def arrive(self):
        for j in range(1, self.ranks):
            self.copy(j).wait()

    def totals(self, some, body):
        @pl.loop(0, self.rows // some)
        def _(i):
            at = pl.ds(pl.multiple_of(i * some, some), some)
            total = None
            for j in range(self.ranks):
                src = slab(self.parts, self.rank * (self.rows // some) + i, some) if j == 0 else self.land.at[j, at]
                copy = pltpu.make_async_copy(src, self.temp.at[j % 2, pl.ds(0, some)], self.tsem.at[j % 2])
                copy.start()
                copy.wait()
                v = self.temp[j % 2, pl.ds(0, some)].astype(f32)
                total = v if total is None else total + v
            body(at, total)


class SmallScatter:
    def __init__(self, parts, swap, land, send, recv, chips):
        self.parts, self.swap, self.land, self.send, self.recv = parts, swap, land, send, recv
        self.chips, self.rows = chips, parts.shape[0] // (2 * chips)
        self.chip, self.core, self.rank = place()

    @staticmethod
    def scratch(chips, shape, dtype):
        block = pltpu.VMEM((chips, shape[0] // (2 * chips), shape[1]), dtype)
        return [
            block, block, pltpu.SemaphoreType.DMA((2, chips)), pltpu.SemaphoreType.DMA((2, chips)),
        ]

    def over(self, c):
        return remote(
            slab(self.parts, 2 * c + 1 - self.core, self.rows), self.swap.at[c], self.send.at[0, c],
            self.recv.at[0, c], self.chip * 2 + 1 - self.core, self.rank,
        )

    def straight(self, k):
        to = lax.rem(self.chip + k, self.chips)
        return remote(
            self.swap.at[to], self.land.at[self.chip], self.send.at[1, k], self.recv.at[1, k],
            2 * to + self.core, self.rank,
        )

    def step(self, k):
        if k == 0:
            for c in range(self.chips):
                self.over(c).start()
            return
        for c in range(self.chips):
            self.over(c).wait()
            add_rows(self.swap.at[c], [slab(self.parts, 2 * c + self.core, self.rows)])
        for j in range(1, self.chips):
            self.straight(j).start()

    def finish(self, out):
        for j in range(1, self.chips):
            self.straight(j).wait()
        total = self.swap[self.chip].astype(f32)
        for j in range(1, self.chips):
            total = total + self.land[lax.rem(self.chip + j, self.chips)].astype(f32)
        out[...] = total.astype(out.dtype)


class SmallGather:
    def __init__(self, own, slots, send, recv, chips):
        self.own, self.slots, self.send, self.recv = own, slots, send, recv
        self.chips, self.rows = chips, own.shape[0]
        self.chip, self.core, self.rank = place()
        self.me = self.chip * 2 + self.core

    @staticmethod
    def scratch(chips):
        return [pltpu.SemaphoreType.DMA((2, chips)), pltpu.SemaphoreType.DMA((2, chips))]

    def straight(self, k):
        slot = slab(self.slots, self.me, self.rows)
        return remote(
            self.own, slot, self.send.at[0, k], self.recv.at[0, k],
            2 * lax.rem(self.chip + k, self.chips) + self.core, self.rank,
        )

    def over(self, k):
        slot = slab(
            self.slots, 2 * lax.rem(self.chip + self.chips - k, self.chips) + self.core, self.rows
        )
        return remote(
            self.own if k == 0 else slot, slot, self.send.at[1, k], self.recv.at[1, k],
            self.chip * 2 + 1 - self.core, self.rank,
        )

    def step(self, k):
        if k == 0:
            for j in range(1, self.chips):
                self.straight(j).start()
            self.over(0).start()
            self.slots[pl.ds(pl.multiple_of(self.me * self.rows, self.rows), self.rows)] = self.own[...]
            return
        for j in range(1, self.chips):
            self.straight(j).wait_recv()
            self.over(j).start()

    def finish(self):
        for j in range(1, self.chips):
            self.straight(j).wait_send()
        for j in range(self.chips):
            self.over(j).wait()


class HalvesScatter:
    def __init__(self, parts, land, temp, send, recv, tsem):
        self.parts, self.land, self.temp, self.send, self.recv, self.tsem = parts, land, temp, send, recv, tsem
        chip, core, self.rank = place()
        self.me = chip * 2 + core
        self.rows = parts.shape[0] // 4
        self.half, self.wide = self.rows // 2, parts.shape[1] // 2
        x, y = self.rank % 2, self.rank // 2
        self.across = (y * 2 + 1 - x, (1 - y) * 2 + x)
        self.far = (1 - y) * 2 + 1 - x

    @staticmethod
    def scratch(shape):
        return [
            pltpu.VMEM((2, 6, shape[0] // 8, shape[1] // 2), bf16),
            *[pltpu.SemaphoreType.DMA((2, n)) for n in (6, 6, 2)],
        ]

    @staticmethod
    def temp(shape):
        return pltpu.VMEM((2, 2, shape[0] // 8, shape[1] // 2), bf16)

    def part(self, g, owner, way):
        return slab(self.parts.at[:, pl.ds(g * self.wide, self.wide)], owner * 2 + way, self.half)

    def copy(self, g, i):
        if i < 4:
            way = i // 2
            src = self.part(g, self.across[way] if i % 2 == 0 else self.far, way)
            to = self.across[way]
        else:
            way = i - 4
            src, to = self.land.at[g, 2 * way + 1], self.across[1 - way]
        return remote(
            src, self.land.at[g, i], self.send.at[g, i], self.recv.at[g, i], self.me, to
        )

    def fetch(self, g, owner, way):
        return pltpu.make_async_copy(
            self.part(g, owner, way), self.temp.at[g, way], self.tsem.at[g, way]
        )

    def step(self, k, g):
        if k == 0:
            for i in (1, 3, 0, 2):
                self.copy(g, i).start()
            return
        for way in (0, 1):
            self.fetch(g, self.across[1 - way], way).start()
        for way in (0, 1):
            self.copy(g, 2 * way + 1).wait_recv()
            self.fetch(g, self.across[1 - way], way).wait()
            add_rows(self.land.at[g, 2 * way + 1], [self.temp.at[g, way]])
            self.copy(g, 4 + way).start()
        for way in (0, 1):
            self.fetch(g, self.rank, way).start()

    def arrive(self):
        for g in (0, 1):
            for way in (0, 1):
                self.copy(g, 2 * way + 1).wait_send()
                self.copy(g, 2 * way).wait()
                self.copy(g, 4 + way).wait()
                self.fetch(g, self.rank, way).wait()

    def totals(self, some, body):
        for way in (0, 1):
            def add(i):
                at = pl.ds(pl.multiple_of(i * some, some), some)
                total = jnp.concatenate(
                    [
                        self.temp[g, way, at].astype(f32)
                        + self.land[g, 2 * way, at].astype(f32)
                        + self.land[g, 4 + way, at].astype(f32)
                        for g in (0, 1)
                    ],
                    axis=1,
                )
                body(pl.ds(pl.multiple_of(way * self.half + i * some, some), some), total)

            pl.loop(0, self.half // some)(add)


def row_loop(rows, some, body):
    @pl.loop(0, rows // some)
    def _(i):
        body(pl.ds(pl.multiple_of(i * some, some), some))


def params(number):
    return pltpu.CompilerParams(
        collective_id=number, has_side_effects=True, vmem_limit_bytes=VMEM_BYTES
    )


ANY = pl.BlockSpec(memory_space=pl.ANY)
ONCHIP = pl.BlockSpec(memory_space=pltpu.VMEM)


epsilon = 1e-05
CHUNK = 256


def shaped(shape, dtype):
    return jax.ShapeDtypeStruct(shape, dtype)


def dma(count=None):
    return pltpu.SemaphoreType.DMA if count is None else pltpu.SemaphoreType.DMA((count,))


def exact_mm(v, picks):
    high = v.astype(bf16)
    rest = v - high.astype(f32)
    middle = rest.astype(bf16)
    low = (rest - middle.astype(f32)).astype(bf16)
    return mm(high, picks) + mm(middle, picks) + mm(low, picks)


def prepare(
    rank, heads, seg_in, taps_in, bias_in, heads_in, gain_in,
    seg_out, tapx_out, tapbc_out, par_out, skip_out, gain_out, spread_out,
):
    width, inner = tapx_out.shape[1], gain_in.shape[1]
    length = seg_in.shape[1]
    for s in range(seg_in.shape[0]):
        for r in range(0, length, LANES):
            row = jnp.broadcast_to(seg_in[s : s + 1, r : r + LANES], (LANES, LANES))
            at = s * length + r
            seg_out[at : at + LANES] = jnp.transpose(row.astype(f32)).astype(jnp.int32)
    own = pl.ds(pl.multiple_of(rank * width, LANES), width)
    tapx_out[...] = jnp.zeros_like(tapx_out)
    tapbc_out[...] = jnp.zeros_like(tapbc_out)
    tapx_out[0:4], tapx_out[4:5] = taps_in[:, own], bias_in[:, own]
    tapbc_out[0:4], tapbc_out[4:5] = taps_in[:, inner:], bias_in[:, inner:]
    gain_out[...] = jnp.broadcast_to(gain_in[:, own], gain_out.shape)
    row = lax.broadcasted_iota(jnp.int32, spread_out.shape, 0)
    col = lax.broadcasted_iota(jnp.int32, spread_out.shape, 1)
    half = LANES // 2
    folded = jnp.where(row >= half, row - half, row)
    start = folded * WIDTH
    spread_out[...] = ((col >= start) & (col < start + WIDTH)).astype(bf16)
    row = lax.broadcasted_iota(jnp.int32, (LANES, LANES), 0)
    col = lax.broadcasted_iota(jnp.int32, (LANES, LANES), 1)
    lane = jnp.where(col >= half, col - half, col)
    picked = exact_mm(
        heads_in[...], ((row == rank * heads + lane) & (lane < heads)).astype(bf16)
    )
    lane = lax.broadcasted_iota(jnp.int32, (1, LANES), 1)
    there = jnp.where(lane >= half, lane - half, lane) < heads
    par_out[...] = jnp.zeros_like(par_out)
    par_out[0:1] = picked[0:1]
    par_out[1:2] = jnp.where(there, -jnp.exp(picked[1:2]), 0.0)
    skip = jnp.where(lane < half, picked[2:3], 0.0)
    skip_out[...] = exact_mm(jnp.broadcast_to(skip, (8, LANES)), spread_out[...])


def project_kernel(
    chips, ranks, heads, res_ref, gain_ref, ws_ref, seg_in, taps_in, bias_in, heads_in, gated_in, wx_own,
    x_ref, st_ref, bc_ref, seg_out, tapx_out, tapbc_out, par_out, skip_out, gain_out, spread_out,
    normed_out, wx_out, own, normed, wx, *sems
):
    greet(chips, ranks)
    line = LineGather(wx_own, wx, *sems[:3], chips)
    tensor = TensorGather(own, normed, *sems[3:6], ranks)
    line.step(0)
    gain = gain_ref[...]

    def norm(at):
        v = res_ref[at].astype(f32)
        scaling = lax.rsqrt(jnp.mean(v * v, axis=1, keepdims=True) + epsilon)
        own[at] = (v * scaling * gain).astype(bf16)

    row_loop(own.shape[0], 32, norm)
    tensor.step(0)
    prepare(
        line.rank, heads, seg_in, taps_in, bias_in, heads_in, gated_in,
        seg_out, tapx_out, tapbc_out, par_out, skip_out, gain_out, spread_out,
    )
    line.step(1)
    tensor.step(1)
    if chips > 2:
        line.step(2)
    tokens, width = x_ref.shape
    deep, some = 2 * line.rows, own.shape[0]

    def states(blocks):
        for r in blocks:
            at = pl.ds(pl.multiple_of(r * some, some), some)
            bc_ref[at] = mm(normed[at], ws_ref[...])

    def use(first, blocks, chip):
        ks = pl.ds(pl.multiple_of(chip * deep, deep), deep)
        for r in blocks:
            at = pl.ds(pl.multiple_of(r * some, some), some)
            left = normed[at, ks]
            x, st = mm(left, wx[ks, :width]), mm(left, wx[ks, width:])
            if first:
                x_ref[at], st_ref[at] = x, st
            else:
                x_ref[at] += x
                st_ref[at] += st

    every = list(range(ranks))
    early, late = tensor.near_rows() if ranks == 4 else ([], every)
    for k in (0, 1):
        line.arrive(k, functools.partial(use, k == 0, early))
    states(early)
    tensor.finish()
    keep_normed = pltpu.make_async_copy(normed, normed_out, sems[6])
    keep_normed.start()
    for k in (0, 1):
        line.each(k, functools.partial(use, k == 0, late))
    states(late)
    for k in range(2, chips):
        if k + 1 < chips:
            line.step(k + 1)
        line.arrive(k, functools.partial(use, False, every))
    keep_wx = pltpu.make_async_copy(wx, wx_out, sems[7])
    keep_wx.start()
    line.sent()
    keep_normed.wait()
    keep_wx.wait()


def project(
    number, chips, ranks, heads, residual, norm_gain, ws, segments, taps, bias, by_head, gated_gain, wx_own
):
    rows, model = residual.shape
    tokens, width = rows * ranks, wx_own.shape[1]
    inner = width - LANES
    return pl.pallas_call(
        functools.partial(project_kernel, chips, ranks, heads),
        in_specs=[ONCHIP] * 8 + [ANY],
        out_specs=[ONCHIP] * 10 + [ANY, ANY],
        out_shape=[
            shaped((tokens, inner), f32), shaped((tokens, LANES), f32),
            shaped((tokens, ws.shape[1]), f32),
            shaped((tokens, LANES), jnp.int32), shaped((8, inner), f32), shaped((8, ws.shape[1]), f32),
            shaped((8, LANES), f32), shaped((8, inner), f32), shaped((8, inner), f32),
            shaped((LANES, inner), bf16),
            shaped((tokens, model), bf16), shaped((model, width), bf16),
        ],
        scratch_shapes=[
            pltpu.VMEM((rows, model), bf16), pltpu.VMEM((tokens, model), bf16),
            pltpu.VMEM((model, width), bf16),
            *LineGather.scratch(chips), *TensorGather.scratch(ranks), dma(), dma(),
        ],
        compiler_params=params(number),
        name="project",
    )(residual, norm_gain, ws, segments, taps, bias, by_head, gated_gain, wx_own)


def scan_gather_kernel(blocks, total, chips, ranks, *refs):
    own, (wz_own, cot_own) = refs[:9], refs[9:11]
    outs, (wz_out, cot_out) = refs[11:15], refs[15:17]
    scratch, sems = refs[17:21], refs[21:]
    now = pl.program_id(0) * blocks + pl.program_id(1)
    line = LineGather(wz_own, wz_out, *sems[:3], chips)
    tensor = TensorGather(cot_own, cot_out, *sems[3:], ranks)

    @pl.when(now == 0)
    def _():
        greet(chips, ranks)
        line.step(0)
        tensor.step(0)

    @pl.when(now == total - 2)
    def _():
        line.step(1)

    scan_fwd_kernel(blocks, *own, *outs, *scratch)

    @pl.when(now == total - 1)
    def _():
        tensor.step(1)
        for k in range(2, chips):
            line.step(k)
        line.finish()
        tensor.finish()


def scan_forward_gather(
    number, chips, ranks, wz_own, cot_own, x, bc, st, seg, tapx, tapbc, par, spread, skip, nseq
):
    tokens, width = x.shape
    n = BLOCK
    blocks = tokens // nseq // n
    at = lambda s, i: (s * blocks + i, 0)
    whole = lambda s, i: (0, 0)
    states = LANES
    return pl.pallas_call(
        functools.partial(scan_gather_kernel, blocks, nseq * blocks, chips, ranks),
        grid=(nseq, blocks),
        in_specs=[
            pl.BlockSpec((n, width), at),
            pl.BlockSpec((n, 2 * states), at),
            pl.BlockSpec((n, LANES), at),
            pl.BlockSpec((n, LANES), at),
            pl.BlockSpec(tapx.shape, whole),
            pl.BlockSpec(tapbc.shape, whole),
            pl.BlockSpec(par.shape, whole),
            pl.BlockSpec(spread.shape, whole),
            pl.BlockSpec(skip.shape, whole),
            pl.BlockSpec(wz_own.shape, whole),
            pl.BlockSpec(cot_own.shape, whole),
        ],
        out_specs=[
            pl.BlockSpec((n, width), at), pl.BlockSpec((states, width), at),
            pl.BlockSpec((n, width), at), pl.BlockSpec((n, 2 * states), at), ANY, ANY,
        ],
        out_shape=[
            shaped((tokens, width), f32),
            shaped((tokens // n * states, width), bf16),
            shaped((tokens, width), f32),
            shaped((tokens, 2 * states), f32),
            shaped((wz_own.shape[0] * 2 * chips, width), bf16),
            shaped((tokens, cot_own.shape[1]), bf16),
        ],
        scratch_shapes=[
            pltpu.VMEM((states, width), f32),
            pltpu.VMEM((8, width), f32),
            pltpu.VMEM((8, 2 * states), f32),
            pltpu.VMEM((8, LANES), jnp.int32),
            *LineGather.scratch(chips), *TensorGather.scratch(ranks),
        ],
        compiler_params=params(number),
        name="scan_forward",
    )(x, bc, st, seg, tapx, tapbc, par, spread, skip, wz_own, cot_own)


def lane_sums(v):
    total = v[:, :LANES]
    for i in range(LANES, v.shape[1], LANES):
        total = total + v[:, i : i + LANES]
    return total


def row_sums(picks, v):
    high = v.astype(bf16)
    low = (v - high.astype(f32)).astype(bf16)
    return mm_nt(picks, high) + mm_nt(picks, low)


def gate_kernel(
    chips, ranks, gain_ref, wo_own, normed_in, wz_in, y_in, cot_in,
    gz_ref, gy_ref, ng_ref, ggain_ref, wo_out,
    wo, normed, wz, y, cot, z, gng, squares, dots, columns, land, send, recv, loads, *sems
):
    line = LineGather(wo_own, wo, *sems[:3], chips)
    tokens, width = y.shape
    inner = width * ranks
    rank = line.rank
    load = [
        pltpu.make_async_copy(src, dst, loads.at[i])
        for i, (src, dst) in enumerate(((normed_in, normed), (wz_in, wz), (y_in, y), (cot_in, cot)))
    ]
    greet(chips, ranks)
    line.step(0)
    for copy in load:
        copy.start()
    load[0].wait()
    load[1].wait()

    def gate(at):
        z[at] = mm(normed[at], wz[...])

    row_loop(tokens, CHUNK, gate)
    load[2].wait()

    def square(at):
        zz = z[at]
        gated = y[at] * (zz * sigmoid(zz))
        squares[at] = lane_sums(gated * gated)

    row_loop(tokens, 32, square)
    load[3].wait()
    deep = 2 * line.rows

    def use(first, chip):
        ks = pl.ds(pl.multiple_of(chip * deep, deep), deep)

        def rows(at):
            v = mm(cot[at, ks], wo[ks])
            if first:
                gng[at] = v
            else:
                gng[at] += v

        row_loop(tokens, CHUNK, rows)

    line.arrive(0, functools.partial(use, True))
    for k in range(1, chips):
        line.step(k)
        line.arrive(k, functools.partial(use, False))
    keep = pltpu.make_async_copy(wo, wo_out, loads.at[4])
    keep.start()
    gain = gain_ref[0:1]

    def sums(at):
        zz = z[at]
        dots[at] = lane_sums(gng[at] * gain * (y[at] * (zz * sigmoid(zz))))

    row_loop(tokens, 32, sums)
    half = lax.broadcasted_iota(jnp.int32, (8, LANES), 0) < 4
    one, other = half.astype(bf16), jnp.logical_not(half).astype(bf16)
    for r in range(0, tokens, CHUNK):
        at = slice(r, r + CHUNK)
        land[rank, :, at] = row_sums(one, squares[at]) + row_sums(other, dots[at])
    copies = [
        remote(
            land.at[rank], land.at[rank], send.at[k], recv.at[k], line.me, lax.rem(rank + k, ranks)
        )
        for k in range(1, ranks)
    ]
    for copy in copies:
        copy.start()
    line.sent()
    for copy in copies:
        copy.wait()
    for r in range(0, tokens, LANES):
        at = slice(r, r + LANES)
        total = land[0, :, at]
        for k in range(1, ranks):
            total = total + land[k, :, at]
        columns[at] = jnp.transpose(jnp.concatenate([total] * (LANES // 8), axis=0))
    ggain_ref[...] = jnp.zeros_like(ggain_ref)

    def grads(at):
        zz, yy, gg = z[at], y[at], gng[at]
        sig = sigmoid(zz)
        silu = zz * sig
        gated = yy * silu
        scale = lax.rsqrt(columns[at, 0:1] / inner + epsilon)
        ng_ref[at] = (gated * scale * gain).astype(bf16)
        weight = scale * scale * scale * columns[at, 4:5] / inner
        ggain_ref[...] += fold(gg * gated * scale)
        grad = scale * gain * gg - gated * weight
        gz_ref[at] = (grad * yy * (sig * (1.0 + zz * (1.0 - sig)))).astype(bf16)
        gy_ref[at] = grad * silu

    row_loop(tokens, 32, grads)
    keep.wait()


def gate(number, chips, ranks, gain, wo_own, normed, wz, y, cot):
    tokens, width = y.shape
    model = normed.shape[1]
    return pl.pallas_call(
        functools.partial(gate_kernel, chips, ranks),
        in_specs=[ONCHIP] + [ANY] * 5,
        out_specs=[ONCHIP] * 4 + [ANY],
        out_shape=[
            shaped((tokens, width), bf16), shaped((tokens, width), f32), shaped((tokens, width), bf16),
            shaped((8, width), f32), shaped((model, width), bf16),
        ],
        scratch_shapes=[
            pltpu.VMEM((model, width), bf16), pltpu.VMEM((tokens, model), bf16),
            pltpu.VMEM((model, width), bf16), pltpu.VMEM((tokens, width), f32),
            pltpu.VMEM((tokens, model), bf16), pltpu.VMEM((tokens, width), f32),
            pltpu.VMEM((tokens, width), f32), pltpu.VMEM((tokens, LANES), f32),
            pltpu.VMEM((tokens, LANES), f32), pltpu.VMEM((tokens, LANES), f32),
            pltpu.VMEM((ranks, 8, tokens), f32), dma(ranks), dma(ranks), dma(5),
            *LineGather.scratch(chips),
        ],
        compiler_params=params(number),
        name="gate",
    )(gain, wo_own, normed, wz, y, cot)


class Grads:
    def __init__(self, src, grad, parts, cbuf, csem):
        self.src, self.grad, self.parts, self.cbuf, self.csem = src, grad, parts, cbuf, csem
        self.count = src.shape[1] // CHUNK

    def load(self, j):
        slot = lax.rem(j, 2)
        columns = pl.ds(pl.multiple_of(j * CHUNK, CHUNK), CHUNK)
        return pltpu.make_async_copy(
            self.src.at[:, columns], self.cbuf.at[slot], self.csem.at[slot]
        )

    def begin(self):
        self.load(0).start()

    def run(self):
        @pl.loop(0, self.count)
        def _(j):
            @pl.when(j + 1 < self.count)
            def _():
                self.load(j + 1).start()

            self.load(j).wait()
            at = pl.ds(pl.multiple_of(j * CHUNK, CHUNK), CHUNK)
            self.parts[at] = mm_tn(self.cbuf[lax.rem(j, 2)], self.grad[...]).astype(bf16)


class Back:
    def __init__(self, terms, parts, stage, ssem):
        self.terms, self.parts, self.stage, self.ssem = terms, parts, stage, ssem
        self.count = parts.shape[1] // CHUNK

    def loads(self, j):
        slot = lax.rem(j, 2)
        return [
            pltpu.make_async_copy(slab(right, j, CHUNK), buffer.at[slot], sem.at[slot])
            for _, right, buffer, sem in self.terms
        ]

    def store(self, j):
        slot = lax.rem(j, 2)
        columns = pl.ds(pl.multiple_of(j * CHUNK, CHUNK), CHUNK)
        return pltpu.make_async_copy(
            self.stage.at[slot], self.parts.at[:, columns], self.ssem.at[slot]
        )

    def begin(self):
        for copy in self.loads(0):
            copy.start()

    def run(self, between=None):
        count = self.count

        @pl.loop(0, count)
        def _(j):
            slot = lax.rem(j, 2)

            @pl.when(j + 1 < count)
            def _():
                for copy in self.loads(j + 1):
                    copy.start()

            for copy in self.loads(j):
                copy.wait()

            @pl.when(j >= 2)
            def _():
                self.store(j - 2).wait()

            if between is not None:
                pl.when(j == count // 2 + 1)(between)

            for r in range(0, self.parts.shape[0], CHUNK):
                at = slice(r, r + CHUNK)
                total = jnp.zeros((CHUNK, CHUNK), f32)
                for left, _, buffer, _ in self.terms:
                    total = total + mm_nt(left[at], buffer[slot])
                self.stage[slot, at] = total.astype(bf16)
            self.store(j).start()

        for j in (count - 2, count - 1):
            self.store(j).wait()


def everyone(buffer, mine, count, send, recv, device):
    row = buffer.at[mine]
    return [
        remote(row, row, send.at[k], recv.at[k], *device(lax.rem(mine + k, count)))
        for k in range(1, count)
    ]


def added(buffer, count):
    total = buffer[0]
    for k in range(1, count):
        total = total + buffer[k]
    return total


def backward_kernel(blocks, total, chips, ranks, *refs):
    ins, refs = refs[:15], refs[15:]
    (ggain_ref, gain_ref), refs = refs[:2], refs[2:]
    (res_in, cot_own_in, ws_in, gz_in, ng_in, normed_in, cot_in, wo_in, wz_in, wx_in), refs = refs[:10], refs[10:]
    (sums_ref, norm_ref), refs = refs[:2], refs[2:]
    (z_sum, o_sum, x_sum, block_out, res_grad, state_out), refs = refs[:6], refs[6:]
    (tparts, pparts, pland, tland), refs = refs[:4], refs[4:]
    scratch, refs = refs[:11], refs[11:]
    (gxs, gbc_own, gtapx, gtapbc, gpar, gz, ng, cbuf, parts, back, wbuf, xbuf), refs = refs[:12], refs[12:]
    (gbc_slots, sbuf, wide_out, line_out, sparts, state_f, state_g), refs = refs[:7], refs[7:]
    (state_own, state_line, state_low, land_core, land_chip, land_rank), refs = refs[:6], refs[6:]
    (norm_rank, norm_dp, norm_acc), refs = refs[:3], refs[3:]
    (loads, csem, bsem, wsem, xsem, ysem, osem, fsem), refs = refs[:8], refs[8:]
    (psem, qsem, rsem, nsem, msem), refs = refs[:5], refs[5:]
    half_parts = parts.at[:, pl.ds(0, gz.shape[1])]
    z_job = LineScatter(half_parts, *refs[:4], chips)
    o_job = LineScatter(half_parts, *refs[4:8], chips)
    x_job = LineScatter(parts, *refs[8:12], chips)
    s_job = SmallScatter(sparts, *refs[12:16], chips)
    refs = refs[16:]
    around = TensorGather(gbc_own, gbc_slots, *refs[:3], ranks)
    s_line = SmallGather(state_own, state_line, *refs[3:5], chips)
    state_all = gbc_slots.at[pl.ds(gz.shape[0], normed_in.shape[1])]
    s_rank = TensorGather(state_low, state_all, *refs[5:8], ranks)
    temp, refs = refs[8], refs[9:]
    if ranks == 4:
        first = HalvesScatter(pparts, refs[0], temp, *refs[1:4])
        second = HalvesScatter(tparts, refs[4], temp, *refs[5:8])
    else:
        first = DirectScatter(pparts, pland, temp, *refs[:3], ranks)
        second = DirectScatter(tparts, tland, temp, *refs[3:6], ranks)
    now = pl.program_id(0) * blocks + pl.program_id(1)
    tokens, width = gz.shape
    model = normed_in.shape[1]
    rank, me, devices = first.rank, first.me, 2 * chips
    chip, core = z_job.chip, z_job.core
    over_dp = lambda d: (d, rank)
    over_rank = lambda r: (me, r)
    by_core = everyone(land_core, core, 2, psem.at[0], psem.at[1], lambda c: (chip * 2 + c, rank))
    by_chip = everyone(land_chip, chip, chips, qsem.at[0], qsem.at[1], lambda c: (c * 2 + core, rank))
    by_rank = everyone(land_rank, rank, ranks, rsem.at[0], rsem.at[1], over_rank)
    norm_by_rank = everyone(norm_rank, rank, ranks, nsem.at[0], nsem.at[1], over_rank)
    norm_by_dp = everyone(norm_dp, me, devices, msem.at[0], msem.at[1], over_dp)

    def begin(copies):
        for copy in copies:
            copy.start()

    def end(copies):
        for copy in copies:
            copy.wait()
    fetch = [
        pltpu.make_async_copy(src, dst, loads.at[i])
        for i, (src, dst) in enumerate(((gz_in, gz), (ng_in, ng)))
    ]
    pieces = model // width
    own_rows = first.rows

    def piece(ref, p, at):
        return ref[pl.ds(pl.multiple_of(at.start + p * own_rows, 16), at.size)]

    def pieced(ref, at):
        return jnp.concatenate([piece(ref, p, at) for p in range(pieces)], axis=1).astype(f32)

    def own_copies(src, ref, sems):
        return [
            pltpu.make_async_copy(
                src.at[:, pl.ds(p * width, width)], ref.at[pl.ds(p * own_rows, own_rows)], sems.at[p]
            )
            for p in range(pieces)
        ]

    own_res = own_copies(res_in, gz, fsem.at[0])
    own_cot = own_copies(cot_own_in, ng, fsem.at[1])
    half_out = line_out.at[:, pl.ds(0, width)]
    keep_z = pltpu.make_async_copy(half_out, z_sum, osem.at[0])
    keep_o = pltpu.make_async_copy(half_out, o_sum, osem.at[0])
    keep_x = pltpu.make_async_copy(line_out, x_sum, osem.at[0])
    keep_block = pltpu.make_async_copy(wide_out, block_out, osem.at[2])
    keep_grad = pltpu.make_async_copy(wide_out, res_grad, osem.at[2])

    z_part = Grads(normed_in, gz, half_parts, cbuf, csem)
    o_part = Grads(cot_in, ng, half_parts, cbuf, csem)
    x_part = Grads(normed_in, gxs, parts, cbuf, csem)
    out_part = Back([(ng, wo_in, wbuf, wsem)], pparts, back, bsem)
    in_part = Back(
        [(gz, wz_in, wbuf, wsem), (gxs, wx_in, xbuf, xsem), (gbc_own, ws_in, sbuf, ysem)],
        tparts, back, bsem,
    )

    @pl.when(now == 0)
    def _():
        z_part.begin()
        for copy in fetch:
            copy.start()
        out_part.begin()
        greet_all(chips, ranks)
        fetch[0].wait()
        z_part.run()
        z_job.step(0)
        fetch[1].wait()
        o_part.begin()
        out_part.run(lambda: z_job.step(1))
        first.step(0, 0)
        first.step(0, 1)

    early = [k for k in range(2, chips) if 2 * k - 2 < total - 1]

    @pl.when(now == 1)
    def _():
        o_part.run()
        o_job.step(0)

    for k in early:
        @pl.when(now == 2 * k - 2)
        def _():
            z_job.step(k)

    @pl.when(now == 3)
    def _():
        o_job.step(1)

    @pl.when(now == 5)
    def _():
        first.step(1, 0)
        first.step(1, 1)

    @pl.when(now == total - 1)
    def _():
        x_part.begin()
        in_part.begin()

    row = pl.multiple_of(
        (pl.program_id(0) * blocks + blocks - 1 - pl.program_id(1)) * BLOCK, BLOCK
    )
    here = pl.ds(row, BLOCK)
    outs = (
        gxs.at[here, pl.ds(0, width)], gbc_own.at[here], gxs.at[here, pl.ds(width, LANES)],
        gtapx, gtapbc, gpar,
    )
    scan_bwd_kernel(blocks, *ins, *outs, *scratch)

    @pl.when(now == total - 1)
    def _():
        around.step(0)
        begin(own_cot)
        pack = land_core.at[core]
        pack[...] = jnp.zeros(land_core.shape[1:], f32)
        for k in range(5):
            rows = slice(8 * k, 8 * k + 8)
            pack[k : k + 1, :width] = jnp.sum(gtapx[rows], axis=0, keepdims=True)
            pack[k : k + 1, width:] = jnp.sum(gtapbc[rows], axis=0, keepdims=True)
        pack[5:6, :width] = jnp.sum(ggain_ref[...], axis=0, keepdims=True)
        for k in range(3):
            pack[6:7, k * LANES : (k + 1) * LANES] = jnp.sum(
                gpar[8 * k : 8 * k + 8], axis=0, keepdims=True
            )
        begin(by_core)
        x_part.run()
        x_job.step(0)
        end(by_core)
        land_chip[chip] = added(land_core, 2)
        begin(by_chip)
        depth = sparts.shape[0]

        def own_columns(i):
            columns = pl.ds(pl.multiple_of(rank * depth + i * CHUNK, CHUNK), CHUNK)
            return pltpu.make_async_copy(normed_in.at[:, columns], cbuf.at[i], csem.at[i])

        for i in range(depth // CHUNK):
            own_columns(i).start()
        for k in range(2, chips):
            if k not in early:
                z_job.step(k)
        if chips > 2:
            o_job.step(2)
        around.step(1)

        def between():
            second.step(0, 0)
            around.finish()

            def add(at):
                total = gbc_slots[at].astype(f32)
                for r in range(1, ranks):
                    there = pl.ds(pl.multiple_of(at.start + r * tokens, 128), at.size)
                    total = total + gbc_slots[there].astype(f32)
                gbc_slots[at] = total.astype(bf16)

            row_loop(tokens, 128, add)
            for i in range(depth // CHUNK):
                own_columns(i).wait()
                sparts[i * CHUNK : (i + 1) * CHUNK] = mm_tn(cbuf[i], gbc_slots[:tokens]).astype(
                    sparts.dtype
                )
            s_job.step(0)
            for k in range(3, chips):
                o_job.step(k)
            s_job.step(1)
            x_job.step(1, True)

        in_part.run(between)
        second.step(0, 1)
        begin(own_res)
        s_job.finish(state_own)
        s_line.step(0)
        x_job.send_rest()
        z_job.finish(half_out)
        keep_z.start()
        first.arrive()
        end(own_res)

        def plus(at, total):
            wide_out[at] = pieced(gz, at) + total

        first.totals(32, plus)
        keep_block.start()
        second.step(1, 0)
        end(by_chip)
        land_rank[rank] = added(land_chip, chips)
        begin(by_rank)
        keep_z.wait()
        o_job.finish(half_out)
        keep_o.start()
        s_line.step(1)
        s_line.finish()

        def lower(at):
            state_low[at] = state_line[at].astype(bf16)

        row_loop(depth, 64, lower)
        end(by_rank)
        s_rank.step(0)
        shared = land_rank[0, :, width:]
        for r in range(1, ranks):
            shared = shared + land_rank[r, :, width:]
        for r in range(ranks):
            sums_ref[:, r * width : (r + 1) * width] = land_rank[r, :, :width]
        sums_ref[:, ranks * width :] = shared
        if chips > 2:
            x_job.step(2)
        second.step(1, 1)
        s_rank.step(1)
        for k in range(3, chips):
            x_job.step(k)
        keep_block.wait()
        end(own_cot)
        second.arrive()
        norm_acc[...] = jnp.zeros_like(norm_acc)
        gain = gain_ref[...]

        def last(at, grad):
            v = pieced(gz, at)
            scaling = lax.rsqrt(jnp.mean(v * v, axis=1, keepdims=True) + epsilon)
            norm_acc[...] += fold(grad * v * scaling)
            grad = grad * gain
            along = jnp.sum(grad * v, axis=1, keepdims=True)
            weight = scaling * scaling * scaling * along / model
            wide_out[at] = pieced(ng, at) + scaling * grad - v * weight

        second.totals(32, last)
        keep_grad.start()
        line = jnp.sum(norm_acc[...], axis=0, keepdims=True)
        eighth = model // 8
        for i in range(8):
            norm_rank[rank, i : i + 1, :] = line[:, i * eighth : (i + 1) * eighth]
        begin(norm_by_rank)
        s_rank.finish()
        buffers = (state_f, state_g)
        stored = []
        some = depth // 2
        for r in range(2 * ranks):
            if r >= 2:
                stored[r - 2].wait()

            def state(at):
                low = pl.ds(pl.multiple_of(at.start + r * some, 64), at.size)
                buffers[r % 2][at] = state_all[low].astype(f32)

            row_loop(some, 64, state)
            copy = pltpu.make_async_copy(
                buffers[r % 2], state_out.at[pl.ds(r * some, some)], osem.at[1 + r % 2 * 2]
            )
            copy.start()
            stored.append(copy)
        end(norm_by_rank)
        norm_dp[me] = added(norm_rank, ranks)
        begin(norm_by_dp)
        keep_o.wait()
        x_job.finish(line_out)
        keep_x.start()
        end(stored[-2:])
        end(norm_by_dp)
        norm_ref[...] = added(norm_dp, devices)
        keep_x.wait()
        keep_grad.wait()


def backward(
    number, chips, ranks, ggain, norm_gain, residual, cot_own, ws, gz, ng, normed, cot, wo, wz, wx,
    x, conv, bc, convbc, st, seg, gy, y, h, tapx, tapbc, par, spread, skip, nseq,
):
    tokens, width = x.shape
    rows, model = residual.shape
    n = BLOCK
    blocks = tokens // nseq // n
    at = lambda s, i: (s * blocks + blocks - 1 - i, 0)
    tail = lambda s, i: (jnp.maximum((s * blocks + blocks - 1 - i) * (n // 8) - 1, 0), 0)
    whole = lambda s, i: (0, 0)
    states = LANES
    full = lambda v: pl.BlockSpec(v.shape, whole)
    once = lambda shape: pl.BlockSpec(shape, whole)
    devices = 2 * chips
    own, depth, wide = model // devices, model // ranks, width + 2 * states
    kind = bf16 if depth // devices % 16 == 0 else f32
    return pl.pallas_call(
        functools.partial(backward_kernel, blocks, nseq * blocks, chips, ranks),
        grid=(nseq, blocks),
        in_specs=[
            pl.BlockSpec((n, width), at),
            pl.BlockSpec((n, width), at),
            pl.BlockSpec((n, 2 * states), at),
            pl.BlockSpec((n, 2 * states), at),
            pl.BlockSpec((n, LANES), at),
            pl.BlockSpec((n, LANES), at),
            pl.BlockSpec((8, LANES), tail),
            pl.BlockSpec((n, width), at),
            pl.BlockSpec((n, width), at),
            pl.BlockSpec((states, width), at),
            full(tapx), full(tapbc), full(par), full(spread), full(skip), full(ggain), full(norm_gain),
        ]
        + [ANY] * 10,
        out_specs=[
            once((8, width * ranks + 2 * states)), once((8, model // 8)),
        ]
        + [ANY] * 10,
        out_shape=[
            shaped((8, width * ranks + 2 * states), f32), shaped((8, model // 8), f32),
            shaped((own, width), f32), shaped((own, width), f32), shaped((own, width + LANES), f32),
            shaped((rows, model), f32), shaped((rows, model), f32), shaped((model, 2 * states), f32),
            shaped((tokens, model), bf16), shaped((tokens, model), bf16),
            *[shaped((ranks, rows, model) if ranks != 4 else (8, LANES), bf16)] * 2,
        ],
        scratch_shapes=[
            *scan_bwd_scratch(width, states),
            pltpu.VMEM((tokens, width + LANES), bf16),
            pltpu.VMEM((tokens, 2 * states), bf16),
            pltpu.VMEM((40, width), f32),
            pltpu.VMEM((40, 2 * states), f32),
            pltpu.VMEM((24, LANES), f32),
            pltpu.VMEM((tokens, width), bf16),
            pltpu.VMEM((tokens, width), bf16),
            pltpu.VMEM((2, tokens, CHUNK), bf16),
            pltpu.VMEM((model, width + LANES), bf16),
            pltpu.VMEM((2, tokens, CHUNK), bf16),
            pltpu.VMEM((2, CHUNK, width), bf16),
            pltpu.VMEM((2, CHUNK, width + LANES), bf16),
            pltpu.VMEM((ranks * tokens, 2 * states), bf16),
            pltpu.VMEM((2, CHUNK, 2 * states), bf16),
            pltpu.VMEM((rows, model), f32),
            pltpu.VMEM((own, width + LANES), f32),
            pltpu.VMEM((depth, 2 * states), kind),
            pltpu.VMEM((depth // 2, 2 * states), f32),
            pltpu.VMEM((depth // 2, 2 * states), f32),
            pltpu.VMEM((depth // devices, 2 * states), kind),
            pltpu.VMEM((depth, 2 * states), kind),
            pltpu.VMEM((depth, 2 * states), bf16),
            pltpu.VMEM((2, 8, wide), f32),
            pltpu.VMEM((chips, 8, wide), f32),
            pltpu.VMEM((ranks, 8, wide), f32),
            pltpu.VMEM((ranks, 8, model // 8), f32),
            pltpu.VMEM((devices, 8, model // 8), f32),
            pltpu.VMEM((8, model), f32),
            dma(2), *[dma(2)] * 5, dma(4), pltpu.SemaphoreType.DMA((2, model // width)),
            *[pltpu.SemaphoreType.DMA((2, n)) for n in (2, chips, ranks, ranks, devices)],
            *LineScatter.scratch(chips, (model, width)),
            *LineScatter.scratch(chips, (model, width)),
            *LineScatter.scratch(chips, (model, width + LANES)),
            *SmallScatter.scratch(chips, (depth, 2 * states), kind),
            *TensorGather.scratch(ranks), *SmallGather.scratch(chips), *TensorGather.scratch(ranks),
            HalvesScatter.temp((tokens, model)) if ranks == 4 else pltpu.VMEM((2, rows // 2, model), bf16),
            *(HalvesScatter.scratch((tokens, model)) if ranks == 4 else DirectScatter.scratch(ranks)) * 2,
        ],
        compiler_params=params(number),
        name="backward",
    )(
        x, conv, bc, convbc, st, seg, seg, gy, y, h, tapx, tapbc, par, spread, skip, ggain, norm_gain,
        residual, cot_own, ws, gz, ng, normed, cot, wo, wz, wx,
    )


def emit_kernel(
    ranks, heads, sums_ref, norm_ref, z_ref, x_ref, o_ref, block_in, res_in, state_in,
    inner_ref, step_ref, out_ref, taps_ref, bias_ref, gated_ref, norm_out, a_ref, b_ref, c_ref,
    block_out, res_out, state_out, block, res, state, sems
):
    moves = [
        (
            pltpu.make_async_copy(src, held, sems.at[0, i]),
            pltpu.make_async_copy(held, dst, sems.at[1, i]),
        )
        for i, (src, held, dst) in enumerate(
            ((block_in, block, block_out), (res_in, res, res_out), (state_in, state, state_out))
        )
    ]
    for come, _ in moves:
        come.start()
    width, inner = z_ref.shape[1], gated_ref.shape[0]
    row = lax.broadcasted_iota(jnp.int32, (LANES, LANES), 0)
    col = lax.broadcasted_iota(jnp.int32, (LANES, LANES), 1)
    total = jnp.zeros((8, LANES), f32)
    for r in range(ranks):
        line = [sums_ref[6:7, r * width + k * LANES : r * width + (k + 1) * LANES] for k in range(3)]
        picks = ((col == r * heads + row) & (row < heads)).astype(bf16)
        total = total + exact_mm(
            jnp.concatenate(line + [jnp.zeros((5, LANES), f32)], axis=0), picks
        )
    for k, ref in enumerate((a_ref, b_ref, c_ref)):
        ref[...] = total[k, : ranks * heads]
    taps_ref[...] = sums_ref[0:4]
    bias_ref[...] = sums_ref[4]
    gated_ref[...] = sums_ref[5, :inner]
    eighth = norm_ref.shape[1]
    for i in range(8):
        norm_out[i * eighth : (i + 1) * eighth] = norm_ref[i]
    step_ref[...] = x_ref[:, width : width + heads]
    for come, go in moves:
        come.wait()
        go.start()
    inner_ref[:, 0, :] = z_ref[...]
    inner_ref[:, 1, :] = x_ref[:, :width]
    out_ref[...] = jnp.transpose(o_ref[...])
    for _, go in moves:
        go.wait()


def emit(ranks, heads, sums, norm, z, x, o, block, res, state):
    own, width = z.shape
    inner = width * ranks
    vector = lambda n: shaped((n,), f32)
    return pl.pallas_call(
        functools.partial(emit_kernel, ranks, heads),
        in_specs=[ONCHIP] * 5 + [ANY] * 3,
        out_specs=[ONCHIP] * 10 + [ANY] * 3,
        out_shape=[
            shaped((own, 2, width), f32), shaped((own, heads), f32), shaped((width, own), f32),
            shaped((4, sums.shape[1]), f32), vector(sums.shape[1]), vector(inner),
            vector(norm.size), *[vector(ranks * heads)] * 3,
            shaped(block.shape, f32), shaped(res.shape, f32), shaped(state.shape, f32),
        ],
        scratch_shapes=[
            pltpu.VMEM(block.shape, f32), pltpu.VMEM(res.shape, f32), pltpu.VMEM(state.shape, f32),
            pltpu.SemaphoreType.DMA((2, 3)),
        ],
        compiler_params=pltpu.CompilerParams(vmem_limit_bytes=VMEM_BYTES),
        name="emit",
    )(sums, norm, z, x, o, block, res, state)


def per_device(
    residual, segment_ids, norm_gain, inner_weight, state_weight, step_weight, conv_weight,
    conv_bias, step_bias, decay_log, skip_gain, gated_gain, out_weight, cotangent,
):
    chips, ranks = lax.axis_size("dp") // 2, lax.axis_size("tensor")
    width = inner_weight.shape[2]
    heads = step_weight.shape[1]
    inner_width = gated_gain.shape[0]
    nseq = segment_ids.shape[0]
    wx_own = jnp.concatenate([inner_weight[:, 1], on_lanes(step_weight)], axis=1)
    by_head = jnp.stack([step_bias, decay_log, skip_gain])
    by_head = jnp.pad(by_head, ((0, 5), (0, LANES - by_head.shape[1])))
    x, st, bc, seg, tapx, tapbc, par, skip, gain, spread, normed, wx = project(
        1, chips, ranks, heads, residual, norm_gain[None], state_weight, segment_ids,
        conv_weight, conv_bias[None], by_head, gated_gain[None], wx_own,
    )
    y, h, conv, convbc, wz, cot = scan_forward_gather(
        2, chips, ranks, inner_weight[:, 0], cotangent,
        x, bc, st, seg, tapx, tapbc, par, spread, skip, nseq,
    )
    gz, gy, ng, ggain, wo = gate(3, chips, ranks, gain, out_weight.T, normed, wz, y, cot)
    sums, norm_grad, z_grad, out_grad, x_grad, block_out, residual_grad, state_grad, *_ = backward(
        4, chips, ranks, ggain, norm_gain[None], residual, cotangent, state_weight,
        gz, ng, normed, cot, wo, wz, wx,
        x, conv, bc, convbc, st, seg, gy, y, h, tapx, tapbc, par, spread, skip, nseq,
    )
    (
        inner_grad, step_grad, out_grad, tap_grad, bias_grad, gated_grad, norm_grad,
        step_bias_grad, decay_grad, skip_grad, block_out, residual_grad, state_grad,
    ) = emit(
        ranks, heads, sums, norm_grad, z_grad, x_grad, out_grad, block_out, residual_grad, state_grad
    )
    return (
        block_out, residual_grad, norm_grad, inner_grad, state_grad, step_grad, tap_grad, bias_grad,
        step_bias_grad, decay_grad, skip_grad, gated_grad, out_grad,
    )


def solution(mesh):
    rows, both = P("dp", "tensor"), P(("dp", "tensor"), None)
    inner, out = P("dp", None, "tensor"), P("tensor", "dp")
    return jax.shard_map(
        per_device,
        mesh=mesh,
        in_specs=(
            both, P("dp", None), P(), inner, P(), rows, P(), P(), P(), P(), P(), P(), out, both,
        ),
        out_specs=(both, both, P(), inner, P(), rows, P(), P(), P(), P(), P(), P(), out),
        check_vma=False,
    )
```

```python
import functools
import jax
import jax.numpy as jnp
from jax import lax
from jax.experimental import pallas as pl
from jax.experimental.pallas import tpu as pltpu
from jax.sharding import PartitionSpec as P

LANES = 128
BLOCK = 128
WIDTH = 64
VMEM_BYTES = 60 * 1024 * 1024
f32, bf16 = jnp.float32, jnp.bfloat16
ROWS0 = (((0,), (0,)), ((), ()))
COLS1 = (((1,), (1,)), ((), ()))


def mm(a, b):
    return jnp.dot(a, b, preferred_element_type=f32)


def mm_tn(a, b):
    return lax.dot_general(a, b, ROWS0, preferred_element_type=f32)


def mm_nt(a, b):
    return lax.dot_general(a, b, COLS1, preferred_element_type=f32)


def sigmoid(v):
    return 0.5 + 0.5 * jnp.tanh(0.5 * v)


def two_parts(v, low_lanes):
    high = v.astype(bf16)
    return jnp.where(low_lanes, (v - high.astype(f32)).astype(bf16), high)


def head_sums(v, spread):
    high = v.astype(bf16)
    low = (v - high.astype(f32)).astype(bf16)
    return mm_nt(high, spread) + mm_nt(low, spread)


def shifted_masks(seg_ext, seg):
    n = seg.shape[0]
    return [None] + [seg_ext[8 - k : 8 - k + n] == seg for k in (1, 2, 3)]


def convolve(tail, part, masks, taps):
    n = part.shape[0]
    ext = jnp.concatenate([tail, part], axis=0)
    total = taps[4:5] + taps[3:4] * part
    for k in (1, 2, 3):
        total = total + taps[3 - k : 4 - k] * jnp.where(masks[k], ext[8 - k : 8 - k + n], 0.0)
    return total


def wide(v):
    return jnp.concatenate([v, v], axis=1)


def step_state(raw, params, seg, prev_seg, end_seg, n):
    row = lax.broadcasted_iota(jnp.int32, (n, n), 0)
    col = lax.broadcasted_iota(jnp.int32, (n, n), 1)
    v = raw + params[0:1]
    dt = jnp.maximum(v, 0.0) + jnp.log1p(jnp.exp(-jnp.abs(v)))
    a = params[1:2]
    cum = jnp.dot(
        (row >= col).astype(f32), dt * a, precision=lax.Precision.HIGHEST, preferred_element_type=f32
    )
    last = cum[n - 1 : n]
    into = jnp.where(seg == prev_seg, jnp.exp(cum), 0.0)
    onto = jnp.where(seg == end_seg, jnp.exp(last - cum), 0.0)
    through = jnp.where(end_seg == prev_seg, jnp.exp(last), 0.0)
    bias = jnp.where((row >= col) & (seg == jnp.transpose(seg)), 0.0, -1e30)
    return v, dt, a, cum, into, onto, through, bias


def scan_fwd_kernel(
    blocks, x_ref, bc_ref, st_ref, seg_ref, tapx_ref, tapbc_ref, par_ref, spread_ref, skip_ref,
    y_ref, h_ref, conv_ref, convbc_ref, state, tail_x, tail_bc, tail_seg,
):
    n = BLOCK
    block = pl.program_id(1)

    @pl.when(block == 0)
    def _():
        state[...] = jnp.zeros_like(state)
        tail_x[...] = jnp.zeros_like(tail_x)
        tail_bc[...] = jnp.zeros_like(tail_bc)
        tail_seg[...] = jnp.full_like(tail_seg, -1)

    seg = seg_ref[...]
    masks = shifted_masks(jnp.concatenate([tail_seg[...], seg], axis=0), seg)
    prev_seg, end_seg = tail_seg[7:8], seg[n - 1 : n]
    v, dt, a, cum, into, onto, through, bias = step_state(
        st_ref[...], par_ref[...], seg, prev_seg, end_seg, n
    )
    cum_t = jnp.transpose(cum)
    low_lanes = lax.broadcasted_iota(jnp.int32, (n, LANES), 1) >= LANES // 2
    spread = spread_ref[...]
    dt_w = mm(two_parts(dt, low_lanes), spread)
    into_w = mm(two_parts(into, low_lanes), spread)
    onto_w = mm(two_parts(onto, low_lanes), spread)
    through_w = mm(two_parts(jnp.broadcast_to(through, (8, LANES)), low_lanes[:8]), spread)[0:1]
    bc_masks = [None] + [wide(m) for m in masks[1:]]
    conv_bc = convolve(tail_bc[...], bc_ref[...], bc_masks, tapbc_ref[...])
    convbc_ref[...] = conv_bc
    act_bc = conv_bc * sigmoid(conv_bc)
    b, c = act_bc[:, :LANES].astype(bf16), act_bc[:, LANES:].astype(bf16)
    cross = mm_nt(c, b)
    entering = state[...].astype(bf16)
    h_ref[...] = entering
    first_half = lax.broadcasted_iota(jnp.int32, (n, LANES), 1) < WIDTH
    for pair in range(x_ref.shape[1] // LANES):
        sl = slice(pair * LANES, (pair + 1) * LANES)
        conv = convolve(tail_x[:, sl], x_ref[:, sl], masks, tapx_ref[:, sl])
        conv_ref[:, sl] = conv
        xs = conv * sigmoid(conv)
        xd = xs * dt_w[:, sl]
        outside = mm(c, entering[:, sl]) * into_w[:, sl]
        mixes = []
        for h in (2 * pair, 2 * pair + 1):
            decay = jnp.exp(cum[:, h : h + 1] - cum_t[h : h + 1, :] + bias)
            mixes.append((decay * cross).astype(bf16))
        stacked = jnp.concatenate(
            [jnp.where(first_half, xd, 0.0), jnp.where(first_half, 0.0, xd)], axis=0
        ).astype(bf16)
        inside = mm(jnp.concatenate(mixes, axis=1), stacked)
        y_ref[:, sl] = inside + outside + skip_ref[0:1, sl] * xs
        local = mm_tn(b, (onto_w[:, sl] * xd).astype(bf16))
        state[:, sl] = through_w[:, sl] * state[:, sl] + local
    tail_x[...] = x_ref[n - 8 :, :]
    tail_bc[...] = bc_ref[n - 8 :, :]
    tail_seg[...] = seg_ref[n - 8 :, :]


def fold(v):
    total = v[0:8]
    for r in range(8, v.shape[0], 8):
        total = total + v[r : r + 8]
    return total


def scan_bwd_kernel(
    blocks, x_ref, conv_ref, bc_ref, convbc_ref, st_ref, seg_ref, segt_ref, gy_ref, y_ref, h_ref,
    tapx_ref, tapbc_ref, par_ref, spread_ref, skip_ref,
    gx_ref, gbc_ref, gst_ref, gtapx_ref, gtapbc_ref, gpar_ref,
    gstate, head_x, head_bc, head_seg, xs_s, slope_s, back_s, dt_s, onto_s, xd_s, sums_s,
):
    n = BLOCK
    step = pl.program_id(1)
    block = blocks - 1 - step

    @pl.when((step == 0) & (pl.program_id(0) == 0))
    def _():
        gtapx_ref[...] = jnp.zeros_like(gtapx_ref)
        gtapbc_ref[...] = jnp.zeros_like(gtapbc_ref)
        gpar_ref[...] = jnp.zeros_like(gpar_ref)

    @pl.when(step == 0)
    def _():
        gstate[...] = jnp.zeros_like(gstate)
        head_x[...] = jnp.zeros_like(head_x)
        head_bc[...] = jnp.zeros_like(head_bc)
        head_seg[...] = jnp.full_like(head_seg, -1)

    seg = seg_ref[...]
    first = block == 0
    seg_next = jnp.concatenate([seg, head_seg[...]], axis=0)
    ahead = [None] + [seg_next[k : k + n] == seg for k in (1, 2, 3)]
    prev_seg = jnp.where(first, -1, segt_ref[7:8])
    end_seg = seg[n - 1 : n]
    v, dt, a, cum, into, onto, through, bias = step_state(
        st_ref[...], par_ref[...], seg, prev_seg, end_seg, n
    )
    cum_t = jnp.transpose(cum)
    low_lanes = lax.broadcasted_iota(jnp.int32, (n, LANES), 1) >= LANES // 2
    spread = spread_ref[...]
    dt_s[...] = mm(two_parts(dt, low_lanes), spread)
    into_w = mm(two_parts(into, low_lanes), spread)
    onto_s[...] = mm(two_parts(onto, low_lanes), spread)
    through_w = mm(two_parts(jnp.broadcast_to(through, (8, LANES)), low_lanes[:8]), spread)[0:1]
    conv_bc = convbc_ref[...]
    sig_bc = sigmoid(conv_bc)
    act_bc = conv_bc * sig_bc
    b, c = act_bc[:, :LANES].astype(bf16), act_bc[:, LANES:].astype(bf16)
    cross = mm_nt(c, b)
    first_half = lax.broadcasted_iota(jnp.int32, (n, LANES), 1) < WIDTH
    halves = lambda t: jnp.concatenate(
        [jnp.where(first_half, t, 0.0), jnp.where(first_half, 0.0, t)], axis=0
    ).astype(bf16)
    into_s, onto_low = sums_s.at[0:n], sums_s.at[n : 2 * n]
    pairs = [slice(i, i + LANES) for i in range(0, x_ref.shape[1], LANES)]

    for sl in pairs:
        conv = conv_ref[:, sl]
        sig = sigmoid(conv)
        xs = conv * sig
        xs_s[:, sl] = xs
        slope_s[:, sl] = sig + xs * (1.0 - sig)
        xd = xs * dt_s[:, sl]
        xd_s[:, sl] = xd.astype(bf16)
        onto_low[:, sl] = (xd * onto_s[:, sl]).astype(bf16)
        into_s[:, sl] = (gy_ref[:, sl] * into_w[:, sl]).astype(bf16)
    before = h_ref[...]
    gstate_low = gstate[...].astype(bf16)
    gy_into = into_s[...]
    gc = mm_nt(gy_into, before)
    gb = mm_nt(onto_low[...], gstate_low)
    back_s[...] = mm(b, gstate_low)
    edges = 5 * n
    for sl in pairs:
        old = through_w[:, sl] * gstate[:, sl]
        last = fold(old * before[:, sl].astype(f32))
        skips = fold(gy_ref[:, sl] * xs_s[:, sl])
        both = jnp.concatenate([last, skips], axis=0)
        high = both.astype(bf16)
        sums_s[edges : edges + 16, sl] = high
        sums_s[edges + 16 : edges + 32, sl] = (both - high.astype(f32)).astype(bf16)
        gstate[:, sl] = old + mm_tn(c, gy_into[:, sl])
    gcross = jnp.zeros((n, n), f32)
    for pair, sl in enumerate(pairs):
        xs = xs_s[:, sl]
        xd_low = xd_s[:, sl]
        gy = gy_ref[:, sl]
        skip = skip_ref[0:1, sl]
        inner = y_ref[:, sl] - skip * xs
        g_state = onto_s[:, sl] * back_s[:, sl]
        gy_halves = halves(gy)
        gmix = mm_nt(gy_halves, xd_low)
        mixes = []
        for i, h in enumerate((2 * pair, 2 * pair + 1)):
            decay = jnp.exp(cum[:, h : h + 1] - cum_t[h : h + 1, :] + bias)
            mixes.append((decay * cross).astype(bf16))
            gcross = gcross + decay * gmix[i * n : (i + 1) * n]
        gxd = mm_tn(jnp.concatenate(mixes, axis=0), gy_halves) + g_state
        xd_r, gy_r = xd_low.astype(f32), gy.astype(bf16).astype(f32)
        q = gy_r * inner - xd_r * gxd
        high = q.astype(bf16)
        sums_s[0:n, sl] = high
        sums_s[n : 2 * n, sl] = (q - high.astype(f32)).astype(bf16)
        q = xd_r * g_state
        high = q.astype(bf16)
        sums_s[2 * n : 3 * n, sl] = high
        sums_s[3 * n : 4 * n, sl] = (q - high.astype(f32)).astype(bf16)
        sums_s[4 * n : 5 * n, sl] = (xs * gxd).astype(bf16)
        gconv = (dt_s[:, sl] * gxd + skip * gy) * slope_s[:, sl]
        taps = tapx_ref[:, sl]
        part = x_ref[:, sl]
        ext = jnp.concatenate([gconv, head_x[:, sl]], axis=0)
        gu = taps[3:4] * gconv
        gtapx_ref[24:32, sl] += fold(gconv * part)
        for k in (1, 2, 3):
            later = jnp.where(ahead[k], ext[k : k + n], 0.0)
            gu = gu + taps[3 - k : 4 - k] * later
            gtapx_ref[8 * (3 - k) : 8 * (4 - k), sl] += fold(later * part)
        gx_ref[:, sl] = gu.astype(bf16)
        gtapx_ref[32:40, sl] += fold(gconv)
        head_x[:, sl] = gconv[0:8]
    sums = mm_nt(sums_s[...], spread)
    sum_q = sums[0:n] + sums[n : 2 * n]
    sum_state = sums[2 * n : 3 * n] + sums[3 * n : 4 * n]
    sum_dt = sums[4 * n : 5 * n]
    sum_last = sums[edges : edges + 8] + sums[edges + 16 : edges + 24]
    sum_skip = sums[edges + 8 : edges + 16] + sums[edges + 24 : edges + 32]
    gcross_low = gcross.astype(bf16)
    gc = gc + mm(gcross_low, b)
    gb = gb + mm_tn(gcross_low, c)
    gconv = jnp.concatenate([gb, gc], axis=1) * (sig_bc + act_bc * (1.0 - sig_bc))
    ext = jnp.concatenate([gconv, head_bc[...]], axis=0)
    taps = tapbc_ref[...]
    part = bc_ref[...]
    gu = taps[3:4] * gconv
    gtapbc_ref[24:32, :] += fold(gconv * part)
    for k in (1, 2, 3):
        later = jnp.where(wide(ahead[k]), ext[k : k + n], 0.0)
        gu = gu + taps[3 - k : 4 - k] * later
        gtapbc_ref[8 * (3 - k) : 8 * (4 - k), :] += fold(later * part)
    gbc_ref[...] = gu.astype(gbc_ref.dtype)
    gtapbc_ref[32:40, :] += fold(gconv)
    head_bc[...] = gconv[0:8]
    head_seg[...] = seg[0:8]
    rows = lax.broadcasted_iota(jnp.int32, (n, n), 0)
    cols = lax.broadcasted_iota(jnp.int32, (n, n), 1)
    after = jnp.dot(
        (cols >= rows).astype(f32), sum_q, precision=lax.Precision.HIGHEST, preferred_element_type=f32
    )
    edge = jnp.sum(sum_state, axis=0, keepdims=True) + jnp.sum(sum_last, axis=0, keepdims=True)
    glog = after + edge
    gdt = sum_dt + a * glog
    gst = gdt * sigmoid(v)
    gst_ref[...] = jnp.where(low_lanes, 0.0, gst).astype(bf16)
    gpar_ref[0:8] += fold(gst)
    gpar_ref[8:16] += fold(a * dt * glog)
    gpar_ref[16:24] += sum_skip


def scan_bwd_scratch(width, states):
    n = BLOCK
    return [
        pltpu.VMEM((states, width), f32),
        pltpu.VMEM((8, width), f32),
        pltpu.VMEM((8, 2 * states), f32),
        pltpu.VMEM((8, LANES), jnp.int32),
        *[pltpu.VMEM((n, width), f32)] * 5,
        pltpu.VMEM((n, width), bf16),
        pltpu.VMEM((5 * n + 32, width), bf16),
    ]


def on_lanes(v):
    half = jnp.pad(v, [(0, 0)] * (v.ndim - 1) + [(0, LANES // 2 - v.shape[-1])])
    return jnp.concatenate([half, half], axis=-1)


MESH = pl.DeviceIdType.MESH


def place():
    dp, rank = lax.axis_index("dp"), lax.axis_index("tensor")
    return dp // 2, dp % 2, rank


def remote(src, dst, send, recv, dp, rank):
    return pltpu.make_async_remote_copy(
        src_ref=src, dst_ref=dst, send_sem=send, recv_sem=recv, device_id=(dp, rank),
        device_id_type=MESH,
    )


def greet(chips, ranks):
    chip, core, rank = place()
    sem = pltpu.get_barrier_semaphore()
    me = chip * 2 + core

    def signal(dp, r):
        pl.semaphore_signal(sem, inc=1, device_id=(dp, r), device_id_type=MESH)

    signal(chip * 2 + 1 - core, rank)
    for step in (1, -1):
        @pl.when((chip + step >= 0) & (chip + step < chips))
        def _():
            signal(me + 2 * step, rank)
    for k in range(1, ranks):
        signal(me, lax.rem(rank + k, ranks))
    pl.semaphore_wait(sem, ranks + (chip + chips - 1) // chips + (2 * chips - 2 - chip) // chips)


def greet_all(chips, ranks):
    chip, core, rank = place()
    sem = pltpu.get_barrier_semaphore()
    me, devices = chip * 2 + core, 2 * chips
    for k in range(1, devices):
        pl.semaphore_signal(
            sem, inc=1, device_id=(lax.rem(me + k, devices), rank), device_id_type=MESH
        )
    for k in range(1, ranks):
        pl.semaphore_signal(
            sem, inc=1, device_id=(me, lax.rem(rank + k, ranks)), device_id_type=MESH
        )
    pl.semaphore_wait(sem, devices + ranks - 2)


def slab(ref, index, rows):
    return ref.at[pl.ds(pl.multiple_of(index * rows, rows), rows)]


class LineGather:
    def __init__(self, own, slots, send, recv, local, chips):
        self.own, self.slots, self.send, self.recv, self.local = own, slots, send, recv, local
        self.chips, self.rows = chips, own.shape[0]
        self.chip, self.core, self.rank = place()
        self.me = self.chip * 2 + self.core
        self.partner = self.chip * 2 + 1 - self.core
        self.steps = chips

    @staticmethod
    def scratch(chips):
        n = 2 * chips
        return [
            pltpu.SemaphoreType.DMA((3, n)), pltpu.SemaphoreType.DMA((n,)), pltpu.SemaphoreType.DMA,
        ]

    def copy(self, way, origin, src=None):
        target = (self.me + 2, self.me - 2, self.partner)[way]
        slot = slab(self.slots, origin, self.rows)
        return remote(
            slot if src is None else src, slot, self.send.at[way, origin], self.recv.at[origin],
            target, self.rank,
        )

    def pass_on(self, way, origin, src=None, wait=False):
        def go():
            copy = self.copy(way, origin, src)
            copy.wait_send() if wait else copy.start()

        if way == 0:
            pl.when(self.chip + 1 < self.chips)(go)
        elif way == 1:
            pl.when(self.chip > 0)(go)
        else:
            go()

    def keep(self):
        return pltpu.make_async_copy(self.own, slab(self.slots, self.me, self.rows), self.local)

    def sides(self, k):
        return ((0, self.chip - k >= 0, -k), (1, self.chip + k < self.chips, k))

    def step(self, k):
        if k == 0:
            for way in (0, 1, 2):
                self.pass_on(way, self.me, self.own)
            self.keep().start()
            return
        for way, there, shift in self.sides(k):
            @pl.when(there)
            def _():
                origin = self.me + 2 * shift
                self.copy(2, origin).wait_recv()
                self.pass_on(way, origin)
                self.pass_on(2, origin)

    def arrive(self, k, use=None):
        if k == 0:
            self.keep().wait()
            self.copy(2, self.partner).wait_recv()
            if use is not None:
                use(self.chip)
            return
        for way, there, shift in self.sides(k):
            @pl.when(there)
            def _():
                self.copy(2, self.partner + 2 * shift).wait_recv()
                if use is not None:
                    use(self.chip + shift)

    def each(self, k, use):
        if k == 0:
            use(self.chip)
            return
        for way, there, shift in self.sides(k):
            @pl.when(there)
            def _():
                use(self.chip + shift)

    def sent(self):
        for way in (0, 1, 2):
            self.pass_on(way, self.me, self.own, wait=True)
        for k in range(1, self.chips):
            for way, there, shift in self.sides(k):
                @pl.when(there)
                def _():
                    origin = self.me + 2 * shift
                    self.pass_on(way, origin, wait=True)
                    self.pass_on(2, origin, wait=True)

    def finish(self):
        for k in range(self.chips):
            self.arrive(k)
        self.sent()


class TensorGather:
    def __init__(self, own, slots, send, recv, local, ranks):
        self.own, self.slots, self.send, self.recv, self.local = own, slots, send, recv, local
        self.ranks, self.rows = ranks, own.shape[0]
        chip, core, self.rank = place()
        self.me = chip * 2 + core
        self.kept = False

    @staticmethod
    def scratch(ranks):
        return [
            pltpu.SemaphoreType.DMA((ranks,)), pltpu.SemaphoreType.DMA((ranks,)), pltpu.SemaphoreType.DMA,
        ]

    def near(self, k):
        x = self.rank % 2
        y = self.rank // 2
        across = (y * 2 + 1 - x, (1 - y) * 2 + x)
        if k < 2:
            return remote(
                self.own, slab(self.slots, self.rank, self.rows), self.send.at[k], self.recv.at[k],
                self.me, across[k],
            )
        half = slab(self.slots, across[k - 2] * 2 + (k - 2), self.rows // 2)
        return remote(half, half, self.send.at[k], self.recv.at[k], self.me, across[3 - k])

    def direct(self, k):
        return remote(
            self.own, slab(self.slots, self.rank, self.rows), self.send.at[k], self.recv.at[k],
            self.me, lax.rem(self.rank + k, self.ranks),
        )

    def keep(self):
        return pltpu.make_async_copy(self.own, slab(self.slots, self.rank, self.rows), self.local)

    def step(self, k):
        if k == 0:
            if self.ranks == 4:
                self.near(0).start()
                self.near(1).start()
            else:
                for j in range(1, self.ranks):
                    self.direct(j).start()
            self.keep().start()
        elif self.ranks == 4:
            for j in (0, 1):
                self.near(j).wait_recv()
                self.near(2 + j).start()

    def near_rows(self):
        self.keep().wait()
        self.kept = True
        x, y = self.rank % 2, self.rank // 2
        return [self.rank, y * 2 + 1 - x, (1 - y) * 2 + x], [(1 - y) * 2 + 1 - x]

    def finish(self):
        if not self.kept:
            self.keep().wait()
        if self.ranks == 4:
            for j in (0, 1):
                self.near(j).wait_send()
                self.near(2 + j).wait()
        else:
            for j in range(1, self.ranks):
                self.direct(j).wait()


def add_rows(target, others, out=None):
    out = target if out is None else out
    rows = target.shape[0]
    some = 64 if rows % 64 == 0 else rows
    kind = out.dtype if len(others) == 1 else f32

    def add(at):
        total = target[at].astype(kind)
        for other in others:
            total = total + other[at].astype(kind)
        out[at] = total.astype(out.dtype)

    row_loop(rows, some, add)


class LineScatter:
    def __init__(self, parts, swap, flow, send, recv, chips):
        self.parts, self.swap, self.flow = parts, swap, flow
        self.send, self.recv, self.chips = send, recv, chips
        self.rows = parts.shape[0] // (2 * chips)
        self.chip, self.core, self.rank = place()
        self.me = self.chip * 2 + self.core
        self.partner = self.chip * 2 + 1 - self.core

    @staticmethod
    def scratch(chips, shape, dtype=bf16):
        block = (shape[0] // (2 * chips),) + tuple(shape[1:])
        return [
            pltpu.VMEM((chips,) + block, dtype), pltpu.VMEM((chips + 1,) + block, dtype),
            pltpu.SemaphoreType.DMA((3, chips)), pltpu.SemaphoreType.DMA((3, chips)),
        ]

    def order(self):
        n = self.chips
        return [c for k in range(n // 2) for c in (n - 1 - k, k)]

    def over(self, c):
        return remote(
            slab(self.parts, 2 * c + 1 - self.core, self.rows), self.swap.at[c], self.send.at[2, c],
            self.recv.at[2, c], self.partner, self.rank,
        )

    def along(self, way, c, first=False):
        if way == 0:
            here = there = c
        else:
            here, there = c, jnp.where(c == self.chip - 1, self.chips, c)
        src = self.swap.at[c] if first else self.flow.at[here]
        return remote(
            src, self.flow.at[there], self.send.at[way, c], self.recv.at[way, c],
            self.me + (2, -2)[way], self.rank,
        )

    def send_off(self, c):
        n, chip = self.chips, self.chip

        @pl.when((chip == 0) & (c > 0))
        def _():
            self.along(0, c, True).start()

        @pl.when((chip == n - 1) & (c < n - 1))
        def _():
            self.along(1, c, True).start()

    def send_rest(self):
        for c in self.order()[2:]:
            self.send_off(c)

    def step(self, k, hold=False):
        n, chip = self.chips, self.chip
        if k == 0:
            for c in self.order():
                self.over(c).start()
            return
        if k == 1:
            for i, c in enumerate(self.order()):
                self.over(c).wait()
                add_rows(self.swap.at[c], [slab(self.parts, 2 * c + self.core, self.rows)])
                if i < 2 or not hold:
                    self.send_off(c)
            return
        t = k - 1
        c = n - 1 - (t - chip)

        @pl.when((chip > 0) & (t >= chip) & (c > chip))
        def _():
            self.along(0, c).wait_recv()
            add_rows(self.flow.at[c], [self.swap.at[c]])
            self.along(0, c).start()

        d = t - (n - 1 - chip)

        @pl.when((chip < n - 1) & (d >= 0) & (d < chip))
        def _():
            self.along(1, d).wait_recv()
            add_rows(self.flow.at[d], [self.swap.at[d]])
            self.along(1, d).start()

    def finish(self, out):
        n, chip = self.chips, self.chip
        mine, up, down = self.swap.at[chip], self.flow.at[chip], self.flow.at[n]

        @pl.when(chip == 0)
        def _():
            self.along(1, chip).wait_recv()
            add_rows(mine, [down], out)

        @pl.when(chip == n - 1)
        def _():
            self.along(0, chip).wait_recv()
            add_rows(mine, [up], out)

        @pl.when((chip > 0) & (chip < n - 1))
        def _():
            self.along(0, chip).wait_recv()
            self.along(1, chip).wait_recv()
            add_rows(mine, [up, down], out)

        for c in range(n):
            @pl.when((chip < n - 1) & (c > chip))
            def _():
                self.along(0, c).wait_send()

            @pl.when((chip > 0) & (c < chip))
            def _():
                self.along(1, c).wait_send()


class DirectScatter:
    def __init__(self, parts, land, temp, send, recv, tsem, ranks):
        self.parts, self.land, self.temp = parts, land, temp
        self.send, self.recv, self.tsem, self.ranks = send, recv, tsem, ranks
        self.rows = parts.shape[0] // ranks
        chip, core, self.rank = place()
        self.me = chip * 2 + core

    @staticmethod
    def scratch(ranks):
        return [dma(ranks), dma(ranks), dma(2)]

    def copy(self, k):
        to = lax.rem(self.rank + k, self.ranks)
        return remote(
            slab(self.parts, to, self.rows), self.land.at[k], self.send.at[k], self.recv.at[k],
            self.me, to,
        )

    def step(self, k, g):
        if k == 0 and g == 1:
            for j in range(1, self.ranks):
                self.copy(j).start()

    def arrive(self):
        for j in range(1, self.ranks):
            self.copy(j).wait()

    def totals(self, some, body):
        @pl.loop(0, self.rows // some)
        def _(i):
            at = pl.ds(pl.multiple_of(i * some, some), some)
            total = None
            for j in range(self.ranks):
                src = slab(self.parts, self.rank * (self.rows // some) + i, some) if j == 0 else self.land.at[j, at]
                copy = pltpu.make_async_copy(src, self.temp.at[j % 2, pl.ds(0, some)], self.tsem.at[j % 2])
                copy.start()
                copy.wait()
                v = self.temp[j % 2, pl.ds(0, some)].astype(f32)
                total = v if total is None else total + v
            body(at, total)


class SmallScatter:
    def __init__(self, parts, swap, land, send, recv, chips):
        self.parts, self.swap, self.land, self.send, self.recv = parts, swap, land, send, recv
        self.chips, self.rows = chips, parts.shape[0] // (2 * chips)
        self.chip, self.core, self.rank = place()

    @staticmethod
    def scratch(chips, shape, dtype):
        block = pltpu.VMEM((chips, shape[0] // (2 * chips), shape[1]), dtype)
        return [
            block, block, pltpu.SemaphoreType.DMA((2, chips)), pltpu.SemaphoreType.DMA((2, chips)),
        ]

    def over(self, c):
        return remote(
            slab(self.parts, 2 * c + 1 - self.core, self.rows), self.swap.at[c], self.send.at[0, c],
            self.recv.at[0, c], self.chip * 2 + 1 - self.core, self.rank,
        )

    def straight(self, k):
        to = lax.rem(self.chip + k, self.chips)
        return remote(
            self.swap.at[to], self.land.at[self.chip], self.send.at[1, k], self.recv.at[1, k],
            2 * to + self.core, self.rank,
        )

    def step(self, k):
        if k == 0:
            for c in range(self.chips):
                self.over(c).start()
            return
        for c in range(self.chips):
            self.over(c).wait()
            add_rows(self.swap.at[c], [slab(self.parts, 2 * c + self.core, self.rows)])
        for j in range(1, self.chips):
            self.straight(j).start()

    def finish(self, out):
        for j in range(1, self.chips):
            self.straight(j).wait()
        total = self.swap[self.chip].astype(f32)
        for j in range(1, self.chips):
            total = total + self.land[lax.rem(self.chip + j, self.chips)].astype(f32)
        out[...] = total.astype(out.dtype)


class SmallGather:
    def __init__(self, own, slots, send, recv, chips):
        self.own, self.slots, self.send, self.recv = own, slots, send, recv
        self.chips, self.rows = chips, own.shape[0]
        self.chip, self.core, self.rank = place()
        self.me = self.chip * 2 + self.core

    @staticmethod
    def scratch(chips):
        return [pltpu.SemaphoreType.DMA((2, chips)), pltpu.SemaphoreType.DMA((2, chips))]

    def straight(self, k):
        slot = slab(self.slots, self.me, self.rows)
        return remote(
            self.own, slot, self.send.at[0, k], self.recv.at[0, k],
            2 * lax.rem(self.chip + k, self.chips) + self.core, self.rank,
        )

    def over(self, k):
        slot = slab(
            self.slots, 2 * lax.rem(self.chip + self.chips - k, self.chips) + self.core, self.rows
        )
        return remote(
            self.own if k == 0 else slot, slot, self.send.at[1, k], self.recv.at[1, k],
            self.chip * 2 + 1 - self.core, self.rank,
        )

    def step(self, k):
        if k == 0:
            for j in range(1, self.chips):
                self.straight(j).start()
            self.over(0).start()
            self.slots[pl.ds(pl.multiple_of(self.me * self.rows, self.rows), self.rows)] = self.own[...]
            return
        for j in range(1, self.chips):
            self.straight(j).wait_recv()
            self.over(j).start()

    def finish(self):
        for j in range(1, self.chips):
            self.straight(j).wait_send()
        for j in range(self.chips):
            self.over(j).wait()


class HalvesScatter:
    def __init__(self, parts, land, temp, send, recv, tsem):
        self.parts, self.land, self.temp, self.send, self.recv, self.tsem = parts, land, temp, send, recv, tsem
        chip, core, self.rank = place()
        self.me = chip * 2 + core
        self.rows = parts.shape[0] // 4
        self.half, self.wide = self.rows // 2, parts.shape[1] // 2
        x, y = self.rank % 2, self.rank // 2
        self.across = (y * 2 + 1 - x, (1 - y) * 2 + x)
        self.far = (1 - y) * 2 + 1 - x

    @staticmethod
    def scratch(shape):
        return [
            pltpu.VMEM((2, 6, shape[0] // 8, shape[1] // 2), bf16),
            *[pltpu.SemaphoreType.DMA((2, n)) for n in (6, 6, 2)],
        ]

    @staticmethod
    def temp(shape):
        return pltpu.VMEM((2, 2, shape[0] // 8, shape[1] // 2), bf16)

    def part(self, g, owner, way):
        return slab(self.parts.at[:, pl.ds(g * self.wide, self.wide)], owner * 2 + way, self.half)

    def copy(self, g, i):
        if i < 4:
            way = i // 2
            src = self.part(g, self.across[way] if i % 2 == 0 else self.far, way)
            to = self.across[way]
        else:
            way = i - 4
            src, to = self.land.at[g, 2 * way + 1], self.across[1 - way]
        return remote(
            src, self.land.at[g, i], self.send.at[g, i], self.recv.at[g, i], self.me, to
        )

    def fetch(self, g, owner, way):
        return pltpu.make_async_copy(
            self.part(g, owner, way), self.temp.at[g, way], self.tsem.at[g, way]
        )

    def step(self, k, g):
        if k == 0:
            for i in (1, 3, 0, 2):
                self.copy(g, i).start()
            return
        for way in (0, 1):
            self.fetch(g, self.across[1 - way], way).start()
        for way in (0, 1):
            self.copy(g, 2 * way + 1).wait_recv()
            self.fetch(g, self.across[1 - way], way).wait()
            add_rows(self.land.at[g, 2 * way + 1], [self.temp.at[g, way]])
            self.copy(g, 4 + way).start()
        for way in (0, 1):
            self.fetch(g, self.rank, way).start()

    def arrive(self):
        for g in (0, 1):
            for way in (0, 1):
                self.copy(g, 2 * way + 1).wait_send()
                self.copy(g, 2 * way).wait()
                self.copy(g, 4 + way).wait()
                self.fetch(g, self.rank, way).wait()

    def totals(self, some, body):
        for way in (0, 1):
            def add(i):
                at = pl.ds(pl.multiple_of(i * some, some), some)
                total = jnp.concatenate(
                    [
                        self.temp[g, way, at].astype(f32)
                        + self.land[g, 2 * way, at].astype(f32)
                        + self.land[g, 4 + way, at].astype(f32)
                        for g in (0, 1)
                    ],
                    axis=1,
                )
                body(pl.ds(pl.multiple_of(way * self.half + i * some, some), some), total)

            pl.loop(0, self.half // some)(add)


def row_loop(rows, some, body):
    @pl.loop(0, rows // some)
    def _(i):
        body(pl.ds(pl.multiple_of(i * some, some), some))


def params(number):
    return pltpu.CompilerParams(
        collective_id=number, has_side_effects=True, vmem_limit_bytes=VMEM_BYTES
    )


ANY = pl.BlockSpec(memory_space=pl.ANY)
ONCHIP = pl.BlockSpec(memory_space=pltpu.VMEM)


epsilon = 1e-05
CHUNK = 256


def shaped(shape, dtype):
    return jax.ShapeDtypeStruct(shape, dtype)


def dma(count=None):
    return pltpu.SemaphoreType.DMA if count is None else pltpu.SemaphoreType.DMA((count,))


def exact_mm(v, picks):
    high = v.astype(bf16)
    rest = v - high.astype(f32)
    middle = rest.astype(bf16)
    low = (rest - middle.astype(f32)).astype(bf16)
    return mm(high, picks) + mm(middle, picks) + mm(low, picks)


def prepare(
    rank, heads, seg_in, taps_in, bias_in, heads_in, gain_in, wo_in, bias_row, wo_out,
    seg_out, tapx_out, tapbc_out, par_out, skip_out, gain_out, spread_out,
):
    width, inner = tapx_out.shape[1], gain_in.shape[1]
    bias_row[0:1] = bias_in[...][None]
    wo_out[...] = jnp.transpose(wo_in[...].astype(f32)).astype(bf16)
    length = seg_in.shape[1]
    for s in range(seg_in.shape[0]):
        for r in range(0, length, LANES):
            row = jnp.broadcast_to(seg_in[s : s + 1, r : r + LANES], (LANES, LANES))
            at = s * length + r
            seg_out[at : at + LANES] = jnp.transpose(row.astype(f32)).astype(jnp.int32)
    own = pl.ds(pl.multiple_of(rank * width, LANES), width)
    tapx_out[...] = jnp.zeros_like(tapx_out)
    tapbc_out[...] = jnp.zeros_like(tapbc_out)
    tapx_out[0:4], tapx_out[4:5] = taps_in[:, own], bias_row[0:1, own]
    tapbc_out[0:4], tapbc_out[4:5] = taps_in[:, inner:], bias_row[0:1, inner:]
    gain_out[...] = jnp.broadcast_to(gain_in[:, own], gain_out.shape)
    row = lax.broadcasted_iota(jnp.int32, spread_out.shape, 0)
    col = lax.broadcasted_iota(jnp.int32, spread_out.shape, 1)
    half = LANES // 2
    folded = jnp.where(row >= half, row - half, row)
    start = folded * WIDTH
    spread_out[...] = ((col >= start) & (col < start + WIDTH)).astype(bf16)
    row = lax.broadcasted_iota(jnp.int32, (LANES, LANES), 0)
    col = lax.broadcasted_iota(jnp.int32, (LANES, LANES), 1)
    lane = jnp.where(col >= half, col - half, col)
    lines = [ref[...][None] for ref in heads_in]
    lines = jnp.concatenate(lines + [jnp.zeros((5, lines[0].shape[1]), f32)], axis=0)
    if lines.shape[1] < LANES:
        lines = jnp.concatenate([lines, jnp.zeros((8, LANES - lines.shape[1]), f32)], axis=1)
    picked = exact_mm(
        lines, ((row == rank * heads + lane) & (lane < heads)).astype(bf16)
    )
    lane = lax.broadcasted_iota(jnp.int32, (1, LANES), 1)
    there = jnp.where(lane >= half, lane - half, lane) < heads
    par_out[...] = jnp.zeros_like(par_out)
    par_out[0:1] = picked[0:1]
    par_out[1:2] = jnp.where(there, -jnp.exp(picked[1:2]), 0.0)
    skip = jnp.where(lane < half, picked[2:3], 0.0)
    skip_out[...] = exact_mm(jnp.broadcast_to(skip, (8, LANES)), spread_out[...])


def project_kernel(
    chips, ranks, heads, res_ref, gain_ref, ws_ref, seg_in, taps_in, bias_in, a_in, b_in, c_in, gated_in, wo_in,
    wx_own,
    x_ref, st_ref, bc_ref, seg_out, tapx_out, tapbc_out, par_out, skip_out, gain_out, spread_out,
    wo_out, normed_out, wx_out, own, normed, wx, bias_row, *sems
):
    greet(chips, ranks)
    line = LineGather(wx_own, wx, *sems[:3], chips)
    tensor = TensorGather(own, normed, *sems[3:6], ranks)
    line.step(0)
    gain = gain_ref[...]

    def norm(at):
        v = res_ref[at].astype(f32)
        scaling = lax.rsqrt(jnp.mean(v * v, axis=1, keepdims=True) + epsilon)
        own[at] = (v * scaling * gain).astype(bf16)

    row_loop(own.shape[0], 32, norm)
    tensor.step(0)
    prepare(
        line.rank, heads, seg_in, taps_in, bias_in, (a_in, b_in, c_in), gated_in, wo_in, bias_row, wo_out,
        seg_out, tapx_out, tapbc_out, par_out, skip_out, gain_out, spread_out,
    )
    line.step(1)
    tensor.step(1)
    if chips > 2:
        line.step(2)
    tokens, width = x_ref.shape
    deep, some = 2 * line.rows, own.shape[0]

    def states(blocks):
        for r in blocks:
            at = pl.ds(pl.multiple_of(r * some, some), some)
            bc_ref[at] = mm(normed[at], ws_ref[...])

    def use(first, blocks, chip):
        ks = pl.ds(pl.multiple_of(chip * deep, deep), deep)
        for r in blocks:
            at = pl.ds(pl.multiple_of(r * some, some), some)
            left = normed[at, ks]
            x, st = mm(left, wx[ks, :width]), mm(left, wx[ks, width:])
            if first:
                x_ref[at], st_ref[at] = x, st
            else:
                x_ref[at] += x
                st_ref[at] += st

    every = list(range(ranks))
    early, late = tensor.near_rows() if ranks == 4 else ([], every)
    for k in (0, 1):
        line.arrive(k, functools.partial(use, k == 0, early))
    states(early)
    tensor.finish()
    keep_normed = pltpu.make_async_copy(normed, normed_out, sems[6])
    keep_normed.start()
    for k in (0, 1):
        line.each(k, functools.partial(use, k == 0, late))
    states(late)
    for k in range(2, chips):
        if k + 1 < chips:
            line.step(k + 1)
        line.arrive(k, functools.partial(use, False, every))
    keep_wx = pltpu.make_async_copy(wx, wx_out, sems[7])
    keep_wx.start()
    line.sent()
    keep_normed.wait()
    keep_wx.wait()


def project(
    number, chips, ranks, heads, residual, norm_gain, ws, segments, taps, bias, by_head, gated_gain,
    out_weight, wx_own,
):
    rows, model = residual.shape
    tokens, width = rows * ranks, wx_own.shape[1]
    inner = width - LANES
    return pl.pallas_call(
        functools.partial(project_kernel, chips, ranks, heads),
        in_specs=[ONCHIP] * 11 + [ANY],
        out_specs=[ONCHIP] * 11 + [ANY, ANY],
        out_shape=[
            shaped((tokens, inner), f32), shaped((tokens, LANES), f32),
            shaped((tokens, ws.shape[1]), f32),
            shaped((tokens, LANES), jnp.int32), shaped((8, inner), f32), shaped((8, ws.shape[1]), f32),
            shaped((8, LANES), f32), shaped((8, inner), f32), shaped((8, inner), f32),
            shaped((LANES, inner), bf16), shaped(out_weight.shape[::-1], bf16),
            shaped((tokens, model), bf16), shaped((model, width), bf16),
        ],
        scratch_shapes=[
            pltpu.VMEM((rows, model), bf16), pltpu.VMEM((tokens, model), bf16),
            pltpu.VMEM((model, width), bf16), pltpu.VMEM((8, taps.shape[1]), f32),
            *LineGather.scratch(chips), *TensorGather.scratch(ranks), dma(), dma(),
        ],
        compiler_params=params(number),
        name="project",
    )(residual, norm_gain, ws, segments, taps, bias, *by_head, gated_gain, out_weight, wx_own)


def scan_gather_kernel(blocks, total, chips, ranks, *refs):
    own, (wz_own, cot_own) = refs[:9], refs[9:11]
    outs, (wz_out, cot_out) = refs[11:15], refs[15:17]
    scratch, sems = refs[17:21], refs[21:]
    now = pl.program_id(0) * blocks + pl.program_id(1)
    line = LineGather(wz_own, wz_out, *sems[:3], chips)
    tensor = TensorGather(cot_own, cot_out, *sems[3:], ranks)

    @pl.when(now == 0)
    def _():
        greet(chips, ranks)
        line.step(0)
        tensor.step(0)

    @pl.when(now == total - 2)
    def _():
        line.step(1)

    scan_fwd_kernel(blocks, *own, *outs, *scratch)

    @pl.when(now == total - 1)
    def _():
        tensor.step(1)
        for k in range(2, chips):
            line.step(k)
        line.finish()
        tensor.finish()


def scan_forward_gather(
    number, chips, ranks, wz_own, cot_own, x, bc, st, seg, tapx, tapbc, par, spread, skip, nseq
):
    tokens, width = x.shape
    n = BLOCK
    blocks = tokens // nseq // n
    at = lambda s, i: (s * blocks + i, 0)
    whole = lambda s, i: (0, 0)
    states = LANES
    return pl.pallas_call(
        functools.partial(scan_gather_kernel, blocks, nseq * blocks, chips, ranks),
        grid=(nseq, blocks),
        in_specs=[
            pl.BlockSpec((n, width), at),
            pl.BlockSpec((n, 2 * states), at),
            pl.BlockSpec((n, LANES), at),
            pl.BlockSpec((n, LANES), at),
            pl.BlockSpec(tapx.shape, whole),
            pl.BlockSpec(tapbc.shape, whole),
            pl.BlockSpec(par.shape, whole),
            pl.BlockSpec(spread.shape, whole),
            pl.BlockSpec(skip.shape, whole),
            pl.BlockSpec(wz_own.shape, whole),
            pl.BlockSpec(cot_own.shape, whole),
        ],
        out_specs=[
            pl.BlockSpec((n, width), at), pl.BlockSpec((states, width), at),
            pl.BlockSpec((n, width), at), pl.BlockSpec((n, 2 * states), at), ANY, ANY,
        ],
        out_shape=[
            shaped((tokens, width), f32),
            shaped((tokens // n * states, width), bf16),
            shaped((tokens, width), f32),
            shaped((tokens, 2 * states), f32),
            shaped((wz_own.shape[0] * 2 * chips, width), bf16),
            shaped((tokens, cot_own.shape[1]), bf16),
        ],
        scratch_shapes=[
            pltpu.VMEM((states, width), f32),
            pltpu.VMEM((8, width), f32),
            pltpu.VMEM((8, 2 * states), f32),
            pltpu.VMEM((8, LANES), jnp.int32),
            *LineGather.scratch(chips), *TensorGather.scratch(ranks),
        ],
        compiler_params=params(number),
        name="scan_forward",
    )(x, bc, st, seg, tapx, tapbc, par, spread, skip, wz_own, cot_own)


def lane_sums(v):
    total = v[:, :LANES]
    for i in range(LANES, v.shape[1], LANES):
        total = total + v[:, i : i + LANES]
    return total


def row_sums(picks, v):
    high = v.astype(bf16)
    low = (v - high.astype(f32)).astype(bf16)
    return mm_nt(picks, high) + mm_nt(picks, low)


def gate_kernel(
    chips, ranks, gain_ref, wo_own, normed_in, wz_in, y_in, cot_in,
    gz_ref, gy_ref, ng_ref, ggain_ref, wo_out,
    wo, normed, wz, y, cot, z, gng, squares, dots, columns, land, send, recv, loads, *sems
):
    line = LineGather(wo_own, wo, *sems[:3], chips)
    tokens, width = y.shape
    inner = width * ranks
    rank = line.rank
    load = [
        pltpu.make_async_copy(src, dst, loads.at[i])
        for i, (src, dst) in enumerate(((normed_in, normed), (wz_in, wz), (y_in, y), (cot_in, cot)))
    ]
    greet(chips, ranks)
    line.step(0)
    for copy in load:
        copy.start()
    load[0].wait()
    load[1].wait()

    def gate(at):
        z[at] = mm(normed[at], wz[...])

    row_loop(tokens, CHUNK, gate)
    load[2].wait()

    def square(at):
        zz = z[at]
        gated = y[at] * (zz * sigmoid(zz))
        squares[at] = lane_sums(gated * gated)

    row_loop(tokens, 32, square)
    load[3].wait()
    deep = 2 * line.rows

    def use(first, chip):
        ks = pl.ds(pl.multiple_of(chip * deep, deep), deep)

        def rows(at):
            v = mm(cot[at, ks], wo[ks])
            if first:
                gng[at] = v
            else:
                gng[at] += v

        row_loop(tokens, CHUNK, rows)

    line.arrive(0, functools.partial(use, True))
    for k in range(1, chips):
        line.step(k)
        line.arrive(k, functools.partial(use, False))
    keep = pltpu.make_async_copy(wo, wo_out, loads.at[4])
    keep.start()
    gain = gain_ref[0:1]

    def sums(at):
        zz = z[at]
        dots[at] = lane_sums(gng[at] * gain * (y[at] * (zz * sigmoid(zz))))

    row_loop(tokens, 32, sums)
    half = lax.broadcasted_iota(jnp.int32, (8, LANES), 0) < 4
    one, other = half.astype(bf16), jnp.logical_not(half).astype(bf16)
    for r in range(0, tokens, CHUNK):
        at = slice(r, r + CHUNK)
        land[rank, :, at] = row_sums(one, squares[at]) + row_sums(other, dots[at])
    copies = [
        remote(
            land.at[rank], land.at[rank], send.at[k], recv.at[k], line.me, lax.rem(rank + k, ranks)
        )
        for k in range(1, ranks)
    ]
    for copy in copies:
        copy.start()
    line.sent()
    for copy in copies:
        copy.wait()
    for r in range(0, tokens, LANES):
        at = slice(r, r + LANES)
        total = land[0, :, at]
        for k in range(1, ranks):
            total = total + land[k, :, at]
        columns[at] = jnp.transpose(jnp.concatenate([total] * (LANES // 8), axis=0))
    ggain_ref[...] = jnp.zeros_like(ggain_ref)

    def grads(at):
        zz, yy, gg = z[at], y[at], gng[at]
        sig = sigmoid(zz)
        silu = zz * sig
        gated = yy * silu
        scale = lax.rsqrt(columns[at, 0:1] / inner + epsilon)
        ng_ref[at] = (gated * scale * gain).astype(bf16)
        weight = scale * scale * scale * columns[at, 4:5] / inner
        ggain_ref[...] += fold(gg * gated * scale)
        grad = scale * gain * gg - gated * weight
        gz_ref[at] = (grad * yy * (sig * (1.0 + zz * (1.0 - sig)))).astype(bf16)
        gy_ref[at] = grad * silu

    row_loop(tokens, 32, grads)
    keep.wait()


def gate(number, chips, ranks, gain, wo_own, normed, wz, y, cot):
    tokens, width = y.shape
    model = normed.shape[1]
    return pl.pallas_call(
        functools.partial(gate_kernel, chips, ranks),
        in_specs=[ONCHIP] + [ANY] * 5,
        out_specs=[ONCHIP] * 4 + [ANY],
        out_shape=[
            shaped((tokens, width), bf16), shaped((tokens, width), f32), shaped((tokens, width), bf16),
            shaped((8, width), f32), shaped((model, width), bf16),
        ],
        scratch_shapes=[
            pltpu.VMEM((model, width), bf16), pltpu.VMEM((tokens, model), bf16),
            pltpu.VMEM((model, width), bf16), pltpu.VMEM((tokens, width), f32),
            pltpu.VMEM((tokens, model), bf16), pltpu.VMEM((tokens, width), f32),
            pltpu.VMEM((tokens, width), f32), pltpu.VMEM((tokens, LANES), f32),
            pltpu.VMEM((tokens, LANES), f32), pltpu.VMEM((tokens, LANES), f32),
            pltpu.VMEM((ranks, 8, tokens), f32), dma(ranks), dma(ranks), dma(5),
            *LineGather.scratch(chips),
        ],
        compiler_params=params(number),
        name="gate",
    )(gain, wo_own, normed, wz, y, cot)


class Grads:
    def __init__(self, src, grad, parts, cbuf, csem):
        self.src, self.grad, self.parts, self.cbuf, self.csem = src, grad, parts, cbuf, csem
        self.count = src.shape[1] // CHUNK

    def load(self, j):
        slot = lax.rem(j, 2)
        columns = pl.ds(pl.multiple_of(j * CHUNK, CHUNK), CHUNK)
        return pltpu.make_async_copy(
            self.src.at[:, columns], self.cbuf.at[slot], self.csem.at[slot]
        )

    def begin(self):
        self.load(0).start()

    def run(self):
        @pl.loop(0, self.count)
        def _(j):
            @pl.when(j + 1 < self.count)
            def _():
                self.load(j + 1).start()

            self.load(j).wait()
            at = pl.ds(pl.multiple_of(j * CHUNK, CHUNK), CHUNK)
            self.parts[at] = mm_tn(self.cbuf[lax.rem(j, 2)], self.grad[...]).astype(bf16)


class Back:
    def __init__(self, terms, parts, stage, ssem):
        self.terms, self.parts, self.stage, self.ssem = terms, parts, stage, ssem
        self.count = parts.shape[1] // CHUNK

    def loads(self, j):
        slot = lax.rem(j, 2)
        return [
            pltpu.make_async_copy(slab(right, j, CHUNK), buffer.at[slot], sem.at[slot])
            for _, right, buffer, sem in self.terms
        ]

    def store(self, j):
        slot = lax.rem(j, 2)
        columns = pl.ds(pl.multiple_of(j * CHUNK, CHUNK), CHUNK)
        return pltpu.make_async_copy(
            self.stage.at[slot], self.parts.at[:, columns], self.ssem.at[slot]
        )

    def begin(self):
        for copy in self.loads(0):
            copy.start()

    def run(self, between=None):
        count = self.count

        @pl.loop(0, count)
        def _(j):
            slot = lax.rem(j, 2)

            @pl.when(j + 1 < count)
            def _():
                for copy in self.loads(j + 1):
                    copy.start()

            for copy in self.loads(j):
                copy.wait()

            @pl.when(j >= 2)
            def _():
                self.store(j - 2).wait()

            if between is not None:
                pl.when(j == count // 2 + 1)(between)

            for r in range(0, self.parts.shape[0], CHUNK):
                at = slice(r, r + CHUNK)
                total = jnp.zeros((CHUNK, CHUNK), f32)
                for left, _, buffer, _ in self.terms:
                    total = total + mm_nt(left[at], buffer[slot])
                self.stage[slot, at] = total.astype(bf16)
            self.store(j).start()

        for j in (count - 2, count - 1):
            self.store(j).wait()


def everyone(buffer, mine, count, send, recv, device):
    row = buffer.at[mine]
    return [
        remote(row, row, send.at[k], recv.at[k], *device(lax.rem(mine + k, count)))
        for k in range(1, count)
    ]


def added(buffer, count):
    total = buffer[0]
    for k in range(1, count):
        total = total + buffer[k]
    return total


def backward_kernel(blocks, total, chips, ranks, *refs):
    ins, refs = refs[:15], refs[15:]
    (ggain_ref, gain_ref), refs = refs[:2], refs[2:]
    (res_in, cot_own_in, ws_in, gz_in, ng_in, normed_in, cot_in, wo_in, wz_in, wx_in), refs = refs[:10], refs[10:]
    (sums_ref, norm_ref), refs = refs[:2], refs[2:]
    (z_sum, o_sum, x_sum, block_out, res_grad, state_out), refs = refs[:6], refs[6:]
    (tparts, pparts, pland, tland), refs = refs[:4], refs[4:]
    scratch, refs = refs[:11], refs[11:]
    (gxs, gbc_own, gtapx, gtapbc, gpar, gz, ng, cbuf, parts, back, wbuf, xbuf), refs = refs[:12], refs[12:]
    (gbc_slots, sbuf, wide_out, line_out, sparts, state_f, state_g), refs = refs[:7], refs[7:]
    (state_own, state_line, state_low, land_core, land_chip, land_rank), refs = refs[:6], refs[6:]
    (norm_rank, norm_dp, norm_acc), refs = refs[:3], refs[3:]
    (loads, csem, bsem, wsem, xsem, ysem, osem, fsem), refs = refs[:8], refs[8:]
    (psem, qsem, rsem, nsem, msem), refs = refs[:5], refs[5:]
    half_parts = parts.at[:, pl.ds(0, gz.shape[1])]
    z_job = LineScatter(half_parts, *refs[:4], chips)
    o_job = LineScatter(half_parts, *refs[4:8], chips)
    x_job = LineScatter(parts, *refs[8:12], chips)
    s_job = SmallScatter(sparts, *refs[12:16], chips)
    refs = refs[16:]
    around = TensorGather(gbc_own, gbc_slots, *refs[:3], ranks)
    s_line = SmallGather(state_own, state_line, *refs[3:5], chips)
    state_all = gbc_slots.at[pl.ds(gz.shape[0], normed_in.shape[1])]
    s_rank = TensorGather(state_low, state_all, *refs[5:8], ranks)
    temp, refs = refs[8], refs[9:]
    if ranks == 4:
        first = HalvesScatter(pparts, refs[0], temp, *refs[1:4])
        second = HalvesScatter(tparts, refs[4], temp, *refs[5:8])
    else:
        first = DirectScatter(pparts, pland, temp, *refs[:3], ranks)
        second = DirectScatter(tparts, tland, temp, *refs[3:6], ranks)
    now = pl.program_id(0) * blocks + pl.program_id(1)
    tokens, width = gz.shape
    model = normed_in.shape[1]
    rank, me, devices = first.rank, first.me, 2 * chips
    chip, core = z_job.chip, z_job.core
    over_dp = lambda d: (d, rank)
    over_rank = lambda r: (me, r)
    by_core = everyone(land_core, core, 2, psem.at[0], psem.at[1], lambda c: (chip * 2 + c, rank))
    by_chip = everyone(land_chip, chip, chips, qsem.at[0], qsem.at[1], lambda c: (c * 2 + core, rank))
    by_rank = everyone(land_rank, rank, ranks, rsem.at[0], rsem.at[1], over_rank)
    norm_by_rank = everyone(norm_rank, rank, ranks, nsem.at[0], nsem.at[1], over_rank)
    norm_by_dp = everyone(norm_dp, me, devices, msem.at[0], msem.at[1], over_dp)

    def begin(copies):
        for copy in copies:
            copy.start()

    def end(copies):
        for copy in copies:
            copy.wait()
    fetch = [
        pltpu.make_async_copy(src, dst, loads.at[i])
        for i, (src, dst) in enumerate(((gz_in, gz), (ng_in, ng)))
    ]
    pieces = model // width
    own_rows = first.rows

    def piece(ref, p, at):
        return ref[pl.ds(pl.multiple_of(at.start + p * own_rows, 16), at.size)]

    def pieced(ref, at):
        return jnp.concatenate([piece(ref, p, at) for p in range(pieces)], axis=1).astype(f32)

    def own_copies(src, ref, sems):
        return [
            pltpu.make_async_copy(
                src.at[:, pl.ds(p * width, width)], ref.at[pl.ds(p * own_rows, own_rows)], sems.at[p]
            )
            for p in range(pieces)
        ]

    own_res = own_copies(res_in, gz, fsem.at[0])
    own_cot = own_copies(cot_own_in, ng, fsem.at[1])
    half_out = line_out.at[:, pl.ds(0, width)]
    keep_z = pltpu.make_async_copy(half_out, z_sum, osem.at[0])
    keep_o = pltpu.make_async_copy(half_out, o_sum, osem.at[0])
    keep_x = pltpu.make_async_copy(line_out, x_sum, osem.at[0])
    keep_block = pltpu.make_async_copy(wide_out, block_out, osem.at[2])
    keep_grad = pltpu.make_async_copy(wide_out, res_grad, osem.at[2])

    z_part = Grads(normed_in, gz, half_parts, cbuf, csem)
    o_part = Grads(cot_in, ng, half_parts, cbuf, csem)
    x_part = Grads(normed_in, gxs, parts, cbuf, csem)
    out_part = Back([(ng, wo_in, wbuf, wsem)], pparts, back, bsem)
    in_part = Back(
        [(gz, wz_in, wbuf, wsem), (gxs, wx_in, xbuf, xsem), (gbc_own, ws_in, sbuf, ysem)],
        tparts, back, bsem,
    )

    @pl.when(now == 0)
    def _():
        z_part.begin()
        for copy in fetch:
            copy.start()
        out_part.begin()
        greet_all(chips, ranks)
        fetch[0].wait()
        z_part.run()
        z_job.step(0)
        fetch[1].wait()
        o_part.begin()
        out_part.run(lambda: z_job.step(1))
        first.step(0, 0)
        first.step(0, 1)

    early = [k for k in range(2, chips) if 2 * k - 2 < total - 1]

    @pl.when(now == 1)
    def _():
        o_part.run()
        o_job.step(0)

    for k in early:
        @pl.when(now == 2 * k - 2)
        def _():
            z_job.step(k)

    @pl.when(now == 3)
    def _():
        o_job.step(1)

    @pl.when(now == 5)
    def _():
        first.step(1, 0)
        first.step(1, 1)

    @pl.when(now == total - 1)
    def _():
        x_part.begin()
        in_part.begin()

    row = pl.multiple_of(
        (pl.program_id(0) * blocks + blocks - 1 - pl.program_id(1)) * BLOCK, BLOCK
    )
    here = pl.ds(row, BLOCK)
    outs = (
        gxs.at[here, pl.ds(0, width)], gbc_own.at[here], gxs.at[here, pl.ds(width, LANES)],
        gtapx, gtapbc, gpar,
    )
    scan_bwd_kernel(blocks, *ins, *outs, *scratch)

    @pl.when(now == total - 1)
    def _():
        around.step(0)
        begin(own_cot)
        pack = land_core.at[core]
        pack[...] = jnp.zeros(land_core.shape[1:], f32)
        for k in range(5):
            rows = slice(8 * k, 8 * k + 8)
            pack[k : k + 1, :width] = jnp.sum(gtapx[rows], axis=0, keepdims=True)
            pack[k : k + 1, width:] = jnp.sum(gtapbc[rows], axis=0, keepdims=True)
        pack[5:6, :width] = jnp.sum(ggain_ref[...], axis=0, keepdims=True)
        for k in range(3):
            pack[6:7, k * LANES : (k + 1) * LANES] = jnp.sum(
                gpar[8 * k : 8 * k + 8], axis=0, keepdims=True
            )
        begin(by_core)
        x_part.run()
        x_job.step(0)
        end(by_core)
        land_chip[chip] = added(land_core, 2)
        begin(by_chip)
        depth = sparts.shape[0]

        def own_columns(i):
            columns = pl.ds(pl.multiple_of(rank * depth + i * CHUNK, CHUNK), CHUNK)
            return pltpu.make_async_copy(normed_in.at[:, columns], cbuf.at[i], csem.at[i])

        for i in range(depth // CHUNK):
            own_columns(i).start()
        for k in range(2, chips):
            if k not in early:
                z_job.step(k)
        if chips > 2:
            o_job.step(2)
        around.step(1)

        def between():
            second.step(0, 0)
            around.finish()

            def add(at):
                total = gbc_slots[at].astype(f32)
                for r in range(1, ranks):
                    there = pl.ds(pl.multiple_of(at.start + r * tokens, 128), at.size)
                    total = total + gbc_slots[there].astype(f32)
                gbc_slots[at] = total.astype(bf16)

            row_loop(tokens, 128, add)
            for i in range(depth // CHUNK):
                own_columns(i).wait()
                sparts[i * CHUNK : (i + 1) * CHUNK] = mm_tn(cbuf[i], gbc_slots[:tokens]).astype(
                    sparts.dtype
                )
            s_job.step(0)
            for k in range(3, chips):
                o_job.step(k)
            s_job.step(1)
            x_job.step(1, True)

        in_part.run(between)
        second.step(0, 1)
        begin(own_res)
        s_job.finish(state_own)
        s_line.step(0)
        x_job.send_rest()
        z_job.finish(half_out)
        keep_z.start()
        first.arrive()
        end(own_res)

        def plus(at, total):
            wide_out[at] = pieced(gz, at) + total

        first.totals(32, plus)
        keep_block.start()
        second.step(1, 0)
        end(by_chip)
        land_rank[rank] = added(land_chip, chips)
        begin(by_rank)
        keep_z.wait()
        o_job.finish(half_out)
        keep_o.start()
        s_line.step(1)
        s_line.finish()

        def lower(at):
            state_low[at] = state_line[at].astype(bf16)

        row_loop(depth, 64, lower)
        end(by_rank)
        s_rank.step(0)
        shared = land_rank[0, :, width:]
        for r in range(1, ranks):
            shared = shared + land_rank[r, :, width:]
        for r in range(ranks):
            sums_ref[:, r * width : (r + 1) * width] = land_rank[r, :, :width]
        sums_ref[:, ranks * width :] = shared
        if chips > 2:
            x_job.step(2)
        second.step(1, 1)
        s_rank.step(1)
        for k in range(3, chips):
            x_job.step(k)
        keep_block.wait()
        end(own_cot)
        second.arrive()
        norm_acc[...] = jnp.zeros_like(norm_acc)
        gain = gain_ref[...]

        def last(at, grad):
            v = pieced(gz, at)
            scaling = lax.rsqrt(jnp.mean(v * v, axis=1, keepdims=True) + epsilon)
            norm_acc[...] += fold(grad * v * scaling)
            grad = grad * gain
            along = jnp.sum(grad * v, axis=1, keepdims=True)
            weight = scaling * scaling * scaling * along / model
            wide_out[at] = pieced(ng, at) + scaling * grad - v * weight

        second.totals(32, last)
        keep_grad.start()
        line = jnp.sum(norm_acc[...], axis=0, keepdims=True)
        eighth = model // 8
        for i in range(8):
            norm_rank[rank, i : i + 1, :] = line[:, i * eighth : (i + 1) * eighth]
        begin(norm_by_rank)
        s_rank.finish()
        buffers = (state_f, state_g)
        stored = []
        some = depth // 2
        for r in range(2 * ranks):
            if r >= 2:
                stored[r - 2].wait()

            def state(at):
                low = pl.ds(pl.multiple_of(at.start + r * some, 64), at.size)
                buffers[r % 2][at] = state_all[low].astype(f32)

            row_loop(some, 64, state)
            copy = pltpu.make_async_copy(
                buffers[r % 2], state_out.at[pl.ds(r * some, some)], osem.at[1 + r % 2 * 2]
            )
            copy.start()
            stored.append(copy)
        end(norm_by_rank)
        norm_dp[me] = added(norm_rank, ranks)
        begin(norm_by_dp)
        keep_o.wait()
        x_job.finish(line_out)
        keep_x.start()
        end(stored[-2:])
        end(norm_by_dp)
        norm_ref[...] = added(norm_dp, devices)
        keep_x.wait()
        keep_grad.wait()


def backward(
    number, chips, ranks, ggain, norm_gain, residual, cot_own, ws, gz, ng, normed, cot, wo, wz, wx,
    x, conv, bc, convbc, st, seg, gy, y, h, tapx, tapbc, par, spread, skip, nseq,
):
    tokens, width = x.shape
    rows, model = residual.shape
    n = BLOCK
    blocks = tokens // nseq // n
    at = lambda s, i: (s * blocks + blocks - 1 - i, 0)
    tail = lambda s, i: (jnp.maximum((s * blocks + blocks - 1 - i) * (n // 8) - 1, 0), 0)
    whole = lambda s, i: (0, 0)
    states = LANES
    full = lambda v: pl.BlockSpec(v.shape, whole)
    once = lambda shape: pl.BlockSpec(shape, whole)
    devices = 2 * chips
    own, depth, wide = model // devices, model // ranks, width + 2 * states
    kind = bf16 if depth // devices % 16 == 0 else f32
    return pl.pallas_call(
        functools.partial(backward_kernel, blocks, nseq * blocks, chips, ranks),
        grid=(nseq, blocks),
        in_specs=[
            pl.BlockSpec((n, width), at),
            pl.BlockSpec((n, width), at),
            pl.BlockSpec((n, 2 * states), at),
            pl.BlockSpec((n, 2 * states), at),
            pl.BlockSpec((n, LANES), at),
            pl.BlockSpec((n, LANES), at),
            pl.BlockSpec((8, LANES), tail),
            pl.BlockSpec((n, width), at),
            pl.BlockSpec((n, width), at),
            pl.BlockSpec((states, width), at),
            full(tapx), full(tapbc), full(par), full(spread), full(skip), full(ggain), full(norm_gain),
        ]
        + [ANY] * 10,
        out_specs=[
            once((8, width * ranks + 2 * states)), once((8, model // 8)),
        ]
        + [ANY] * 10,
        out_shape=[
            shaped((8, width * ranks + 2 * states), f32), shaped((8, model // 8), f32),
            shaped((own, width), f32), shaped((own, width), f32), shaped((own, width + LANES), f32),
            shaped((rows, model), f32), shaped((rows, model), f32), shaped((model, 2 * states), f32),
            shaped((tokens, model), bf16), shaped((tokens, model), bf16),
            *[shaped((ranks, rows, model) if ranks != 4 else (8, LANES), bf16)] * 2,
        ],
        scratch_shapes=[
            *scan_bwd_scratch(width, states),
            pltpu.VMEM((tokens, width + LANES), bf16),
            pltpu.VMEM((tokens, 2 * states), bf16),
            pltpu.VMEM((40, width), f32),
            pltpu.VMEM((40, 2 * states), f32),
            pltpu.VMEM((24, LANES), f32),
            pltpu.VMEM((tokens, width), bf16),
            pltpu.VMEM((tokens, width), bf16),
            pltpu.VMEM((2, tokens, CHUNK), bf16),
            pltpu.VMEM((model, width + LANES), bf16),
            pltpu.VMEM((2, tokens, CHUNK), bf16),
            pltpu.VMEM((2, CHUNK, width), bf16),
            pltpu.VMEM((2, CHUNK, width + LANES), bf16),
            pltpu.VMEM((ranks * tokens, 2 * states), bf16),
            pltpu.VMEM((2, CHUNK, 2 * states), bf16),
            pltpu.VMEM((rows, model), f32),
            pltpu.VMEM((own, width + LANES), f32),
            pltpu.VMEM((depth, 2 * states), kind),
            pltpu.VMEM((depth // 2, 2 * states), f32),
            pltpu.VMEM((depth // 2, 2 * states), f32),
            pltpu.VMEM((depth // devices, 2 * states), kind),
            pltpu.VMEM((depth, 2 * states), kind),
            pltpu.VMEM((depth, 2 * states), bf16),
            pltpu.VMEM((2, 8, wide), f32),
            pltpu.VMEM((chips, 8, wide), f32),
            pltpu.VMEM((ranks, 8, wide), f32),
            pltpu.VMEM((ranks, 8, model // 8), f32),
            pltpu.VMEM((devices, 8, model // 8), f32),
            pltpu.VMEM((8, model), f32),
            dma(2), *[dma(2)] * 5, dma(4), pltpu.SemaphoreType.DMA((2, model // width)),
            *[pltpu.SemaphoreType.DMA((2, n)) for n in (2, chips, ranks, ranks, devices)],
            *LineScatter.scratch(chips, (model, width)),
            *LineScatter.scratch(chips, (model, width)),
            *LineScatter.scratch(chips, (model, width + LANES)),
            *SmallScatter.scratch(chips, (depth, 2 * states), kind),
            *TensorGather.scratch(ranks), *SmallGather.scratch(chips), *TensorGather.scratch(ranks),
            HalvesScatter.temp((tokens, model)) if ranks == 4 else pltpu.VMEM((2, rows // 2, model), bf16),
            *(HalvesScatter.scratch((tokens, model)) if ranks == 4 else DirectScatter.scratch(ranks)) * 2,
        ],
        compiler_params=params(number),
        name="backward",
    )(
        x, conv, bc, convbc, st, seg, seg, gy, y, h, tapx, tapbc, par, spread, skip, ggain, norm_gain,
        residual, cot_own, ws, gz, ng, normed, cot, wo, wz, wx,
    )


def emit_kernel(
    ranks, heads, sums_ref, norm_ref, z_ref, x_ref, o_ref, block_in, res_in, state_in,
    inner_ref, step_ref, out_ref, taps_ref, bias_ref, gated_ref, norm_out, a_ref, b_ref, c_ref,
    block_out, res_out, state_out, block, res, state, sems
):
    moves = [
        (
            pltpu.make_async_copy(src, held, sems.at[0, i]),
            pltpu.make_async_copy(held, dst, sems.at[1, i]),
        )
        for i, (src, held, dst) in enumerate(
            ((block_in, block, block_out), (res_in, res, res_out), (state_in, state, state_out))
        )
    ]
    for come, _ in moves:
        come.start()
    width, inner = z_ref.shape[1], gated_ref.shape[0]
    row = lax.broadcasted_iota(jnp.int32, (LANES, LANES), 0)
    col = lax.broadcasted_iota(jnp.int32, (LANES, LANES), 1)
    total = jnp.zeros((8, LANES), f32)
    for r in range(ranks):
        line = [sums_ref[6:7, r * width + k * LANES : r * width + (k + 1) * LANES] for k in range(3)]
        picks = ((col == r * heads + row) & (row < heads)).astype(bf16)
        total = total + exact_mm(
            jnp.concatenate(line + [jnp.zeros((5, LANES), f32)], axis=0), picks
        )
    for k, ref in enumerate((a_ref, b_ref, c_ref)):
        ref[...] = total[k, : ranks * heads]
    taps_ref[...] = sums_ref[0:4]
    bias_ref[...] = sums_ref[4]
    gated_ref[...] = sums_ref[5, :inner]
    eighth = norm_ref.shape[1]
    for i in range(8):
        norm_out[i * eighth : (i + 1) * eighth] = norm_ref[i]
    step_ref[...] = x_ref[:, width : width + heads]
    for come, go in moves:
        come.wait()
        go.start()
    inner_ref[:, 0, :] = z_ref[...]
    inner_ref[:, 1, :] = x_ref[:, :width]
    out_ref[...] = jnp.transpose(o_ref[...])
    for _, go in moves:
        go.wait()


def emit(ranks, heads, sums, norm, z, x, o, block, res, state):
    own, width = z.shape
    inner = width * ranks
    vector = lambda n: shaped((n,), f32)
    return pl.pallas_call(
        functools.partial(emit_kernel, ranks, heads),
        in_specs=[ONCHIP] * 5 + [ANY] * 3,
        out_specs=[ONCHIP] * 10 + [ANY] * 3,
        out_shape=[
            shaped((own, 2, width), f32), shaped((own, heads), f32), shaped((width, own), f32),
            shaped((4, sums.shape[1]), f32), vector(sums.shape[1]), vector(inner),
            vector(norm.size), *[vector(ranks * heads)] * 3,
            shaped(block.shape, f32), shaped(res.shape, f32), shaped(state.shape, f32),
        ],
        scratch_shapes=[
            pltpu.VMEM(block.shape, f32), pltpu.VMEM(res.shape, f32), pltpu.VMEM(state.shape, f32),
            pltpu.SemaphoreType.DMA((2, 3)),
        ],
        compiler_params=pltpu.CompilerParams(vmem_limit_bytes=VMEM_BYTES),
        name="emit",
    )(sums, norm, z, x, o, block, res, state)


def per_device(
    residual, segment_ids, norm_gain, inner_weight, state_weight, step_weight, conv_weight,
    conv_bias, step_bias, decay_log, skip_gain, gated_gain, out_weight, cotangent,
):
    chips, ranks = lax.axis_size("dp") // 2, lax.axis_size("tensor")
    width = inner_weight.shape[2]
    heads = step_weight.shape[1]
    inner_width = gated_gain.shape[0]
    nseq = segment_ids.shape[0]
    wx_own = jnp.concatenate([inner_weight[:, 1], on_lanes(step_weight)], axis=1)
    x, st, bc, seg, tapx, tapbc, par, skip, gain, spread, wo_own, normed, wx = project(
        1, chips, ranks, heads, residual, norm_gain[None], state_weight, segment_ids,
        conv_weight, conv_bias, (step_bias, decay_log, skip_gain), gated_gain[None], out_weight, wx_own,
    )
    y, h, conv, convbc, wz, cot = scan_forward_gather(
        2, chips, ranks, inner_weight[:, 0], cotangent,
        x, bc, st, seg, tapx, tapbc, par, spread, skip, nseq,
    )
    gz, gy, ng, ggain, wo = gate(3, chips, ranks, gain, wo_own, normed, wz, y, cot)
    sums, norm_grad, z_grad, out_grad, x_grad, block_out, residual_grad, state_grad, *_ = backward(
        4, chips, ranks, ggain, norm_gain[None], residual, cotangent, state_weight,
        gz, ng, normed, cot, wo, wz, wx,
        x, conv, bc, convbc, st, seg, gy, y, h, tapx, tapbc, par, spread, skip, nseq,
    )
    (
        inner_grad, step_grad, out_grad, tap_grad, bias_grad, gated_grad, norm_grad,
        step_bias_grad, decay_grad, skip_grad, block_out, residual_grad, state_grad,
    ) = emit(
        ranks, heads, sums, norm_grad, z_grad, x_grad, out_grad, block_out, residual_grad, state_grad
    )
    return (
        block_out, residual_grad, norm_grad, inner_grad, state_grad, step_grad, tap_grad, bias_grad,
        step_bias_grad, decay_grad, skip_grad, gated_grad, out_grad,
    )


def solution(mesh):
    rows, both = P("dp", "tensor"), P(("dp", "tensor"), None)
    inner, out = P("dp", None, "tensor"), P("tensor", "dp")
    return jax.shard_map(
        per_device,
        mesh=mesh,
        in_specs=(
            both, P("dp", None), P(), inner, P(), rows, P(), P(), P(), P(), P(), P(), out, both,
        ),
        out_specs=(both, both, P(), inner, P(), rows, P(), P(), P(), P(), P(), P(), out),
        check_vma=False,
    )
```

```python
import functools
import jax
import jax.numpy as jnp
from jax import lax
from jax.experimental import pallas as pl
from jax.experimental.pallas import tpu as pltpu
from jax.sharding import PartitionSpec as P

LANES = 128
BLOCK = 128
WIDTH = 64
VMEM_BYTES = 60 * 1024 * 1024
f32, bf16 = jnp.float32, jnp.bfloat16
ROWS0 = (((0,), (0,)), ((), ()))
COLS1 = (((1,), (1,)), ((), ()))


def mm(a, b):
    return jnp.dot(a, b, preferred_element_type=f32)


def mm_tn(a, b):
    return lax.dot_general(a, b, ROWS0, preferred_element_type=f32)


def mm_nt(a, b):
    return lax.dot_general(a, b, COLS1, preferred_element_type=f32)


def sigmoid(v):
    return 0.5 + 0.5 * jnp.tanh(0.5 * v)


def two_parts(v, low_lanes):
    high = v.astype(bf16)
    return jnp.where(low_lanes, (v - high.astype(f32)).astype(bf16), high)


def head_sums(v, spread):
    high = v.astype(bf16)
    low = (v - high.astype(f32)).astype(bf16)
    return mm_nt(high, spread) + mm_nt(low, spread)


def shifted_masks(seg_ext, seg):
    n = seg.shape[0]
    return [None] + [seg_ext[8 - k : 8 - k + n] == seg for k in (1, 2, 3)]


def convolve(tail, part, masks, taps):
    n = part.shape[0]
    ext = jnp.concatenate([tail, part], axis=0)
    total = taps[4:5] + taps[3:4] * part
    for k in (1, 2, 3):
        total = total + taps[3 - k : 4 - k] * jnp.where(masks[k], ext[8 - k : 8 - k + n], 0.0)
    return total


def wide(v):
    return jnp.concatenate([v, v], axis=1)


def step_state(raw, params, seg, prev_seg, end_seg, n):
    row = lax.broadcasted_iota(jnp.int32, (n, n), 0)
    col = lax.broadcasted_iota(jnp.int32, (n, n), 1)
    v = raw + params[0:1]
    dt = jnp.maximum(v, 0.0) + jnp.log1p(jnp.exp(-jnp.abs(v)))
    a = params[1:2]
    cum = jnp.dot(
        (row >= col).astype(f32), dt * a, precision=lax.Precision.HIGHEST, preferred_element_type=f32
    )
    last = cum[n - 1 : n]
    into = jnp.where(seg == prev_seg, jnp.exp(cum), 0.0)
    onto = jnp.where(seg == end_seg, jnp.exp(last - cum), 0.0)
    through = jnp.where(end_seg == prev_seg, jnp.exp(last), 0.0)
    bias = jnp.where((row >= col) & (seg == jnp.transpose(seg)), 0.0, -1e30)
    return v, dt, a, cum, into, onto, through, bias


def scan_fwd_kernel(
    blocks, x_ref, bc_ref, st_ref, seg_ref, tapx_ref, tapbc_ref, par_ref, spread_ref, skip_ref,
    y_ref, h_ref, conv_ref, convbc_ref, state, tail_x, tail_bc, tail_seg,
):
    n = BLOCK
    block = pl.program_id(1)

    @pl.when(block == 0)
    def _():
        state[...] = jnp.zeros_like(state)
        tail_x[...] = jnp.zeros_like(tail_x)
        tail_bc[...] = jnp.zeros_like(tail_bc)
        tail_seg[...] = jnp.full_like(tail_seg, -1)

    seg = seg_ref[...]
    masks = shifted_masks(jnp.concatenate([tail_seg[...], seg], axis=0), seg)
    prev_seg, end_seg = tail_seg[7:8], seg[n - 1 : n]
    v, dt, a, cum, into, onto, through, bias = step_state(
        st_ref[...], par_ref[...], seg, prev_seg, end_seg, n
    )
    cum_t = jnp.transpose(cum)
    low_lanes = lax.broadcasted_iota(jnp.int32, (n, LANES), 1) >= LANES // 2
    spread = spread_ref[...]
    dt_w = mm(two_parts(dt, low_lanes), spread)
    into_w = mm(two_parts(into, low_lanes), spread)
    onto_w = mm(two_parts(onto, low_lanes), spread)
    through_w = mm(two_parts(jnp.broadcast_to(through, (8, LANES)), low_lanes[:8]), spread)[0:1]
    bc_masks = [None] + [wide(m) for m in masks[1:]]
    conv_bc = convolve(tail_bc[...], bc_ref[...], bc_masks, tapbc_ref[...])
    convbc_ref[...] = conv_bc
    act_bc = conv_bc * sigmoid(conv_bc)
    b, c = act_bc[:, :LANES].astype(bf16), act_bc[:, LANES:].astype(bf16)
    cross = mm_nt(c, b)
    entering = state[...].astype(bf16)
    h_ref[...] = entering
    first_half = lax.broadcasted_iota(jnp.int32, (n, LANES), 1) < WIDTH
    for pair in range(x_ref.shape[1] // LANES):
        sl = slice(pair * LANES, (pair + 1) * LANES)
        conv = convolve(tail_x[:, sl], x_ref[:, sl], masks, tapx_ref[:, sl])
        conv_ref[:, sl] = conv
        xs = conv * sigmoid(conv)
        xd = xs * dt_w[:, sl]
        outside = mm(c, entering[:, sl]) * into_w[:, sl]
        mixes = []
        for h in (2 * pair, 2 * pair + 1):
            decay = jnp.exp(cum[:, h : h + 1] - cum_t[h : h + 1, :] + bias)
            mixes.append((decay * cross).astype(bf16))
        stacked = jnp.concatenate(
            [jnp.where(first_half, xd, 0.0), jnp.where(first_half, 0.0, xd)], axis=0
        ).astype(bf16)
        inside = mm(jnp.concatenate(mixes, axis=1), stacked)
        y_ref[:, sl] = inside + outside + skip_ref[0:1, sl] * xs
        local = mm_tn(b, (onto_w[:, sl] * xd).astype(bf16))
        state[:, sl] = through_w[:, sl] * state[:, sl] + local
    tail_x[...] = x_ref[n - 8 :, :]
    tail_bc[...] = bc_ref[n - 8 :, :]
    tail_seg[...] = seg_ref[n - 8 :, :]


def fold(v):
    total = v[0:8]
    for r in range(8, v.shape[0], 8):
        total = total + v[r : r + 8]
    return total


def scan_bwd_kernel(
    blocks, x_ref, conv_ref, bc_ref, convbc_ref, st_ref, seg_ref, segt_ref, gy_ref, y_ref, h_ref,
    tapx_ref, tapbc_ref, par_ref, spread_ref, skip_ref,
    gx_ref, gbc_ref, gst_ref, gtapx_ref, gtapbc_ref, gpar_ref,
    gstate, head_x, head_bc, head_seg, xs_s, slope_s, back_s, dt_s, onto_s, xd_s, sums_s,
):
    n = BLOCK
    step = pl.program_id(1)
    block = blocks - 1 - step

    @pl.when((step == 0) & (pl.program_id(0) == 0))
    def _():
        gtapx_ref[...] = jnp.zeros_like(gtapx_ref)
        gtapbc_ref[...] = jnp.zeros_like(gtapbc_ref)
        gpar_ref[...] = jnp.zeros_like(gpar_ref)

    @pl.when(step == 0)
    def _():
        gstate[...] = jnp.zeros_like(gstate)
        head_x[...] = jnp.zeros_like(head_x)
        head_bc[...] = jnp.zeros_like(head_bc)
        head_seg[...] = jnp.full_like(head_seg, -1)

    seg = seg_ref[...]
    first = block == 0
    seg_next = jnp.concatenate([seg, head_seg[...]], axis=0)
    ahead = [None] + [seg_next[k : k + n] == seg for k in (1, 2, 3)]
    prev_seg = jnp.where(first, -1, segt_ref[7:8])
    end_seg = seg[n - 1 : n]
    v, dt, a, cum, into, onto, through, bias = step_state(
        st_ref[...], par_ref[...], seg, prev_seg, end_seg, n
    )
    cum_t = jnp.transpose(cum)
    low_lanes = lax.broadcasted_iota(jnp.int32, (n, LANES), 1) >= LANES // 2
    spread = spread_ref[...]
    dt_s[...] = mm(two_parts(dt, low_lanes), spread)
    into_w = mm(two_parts(into, low_lanes), spread)
    onto_s[...] = mm(two_parts(onto, low_lanes), spread)
    through_w = mm(two_parts(jnp.broadcast_to(through, (8, LANES)), low_lanes[:8]), spread)[0:1]
    conv_bc = convbc_ref[...]
    sig_bc = sigmoid(conv_bc)
    act_bc = conv_bc * sig_bc
    b, c = act_bc[:, :LANES].astype(bf16), act_bc[:, LANES:].astype(bf16)
    cross = mm_nt(c, b)
    first_half = lax.broadcasted_iota(jnp.int32, (n, LANES), 1) < WIDTH
    halves = lambda t: jnp.concatenate(
        [jnp.where(first_half, t, 0.0), jnp.where(first_half, 0.0, t)], axis=0
    ).astype(bf16)
    into_s, onto_low = sums_s.at[0:n], sums_s.at[n : 2 * n]
    pairs = [slice(i, i + LANES) for i in range(0, x_ref.shape[1], LANES)]

    for sl in pairs:
        conv = conv_ref[:, sl]
        sig = sigmoid(conv)
        xs = conv * sig
        xs_s[:, sl] = xs
        slope_s[:, sl] = sig + xs * (1.0 - sig)
        xd = xs * dt_s[:, sl]
        xd_s[:, sl] = xd.astype(bf16)
        onto_low[:, sl] = (xd * onto_s[:, sl]).astype(bf16)
        into_s[:, sl] = (gy_ref[:, sl] * into_w[:, sl]).astype(bf16)
    before = h_ref[...]
    gstate_low = gstate[...].astype(bf16)
    gy_into = into_s[...]
    gc = mm_nt(gy_into, before)
    gb = mm_nt(onto_low[...], gstate_low)
    back_s[...] = mm(b, gstate_low)
    edges = 5 * n
    for sl in pairs:
        old = through_w[:, sl] * gstate[:, sl]
        last = fold(old * before[:, sl].astype(f32))
        skips = fold(gy_ref[:, sl] * xs_s[:, sl])
        both = jnp.concatenate([last, skips], axis=0)
        high = both.astype(bf16)
        sums_s[edges : edges + 16, sl] = high
        sums_s[edges + 16 : edges + 32, sl] = (both - high.astype(f32)).astype(bf16)
        gstate[:, sl] = old + mm_tn(c, gy_into[:, sl])
    gcross = jnp.zeros((n, n), f32)
    for pair, sl in enumerate(pairs):
        xs = xs_s[:, sl]
        xd_low = xd_s[:, sl]
        gy = gy_ref[:, sl]
        skip = skip_ref[0:1, sl]
        inner = y_ref[:, sl] - skip * xs
        g_state = onto_s[:, sl] * back_s[:, sl]
        gy_halves = halves(gy)
        gmix = mm_nt(gy_halves, xd_low)
        mixes = []
        for i, h in enumerate((2 * pair, 2 * pair + 1)):
            decay = jnp.exp(cum[:, h : h + 1] - cum_t[h : h + 1, :] + bias)
            mixes.append((decay * cross).astype(bf16))
            gcross = gcross + decay * gmix[i * n : (i + 1) * n]
        gxd = mm_tn(jnp.concatenate(mixes, axis=0), gy_halves) + g_state
        xd_r, gy_r = xd_low.astype(f32), gy.astype(bf16).astype(f32)
        q = gy_r * inner - xd_r * gxd
        high = q.astype(bf16)
        sums_s[0:n, sl] = high
        sums_s[n : 2 * n, sl] = (q - high.astype(f32)).astype(bf16)
        q = xd_r * g_state
        high = q.astype(bf16)
        sums_s[2 * n : 3 * n, sl] = high
        sums_s[3 * n : 4 * n, sl] = (q - high.astype(f32)).astype(bf16)
        sums_s[4 * n : 5 * n, sl] = (xs * gxd).astype(bf16)
        gconv = (dt_s[:, sl] * gxd + skip * gy) * slope_s[:, sl]
        taps = tapx_ref[:, sl]
        part = x_ref[:, sl]
        ext = jnp.concatenate([gconv, head_x[:, sl]], axis=0)
        gu = taps[3:4] * gconv
        gtapx_ref[24:32, sl] += fold(gconv * part)
        for k in (1, 2, 3):
            later = jnp.where(ahead[k], ext[k : k + n], 0.0)
            gu = gu + taps[3 - k : 4 - k] * later
            gtapx_ref[8 * (3 - k) : 8 * (4 - k), sl] += fold(later * part)
        gx_ref[:, sl] = gu.astype(bf16)
        gtapx_ref[32:40, sl] += fold(gconv)
        head_x[:, sl] = gconv[0:8]
    sums = mm_nt(sums_s[...], spread)
    sum_q = sums[0:n] + sums[n : 2 * n]
    sum_state = sums[2 * n : 3 * n] + sums[3 * n : 4 * n]
    sum_dt = sums[4 * n : 5 * n]
    sum_last = sums[edges : edges + 8] + sums[edges + 16 : edges + 24]
    sum_skip = sums[edges + 8 : edges + 16] + sums[edges + 24 : edges + 32]
    gcross_low = gcross.astype(bf16)
    gc = gc + mm(gcross_low, b)
    gb = gb + mm_tn(gcross_low, c)
    gconv = jnp.concatenate([gb, gc], axis=1) * (sig_bc + act_bc * (1.0 - sig_bc))
    ext = jnp.concatenate([gconv, head_bc[...]], axis=0)
    taps = tapbc_ref[...]
    part = bc_ref[...]
    gu = taps[3:4] * gconv
    gtapbc_ref[24:32, :] += fold(gconv * part)
    for k in (1, 2, 3):
        later = jnp.where(wide(ahead[k]), ext[k : k + n], 0.0)
        gu = gu + taps[3 - k : 4 - k] * later
        gtapbc_ref[8 * (3 - k) : 8 * (4 - k), :] += fold(later * part)
    gbc_ref[...] = gu.astype(gbc_ref.dtype)
    gtapbc_ref[32:40, :] += fold(gconv)
    head_bc[...] = gconv[0:8]
    head_seg[...] = seg[0:8]
    rows = lax.broadcasted_iota(jnp.int32, (n, n), 0)
    cols = lax.broadcasted_iota(jnp.int32, (n, n), 1)
    after = jnp.dot(
        (cols >= rows).astype(f32), sum_q, precision=lax.Precision.HIGHEST, preferred_element_type=f32
    )
    edge = jnp.sum(sum_state, axis=0, keepdims=True) + jnp.sum(sum_last, axis=0, keepdims=True)
    glog = after + edge
    gdt = sum_dt + a * glog
    gst = gdt * sigmoid(v)
    gst_ref[...] = jnp.where(low_lanes, 0.0, gst).astype(bf16)
    gpar_ref[0:8] += fold(gst)
    gpar_ref[8:16] += fold(a * dt * glog)
    gpar_ref[16:24] += sum_skip


def scan_bwd_scratch(width, states):
    n = BLOCK
    return [
        pltpu.VMEM((states, width), f32),
        pltpu.VMEM((8, width), f32),
        pltpu.VMEM((8, 2 * states), f32),
        pltpu.VMEM((8, LANES), jnp.int32),
        *[pltpu.VMEM((n, width), f32)] * 5,
        pltpu.VMEM((n, width), bf16),
        pltpu.VMEM((5 * n + 32, width), bf16),
    ]


def on_lanes(v):
    half = jnp.pad(v, [(0, 0)] * (v.ndim - 1) + [(0, LANES // 2 - v.shape[-1])])
    return jnp.concatenate([half, half], axis=-1)


MESH = pl.DeviceIdType.MESH


def place():
    dp, rank = lax.axis_index("dp"), lax.axis_index("tensor")
    return dp // 2, dp % 2, rank


def remote(src, dst, send, recv, dp, rank):
    return pltpu.make_async_remote_copy(
        src_ref=src, dst_ref=dst, send_sem=send, recv_sem=recv, device_id=(dp, rank),
        device_id_type=MESH,
    )


def greet(chips, ranks):
    chip, core, rank = place()
    sem = pltpu.get_barrier_semaphore()
    me = chip * 2 + core

    def signal(dp, r):
        pl.semaphore_signal(sem, inc=1, device_id=(dp, r), device_id_type=MESH)

    signal(chip * 2 + 1 - core, rank)
    for step in (1, -1):
        @pl.when((chip + step >= 0) & (chip + step < chips))
        def _():
            signal(me + 2 * step, rank)
    for k in range(1, ranks):
        signal(me, lax.rem(rank + k, ranks))
    pl.semaphore_wait(sem, ranks + (chip + chips - 1) // chips + (2 * chips - 2 - chip) // chips)


def greet_all(chips, ranks):
    chip, core, rank = place()
    sem = pltpu.get_barrier_semaphore()
    me, devices = chip * 2 + core, 2 * chips
    for k in range(1, devices):
        pl.semaphore_signal(
            sem, inc=1, device_id=(lax.rem(me + k, devices), rank), device_id_type=MESH
        )
    for k in range(1, ranks):
        pl.semaphore_signal(
            sem, inc=1, device_id=(me, lax.rem(rank + k, ranks)), device_id_type=MESH
        )
    pl.semaphore_wait(sem, devices + ranks - 2)


def slab(ref, index, rows):
    return ref.at[pl.ds(pl.multiple_of(index * rows, rows), rows)]


class LineGather:
    def __init__(self, own, slots, send, recv, local, chips):
        self.own, self.slots, self.send, self.recv, self.local = own, slots, send, recv, local
        self.chips, self.rows = chips, own.shape[0]
        self.chip, self.core, self.rank = place()
        self.me = self.chip * 2 + self.core
        self.partner = self.chip * 2 + 1 - self.core
        self.steps = chips

    @staticmethod
    def scratch(chips):
        n = 2 * chips
        return [
            pltpu.SemaphoreType.DMA((3, n)), pltpu.SemaphoreType.DMA((n,)), pltpu.SemaphoreType.DMA,
        ]

    def copy(self, way, origin, src=None):
        target = (self.me + 2, self.me - 2, self.partner)[way]
        slot = slab(self.slots, origin, self.rows)
        return remote(
            slot if src is None else src, slot, self.send.at[way, origin], self.recv.at[origin],
            target, self.rank,
        )

    def pass_on(self, way, origin, src=None, wait=False):
        def go():
            copy = self.copy(way, origin, src)
            copy.wait_send() if wait else copy.start()

        if way == 0:
            pl.when(self.chip + 1 < self.chips)(go)
        elif way == 1:
            pl.when(self.chip > 0)(go)
        else:
            go()

    def keep(self):
        return pltpu.make_async_copy(self.own, slab(self.slots, self.me, self.rows), self.local)

    def sides(self, k):
        return ((0, self.chip - k >= 0, -k), (1, self.chip + k < self.chips, k))

    def step(self, k):
        if k == 0:
            for way in (0, 1, 2):
                self.pass_on(way, self.me, self.own)
            self.keep().start()
            return
        for way, there, shift in self.sides(k):
            @pl.when(there)
            def _():
                origin = self.me + 2 * shift
                self.copy(2, origin).wait_recv()
                self.pass_on(way, origin)
                self.pass_on(2, origin)

    def arrive(self, k, use=None):
        if k == 0:
            self.keep().wait()
            self.copy(2, self.partner).wait_recv()
            if use is not None:
                use(self.chip)
            return
        for way, there, shift in self.sides(k):
            @pl.when(there)
            def _():
                self.copy(2, self.partner + 2 * shift).wait_recv()
                if use is not None:
                    use(self.chip + shift)

    def each(self, k, use):
        if k == 0:
            use(self.chip)
            return
        for way, there, shift in self.sides(k):
            @pl.when(there)
            def _():
                use(self.chip + shift)

    def sent(self):
        for way in (0, 1, 2):
            self.pass_on(way, self.me, self.own, wait=True)
        for k in range(1, self.chips):
            for way, there, shift in self.sides(k):
                @pl.when(there)
                def _():
                    origin = self.me + 2 * shift
                    self.pass_on(way, origin, wait=True)
                    self.pass_on(2, origin, wait=True)

    def finish(self):
        for k in range(self.chips):
            self.arrive(k)
        self.sent()


class TensorGather:
    def __init__(self, own, slots, send, recv, local, ranks):
        self.own, self.slots, self.send, self.recv, self.local = own, slots, send, recv, local
        self.ranks, self.rows = ranks, own.shape[0]
        chip, core, self.rank = place()
        self.me = chip * 2 + core
        self.kept = False

    @staticmethod
    def scratch(ranks):
        return [
            pltpu.SemaphoreType.DMA((ranks,)), pltpu.SemaphoreType.DMA((ranks,)), pltpu.SemaphoreType.DMA,
        ]

    def near(self, k):
        x = self.rank % 2
        y = self.rank // 2
        across = (y * 2 + 1 - x, (1 - y) * 2 + x)
        if k < 2:
            return remote(
                self.own, slab(self.slots, self.rank, self.rows), self.send.at[k], self.recv.at[k],
                self.me, across[k],
            )
        half = slab(self.slots, across[k - 2] * 2 + (k - 2), self.rows // 2)
        return remote(half, half, self.send.at[k], self.recv.at[k], self.me, across[3 - k])

    def direct(self, k):
        return remote(
            self.own, slab(self.slots, self.rank, self.rows), self.send.at[k], self.recv.at[k],
            self.me, lax.rem(self.rank + k, self.ranks),
        )

    def keep(self):
        return pltpu.make_async_copy(self.own, slab(self.slots, self.rank, self.rows), self.local)

    def step(self, k):
        if k == 0:
            if self.ranks == 4:
                self.near(0).start()
                self.near(1).start()
            else:
                for j in range(1, self.ranks):
                    self.direct(j).start()
            self.keep().start()
        elif self.ranks == 4:
            for j in (0, 1):
                self.near(j).wait_recv()
                self.near(2 + j).start()

    def near_rows(self):
        self.keep().wait()
        self.kept = True
        x, y = self.rank % 2, self.rank // 2
        return [self.rank, y * 2 + 1 - x, (1 - y) * 2 + x], [(1 - y) * 2 + 1 - x]

    def finish(self):
        if not self.kept:
            self.keep().wait()
        if self.ranks == 4:
            for j in (0, 1):
                self.near(j).wait_send()
                self.near(2 + j).wait()
        else:
            for j in range(1, self.ranks):
                self.direct(j).wait()


def add_rows(target, others, out=None):
    out = target if out is None else out
    rows = target.shape[0]
    some = 64 if rows % 64 == 0 else rows
    kind = out.dtype if len(others) == 1 else f32

    def add(at):
        total = target[at].astype(kind)
        for other in others:
            total = total + other[at].astype(kind)
        out[at] = total.astype(out.dtype)

    row_loop(rows, some, add)


class LineScatter:
    def __init__(self, parts, swap, flow, send, recv, chips):
        self.parts, self.swap, self.flow = parts, swap, flow
        self.send, self.recv, self.chips = send, recv, chips
        self.rows = parts.shape[0] // (2 * chips)
        self.chip, self.core, self.rank = place()
        self.me = self.chip * 2 + self.core
        self.partner = self.chip * 2 + 1 - self.core

    @staticmethod
    def scratch(chips, shape, dtype=bf16):
        block = (shape[0] // (2 * chips),) + tuple(shape[1:])
        return [
            pltpu.VMEM((chips,) + block, dtype), pltpu.VMEM((chips + 1,) + block, dtype),
            pltpu.SemaphoreType.DMA((3, chips)), pltpu.SemaphoreType.DMA((3, chips)),
        ]

    def order(self):
        n = self.chips
        return [c for k in range(n // 2) for c in (n - 1 - k, k)]

    def over(self, c):
        return remote(
            slab(self.parts, 2 * c + 1 - self.core, self.rows), self.swap.at[c], self.send.at[2, c],
            self.recv.at[2, c], self.partner, self.rank,
        )

    def along(self, way, c, first=False):
        if way == 0:
            here = there = c
        else:
            here, there = c, jnp.where(c == self.chip - 1, self.chips, c)
        src = self.swap.at[c] if first else self.flow.at[here]
        return remote(
            src, self.flow.at[there], self.send.at[way, c], self.recv.at[way, c],
            self.me + (2, -2)[way], self.rank,
        )

    def send_off(self, c):
        n, chip = self.chips, self.chip

        @pl.when((chip == 0) & (c > 0))
        def _():
            self.along(0, c, True).start()

        @pl.when((chip == n - 1) & (c < n - 1))
        def _():
            self.along(1, c, True).start()

    def send_rest(self):
        for c in self.order()[2:]:
            self.send_off(c)

    def step(self, k, hold=False):
        n, chip = self.chips, self.chip
        if k == 0:
            for c in self.order():
                self.over(c).start()
            return
        if k == 1:
            for i, c in enumerate(self.order()):
                self.over(c).wait()
                add_rows(self.swap.at[c], [slab(self.parts, 2 * c + self.core, self.rows)])
                if i < 2 or not hold:
                    self.send_off(c)
            return
        t = k - 1
        c = n - 1 - (t - chip)

        @pl.when((chip > 0) & (t >= chip) & (c > chip))
        def _():
            self.along(0, c).wait_recv()
            add_rows(self.flow.at[c], [self.swap.at[c]])
            self.along(0, c).start()

        d = t - (n - 1 - chip)

        @pl.when((chip < n - 1) & (d >= 0) & (d < chip))
        def _():
            self.along(1, d).wait_recv()
            add_rows(self.flow.at[d], [self.swap.at[d]])
            self.along(1, d).start()

    def finish(self, out):
        n, chip = self.chips, self.chip
        mine, up, down = self.swap.at[chip], self.flow.at[chip], self.flow.at[n]

        @pl.when(chip == 0)
        def _():
            self.along(1, chip).wait_recv()
            add_rows(mine, [down], out)

        @pl.when(chip == n - 1)
        def _():
            self.along(0, chip).wait_recv()
            add_rows(mine, [up], out)

        @pl.when((chip > 0) & (chip < n - 1))
        def _():
            self.along(0, chip).wait_recv()
            self.along(1, chip).wait_recv()
            add_rows(mine, [up, down], out)

        for c in range(n):
            @pl.when((chip < n - 1) & (c > chip))
            def _():
                self.along(0, c).wait_send()

            @pl.when((chip > 0) & (c < chip))
            def _():
                self.along(1, c).wait_send()


class DirectScatter:
    def __init__(self, parts, land, temp, send, recv, tsem, ranks):
        self.parts, self.land, self.temp = parts, land, temp
        self.send, self.recv, self.tsem, self.ranks = send, recv, tsem, ranks
        self.rows = parts.shape[0] // ranks
        chip, core, self.rank = place()
        self.me = chip * 2 + core

    @staticmethod
    def scratch(ranks):
        return [dma(ranks), dma(ranks), dma(2)]

    def copy(self, k):
        to = lax.rem(self.rank + k, self.ranks)
        return remote(
            slab(self.parts, to, self.rows), self.land.at[k], self.send.at[k], self.recv.at[k],
            self.me, to,
        )

    def step(self, k, g):
        if k == 0 and g == 1:
            for j in range(1, self.ranks):
                self.copy(j).start()

    def arrive(self):
        for j in range(1, self.ranks):
            self.copy(j).wait()

    def totals(self, some, body):
        @pl.loop(0, self.rows // some)
        def _(i):
            at = pl.ds(pl.multiple_of(i * some, some), some)
            total = None
            for j in range(self.ranks):
                src = slab(self.parts, self.rank * (self.rows // some) + i, some) if j == 0 else self.land.at[j, at]
                copy = pltpu.make_async_copy(src, self.temp.at[j % 2, pl.ds(0, some)], self.tsem.at[j % 2])
                copy.start()
                copy.wait()
                v = self.temp[j % 2, pl.ds(0, some)].astype(f32)
                total = v if total is None else total + v
            body(at, total)


class SmallScatter:
    def __init__(self, parts, swap, land, send, recv, chips):
        self.parts, self.swap, self.land, self.send, self.recv = parts, swap, land, send, recv
        self.chips, self.rows = chips, parts.shape[0] // (2 * chips)
        self.chip, self.core, self.rank = place()

    @staticmethod
    def scratch(chips, shape, dtype):
        block = pltpu.VMEM((chips, shape[0] // (2 * chips), shape[1]), dtype)
        return [
            block, block, pltpu.SemaphoreType.DMA((2, chips)), pltpu.SemaphoreType.DMA((2, chips)),
        ]

    def over(self, c):
        return remote(
            slab(self.parts, 2 * c + 1 - self.core, self.rows), self.swap.at[c], self.send.at[0, c],
            self.recv.at[0, c], self.chip * 2 + 1 - self.core, self.rank,
        )

    def straight(self, k):
        to = lax.rem(self.chip + k, self.chips)
        return remote(
            self.swap.at[to], self.land.at[self.chip], self.send.at[1, k], self.recv.at[1, k],
            2 * to + self.core, self.rank,
        )

    def step(self, k):
        if k == 0:
            for c in range(self.chips):
                self.over(c).start()
            return
        for c in range(self.chips):
            self.over(c).wait()
            add_rows(self.swap.at[c], [slab(self.parts, 2 * c + self.core, self.rows)])
        for j in range(1, self.chips):
            self.straight(j).start()

    def finish(self, out):
        for j in range(1, self.chips):
            self.straight(j).wait()
        total = self.swap[self.chip].astype(f32)
        for j in range(1, self.chips):
            total = total + self.land[lax.rem(self.chip + j, self.chips)].astype(f32)
        out[...] = total.astype(out.dtype)


class SmallGather:
    def __init__(self, own, slots, send, recv, chips):
        self.own, self.slots, self.send, self.recv = own, slots, send, recv
        self.chips, self.rows = chips, own.shape[0]
        self.chip, self.core, self.rank = place()
        self.me = self.chip * 2 + self.core

    @staticmethod
    def scratch(chips):
        return [pltpu.SemaphoreType.DMA((2, chips)), pltpu.SemaphoreType.DMA((2, chips))]

    def straight(self, k):
        slot = slab(self.slots, self.me, self.rows)
        return remote(
            self.own, slot, self.send.at[0, k], self.recv.at[0, k],
            2 * lax.rem(self.chip + k, self.chips) + self.core, self.rank,
        )

    def over(self, k):
        slot = slab(
            self.slots, 2 * lax.rem(self.chip + self.chips - k, self.chips) + self.core, self.rows
        )
        return remote(
            self.own if k == 0 else slot, slot, self.send.at[1, k], self.recv.at[1, k],
            self.chip * 2 + 1 - self.core, self.rank,
        )

    def step(self, k):
        if k == 0:
            for j in range(1, self.chips):
                self.straight(j).start()
            self.over(0).start()
            self.slots[pl.ds(pl.multiple_of(self.me * self.rows, self.rows), self.rows)] = self.own[...]
            return
        for j in range(1, self.chips):
            self.straight(j).wait_recv()
            self.over(j).start()

    def finish(self):
        for j in range(1, self.chips):
            self.straight(j).wait_send()
        for j in range(self.chips):
            self.over(j).wait()


class HalvesScatter:
    def __init__(self, parts, land, temp, send, recv, tsem):
        self.parts, self.land, self.temp, self.send, self.recv, self.tsem = parts, land, temp, send, recv, tsem
        chip, core, self.rank = place()
        self.me = chip * 2 + core
        self.rows = parts.shape[0] // 4
        self.half, self.wide = self.rows // 2, parts.shape[1] // 2
        x, y = self.rank % 2, self.rank // 2
        self.across = (y * 2 + 1 - x, (1 - y) * 2 + x)
        self.far = (1 - y) * 2 + 1 - x

    @staticmethod
    def scratch(shape):
        return [
            pltpu.VMEM((2, 6, shape[0] // 8, shape[1] // 2), bf16),
            *[pltpu.SemaphoreType.DMA((2, n)) for n in (6, 6, 2)],
        ]

    @staticmethod
    def temp(shape):
        return pltpu.VMEM((2, 2, shape[0] // 8, shape[1] // 2), bf16)

    def part(self, g, owner, way):
        return slab(self.parts.at[:, pl.ds(g * self.wide, self.wide)], owner * 2 + way, self.half)

    def copy(self, g, i):
        if i < 4:
            way = i // 2
            src = self.part(g, self.across[way] if i % 2 == 0 else self.far, way)
            to = self.across[way]
        else:
            way = i - 4
            src, to = self.land.at[g, 2 * way + 1], self.across[1 - way]
        return remote(
            src, self.land.at[g, i], self.send.at[g, i], self.recv.at[g, i], self.me, to
        )

    def fetch(self, g, owner, way):
        return pltpu.make_async_copy(
            self.part(g, owner, way), self.temp.at[g, way], self.tsem.at[g, way]
        )

    def step(self, k, g):
        if k == 0:
            for i in (1, 3, 0, 2):
                self.copy(g, i).start()
            return
        for way in (0, 1):
            self.fetch(g, self.across[1 - way], way).start()
        for way in (0, 1):
            self.copy(g, 2 * way + 1).wait_recv()
            self.fetch(g, self.across[1 - way], way).wait()
            add_rows(self.land.at[g, 2 * way + 1], [self.temp.at[g, way]])
            self.copy(g, 4 + way).start()
        for way in (0, 1):
            self.fetch(g, self.rank, way).start()

    def arrive(self):
        for g in (0, 1):
            for way in (0, 1):
                self.copy(g, 2 * way + 1).wait_send()
                self.copy(g, 2 * way).wait()
                self.copy(g, 4 + way).wait()
                self.fetch(g, self.rank, way).wait()

    def totals(self, some, body):
        for way in (0, 1):
            def add(i):
                at = pl.ds(pl.multiple_of(i * some, some), some)
                total = jnp.concatenate(
                    [
                        self.temp[g, way, at].astype(f32)
                        + self.land[g, 2 * way, at].astype(f32)
                        + self.land[g, 4 + way, at].astype(f32)
                        for g in (0, 1)
                    ],
                    axis=1,
                )
                body(pl.ds(pl.multiple_of(way * self.half + i * some, some), some), total)

            pl.loop(0, self.half // some)(add)


def row_loop(rows, some, body):
    @pl.loop(0, rows // some)
    def _(i):
        body(pl.ds(pl.multiple_of(i * some, some), some))


def params(number):
    return pltpu.CompilerParams(
        collective_id=number, has_side_effects=True, vmem_limit_bytes=VMEM_BYTES
    )


ANY = pl.BlockSpec(memory_space=pl.ANY)
ONCHIP = pl.BlockSpec(memory_space=pltpu.VMEM)


epsilon = 1e-05
CHUNK = 256


def shaped(shape, dtype):
    return jax.ShapeDtypeStruct(shape, dtype)


def dma(count=None):
    return pltpu.SemaphoreType.DMA if count is None else pltpu.SemaphoreType.DMA((count,))


def exact_mm(v, picks):
    high = v.astype(bf16)
    rest = v - high.astype(f32)
    middle = rest.astype(bf16)
    low = (rest - middle.astype(f32)).astype(bf16)
    return mm(high, picks) + mm(middle, picks) + mm(low, picks)


def prepare(
    rank, heads, seg_in, taps_in, bias_in, heads_in, gain_in, wo_in, bias_row, wo_out,
    seg_out, tapx_out, tapbc_out, par_out, skip_out, gain_out, spread_out,
):
    width, inner = tapx_out.shape[1], gain_in.shape[1]
    bias_row[0:1] = bias_in[...][None]
    wo_out[...] = jnp.transpose(wo_in[...].astype(f32)).astype(bf16)
    length = seg_in.shape[1]
    for s in range(seg_in.shape[0]):
        for r in range(0, length, LANES):
            row = jnp.broadcast_to(seg_in[s : s + 1, r : r + LANES], (LANES, LANES))
            at = s * length + r
            seg_out[at : at + LANES] = jnp.transpose(row.astype(f32)).astype(jnp.int32)
    own = pl.ds(pl.multiple_of(rank * width, LANES), width)
    tapx_out[...] = jnp.zeros_like(tapx_out)
    tapbc_out[...] = jnp.zeros_like(tapbc_out)
    tapx_out[0:4], tapx_out[4:5] = taps_in[:, own], bias_row[0:1, own]
    tapbc_out[0:4], tapbc_out[4:5] = taps_in[:, inner:], bias_row[0:1, inner:]
    gain_out[...] = jnp.broadcast_to(gain_in[:, own], gain_out.shape)
    row = lax.broadcasted_iota(jnp.int32, spread_out.shape, 0)
    col = lax.broadcasted_iota(jnp.int32, spread_out.shape, 1)
    half = LANES // 2
    folded = jnp.where(row >= half, row - half, row)
    start = folded * WIDTH
    spread_out[...] = ((col >= start) & (col < start + WIDTH)).astype(bf16)
    row = lax.broadcasted_iota(jnp.int32, (LANES, LANES), 0)
    col = lax.broadcasted_iota(jnp.int32, (LANES, LANES), 1)
    lane = jnp.where(col >= half, col - half, col)
    lines = [ref[...][None] for ref in heads_in]
    lines = jnp.concatenate(lines + [jnp.zeros((5, lines[0].shape[1]), f32)], axis=0)
    if lines.shape[1] < LANES:
        lines = jnp.concatenate([lines, jnp.zeros((8, LANES - lines.shape[1]), f32)], axis=1)
    picked = exact_mm(
        lines, ((row == rank * heads + lane) & (lane < heads)).astype(bf16)
    )
    lane = lax.broadcasted_iota(jnp.int32, (1, LANES), 1)
    there = jnp.where(lane >= half, lane - half, lane) < heads
    par_out[...] = jnp.zeros_like(par_out)
    par_out[0:1] = picked[0:1]
    par_out[1:2] = jnp.where(there, -jnp.exp(picked[1:2]), 0.0)
    skip = jnp.where(lane < half, picked[2:3], 0.0)
    skip_out[...] = exact_mm(jnp.broadcast_to(skip, (8, LANES)), spread_out[...])


def project_kernel(
    chips, ranks, heads, res_ref, gain_ref, ws_ref, seg_in, taps_in, bias_in, a_in, b_in, c_in, gated_in, wo_in,
    inner_in, step_in,
    x_ref, st_ref, bc_ref, seg_out, tapx_out, tapbc_out, par_out, skip_out, gain_out, spread_out,
    wo_out, wz_out, normed_out, wx_out, own, normed, wx, bias_row, wx_own, *sems
):
    step = step_in[...]
    gap = jnp.zeros((step.shape[0], LANES // 2 - heads), bf16)
    wx_own[:, : x_ref.shape[1]] = inner_in[:, 1, :]
    wx_own[:, x_ref.shape[1] :] = jnp.concatenate([step, gap, step, gap], axis=1)
    greet(chips, ranks)
    line = LineGather(wx_own, wx, *sems[:3], chips)
    tensor = TensorGather(own, normed, *sems[3:6], ranks)
    line.step(0)
    gain = gain_ref[...]

    def norm(at):
        v = res_ref[at].astype(f32)
        scaling = lax.rsqrt(jnp.mean(v * v, axis=1, keepdims=True) + epsilon)
        own[at] = (v * scaling * gain).astype(bf16)

    row_loop(own.shape[0], 32, norm)
    tensor.step(0)
    prepare(
        line.rank, heads, seg_in, taps_in, bias_in, (a_in, b_in, c_in), gated_in, wo_in, bias_row, wo_out,
        seg_out, tapx_out, tapbc_out, par_out, skip_out, gain_out, spread_out,
    )
    wz_out[...] = inner_in[:, 0, :]
    line.step(1)
    tensor.step(1)
    if chips > 2:
        line.step(2)
    tokens, width = x_ref.shape
    deep, some = 2 * line.rows, own.shape[0]

    def states(blocks):
        for r in blocks:
            at = pl.ds(pl.multiple_of(r * some, some), some)
            bc_ref[at] = mm(normed[at], ws_ref[...])

    def use(first, blocks, chip):
        ks = pl.ds(pl.multiple_of(chip * deep, deep), deep)
        for r in blocks:
            at = pl.ds(pl.multiple_of(r * some, some), some)
            left = normed[at, ks]
            x, st = mm(left, wx[ks, :width]), mm(left, wx[ks, width:])
            if first:
                x_ref[at], st_ref[at] = x, st
            else:
                x_ref[at] += x
                st_ref[at] += st

    every = list(range(ranks))
    early, late = tensor.near_rows() if ranks == 4 else ([], every)
    for k in (0, 1):
        line.arrive(k, functools.partial(use, k == 0, early))
    states(early)
    tensor.finish()
    keep_normed = pltpu.make_async_copy(normed, normed_out, sems[6])
    keep_normed.start()
    for k in (0, 1):
        line.each(k, functools.partial(use, k == 0, late))
    states(late)
    for k in range(2, chips):
        if k + 1 < chips:
            line.step(k + 1)
        line.arrive(k, functools.partial(use, False, every))
    keep_wx = pltpu.make_async_copy(wx, wx_out, sems[7])
    keep_wx.start()
    line.sent()
    keep_normed.wait()
    keep_wx.wait()


def project(
    number, chips, ranks, heads, residual, norm_gain, ws, segments, taps, bias, by_head, gated_gain,
    out_weight, inner_weight, step_weight,
):
    rows, model = residual.shape
    tokens, inner = rows * ranks, inner_weight.shape[2]
    width = inner + LANES
    return pl.pallas_call(
        functools.partial(project_kernel, chips, ranks, heads),
        in_specs=[ONCHIP] * 13,
        out_specs=[ONCHIP] * 12 + [ANY, ANY],
        out_shape=[
            shaped((tokens, inner), f32), shaped((tokens, LANES), f32),
            shaped((tokens, ws.shape[1]), f32),
            shaped((tokens, LANES), jnp.int32), shaped((8, inner), f32), shaped((8, ws.shape[1]), f32),
            shaped((8, LANES), f32), shaped((8, inner), f32), shaped((8, inner), f32),
            shaped((LANES, inner), bf16), shaped(out_weight.shape[::-1], bf16),
            shaped((inner_weight.shape[0], inner), bf16),
            shaped((tokens, model), bf16), shaped((model, width), bf16),
        ],
        scratch_shapes=[
            pltpu.VMEM((rows, model), bf16), pltpu.VMEM((tokens, model), bf16),
            pltpu.VMEM((model, width), bf16), pltpu.VMEM((8, taps.shape[1]), f32),
            pltpu.VMEM((step_weight.shape[0], width), bf16),
            *LineGather.scratch(chips), *TensorGather.scratch(ranks), dma(), dma(),
        ],
        compiler_params=params(number),
        name="project",
    )(residual, norm_gain, ws, segments, taps, bias, *by_head, gated_gain, out_weight, inner_weight, step_weight)


def scan_gather_kernel(blocks, total, chips, ranks, *refs):
    own, (wz_own, cot_own) = refs[:9], refs[9:11]
    outs, (wz_out, cot_out) = refs[11:15], refs[15:17]
    scratch, sems = refs[17:21], refs[21:]
    now = pl.program_id(0) * blocks + pl.program_id(1)
    line = LineGather(wz_own, wz_out, *sems[:3], chips)
    tensor = TensorGather(cot_own, cot_out, *sems[3:], ranks)

    @pl.when(now == 0)
    def _():
        greet(chips, ranks)
        line.step(0)
        tensor.step(0)

    @pl.when(now == total - 2)
    def _():
        line.step(1)

    scan_fwd_kernel(blocks, *own, *outs, *scratch)

    @pl.when(now == total - 1)
    def _():
        tensor.step(1)
        for k in range(2, chips):
            line.step(k)
        line.finish()
        tensor.finish()


def scan_forward_gather(
    number, chips, ranks, wz_own, cot_own, x, bc, st, seg, tapx, tapbc, par, spread, skip, nseq
):
    tokens, width = x.shape
    n = BLOCK
    blocks = tokens // nseq // n
    at = lambda s, i: (s * blocks + i, 0)
    whole = lambda s, i: (0, 0)
    states = LANES
    return pl.pallas_call(
        functools.partial(scan_gather_kernel, blocks, nseq * blocks, chips, ranks),
        grid=(nseq, blocks),
        in_specs=[
            pl.BlockSpec((n, width), at),
            pl.BlockSpec((n, 2 * states), at),
            pl.BlockSpec((n, LANES), at),
            pl.BlockSpec((n, LANES), at),
            pl.BlockSpec(tapx.shape, whole),
            pl.BlockSpec(tapbc.shape, whole),
            pl.BlockSpec(par.shape, whole),
            pl.BlockSpec(spread.shape, whole),
            pl.BlockSpec(skip.shape, whole),
            pl.BlockSpec(wz_own.shape, whole),
            pl.BlockSpec(cot_own.shape, whole),
        ],
        out_specs=[
            pl.BlockSpec((n, width), at), pl.BlockSpec((states, width), at),
            pl.BlockSpec((n, width), at), pl.BlockSpec((n, 2 * states), at), ANY, ANY,
        ],
        out_shape=[
            shaped((tokens, width), f32),
            shaped((tokens // n * states, width), bf16),
            shaped((tokens, width), f32),
            shaped((tokens, 2 * states), f32),
            shaped((wz_own.shape[0] * 2 * chips, width), bf16),
            shaped((tokens, cot_own.shape[1]), bf16),
        ],
        scratch_shapes=[
            pltpu.VMEM((states, width), f32),
            pltpu.VMEM((8, width), f32),
            pltpu.VMEM((8, 2 * states), f32),
            pltpu.VMEM((8, LANES), jnp.int32),
            *LineGather.scratch(chips), *TensorGather.scratch(ranks),
        ],
        compiler_params=params(number),
        name="scan_forward",
    )(x, bc, st, seg, tapx, tapbc, par, spread, skip, wz_own, cot_own)


def lane_sums(v):
    total = v[:, :LANES]
    for i in range(LANES, v.shape[1], LANES):
        total = total + v[:, i : i + LANES]
    return total


def row_sums(picks, v):
    high = v.astype(bf16)
    low = (v - high.astype(f32)).astype(bf16)
    return mm_nt(picks, high) + mm_nt(picks, low)


def gate_kernel(
    chips, ranks, gain_ref, wo_own, normed_in, wz_in, y_in, cot_in,
    gz_ref, gy_ref, ng_ref, ggain_ref, wo_out,
    wo, normed, wz, y, cot, z, gng, squares, dots, columns, land, send, recv, loads, *sems
):
    line = LineGather(wo_own, wo, *sems[:3], chips)
    tokens, width = y.shape
    inner = width * ranks
    rank = line.rank
    load = [
        pltpu.make_async_copy(src, dst, loads.at[i])
        for i, (src, dst) in enumerate(((normed_in, normed), (wz_in, wz), (y_in, y), (cot_in, cot)))
    ]
    greet(chips, ranks)
    line.step(0)
    for copy in load:
        copy.start()
    load[0].wait()
    load[1].wait()

    def gate(at):
        z[at] = mm(normed[at], wz[...])

    row_loop(tokens, CHUNK, gate)
    load[2].wait()

    def square(at):
        zz = z[at]
        gated = y[at] * (zz * sigmoid(zz))
        squares[at] = lane_sums(gated * gated)

    row_loop(tokens, 32, square)
    load[3].wait()
    deep = 2 * line.rows

    def use(first, chip):
        ks = pl.ds(pl.multiple_of(chip * deep, deep), deep)

        def rows(at):
            v = mm(cot[at, ks], wo[ks])
            if first:
                gng[at] = v
            else:
                gng[at] += v

        row_loop(tokens, CHUNK, rows)

    line.arrive(0, functools.partial(use, True))
    for k in range(1, chips):
        line.step(k)
        line.arrive(k, functools.partial(use, False))
    keep = pltpu.make_async_copy(wo, wo_out, loads.at[4])
    keep.start()
    gain = gain_ref[0:1]

    def sums(at):
        zz = z[at]
        dots[at] = lane_sums(gng[at] * gain * (y[at] * (zz * sigmoid(zz))))

    row_loop(tokens, 32, sums)
    half = lax.broadcasted_iota(jnp.int32, (8, LANES), 0) < 4
    one, other = half.astype(bf16), jnp.logical_not(half).astype(bf16)
    for r in range(0, tokens, CHUNK):
        at = slice(r, r + CHUNK)
        land[rank, :, at] = row_sums(one, squares[at]) + row_sums(other, dots[at])
    copies = [
        remote(
            land.at[rank], land.at[rank], send.at[k], recv.at[k], line.me, lax.rem(rank + k, ranks)
        )
        for k in range(1, ranks)
    ]
    for copy in copies:
        copy.start()
    line.sent()
    for copy in copies:
        copy.wait()
    for r in range(0, tokens, LANES):
        at = slice(r, r + LANES)
        total = land[0, :, at]
        for k in range(1, ranks):
            total = total + land[k, :, at]
        columns[at] = jnp.transpose(jnp.concatenate([total] * (LANES // 8), axis=0))
    ggain_ref[...] = jnp.zeros_like(ggain_ref)

    def grads(at):
        zz, yy, gg = z[at], y[at], gng[at]
        sig = sigmoid(zz)
        silu = zz * sig
        gated = yy * silu
        scale = lax.rsqrt(columns[at, 0:1] / inner + epsilon)
        ng_ref[at] = (gated * scale * gain).astype(bf16)
        weight = scale * scale * scale * columns[at, 4:5] / inner
        ggain_ref[...] += fold(gg * gated * scale)
        grad = scale * gain * gg - gated * weight
        gz_ref[at] = (grad * yy * (sig * (1.0 + zz * (1.0 - sig)))).astype(bf16)
        gy_ref[at] = grad * silu

    row_loop(tokens, 32, grads)
    keep.wait()


def gate(number, chips, ranks, gain, wo_own, normed, wz, y, cot):
    tokens, width = y.shape
    model = normed.shape[1]
    return pl.pallas_call(
        functools.partial(gate_kernel, chips, ranks),
        in_specs=[ONCHIP] + [ANY] * 5,
        out_specs=[ONCHIP] * 4 + [ANY],
        out_shape=[
            shaped((tokens, width), bf16), shaped((tokens, width), f32), shaped((tokens, width), bf16),
            shaped((8, width), f32), shaped((model, width), bf16),
        ],
        scratch_shapes=[
            pltpu.VMEM((model, width), bf16), pltpu.VMEM((tokens, model), bf16),
            pltpu.VMEM((model, width), bf16), pltpu.VMEM((tokens, width), f32),
            pltpu.VMEM((tokens, model), bf16), pltpu.VMEM((tokens, width), f32),
            pltpu.VMEM((tokens, width), f32), pltpu.VMEM((tokens, LANES), f32),
            pltpu.VMEM((tokens, LANES), f32), pltpu.VMEM((tokens, LANES), f32),
            pltpu.VMEM((ranks, 8, tokens), f32), dma(ranks), dma(ranks), dma(5),
            *LineGather.scratch(chips),
        ],
        compiler_params=params(number),
        name="gate",
    )(gain, wo_own, normed, wz, y, cot)


class Grads:
    def __init__(self, src, grad, parts, cbuf, csem):
        self.src, self.grad, self.parts, self.cbuf, self.csem = src, grad, parts, cbuf, csem
        self.count = src.shape[1] // CHUNK

    def load(self, j):
        slot = lax.rem(j, 2)
        columns = pl.ds(pl.multiple_of(j * CHUNK, CHUNK), CHUNK)
        return pltpu.make_async_copy(
            self.src.at[:, columns], self.cbuf.at[slot], self.csem.at[slot]
        )

    def begin(self):
        self.load(0).start()

    def run(self):
        @pl.loop(0, self.count)
        def _(j):
            @pl.when(j + 1 < self.count)
            def _():
                self.load(j + 1).start()

            self.load(j).wait()
            at = pl.ds(pl.multiple_of(j * CHUNK, CHUNK), CHUNK)
            self.parts[at] = mm_tn(self.cbuf[lax.rem(j, 2)], self.grad[...]).astype(bf16)


class Back:
    def __init__(self, terms, parts, stage, ssem):
        self.terms, self.parts, self.stage, self.ssem = terms, parts, stage, ssem
        self.count = parts.shape[1] // CHUNK

    def loads(self, j):
        slot = lax.rem(j, 2)
        return [
            pltpu.make_async_copy(slab(right, j, CHUNK), buffer.at[slot], sem.at[slot])
            for _, right, buffer, sem in self.terms
        ]

    def store(self, j):
        slot = lax.rem(j, 2)
        columns = pl.ds(pl.multiple_of(j * CHUNK, CHUNK), CHUNK)
        return pltpu.make_async_copy(
            self.stage.at[slot], self.parts.at[:, columns], self.ssem.at[slot]
        )

    def begin(self):
        for copy in self.loads(0):
            copy.start()

    def run(self, between=None):
        count = self.count

        @pl.loop(0, count)
        def _(j):
            slot = lax.rem(j, 2)

            @pl.when(j + 1 < count)
            def _():
                for copy in self.loads(j + 1):
                    copy.start()

            for copy in self.loads(j):
                copy.wait()

            @pl.when(j >= 2)
            def _():
                self.store(j - 2).wait()

            if between is not None:
                pl.when(j == count // 2 + 1)(between)

            for r in range(0, self.parts.shape[0], CHUNK):
                at = slice(r, r + CHUNK)
                total = jnp.zeros((CHUNK, CHUNK), f32)
                for left, _, buffer, _ in self.terms:
                    total = total + mm_nt(left[at], buffer[slot])
                self.stage[slot, at] = total.astype(bf16)
            self.store(j).start()

        for j in (count - 2, count - 1):
            self.store(j).wait()


def everyone(buffer, mine, count, send, recv, device):
    row = buffer.at[mine]
    return [
        remote(row, row, send.at[k], recv.at[k], *device(lax.rem(mine + k, count)))
        for k in range(1, count)
    ]


def added(buffer, count):
    total = buffer[0]
    for k in range(1, count):
        total = total + buffer[k]
    return total


def backward_kernel(blocks, total, chips, ranks, *refs):
    ins, refs = refs[:15], refs[15:]
    (ggain_ref, gain_ref), refs = refs[:2], refs[2:]
    (res_in, cot_own_in, ws_in, gz_in, ng_in, normed_in, cot_in, wo_in, wz_in, wx_in), refs = refs[:10], refs[10:]
    (sums_ref, norm_ref), refs = refs[:2], refs[2:]
    (z_sum, o_sum, x_sum, block_out, res_grad, state_out), refs = refs[:6], refs[6:]
    (tparts, pparts, pland, tland), refs = refs[:4], refs[4:]
    scratch, refs = refs[:11], refs[11:]
    (gxs, gbc_own, gtapx, gtapbc, gpar, gz, ng, cbuf, parts, back, wbuf, xbuf), refs = refs[:12], refs[12:]
    (gbc_slots, sbuf, wide_out, line_out, sparts, state_f, state_g), refs = refs[:7], refs[7:]
    (state_own, state_line, state_low, land_core, land_chip, land_rank), refs = refs[:6], refs[6:]
    (norm_rank, norm_dp, norm_acc), refs = refs[:3], refs[3:]
    (loads, csem, bsem, wsem, xsem, ysem, osem, fsem), refs = refs[:8], refs[8:]
    (psem, qsem, rsem, nsem, msem), refs = refs[:5], refs[5:]
    half_parts = parts.at[:, pl.ds(0, gz.shape[1])]
    z_job = LineScatter(half_parts, *refs[:4], chips)
    o_job = LineScatter(half_parts, *refs[4:8], chips)
    x_job = LineScatter(parts, *refs[8:12], chips)
    s_job = SmallScatter(sparts, *refs[12:16], chips)
    refs = refs[16:]
    around = TensorGather(gbc_own, gbc_slots, *refs[:3], ranks)
    s_line = SmallGather(state_own, state_line, *refs[3:5], chips)
    state_all = gbc_slots.at[pl.ds(gz.shape[0], normed_in.shape[1])]
    s_rank = TensorGather(state_low, state_all, *refs[5:8], ranks)
    temp, refs = refs[8], refs[9:]
    if ranks == 4:
        first = HalvesScatter(pparts, refs[0], temp, *refs[1:4])
        second = HalvesScatter(tparts, refs[4], temp, *refs[5:8])
    else:
        first = DirectScatter(pparts, pland, temp, *refs[:3], ranks)
        second = DirectScatter(tparts, tland, temp, *refs[3:6], ranks)
    now = pl.program_id(0) * blocks + pl.program_id(1)
    tokens, width = gz.shape
    model = normed_in.shape[1]
    rank, me, devices = first.rank, first.me, 2 * chips
    chip, core = z_job.chip, z_job.core
    over_dp = lambda d: (d, rank)
    over_rank = lambda r: (me, r)
    by_core = everyone(land_core, core, 2, psem.at[0], psem.at[1], lambda c: (chip * 2 + c, rank))
    by_chip = everyone(land_chip, chip, chips, qsem.at[0], qsem.at[1], lambda c: (c * 2 + core, rank))
    by_rank = everyone(land_rank, rank, ranks, rsem.at[0], rsem.at[1], over_rank)
    norm_by_rank = everyone(norm_rank, rank, ranks, nsem.at[0], nsem.at[1], over_rank)
    norm_by_dp = everyone(norm_dp, me, devices, msem.at[0], msem.at[1], over_dp)

    def begin(copies):
        for copy in copies:
            copy.start()

    def end(copies):
        for copy in copies:
            copy.wait()
    fetch = [
        pltpu.make_async_copy(src, dst, loads.at[i])
        for i, (src, dst) in enumerate(((gz_in, gz), (ng_in, ng)))
    ]
    pieces = model // width
    own_rows = first.rows

    def piece(ref, p, at):
        return ref[pl.ds(pl.multiple_of(at.start + p * own_rows, 16), at.size)]

    def pieced(ref, at):
        return jnp.concatenate([piece(ref, p, at) for p in range(pieces)], axis=1).astype(f32)

    def own_copies(src, ref, sems):
        return [
            pltpu.make_async_copy(
                src.at[:, pl.ds(p * width, width)], ref.at[pl.ds(p * own_rows, own_rows)], sems.at[p]
            )
            for p in range(pieces)
        ]

    own_res = own_copies(res_in, gz, fsem.at[0])
    own_cot = own_copies(cot_own_in, ng, fsem.at[1])
    half_out = line_out.at[:, pl.ds(0, width)]
    keep_z = pltpu.make_async_copy(half_out, z_sum, osem.at[0])
    keep_o = pltpu.make_async_copy(half_out, o_sum, osem.at[0])
    keep_x = pltpu.make_async_copy(line_out, x_sum, osem.at[0])
    keep_block = pltpu.make_async_copy(wide_out, block_out, osem.at[2])
    keep_grad = pltpu.make_async_copy(wide_out, res_grad, osem.at[2])

    z_part = Grads(normed_in, gz, half_parts, cbuf, csem)
    o_part = Grads(cot_in, ng, half_parts, cbuf, csem)
    x_part = Grads(normed_in, gxs, parts, cbuf, csem)
    out_part = Back([(ng, wo_in, wbuf, wsem)], pparts, back, bsem)
    in_part = Back(
        [(gz, wz_in, wbuf, wsem), (gxs, wx_in, xbuf, xsem), (gbc_own, ws_in, sbuf, ysem)],
        tparts, back, bsem,
    )

    @pl.when(now == 0)
    def _():
        z_part.begin()
        for copy in fetch:
            copy.start()
        out_part.begin()
        greet_all(chips, ranks)
        fetch[0].wait()
        z_part.run()
        z_job.step(0)
        fetch[1].wait()
        o_part.begin()
        out_part.run(lambda: z_job.step(1))
        first.step(0, 0)
        first.step(0, 1)

    early = [k for k in range(2, chips) if 2 * k - 2 < total - 1]

    @pl.when(now == 1)
    def _():
        o_part.run()
        o_job.step(0)

    for k in early:
        @pl.when(now == 2 * k - 2)
        def _():
            z_job.step(k)

    @pl.when(now == 3)
    def _():
        o_job.step(1)

    @pl.when(now == 5)
    def _():
        first.step(1, 0)
        first.step(1, 1)

    @pl.when(now == total - 1)
    def _():
        x_part.begin()
        in_part.begin()

    row = pl.multiple_of(
        (pl.program_id(0) * blocks + blocks - 1 - pl.program_id(1)) * BLOCK, BLOCK
    )
    here = pl.ds(row, BLOCK)
    outs = (
        gxs.at[here, pl.ds(0, width)], gbc_own.at[here], gxs.at[here, pl.ds(width, LANES)],
        gtapx, gtapbc, gpar,
    )
    scan_bwd_kernel(blocks, *ins, *outs, *scratch)

    @pl.when(now == total - 1)
    def _():
        around.step(0)
        begin(own_cot)
        pack = land_core.at[core]
        pack[...] = jnp.zeros(land_core.shape[1:], f32)
        for k in range(5):
            rows = slice(8 * k, 8 * k + 8)
            pack[k : k + 1, :width] = jnp.sum(gtapx[rows], axis=0, keepdims=True)
            pack[k : k + 1, width:] = jnp.sum(gtapbc[rows], axis=0, keepdims=True)
        pack[5:6, :width] = jnp.sum(ggain_ref[...], axis=0, keepdims=True)
        for k in range(3):
            pack[6:7, k * LANES : (k + 1) * LANES] = jnp.sum(
                gpar[8 * k : 8 * k + 8], axis=0, keepdims=True
            )
        begin(by_core)
        x_part.run()
        x_job.step(0)
        end(by_core)
        land_chip[chip] = added(land_core, 2)
        begin(by_chip)
        depth = sparts.shape[0]

        def own_columns(i):
            columns = pl.ds(pl.multiple_of(rank * depth + i * CHUNK, CHUNK), CHUNK)
            return pltpu.make_async_copy(normed_in.at[:, columns], cbuf.at[i], csem.at[i])

        for i in range(depth // CHUNK):
            own_columns(i).start()
        for k in range(2, chips):
            if k not in early:
                z_job.step(k)
        if chips > 2:
            o_job.step(2)
        around.step(1)

        def between():
            second.step(0, 0)
            around.finish()

            def add(at):
                total = gbc_slots[at].astype(f32)
                for r in range(1, ranks):
                    there = pl.ds(pl.multiple_of(at.start + r * tokens, 128), at.size)
                    total = total + gbc_slots[there].astype(f32)
                gbc_slots[at] = total.astype(bf16)

            row_loop(tokens, 128, add)
            for i in range(depth // CHUNK):
                own_columns(i).wait()
                sparts[i * CHUNK : (i + 1) * CHUNK] = mm_tn(cbuf[i], gbc_slots[:tokens]).astype(
                    sparts.dtype
                )
            s_job.step(0)
            for k in range(3, chips):
                o_job.step(k)
            s_job.step(1)
            x_job.step(1, True)

        in_part.run(between)
        second.step(0, 1)
        begin(own_res)
        s_job.finish(state_own)
        s_line.step(0)
        x_job.send_rest()
        z_job.finish(half_out)
        keep_z.start()
        first.arrive()
        end(own_res)

        def plus(at, total):
            wide_out[at] = pieced(gz, at) + total

        first.totals(32, plus)
        keep_block.start()
        second.step(1, 0)
        end(by_chip)
        land_rank[rank] = added(land_chip, chips)
        begin(by_rank)
        keep_z.wait()
        o_job.finish(half_out)
        keep_o.start()
        s_line.step(1)
        s_line.finish()

        def lower(at):
            state_low[at] = state_line[at].astype(bf16)

        row_loop(depth, 64, lower)
        end(by_rank)
        s_rank.step(0)
        shared = land_rank[0, :, width:]
        for r in range(1, ranks):
            shared = shared + land_rank[r, :, width:]
        for r in range(ranks):
            sums_ref[:, r * width : (r + 1) * width] = land_rank[r, :, :width]
        sums_ref[:, ranks * width :] = shared
        if chips > 2:
            x_job.step(2)
        second.step(1, 1)
        s_rank.step(1)
        for k in range(3, chips):
            x_job.step(k)
        keep_block.wait()
        end(own_cot)
        second.arrive()
        norm_acc[...] = jnp.zeros_like(norm_acc)
        gain = gain_ref[...]

        def last(at, grad):
            v = pieced(gz, at)
            scaling = lax.rsqrt(jnp.mean(v * v, axis=1, keepdims=True) + epsilon)
            norm_acc[...] += fold(grad * v * scaling)
            grad = grad * gain
            along = jnp.sum(grad * v, axis=1, keepdims=True)
            weight = scaling * scaling * scaling * along / model
            wide_out[at] = pieced(ng, at) + scaling * grad - v * weight

        second.totals(32, last)
        keep_grad.start()
        line = jnp.sum(norm_acc[...], axis=0, keepdims=True)
        eighth = model // 8
        for i in range(8):
            norm_rank[rank, i : i + 1, :] = line[:, i * eighth : (i + 1) * eighth]
        begin(norm_by_rank)
        s_rank.finish()
        buffers = (state_f, state_g)
        stored = []
        some = depth // 2
        for r in range(2 * ranks):
            if r >= 2:
                stored[r - 2].wait()

            def state(at):
                low = pl.ds(pl.multiple_of(at.start + r * some, 64), at.size)
                buffers[r % 2][at] = state_all[low].astype(f32)

            row_loop(some, 64, state)
            copy = pltpu.make_async_copy(
                buffers[r % 2], state_out.at[pl.ds(r * some, some)], osem.at[1 + r % 2 * 2]
            )
            copy.start()
            stored.append(copy)
        end(norm_by_rank)
        norm_dp[me] = added(norm_rank, ranks)
        begin(norm_by_dp)
        keep_o.wait()
        x_job.finish(line_out)
        keep_x.start()
        end(stored[-2:])
        end(norm_by_dp)
        norm_ref[...] = added(norm_dp, devices)
        keep_x.wait()
        keep_grad.wait()


def backward(
    number, chips, ranks, ggain, norm_gain, residual, cot_own, ws, gz, ng, normed, cot, wo, wz, wx,
    x, conv, bc, convbc, st, seg, gy, y, h, tapx, tapbc, par, spread, skip, nseq,
):
    tokens, width = x.shape
    rows, model = residual.shape
    n = BLOCK
    blocks = tokens // nseq // n
    at = lambda s, i: (s * blocks + blocks - 1 - i, 0)
    tail = lambda s, i: (jnp.maximum((s * blocks + blocks - 1 - i) * (n // 8) - 1, 0), 0)
    whole = lambda s, i: (0, 0)
    states = LANES
    full = lambda v: pl.BlockSpec(v.shape, whole)
    once = lambda shape: pl.BlockSpec(shape, whole)
    devices = 2 * chips
    own, depth, wide = model // devices, model // ranks, width + 2 * states
    kind = bf16 if depth // devices % 16 == 0 else f32
    return pl.pallas_call(
        functools.partial(backward_kernel, blocks, nseq * blocks, chips, ranks),
        grid=(nseq, blocks),
        in_specs=[
            pl.BlockSpec((n, width), at),
            pl.BlockSpec((n, width), at),
            pl.BlockSpec((n, 2 * states), at),
            pl.BlockSpec((n, 2 * states), at),
            pl.BlockSpec((n, LANES), at),
            pl.BlockSpec((n, LANES), at),
            pl.BlockSpec((8, LANES), tail),
            pl.BlockSpec((n, width), at),
            pl.BlockSpec((n, width), at),
            pl.BlockSpec((states, width), at),
            full(tapx), full(tapbc), full(par), full(spread), full(skip), full(ggain), full(norm_gain),
        ]
        + [ANY] * 10,
        out_specs=[
            once((8, width * ranks + 2 * states)), once((8, model // 8)),
        ]
        + [ANY] * 10,
        out_shape=[
            shaped((8, width * ranks + 2 * states), f32), shaped((8, model // 8), f32),
            shaped((own, width), f32), shaped((own, width), f32), shaped((own, width + LANES), f32),
            shaped((rows, model), f32), shaped((rows, model), f32), shaped((model, 2 * states), f32),
            shaped((tokens, model), bf16), shaped((tokens, model), bf16),
            *[shaped((ranks, rows, model) if ranks != 4 else (8, LANES), bf16)] * 2,
        ],
        scratch_shapes=[
            *scan_bwd_scratch(width, states),
            pltpu.VMEM((tokens, width + LANES), bf16),
            pltpu.VMEM((tokens, 2 * states), bf16),
            pltpu.VMEM((40, width), f32),
            pltpu.VMEM((40, 2 * states), f32),
            pltpu.VMEM((24, LANES), f32),
            pltpu.VMEM((tokens, width), bf16),
            pltpu.VMEM((tokens, width), bf16),
            pltpu.VMEM((2, tokens, CHUNK), bf16),
            pltpu.VMEM((model, width + LANES), bf16),
            pltpu.VMEM((2, tokens, CHUNK), bf16),
            pltpu.VMEM((2, CHUNK, width), bf16),
            pltpu.VMEM((2, CHUNK, width + LANES), bf16),
            pltpu.VMEM((ranks * tokens, 2 * states), bf16),
            pltpu.VMEM((2, CHUNK, 2 * states), bf16),
            pltpu.VMEM((rows, model), f32),
            pltpu.VMEM((own, width + LANES), f32),
            pltpu.VMEM((depth, 2 * states), kind),
            pltpu.VMEM((depth // 2, 2 * states), f32),
            pltpu.VMEM((depth // 2, 2 * states), f32),
            pltpu.VMEM((depth // devices, 2 * states), kind),
            pltpu.VMEM((depth, 2 * states), kind),
            pltpu.VMEM((depth, 2 * states), bf16),
            pltpu.VMEM((2, 8, wide), f32),
            pltpu.VMEM((chips, 8, wide), f32),
            pltpu.VMEM((ranks, 8, wide), f32),
            pltpu.VMEM((ranks, 8, model // 8), f32),
            pltpu.VMEM((devices, 8, model // 8), f32),
            pltpu.VMEM((8, model), f32),
            dma(2), *[dma(2)] * 5, dma(4), pltpu.SemaphoreType.DMA((2, model // width)),
            *[pltpu.SemaphoreType.DMA((2, n)) for n in (2, chips, ranks, ranks, devices)],
            *LineScatter.scratch(chips, (model, width)),
            *LineScatter.scratch(chips, (model, width)),
            *LineScatter.scratch(chips, (model, width + LANES)),
            *SmallScatter.scratch(chips, (depth, 2 * states), kind),
            *TensorGather.scratch(ranks), *SmallGather.scratch(chips), *TensorGather.scratch(ranks),
            HalvesScatter.temp((tokens, model)) if ranks == 4 else pltpu.VMEM((2, rows // 2, model), bf16),
            *(HalvesScatter.scratch((tokens, model)) if ranks == 4 else DirectScatter.scratch(ranks)) * 2,
        ],
        compiler_params=params(number),
        name="backward",
    )(
        x, conv, bc, convbc, st, seg, seg, gy, y, h, tapx, tapbc, par, spread, skip, ggain, norm_gain,
        residual, cot_own, ws, gz, ng, normed, cot, wo, wz, wx,
    )


def emit_kernel(
    ranks, heads, sums_ref, norm_ref, z_ref, x_ref, o_ref, block_in, res_in, state_in,
    inner_ref, step_ref, out_ref, taps_ref, bias_ref, gated_ref, norm_out, a_ref, b_ref, c_ref,
    block_out, res_out, state_out, block, res, state, sems
):
    moves = [
        (
            pltpu.make_async_copy(src, held, sems.at[0, i]),
            pltpu.make_async_copy(held, dst, sems.at[1, i]),
        )
        for i, (src, held, dst) in enumerate(
            ((block_in, block, block_out), (res_in, res, res_out), (state_in, state, state_out))
        )
    ]
    for come, _ in moves:
        come.start()
    width, inner = z_ref.shape[1], gated_ref.shape[0]
    row = lax.broadcasted_iota(jnp.int32, (LANES, LANES), 0)
    col = lax.broadcasted_iota(jnp.int32, (LANES, LANES), 1)
    total = jnp.zeros((8, LANES), f32)
    for r in range(ranks):
        line = [sums_ref[6:7, r * width + k * LANES : r * width + (k + 1) * LANES] for k in range(3)]
        picks = ((col == r * heads + row) & (row < heads)).astype(bf16)
        total = total + exact_mm(
            jnp.concatenate(line + [jnp.zeros((5, LANES), f32)], axis=0), picks
        )
    for k, ref in enumerate((a_ref, b_ref, c_ref)):
        ref[...] = total[k, : ranks * heads]
    taps_ref[...] = sums_ref[0:4]
    bias_ref[...] = sums_ref[4]
    gated_ref[...] = sums_ref[5, :inner]
    eighth = norm_ref.shape[1]
    for i in range(8):
        norm_out[i * eighth : (i + 1) * eighth] = norm_ref[i]
    step_ref[...] = x_ref[:, width : width + heads]
    for come, go in moves:
        come.wait()
        go.start()
    inner_ref[:, 0, :] = z_ref[...]
    inner_ref[:, 1, :] = x_ref[:, :width]
    out_ref[...] = jnp.transpose(o_ref[...])
    for _, go in moves:
        go.wait()


def emit(ranks, heads, sums, norm, z, x, o, block, res, state):
    own, width = z.shape
    inner = width * ranks
    vector = lambda n: shaped((n,), f32)
    return pl.pallas_call(
        functools.partial(emit_kernel, ranks, heads),
        in_specs=[ONCHIP] * 5 + [ANY] * 3,
        out_specs=[ONCHIP] * 10 + [ANY] * 3,
        out_shape=[
            shaped((own, 2, width), f32), shaped((own, heads), f32), shaped((width, own), f32),
            shaped((4, sums.shape[1]), f32), vector(sums.shape[1]), vector(inner),
            vector(norm.size), *[vector(ranks * heads)] * 3,
            shaped(block.shape, f32), shaped(res.shape, f32), shaped(state.shape, f32),
        ],
        scratch_shapes=[
            pltpu.VMEM(block.shape, f32), pltpu.VMEM(res.shape, f32), pltpu.VMEM(state.shape, f32),
            pltpu.SemaphoreType.DMA((2, 3)),
        ],
        compiler_params=pltpu.CompilerParams(vmem_limit_bytes=VMEM_BYTES),
        name="emit",
    )(sums, norm, z, x, o, block, res, state)


def per_device(
    residual, segment_ids, norm_gain, inner_weight, state_weight, step_weight, conv_weight,
    conv_bias, step_bias, decay_log, skip_gain, gated_gain, out_weight, cotangent,
):
    chips, ranks = lax.axis_size("dp") // 2, lax.axis_size("tensor")
    width = inner_weight.shape[2]
    heads = step_weight.shape[1]
    inner_width = gated_gain.shape[0]
    nseq = segment_ids.shape[0]
    x, st, bc, seg, tapx, tapbc, par, skip, gain, spread, wo_own, wz_own, normed, wx = project(
        1, chips, ranks, heads, residual, norm_gain[None], state_weight, segment_ids,
        conv_weight, conv_bias, (step_bias, decay_log, skip_gain), gated_gain[None], out_weight, inner_weight, step_weight,
    )
    y, h, conv, convbc, wz, cot = scan_forward_gather(
        2, chips, ranks, wz_own, cotangent,
        x, bc, st, seg, tapx, tapbc, par, spread, skip, nseq,
    )
    gz, gy, ng, ggain, wo = gate(3, chips, ranks, gain, wo_own, normed, wz, y, cot)
    sums, norm_grad, z_grad, out_grad, x_grad, block_out, residual_grad, state_grad, *_ = backward(
        4, chips, ranks, ggain, norm_gain[None], residual, cotangent, state_weight,
        gz, ng, normed, cot, wo, wz, wx,
        x, conv, bc, convbc, st, seg, gy, y, h, tapx, tapbc, par, spread, skip, nseq,
    )
    (
        inner_grad, step_grad, out_grad, tap_grad, bias_grad, gated_grad, norm_grad,
        step_bias_grad, decay_grad, skip_grad, block_out, residual_grad, state_grad,
    ) = emit(
        ranks, heads, sums, norm_grad, z_grad, x_grad, out_grad, block_out, residual_grad, state_grad
    )
    return (
        block_out, residual_grad, norm_grad, inner_grad, state_grad, step_grad, tap_grad, bias_grad,
        step_bias_grad, decay_grad, skip_grad, gated_grad, out_grad,
    )


def solution(mesh):
    rows, both = P("dp", "tensor"), P(("dp", "tensor"), None)
    inner, out = P("dp", None, "tensor"), P("tensor", "dp")
    return jax.shard_map(
        per_device,
        mesh=mesh,
        in_specs=(
            both, P("dp", None), P(), inner, P(), rows, P(), P(), P(), P(), P(), P(), out, both,
        ),
        out_specs=(both, both, P(), inner, P(), rows, P(), P(), P(), P(), P(), P(), out),
        check_vma=False,
    )
```
